32 devices in a mesh: dp: 4 (over x, core), tensor: 8 (over z, y).
Axes of the slice: x: 2, y: 2, z: 4, core: 2. Of those that a mesh axis runs over, the one named last changes fastest.
Arguments:
- layer_in: bfloat16 [8192, 2048], P(('dp', 'tensor')), may hold values from -6 to 6
- cotangent: bfloat16 [8192, 2048], P(('dp', 'tensor')), may hold values from -6 to 6
- lengths: int32 [4], P('dp'), may hold values from 1793 to 2048, as said below
- prefix: int32 [4], P('dp'), may hold values from 1 to 1024, as said below
- pad_mask: int32 [8192], P(('dp', 'tensor')), may hold values 0 or 1
- clusters: int32 [4], replicated, may hold values from 0 to 1
- qkv_w: bfloat16 [2048, 3, 2048], P(None, None, 'tensor'), may hold values from -0.125 to 0.125
- out_w: bfloat16 [2048, 2048], P('tensor'), may hold values from -1.5 to 1.5
- gate_up_w: bfloat16 [2048, 2, 5464], P(None, None, 'tensor'), may hold values from -0.125 to 0.125
- down_w: bfloat16 [5464, 2048], P('tensor'), may hold values from -0.078125 to 0.078125
- ln_params: float32 [4, 2048], replicated
- qkv_row: float32 [2048], replicated, may hold values from 204.8 to 819.2
- qkv_col: float32 [3, 2048], P(None, 'tensor'), may hold values from 51.2 to 3276.8
- out_row: float32 [2048], P('tensor'), may hold values from 1.4336 to 91.7504
- out_col: float32 [2048], replicated, may hold values from 5.7344 to 22.9376
- gu_row: float32 [2048], replicated, may hold values from 81.92 to 327.68
- gu_col: float32 [2, 5464], P(None, 'tensor'), may hold values from 20.48 to 1310.72
- down_row: float32 [5464], P('tensor'), may hold values from 22.528 to 1441.792
- down_col: float32 [2048], replicated, may hold values from 90.112 to 368.64
- ln_second: float32 [4, 2048], replicated, may hold values from 409.6 to 1638.4
Outputs:
- layer_out: bfloat16 [8192, 2048], P(('dp', 'tensor'))
- input_grad: bfloat16 [8192, 2048], P(('dp', 'tensor'))
- qkv_grad: float32 [2048, 3, 2048], P(None, None, 'tensor')
- qkv_new: float32 [2048, 3, 2048], P(None, None, 'tensor')
- qkv_row_new: float32 [2048], replicated
- qkv_col_new: float32 [3, 2048], P(None, 'tensor')
- out_grad: float32 [2048, 2048], P('tensor')
- out_new: float32 [2048, 2048], P('tensor')
- out_row_new: float32 [2048], P('tensor')
- out_col_new: float32 [2048], replicated
- gu_grad: float32 [2048, 2, 5464], P(None, None, 'tensor')
- gu_new: float32 [2048, 2, 5464], P(None, None, 'tensor')
- gu_row_new: float32 [2048], replicated
- gu_col_new: float32 [2, 5464], P(None, 'tensor')
- down_grad: float32 [5464, 2048], P('tensor')
- down_new: float32 [5464, 2048], P('tensor')
- down_row_new: float32 [5464], P('tensor')
- down_col_new: float32 [2048], replicated
- ln_grad: float32 [4, 2048], replicated
- ln_second_new: float32 [4, 2048], replicated
- ln_new: float32 [4, 2048], replicated
The draws below stay inside these ranges and needn't reach their ends.
Inputs may be any that keep to these rules, and one draw needn't show every extreme that they name: `lengths`: a sequence's tokens take its first positions; at least one sequence has all 2048. `prefix`: at most half of its sequence's length.
All inputs are finite; a program needn't handle non-finite values. No bound on the sum of `pad_mask` on one device may be relied on, other than what follows from the above.
Results may differ from the reference program's by a relative error of at most 0.014.
Values may be sent and summed in bfloat16 or wider, within the bound.
A program may use at most 320 MiB of HBM per device.

```python
import math
from functools import partial
import jax
import jax.numpy as jnp
from jax import lax

D = 2048
H = 16
HD = 128
FF = 5461
SLOT = 2048
STEP = 10
SEQUENCES = 4
TOKENS = 8192
ROWS_DEV = 256
HHD = 2048
FFP = 5464
NCLUST = 2
N_DP = 4


def length_draw(key):
    chosen = jax.random.randint(jax.random.fold_in(key, 11), (), 0, SEQUENCES)
    shortfall = jax.random.randint(jax.random.fold_in(key, 12), (SEQUENCES,), 0, ROWS_DEV)
    seq_index = jnp.arange(SEQUENCES, dtype=jnp.int32)
    shortfall = jnp.where(seq_index == chosen, 0, shortfall)
    shortfall = jnp.where(seq_index == (chosen + 1) % SEQUENCES, ROWS_DEV - 1, shortfall)
    return ((SLOT - shortfall).astype(jnp.int32), chosen)


def draw_lengths(key, part):
    seq_lengths, chosen = length_draw(key)
    return seq_lengths


def draw_prefix(key, part):
    seq_lengths, chosen = length_draw(key)
    key = jax.random.fold_in(key, 2)
    start_len = 1 + jax.random.randint(key, (SEQUENCES,), 0, seq_lengths // 2)
    seq_index = jnp.arange(SEQUENCES, dtype=jnp.int32)
    start_len = jnp.where(seq_index == chosen, SLOT // 2, start_len)
    start_len = jnp.where(seq_index == (chosen + 2) % SEQUENCES, 1, start_len)
    return start_len.astype(jnp.int32)


def draw_ln_params(key, part):
    key = jax.random.fold_in(key, 3)
    gain_key, shift_key = jax.random.split(key)
    row_index = jnp.arange(4, dtype=jnp.int32)[:, None]
    gains = jax.random.uniform(gain_key, (4, D), jnp.float32, 0.7, 1.3)
    shifts = 0.2 * jax.random.normal(shift_key, (4, D), jnp.float32)
    return jnp.where(row_index % 2 == 0, gains, shifts).astype(jnp.float32)


def falling_stat(key, shape, base, top):
    width = shape[-1]
    place = jnp.arange(width, dtype=jnp.float32) / float(max(width - 1, 1))
    factor = top * jnp.exp(place * jnp.log(0.5 / top))
    spread = jnp.exp(jax.random.uniform(key, shape, jnp.float32, -0.693, 0.693))
    return (base * factor * spread).astype(jnp.float32)


def draw_qkv_col(key, part):
    key = jax.random.fold_in(key, 21)
    return falling_stat(key, (3, HHD), 0.025 * TOKENS, 4.0)


def draw_gu_col(key, part):
    key = jax.random.fold_in(key, 22)
    return falling_stat(key, (2, FFP), 0.01 * TOKENS, 4.0)


def draw_out_row(key, part):
    key = jax.random.fold_in(key, 23)
    return falling_stat(key, (HHD,), 0.0007 * TOKENS, 4.0)


def draw_down_row(key, part):
    key = jax.random.fold_in(key, 24)
    return falling_stat(key, (FFP,), 0.011 * TOKENS, 4.0)


def with_ends(drawn, own_key, low, high):
    shape = drawn.shape
    spot = [jax.random.randint(jax.random.fold_in(own_key, axis), (), 0, shape[axis]) for axis in range(len(shape))]
    drawn = drawn.at[tuple(spot)].set(low)
    longest = shape.index(max(shape))
    spot[longest] = (spot[longest] + 1) % shape[longest]
    return drawn.at[tuple(spot)].set(high)


def block_levels(own_key, shape, shards, least, high):
    level = 1.0
    for dim, blocks in shards:
        draws = jax.random.uniform(jax.random.fold_in(jax.random.fold_in(own_key, 6), dim), (blocks,), jnp.float32, least / len(shards), high / len(shards))
        level = level * jnp.repeat(jnp.exp(draws), shape[dim] // blocks).reshape((-1,) + (1,) * (len(shape) - 1 - dim))
    return level


def bell_draw(stream_key, dims, scale, reach, pieces=(), kind=jnp.bfloat16):
    array = jax.random.normal(stream_key, dims, jnp.float32) * scale
    if len(pieces) > 0:
        array = block_levels(stream_key, dims, pieces, -0.22, 0.18) * array
    return jnp.clip(array, min=-reach, max=reach).astype(kind)


def setup_inputs(seed: int = 0) -> dict:
    streams_of = jax.random.split(jax.random.key(seed), 21)
    return {
        "layer_in": bell_draw(streams_of[0], (TOKENS, D), 1.0, 6.0, ((0, 32),)),
        "cotangent": bell_draw(streams_of[1], (TOKENS, D), 1.0, 6.0, ((0, 32),)),
        "lengths": draw_lengths(jax.random.fold_in(streams_of[20], 71), 0),
        "prefix": draw_prefix(jax.random.fold_in(streams_of[20], 71), 0),
        "pad_mask": with_ends((jax.random.randint(streams_of[4], (TOKENS,), 0, 10) < 9).astype(jnp.int32), jax.random.fold_in(streams_of[4], 1), 0, 1),
        "clusters": with_ends(jax.random.randint(streams_of[5], (SEQUENCES,), 0, NCLUST), jax.random.fold_in(streams_of[5], 1), 0, NCLUST - 1).astype(jnp.int32),
        "qkv_w": bell_draw(streams_of[6], (D, 3, HHD), D ** -0.5, 0.125, ((2, 8),)),
        "out_w": bell_draw(streams_of[7], (HHD, D), (HD // 8) ** -0.5, 1.5, ((0, 8),)),
        "gate_up_w": bell_draw(streams_of[8], (D, 2, FFP), D ** -0.5, 0.125, ((2, 8),)),
        "down_w": bell_draw(streams_of[9], (FFP, D), FF ** -0.5, 0.078125, ((0, 8),)),
        "ln_params": draw_ln_params(jax.random.fold_in(streams_of[20], 71), 0),
        "qkv_row": jnp.clip(jnp.exp(jax.random.uniform(streams_of[11], (D,), jnp.float32, math.log(204.8), math.log(819.2))), 204.8, 819.2),
        "qkv_col": draw_qkv_col(jax.random.fold_in(streams_of[20], 71), 0),
        "out_row": draw_out_row(jax.random.fold_in(streams_of[20], 71), 0),
        "out_col": jnp.clip(jnp.exp(jax.random.uniform(streams_of[14], (D,), jnp.float32, math.log(5.7344), math.log(22.9376))), 5.7344, 22.9376),
        "gu_row": jnp.clip(jnp.exp(jax.random.uniform(streams_of[15], (D,), jnp.float32, math.log(81.92), math.log(327.68))), 81.92, 327.68),
        "gu_col": draw_gu_col(jax.random.fold_in(streams_of[20], 71), 0),
        "down_row": draw_down_row(jax.random.fold_in(streams_of[20], 71), 0),
        "down_col": jnp.clip(jnp.exp(jax.random.uniform(streams_of[18], (D,), jnp.float32, math.log(90.112), math.log(368.64))), 90.112, 368.64),
        "ln_second": jnp.clip(jnp.exp(jax.random.uniform(streams_of[19], (4, D), jnp.float32, math.log(409.6), math.log(1638.4))), 409.6, 1638.4),
    }


ln_eps = 1e-05
eps_one = 1e-30
eps_two = 0.001
clip_bound = 1.0
rate_base = 1.0
masked_score = -1e+30
highest = lax.Precision.HIGHEST

@jax.custom_vjp
def low(v):
    return lax.optimization_barrier(v.astype(jnp.bfloat16)).astype(jnp.float32)

@jax.custom_vjp
def low_back(v):
    return v

def low_keep(v):
    return (low(v), None)

def low_pass(kept, grad):
    return (grad,)

def back_keep(v):
    return (v, None)

def back_low(kept, grad):
    return (low(grad),)
low.defvjp(low_keep, low_pass)
low_back.defvjp(back_keep, back_low)

def layer_norm(rows, gain, shift):
    mean_row = lax.optimization_barrier(jnp.mean(rows, axis=-1, keepdims=True))
    centered = rows - mean_row
    variance = lax.optimization_barrier(jnp.mean(centered * centered, axis=-1, keepdims=True))
    return centered * lax.rsqrt(variance + ln_eps) * gain + shift

def block_mask(q_start, block_len, keys_ok, seq_prefix):
    q_pos = q_start + jnp.arange(block_len, dtype=jnp.int32)
    k_pos = jnp.arange(keys_ok.shape[0], dtype=jnp.int32)
    seen = (k_pos[None, :] <= q_pos[:, None]) | (k_pos[None, :] < seq_prefix)
    return seen & keys_ok[None, :]

def attend_sequence(seq_qkv, keys_ok, seq_prefix):
    query_rows = seq_qkv[:, 0]
    key_rows = seq_qkv[:, 1]
    values = seq_qkv[:, 2]
    block_len = min(512, SLOT)
    n_blocks = SLOT // block_len
    score_scale = HD ** (-0.5)

    def one_block(block_item):
        q_block, q_start = block_item
        allowed = block_mask(q_start, block_len, keys_ok, seq_prefix)
        raw_score = low_back(jnp.einsum('qhd,khd->hqk', q_block, key_rows, precision=highest))
        logits = jnp.where(allowed[None], raw_score * score_scale, masked_score)
        attn_probs = low(jax.nn.softmax(logits, axis=-1))
        return jnp.einsum('hqk,khd->qhd', attn_probs, values, precision=highest)
    q_blocks = query_rows.reshape(n_blocks, block_len, H, HD)
    starts = jnp.arange(n_blocks, dtype=jnp.int32) * block_len
    mixed_rows = lax.map(jax.checkpoint(one_block), (q_blocks, starts))
    return mixed_rows.reshape(SLOT, H * HD)

def forward(inputs, w_qkv, w_out, w_gate_up, w_down, ln_vec, keys_ok, seq_prefix, ff_mask):
    norm_one = low(layer_norm(inputs, ln_vec[0], ln_vec[1]))
    qkv_rows = jnp.einsum('sd,dkc->skc', norm_one, w_qkv, precision=highest)
    qkv_rows = low_back(low(qkv_rows)).reshape(SLOT, 3, H, HD)
    context = low_back(low(attend_sequence(qkv_rows, keys_ok, seq_prefix)))
    attn_out = low_back(jnp.dot(context, w_out, precision=highest))
    hidden = inputs + attn_out
    norm_two = low(layer_norm(hidden, ln_vec[2], ln_vec[3]))
    gate_up = low_back(jnp.einsum('sd,dkf->skf', norm_two, w_gate_up, precision=highest))
    inner_act = low(jax.nn.gelu(gate_up[:, 0]) * gate_up[:, 1] * ff_mask)
    return hidden + low_back(jnp.dot(inner_act, w_down, precision=highest))

def factored_step(grad, weight, row_old, col_old, row_mask, col_mask, decay_rate):
    real_cells = row_mask[:, None] * col_mask[None, :]
    n_rows = jnp.sum(row_mask)
    n_cols = jnp.sum(col_mask)
    squares = (grad * grad + eps_one) * real_cells
    row_new = decay_rate * row_old + (1.0 - decay_rate) * lax.optimization_barrier(jnp.sum(squares, axis=1)) / n_cols
    col_new = decay_rate * col_old + (1.0 - decay_rate) * lax.optimization_barrier(jnp.sum(squares, axis=0)) / n_rows
    row_mean = jnp.sum(row_new * row_mask) / n_rows
    update = grad * lax.rsqrt(row_new[:, None] * col_new[None, :] / row_mean)
    update_rms = jnp.sqrt(jnp.sum(update * update * real_cells) / (n_rows * n_cols))
    weight_rms = jnp.sqrt(jnp.sum(weight * weight * real_cells) / (n_rows * n_cols))
    step_rate = rate_base * jnp.maximum(eps_two, weight_rms)
    weight_new = weight - step_rate * update / jnp.maximum(1.0, update_rms / clip_bound)
    return (row_new, col_new, weight_new)

def reference(layer_in, cotangent, lengths, prefix, pad_mask, clusters, qkv_w, out_w, gate_up_w, down_w, ln_params, qkv_row, qkv_col, out_row, out_col, gu_row, gu_col, down_row, down_col, ln_second):
    onehot = (clusters[:, None] == jnp.arange(NCLUST, dtype=jnp.int32)[None, :]).astype(jnp.float32)
    counts = lax.optimization_barrier(jnp.sum(onehot, axis=0))
    seq_weight = 1.0 / lax.optimization_barrier(jnp.sum(onehot * counts[None, :], axis=1))
    positions = jnp.arange(SLOT, dtype=jnp.int32)
    pads = pad_mask.reshape(N_DP, SLOT)
    in_length = positions[None, :] < lengths[:, None]
    live_rows = (in_length & (pads == 1)).astype(jnp.float32)
    keys_ok = (positions[None, :] == 0) | in_length & (pads == 1)
    row_weight = live_rows * seq_weight[:, None]
    grads_in = cotangent.astype(jnp.float32).reshape(N_DP, SLOT, D) * row_weight[:, :, None]
    ff_mask = (jnp.arange(FFP, dtype=jnp.int32) < FF).astype(jnp.float32)
    w_qkv = qkv_w.astype(jnp.float32)
    w_out = out_w.astype(jnp.float32)
    w_gate_up = gate_up_w.astype(jnp.float32)
    w_down = down_w.astype(jnp.float32)
    inputs_all = layer_in.astype(jnp.float32).reshape(N_DP, SLOT, D)

    def one_sequence(totals, seq_item):
        seq_in, seq_grad, seq_keys, seq_prefix = seq_item
        step_fn = partial(forward, keys_ok=seq_keys, seq_prefix=seq_prefix, ff_mask=ff_mask)
        seq_out, pullback = jax.vjp(step_fn, seq_in, w_qkv, w_out, w_gate_up, w_down, ln_params)
        grad_parts = pullback(seq_grad)
        new_totals = tuple((running + piece_grad for running, piece_grad in zip(totals, grad_parts[1:])))
        return (new_totals, (seq_out.astype(jnp.bfloat16), grad_parts[0].astype(jnp.bfloat16)))
    zero_grads = tuple((jnp.zeros_like(weight_arr) for weight_arr in (w_qkv, w_out, w_gate_up, w_down, ln_params)))
    sums, outputs = lax.scan(one_sequence, zero_grads, (inputs_all, grads_in, keys_ok, prefix))
    g_qkv, g_out, g_gate_up, g_down, g_ln = sums
    layer_out = outputs[0].reshape(TOKENS, D)
    input_grad = outputs[1].reshape(TOKENS, D)
    decay_rate = 1.0 - STEP ** (-0.8)
    ones_d = jnp.ones((D,), jnp.float32)
    qkv_r, qkv_c, qkv_n = factored_step(g_qkv.reshape(D, -1), w_qkv.reshape(D, -1), qkv_row, qkv_col.reshape(-1), ones_d, jnp.ones((3 * H * HD,), jnp.float32), decay_rate)
    out_r, out_c, out_n = factored_step(g_out, w_out, out_row, out_col, jnp.ones((H * HD,), jnp.float32), ones_d, decay_rate)
    gu_r, gu_c, gu_n = factored_step(g_gate_up.reshape(D, -1), w_gate_up.reshape(D, -1), gu_row, gu_col.reshape(-1), ones_d, jnp.concatenate([ff_mask, ff_mask]), decay_rate)
    down_r, down_c, down_n = factored_step(g_down, w_down, down_row, down_col, ff_mask, ones_d, decay_rate)
    ln_second_new = decay_rate * ln_second + (1.0 - decay_rate) * (g_ln * g_ln + eps_one)
    ln_update = g_ln * lax.rsqrt(ln_second_new)
    ln_urms = jnp.sqrt(lax.optimization_barrier(jnp.mean(ln_update * ln_update, axis=1, keepdims=True)))
    ln_wrms = jnp.sqrt(lax.optimization_barrier(jnp.mean(ln_params * ln_params, axis=1, keepdims=True)))
    ln_new = ln_params - rate_base * jnp.maximum(eps_two, ln_wrms) * ln_update / jnp.maximum(1.0, ln_urms / clip_bound)
    return (layer_out, input_grad, g_qkv, qkv_n.reshape(D, 3, H * HD), qkv_r, qkv_c.reshape(3, H * HD), g_out, out_n, out_r, out_c, g_gate_up, gu_n.reshape(D, 2, FFP), gu_r, gu_c.reshape(2, FFP), g_down, down_n, down_r, down_c, g_ln, ln_second_new, ln_new)
```

```python
import functools

import jax
import jax.numpy as jnp
from jax import lax
from jax.experimental import pallas as pl
from jax.experimental.pallas import tpu as pltpu
from jax.sharding import PartitionSpec as P

HD = 128
FF = 5461
SLOT = 2048
STEP = 10
PREFIX_MAX = SLOT // 2
Q_BLOCK = 512

ln_eps = 1e-05
eps_one = 1e-30
eps_two = 0.001
clip_bound = 1.0
rate_base = 1.0
masked_score = -1e30
LOG2E = 1.4426950408889634
BF = jnp.bfloat16
F32 = jnp.float32


def dot(a, b, dims):
    return lax.dot_general(a, b, (dims, ((), ())), preferred_element_type=F32)


def ring_order(n):
    b_size = 2 if n <= 8 else 4
    a_size = n // b_size
    order = []
    for a in range(a_size):
        cols = list(range(1, b_size))
        order += [a * b_size + c for c in (cols[::-1] if a % 2 else cols)]
    for a in range(a_size - 1, -1, -1):
        order.append(a * b_size)
    return order


class Ring:
    def __init__(self, n):
        self.n = n
        order = ring_order(n)
        self.fw = [(order[i], order[(i + 1) % n]) for i in range(n)]
        self.bw = [(order[i], order[(i - 1) % n]) for i in range(n)]
        place = [0] * n
        for p, t in enumerate(order):
            place[t] = p
        self.order = jnp.array(order, jnp.int32)
        self.pos = jnp.array(place, jnp.int32)[lax.axis_index("tensor")]

    def owner(self, step):
        return self.order[lax.rem(self.pos + (2 * self.n - step), self.n)]

    def step(self, a, b):
        return lax.ppermute(a, "tensor", self.fw), lax.ppermute(b, "tensor", self.bw)

    def gather(self, x):
        half = x.shape[0] // 2
        a, b = x[:half], x[half:]
        yield a, b
        for _ in range(self.n - 1):
            a, b = self.step(a, b)
            yield a, b

    def scatter(self, part):
        acc = None
        for s in list(range(1, self.n)) + [0]:
            term = part(s)
            half = term.shape[0] // 2
            ta, tb = term[:half], term[half:]
            if acc is not None:
                ra, rb = self.step(*acc)
                ta, tb = ra.astype(F32) + ta, rb.astype(F32) + tb
            acc = (ta.astype(BF), tb.astype(BF))
        return jnp.concatenate([ta, tb], axis=0)

    def offsets(self, s, rows):
        return self.owner(s) * rows, self.owner(-s) * rows + rows // 2

    def put(self, whole, chunk, s, rows):
        oa, ob = self.offsets(s, rows)
        whole = lax.dynamic_update_slice(whole, chunk[: rows // 2], (oa, 0))
        return lax.dynamic_update_slice(whole, chunk[rows // 2 :], (ob, 0))

    def take(self, whole, s, rows):
        oa, ob = self.offsets(s, rows)
        cols = whole.shape[1]
        return jnp.concatenate(
            [
                lax.dynamic_slice(whole, (oa, 0), (rows // 2, cols)),
                lax.dynamic_slice(whole, (ob, 0), (rows // 2, cols)),
            ],
            axis=0,
        )


def norm_stats(rows):
    mean_row = jnp.mean(rows, axis=-1, keepdims=True)
    centered = rows - mean_row
    variance = jnp.mean(centered * centered, axis=-1, keepdims=True)
    scale = lax.rsqrt(variance + ln_eps)
    return centered * scale, scale


def layer_norm(rows, gain, shift):
    return norm_stats(rows)[0] * gain + shift


def layer_norm_back(rows, gain, e):
    n, scale = norm_stats(rows)
    eg = e * gain
    dv = scale * (
        eg - jnp.mean(eg, axis=-1, keepdims=True) - n * jnp.mean(eg * n, axis=-1, keepdims=True)
    )
    return dv, jnp.stack([jnp.sum(e * n, axis=0), jnp.sum(e, axis=0)])


def seen_mask(thr_ref, q0, shape):
    thr = thr_ref[: shape[0], :]
    thr = jnp.concatenate([thr] * (shape[1] // thr.shape[1]), axis=1)
    q_pos = q0 + lax.broadcasted_iota(jnp.int32, shape, 1)
    return q_pos >= thr


def attn_forward_kernel(q0, thr_ref, q_ref, k_ref, v_ref, o_ref, lse_ref):
    c = HD**-0.5 * LOG2E
    raw = dot(k_ref[...], q_ref[...], ((1,), (1,)))
    raw = jnp.where(seen_mask(thr_ref, q0, raw.shape), raw, masked_score)
    top = jnp.max(raw, axis=0, keepdims=True)
    p = jnp.exp2((raw - top) * c)
    total = jnp.sum(p, axis=0, keepdims=True)
    out = dot(v_ref[...], p.astype(BF), ((0,), (0,))) / total
    o_ref[...] = out.T.astype(BF)
    lse_ref[...] = (top * c + jnp.log2(total))[None]


def attn_backward_kernel(
    q0, thr_ref, q_ref, k_ref, v_ref, do_ref, lse_ref, dq_ref, dk_ref, dv_ref
):
    scale = HD**-0.5
    k, q, do = k_ref[...], q_ref[...], do_ref[...]
    raw = dot(k, q, ((1,), (1,)))
    p = jnp.exp2(raw * (scale * LOG2E) - lse_ref[0])
    p = jnp.where(seen_mask(thr_ref, q0, raw.shape), p, 0.0)
    dv_ref[...] = dot(p.astype(BF), do, ((1,), (0,)))
    dp = dot(v_ref[...], do, ((1,), (1,)))
    delta = jnp.sum(p * dp, axis=0, keepdims=True)
    ds = (p * (dp - delta) * scale).astype(BF)
    dk_ref[...] = dot(ds, q, ((1,), (0,)))
    dq_ref[...] = dot(k, ds, ((0,), (0,))).T.astype(BF)


def key_limit(i):
    return max(PREFIX_MAX, (i + 1) * Q_BLOCK)


def cost(i, products, heads):
    cells = Q_BLOCK * key_limit(i) * heads
    return pl.CostEstimate(
        flops=products * 2 * cells * HD, transcendentals=cells, bytes_accessed=8 * SLOT * HD * heads
    )


def attn_forward(i, thr, q, k, v):
    heads, klim = q.shape[1] // HD, key_limit(i)
    spec = lambda rows, j: pl.BlockSpec((rows, HD), lambda h: (j, h))
    return pl.pallas_call(
        functools.partial(attn_forward_kernel, i * Q_BLOCK),
        grid=(heads,),
        in_specs=[
            pl.BlockSpec((klim, HD), lambda h: (0, 0)),
            spec(Q_BLOCK, i),
            spec(klim, 0),
            spec(klim, 0),
        ],
        out_specs=[spec(Q_BLOCK, 0), pl.BlockSpec((1, 1, Q_BLOCK), lambda h: (h, 0, 0))],
        out_shape=[
            jax.ShapeDtypeStruct((Q_BLOCK, heads * HD), BF),
            jax.ShapeDtypeStruct((heads, 1, Q_BLOCK), F32),
        ],
        compiler_params=pltpu.CompilerParams(vmem_limit_bytes=48 << 20),
        cost_estimate=cost(i, 2, heads),
        name="attn_forward",
    )(thr, q, k, v)


def attn_backward(i, thr, q, k, v, do, lse):
    heads, klim = q.shape[1] // HD, key_limit(i)
    spec = lambda rows, j: pl.BlockSpec((rows, HD), lambda h: (j, h))
    return pl.pallas_call(
        functools.partial(attn_backward_kernel, i * Q_BLOCK),
        grid=(heads,),
        in_specs=[
            pl.BlockSpec((klim, HD), lambda h: (0, 0)),
            spec(Q_BLOCK, i),
            spec(klim, 0),
            spec(klim, 0),
            spec(Q_BLOCK, i),
            pl.BlockSpec((1, 1, Q_BLOCK), lambda h: (h, 0, 0)),
        ],
        out_specs=[spec(Q_BLOCK, 0), spec(klim, 0), spec(klim, 0)],
        out_shape=[
            jax.ShapeDtypeStruct((Q_BLOCK, heads * HD), BF),
            jax.ShapeDtypeStruct((klim, heads * HD), F32),
            jax.ShapeDtypeStruct((klim, heads * HD), F32),
        ],
        compiler_params=pltpu.CompilerParams(vmem_limit_bytes=48 << 20),
        cost_estimate=cost(i, 5, heads),
        name="attn_backward",
    )(thr, q, k, v, do, lse)


def sum_parts(parts):
    done, out = 0, []
    for end in sorted({p.shape[0] for p in parts}):
        out.append(sum(p[done:end] for p in parts if p.shape[0] >= end).astype(BF))
        done = end
    return jnp.concatenate(out, axis=0)


def apply_step(weight, grad, row_new, col_new, row_mean, update_sq, weight_sq, n_real):
    update_rms = jnp.sqrt(update_sq / n_real)
    weight_rms = jnp.sqrt(weight_sq / n_real)
    step_rate = rate_base * jnp.maximum(eps_two, weight_rms) / jnp.maximum(1.0, update_rms / clip_bound)
    return weight.astype(F32) - step_rate * (grad * lax.rsqrt(row_new * col_new / row_mean))


def tie(x, after):
    return lax.optimization_barrier((x, after))[0]


def on_device(
    layer_in,
    cotangent,
    lengths,
    prefix,
    pad_mask,
    clusters,
    qkv_w,
    out_w,
    gate_up_w,
    down_w,
    ln_params,
    qkv_row,
    qkv_col,
    out_row,
    out_col,
    gu_row,
    gu_col,
    down_row,
    down_col,
    ln_second,
):
    n_data = lax.axis_size("dp")
    n_tensor = lax.axis_size("tensor")
    tensor_rank = lax.axis_index("tensor")
    data_rank = lax.axis_index("dp")
    rows_dev, width = layer_in.shape
    cols_dev = qkv_w.shape[2]
    heads_dev = cols_dev // HD
    ff_dev = gate_up_w.shape[2]
    ff_pad = -(-ff_dev // 128) * 128
    n_clusters = max(2, n_data // 2)
    decay_rate = 1.0 - STEP ** (-0.8)
    seq_length = lengths[0]
    seq_prefix = prefix[0]
    ring = Ring(n_tensor)
    chunk_order = list(range(n_tensor))

    onehot = (clusters[:, None] == jnp.arange(n_clusters, dtype=jnp.int32)[None, :]).astype(F32)
    counts = jnp.sum(onehot, axis=0)
    own_row = jnp.sum(
        jnp.where((jnp.arange(n_data, dtype=jnp.int32) == data_rank)[:, None], onehot, 0.0), axis=0
    )
    seq_weight = jnp.sum(own_row / jnp.maximum(counts, 1.0))
    own_pos = tensor_rank * rows_dev + jnp.arange(rows_dev, dtype=jnp.int32)
    live_rows = ((own_pos < seq_length) & (pad_mask == 1)).astype(F32)
    grad_out = cotangent.astype(F32) * (live_rows * seq_weight)[:, None]
    grad_low = grad_out.astype(BF)

    pad_all = lax.all_gather(pad_mask, "tensor", axis=0, tiled=True)
    k_pos = jnp.arange(SLOT, dtype=jnp.int32)
    keys_ok = (k_pos == 0) | (pad_all == 1) & (k_pos < seq_length)
    seen_from = jnp.where(keys_ok, jnp.where(k_pos < seq_prefix, 0, k_pos), jnp.int32(1 << 30))
    thr = jnp.broadcast_to(seen_from[:, None], (SLOT, 128))

    w_qkv = qkv_w.reshape(width, 3 * cols_dev)
    pad = ((0, ff_pad - ff_dev), (0, 0))
    w_gate = jnp.pad(jnp.transpose(gate_up_w[:, 0], (1, 0)), pad)
    w_up = jnp.pad(jnp.transpose(gate_up_w[:, 1], (1, 0)), pad)
    w_gu = jnp.concatenate([w_gate, w_up], axis=0)
    w_down = jnp.pad(down_w, pad)
    col_index = tensor_rank * ff_dev + jnp.arange(ff_pad, dtype=jnp.int32)
    ff_real = ((col_index < FF) & (jnp.arange(ff_pad) < ff_dev)).astype(F32)
    ff_mask = ff_real[:ff_dev]

    layer_own = layer_in.astype(F32)
    act_one = []
    query = key = value = jnp.zeros((SLOT, cols_dev), BF)
    for s, pair in enumerate(ring.gather(layer_in)):
        rows = jnp.concatenate(pair, axis=0).astype(F32)
        act = layer_norm(rows, ln_params[0], ln_params[1]).astype(BF)
        act_one.append(act)
        qkv = dot(act, w_qkv, ((1,), (0,))).astype(BF)
        query = ring.put(query, qkv[:, :cols_dev], s, rows_dev)
        key = ring.put(key, qkv[:, cols_dev : 2 * cols_dev], s, rows_dev)
        value = ring.put(value, qkv[:, 2 * cols_dev :], s, rows_dev)
    last_pair = pair

    grad_chunks = [jnp.concatenate(p, axis=0) for p in ring.gather(tie(grad_low, last_pair))]
    n_blocks = SLOT // Q_BLOCK
    fwd = [attn_forward(i, thr, query, key, value) for i in range(n_blocks)]
    context = jnp.concatenate([f[0] for f in fwd], axis=0)
    context_chunks = [ring.take(context, s, rows_dev) for s in chunk_order]
    attn_own = ring.scatter(lambda s: dot(context_chunks[s], out_w, ((1,), (0,))))
    hidden_own = layer_own + attn_own
    norm_two = layer_norm(hidden_own, ln_params[2], ln_params[3]).astype(BF)

    act_two, inner, d_gu = [], [], []
    for s, pair in enumerate(ring.gather(norm_two)):
        act = jnp.concatenate(pair, axis=0)
        act_two.append(act)
        gate_up = dot(act, w_gu, ((1,), (1,)))
        gate, up = gate_up[:, :ff_pad], gate_up[:, ff_pad:]
        gelu_gate, gelu_back = jax.vjp(jax.nn.gelu, gate)
        inner.append((gelu_gate * up * ff_real).astype(BF))
        d_inner = dot(grad_chunks[s], w_down, ((1,), (1,))) * ff_real
        d_gate = gelu_back(d_inner * up)[0]
        d_gu.append(jnp.concatenate([d_gate, d_inner * gelu_gate], axis=1).astype(BF))
    d_norm_two = ring.scatter(lambda s: dot(d_gu[s], w_gu, ((1,), (0,))))
    grad_all = jnp.concatenate(grad_chunks, axis=0)
    act_two_all = jnp.concatenate(act_two, axis=0)
    down_part = dot(jnp.concatenate(inner, axis=0), grad_all, ((0,), (0,)))[:ff_dev].astype(BF)
    gu_part = dot(jnp.concatenate(d_gu, axis=0), act_two_all, ((0,), (0,))).astype(BF)
    gu_part = jnp.stack([gu_part[:ff_dev], gu_part[ff_pad : ff_pad + ff_dev]])

    d_hidden_ln, ln_two_part = layer_norm_back(hidden_own, ln_params[2], d_norm_two)
    d_hidden = grad_out + d_hidden_ln
    d_hidden_chunks = []
    d_context = jnp.zeros((SLOT, cols_dev), BF)
    for s, pair in enumerate(ring.gather(d_hidden.astype(BF))):
        chunk = jnp.concatenate(pair, axis=0)
        d_hidden_chunks.append(chunk)
        d_context = ring.put(d_context, dot(chunk, out_w, ((1,), (1,))).astype(BF), s, rows_dev)
    out_part = dot(
        jnp.concatenate(context_chunks, axis=0),
        jnp.concatenate(d_hidden_chunks, axis=0),
        ((0,), (0,)),
    ).astype(BF)
    down_low = lax.psum(down_part, "dp")
    gu_low = lax.psum(gu_part, "dp")
    out_low = lax.psum(out_part, "dp")

    ffn_own = ring.scatter(lambda s: dot(tie(inner[s], d_hidden_chunks[-1]), w_down, ((1,), (0,))))
    layer_out = (hidden_own + ffn_own).astype(BF)
    bwd = [
        attn_backward(i, thr, query, key, value, d_context, fwd[i][1]) for i in range(n_blocks)
    ]
    d_query = jnp.concatenate([b[0] for b in bwd], axis=0)
    d_key = sum_parts([b[1] for b in bwd])
    d_value = sum_parts([b[2] for b in bwd])
    d_qkv = jnp.concatenate([d_query, d_key, d_value], axis=1)
    d_qkv_chunks = [ring.take(d_qkv, s, rows_dev) for s in chunk_order]
    act_one_all = jnp.concatenate(act_one, axis=0)
    qkv_part = dot(act_one_all, jnp.concatenate(d_qkv_chunks, axis=0), ((0,), (0,))).astype(BF)
    qkv_part = jnp.transpose(qkv_part.reshape(width, 3, cols_dev), (1, 0, 2))
    qkv_low = lax.psum(qkv_part, "dp")
    d_norm_one = ring.scatter(lambda s: dot(d_qkv_chunks[s], w_qkv, ((1,), (1,))))
    d_input_ln, ln_one_part = layer_norm_back(layer_own, ln_params[0], d_norm_one)
    input_grad = (d_hidden + d_input_ln).astype(BF)

    qkv_sum, gu_sum = qkv_low.astype(F32), gu_low.astype(F32)
    out_sum, down_sum = out_low.astype(F32), down_low.astype(F32)
    gate_up_t = jnp.transpose(gate_up_w, (1, 2, 0))
    qkv_t = jnp.transpose(qkv_w, (1, 0, 2))
    blend = lambda old, total: decay_rate * old + (1.0 - decay_rate) * total
    square = lambda grad: grad * grad + eps_one
    square_sum = lambda w: jnp.sum(jnp.square(w.astype(F32)))

    qkv_sq, gu_sq = square(qkv_sum), square(gu_sum) * ff_mask[None, :, None]
    out_sq, down_sq = square(out_sum), square(down_sum) * ff_mask[:, None]
    qkv_col_new = blend(qkv_col, jnp.sum(qkv_sq, axis=1) / width)
    gu_col_new = blend(gu_col, jnp.sum(gu_sq, axis=2) / width)
    out_row_new = blend(out_row, jnp.sum(out_sq, axis=1) / width)
    down_row_new = blend(down_row, jnp.sum(down_sq, axis=1) / width)
    clean = lambda grad: grad * grad
    vectors = (
        jnp.sum(qkv_sq, axis=(0, 2)),
        jnp.sum(clean(qkv_sum) / qkv_col_new[:, None, :], axis=(0, 2)),
        jnp.sum(gu_sq, axis=(0, 1)),
        jnp.sum(clean(gu_sum) * (ff_mask / gu_col_new)[:, :, None], axis=(0, 1)),
        jnp.sum(out_sq, axis=0),
        jnp.sum(clean(out_sum) / out_row_new[:, None], axis=0),
        jnp.sum(down_sq, axis=0),
        jnp.sum(clean(down_sum) * (ff_mask / down_row_new)[:, None], axis=0),
    )
    scalars = jnp.stack(
        [
            square_sum(qkv_w),
            jnp.sum(jnp.square(gate_up_t.astype(F32)) * ff_mask[None, :, None]),
            square_sum(out_w),
            jnp.sum(jnp.square(down_w.astype(F32)) * ff_mask[:, None]),
            jnp.sum(out_row_new),
            jnp.sum(down_row_new * ff_mask),
        ]
    )
    share = 1.0 / n_data
    packed = jnp.concatenate(
        [jnp.stack(vectors) * share, ln_one_part, ln_two_part]
        + [jnp.pad(scalars * share, (0, width - scalars.shape[0]))[None]],
        axis=0,
    )
    packed = lax.psum(packed, ("dp", "tensor"))
    qkv_tot, qkv_usq, gu_tot, gu_usq, out_tot, out_usq, down_tot, down_usq = (
        packed[i] for i in range(8)
    )
    ln_tot = packed[8:12]
    qkv_wtot, gu_wtot, out_wtot, down_wtot, out_rtot, down_rtot = (packed[12, i] for i in range(6))

    qkv_cols_all = 3 * cols_dev * n_tensor
    out_rows_all = cols_dev * n_tensor
    qkv_row_new = blend(qkv_row, qkv_tot / qkv_cols_all)
    qkv_mean = jnp.sum(qkv_row_new) / width
    gu_row_new = blend(gu_row, gu_tot / (2 * FF))
    gu_mean = jnp.sum(gu_row_new) / width
    out_col_new = blend(out_col, out_tot / out_rows_all)
    out_mean = out_rtot / out_rows_all
    down_col_new = blend(down_col, down_tot / FF)
    down_mean = down_rtot / FF
    qkv_new = apply_step(
        qkv_t, qkv_sum, qkv_row_new[None, :, None], qkv_col_new[:, None, :], qkv_mean,
        jnp.sum(qkv_usq / qkv_row_new) * qkv_mean, qkv_wtot, width * qkv_cols_all,
    )
    gu_new = apply_step(
        gate_up_t, gu_sum, gu_row_new[None, None, :], gu_col_new[:, :, None], gu_mean,
        jnp.sum(gu_usq / gu_row_new) * gu_mean, gu_wtot, width * 2 * FF,
    )
    out_new = apply_step(
        out_w, out_sum, out_row_new[:, None], out_col_new[None, :], out_mean,
        jnp.sum(out_usq / out_col_new) * out_mean, out_wtot, out_rows_all * width,
    )
    down_new = apply_step(
        down_w, down_sum, down_row_new[:, None], down_col_new[None, :], down_mean,
        jnp.sum(down_usq / down_col_new) * down_mean, down_wtot, FF * width,
    )
    ln_second_new = blend(ln_second, ln_tot * ln_tot + eps_one)
    ln_update = ln_tot * lax.rsqrt(ln_second_new)
    ln_urms = jnp.sqrt(jnp.mean(ln_update * ln_update, axis=1, keepdims=True))
    ln_wrms = jnp.sqrt(jnp.mean(ln_params * ln_params, axis=1, keepdims=True))
    ln_new = ln_params - rate_base * jnp.maximum(eps_two, ln_wrms) * ln_update / jnp.maximum(
        1.0, ln_urms / clip_bound
    )
    qkv_back = lambda x: jnp.transpose(x, (1, 0, 2))
    gu_back = lambda x: jnp.transpose(x, (2, 0, 1))
    return (
        layer_out,
        input_grad,
        qkv_back(qkv_sum),
        qkv_back(qkv_new),
        qkv_row_new,
        qkv_col_new,
        out_sum,
        out_new,
        out_row_new,
        out_col_new,
        gu_back(gu_sum),
        gu_back(gu_new),
        gu_row_new,
        gu_col_new,
        down_sum,
        down_new,
        down_row_new,
        down_col_new,
        ln_tot,
        ln_second_new,
        ln_new,
    )


def solution(mesh):
    in_specs = (
        P(("dp", "tensor"), None),
        P(("dp", "tensor"), None),
        P("dp"),
        P("dp"),
        P(("dp", "tensor")),
        P(),
        P(None, None, "tensor"),
        P("tensor", None),
        P(None, None, "tensor"),
        P("tensor", None),
        P(),
        P(),
        P(None, "tensor"),
        P("tensor"),
        P(),
        P(),
        P(None, "tensor"),
        P("tensor"),
        P(),
        P(),
    )
    out_specs = (
        P(("dp", "tensor"), None),
        P(("dp", "tensor"), None),
        P(None, None, "tensor"),
        P(None, None, "tensor"),
        P(),
        P(None, "tensor"),
        P("tensor", None),
        P("tensor", None),
        P("tensor"),
        P(),
        P(None, None, "tensor"),
        P(None, None, "tensor"),
        P(),
        P(None, "tensor"),
        P("tensor", None),
        P("tensor", None),
        P("tensor"),
        P(),
        P(),
        P(),
        P(),
    )
    return jax.shard_map(
        on_device, mesh=mesh, in_specs=in_specs, out_specs=out_specs, check_vma=False
    )
```

```python
import functools

import jax
import jax.numpy as jnp
from jax import lax
from jax.experimental import pallas as pl
from jax.experimental.pallas import tpu as pltpu
from jax.sharding import PartitionSpec as P

HD = 128
FF = 5461
SLOT = 2048
STEP = 10
PREFIX_MAX = SLOT // 2
Q_BLOCK = 512

ln_eps = 1e-05
eps_one = 1e-30
eps_two = 0.001
clip_bound = 1.0
rate_base = 1.0
masked_score = -1e30
LOG2E = 1.4426950408889634
BF = jnp.bfloat16
F32 = jnp.float32


def dot(a, b, dims):
    return lax.dot_general(a, b, (dims, ((), ())), preferred_element_type=F32)


def ring_order(n):
    b_size = 2 if n <= 8 else 4
    a_size = n // b_size
    order = []
    for a in range(a_size):
        cols = list(range(1, b_size))
        order += [a * b_size + c for c in (cols[::-1] if a % 2 else cols)]
    for a in range(a_size - 1, -1, -1):
        order.append(a * b_size)
    return order


class Ring:
    def __init__(self, n):
        self.n = n
        order = ring_order(n)
        self.fw = [(order[i], order[(i + 1) % n]) for i in range(n)]
        self.bw = [(order[i], order[(i - 1) % n]) for i in range(n)]
        place = [0] * n
        for p, t in enumerate(order):
            place[t] = p
        self.order = jnp.array(order, jnp.int32)
        self.pos = jnp.array(place, jnp.int32)[lax.axis_index("tensor")]

    def owner(self, step):
        return self.order[lax.rem(self.pos + (2 * self.n - step), self.n)]

    def step(self, a, b):
        return lax.ppermute(a, "tensor", self.fw), lax.ppermute(b, "tensor", self.bw)

    def gather(self, x):
        half = x.shape[0] // 2
        a, b = x[:half], x[half:]
        yield a, b
        for _ in range(self.n - 1):
            a, b = self.step(a, b)
            yield a, b

    def scatter(self, part):
        acc = None
        for s in list(range(1, self.n)) + [0]:
            term = lax.optimization_barrier(part(s))
            half = term.shape[0] // 2
            ta, tb = term[:half], term[half:]
            if acc is not None:
                ra, rb = self.step(*acc)
                ta, tb = ra.astype(F32) + ta, rb.astype(F32) + tb
            acc = (ta.astype(BF), tb.astype(BF))
        return jnp.concatenate([ta, tb], axis=0)

    def offsets(self, s, rows):
        return self.owner(s) * rows, self.owner(-s) * rows + rows // 2

    def put(self, whole, chunk, s, rows):
        oa, ob = self.offsets(s, rows)
        whole = lax.dynamic_update_slice(whole, chunk[: rows // 2], (oa, 0))
        return lax.dynamic_update_slice(whole, chunk[rows // 2 :], (ob, 0))

    def take(self, whole, s, rows):
        oa, ob = self.offsets(s, rows)
        cols = whole.shape[1]
        return jnp.concatenate(
            [
                lax.dynamic_slice(whole, (oa, 0), (rows // 2, cols)),
                lax.dynamic_slice(whole, (ob, 0), (rows // 2, cols)),
            ],
            axis=0,
        )


def norm_stats(rows):
    mean_row = jnp.mean(rows, axis=-1, keepdims=True)
    centered = rows - mean_row
    variance = jnp.mean(centered * centered, axis=-1, keepdims=True)
    scale = lax.rsqrt(variance + ln_eps)
    return centered * scale, scale


def layer_norm(rows, gain, shift):
    return norm_stats(rows)[0] * gain + shift


def layer_norm_back(rows, gain, e):
    n, scale = norm_stats(rows)
    eg = e * gain
    dv = scale * (
        eg - jnp.mean(eg, axis=-1, keepdims=True) - n * jnp.mean(eg * n, axis=-1, keepdims=True)
    )
    return dv, jnp.stack([jnp.sum(e * n, axis=0), jnp.sum(e, axis=0)])


def seen_mask(thr_ref, q0, shape):
    thr = thr_ref[: shape[0], :]
    thr = jnp.concatenate([thr] * (shape[1] // thr.shape[1]), axis=1)
    q_pos = (q0 + lax.broadcasted_iota(jnp.int32, shape, 1)).astype(F32)
    return q_pos >= thr


def q_blocks():
    return [(q0, max(PREFIX_MAX, q0 + Q_BLOCK)) for q0 in range(0, SLOT, Q_BLOCK)]


def attn_forward_kernel(thr_ref, q_ref, k_ref, v_ref, o_ref, lse_ref):
    c = HD**-0.5 * LOG2E
    for q0, klim in q_blocks():
        raw = dot(k_ref[:klim, :], q_ref[q0 : q0 + Q_BLOCK, :], ((1,), (1,)))
        raw = jnp.where(seen_mask(thr_ref, q0, raw.shape), raw, masked_score)
        top = jnp.max(raw, axis=0, keepdims=True)
        p = jnp.exp2((raw - top) * c)
        total = jnp.sum(p, axis=0, keepdims=True)
        out = dot(v_ref[:klim, :], p.astype(BF), ((0,), (0,))) / total
        o_ref[q0 : q0 + Q_BLOCK, :] = out.T.astype(BF)
        lse_ref[0, :, q0 : q0 + Q_BLOCK] = top * c + jnp.log2(total)


def attn_backward_kernel(
    thr_ref, q_ref, k_ref, v_ref, do_ref, lse_ref, dq_ref, dk_ref, dv_ref, dk_sum, dv_sum
):
    scale = HD**-0.5
    dk_sum[...] = jnp.zeros_like(dk_sum)
    dv_sum[...] = jnp.zeros_like(dv_sum)
    for q0, klim in q_blocks():
        rows = slice(q0, q0 + Q_BLOCK)
        k, q, do = k_ref[:klim, :], q_ref[rows, :], do_ref[rows, :]
        raw = dot(k, q, ((1,), (1,)))
        p = jnp.exp2(raw * (scale * LOG2E) - lse_ref[0, :, rows])
        p = jnp.where(seen_mask(thr_ref, q0, raw.shape), p, 0.0)
        dv_sum[:klim, :] += dot(p.astype(BF), do, ((1,), (0,)))
        dp = dot(v_ref[:klim, :], do, ((1,), (1,)))
        delta = jnp.sum(p * dp, axis=0, keepdims=True)
        ds = (p * (dp - delta) * scale).astype(BF)
        dk_sum[:klim, :] += dot(ds, q, ((1,), (0,)))
        dq_ref[rows, :] = dot(k, ds, ((0,), (0,))).T.astype(BF)
    dk_ref[...] = dk_sum[...].astype(BF)
    dv_ref[...] = dv_sum[...].astype(BF)


def cost(products, heads):
    cells = sum(Q_BLOCK * klim for _, klim in q_blocks()) * heads
    return pl.CostEstimate(
        flops=products * 2 * cells * HD, transcendentals=cells, bytes_accessed=8 * SLOT * HD * heads
    )


def attn_call(kernel, n_wide, products, heads, with_lse, scratch):
    wide = pl.BlockSpec((SLOT, HD), lambda h: (0, h))
    lse = pl.BlockSpec((1, 1, SLOT), lambda h: (h, 0, 0))
    wide_shape = jax.ShapeDtypeStruct((SLOT, heads * HD), BF)
    in_specs = [pl.BlockSpec((SLOT, 128), lambda h: (0, 0))] + [wide] * n_wide
    out_specs, out_shape = [wide] * 3, [wide_shape] * 3
    if with_lse:
        out_specs, out_shape = [wide, lse], [wide_shape, jax.ShapeDtypeStruct((heads, 1, SLOT), F32)]
    else:
        in_specs = in_specs + [lse]
    return pl.pallas_call(
        kernel,
        grid=(heads,),
        in_specs=in_specs,
        out_specs=out_specs,
        out_shape=out_shape,
        scratch_shapes=scratch,
        compiler_params=pltpu.CompilerParams(vmem_limit_bytes=56 << 20),
        cost_estimate=cost(products, heads),
    )


def attn_forward(thr, q, k, v):
    heads = q.shape[1] // HD
    return attn_call(attn_forward_kernel, 3, 2, heads, True, [])(thr, q, k, v)


def attn_backward(thr, q, k, v, do, lse):
    heads = q.shape[1] // HD
    scratch = [pltpu.VMEM((SLOT, HD), F32)] * 2
    return attn_call(attn_backward_kernel, 4, 5, heads, False, scratch)(thr, q, k, v, do, lse)


def apply_step(weight, grad, row_new, col_new, row_mean, update_sq, weight_sq, n_real):
    update_rms = jnp.sqrt(update_sq / n_real)
    weight_rms = jnp.sqrt(weight_sq / n_real)
    step_rate = rate_base * jnp.maximum(eps_two, weight_rms) / jnp.maximum(1.0, update_rms / clip_bound)
    return weight.astype(F32) - step_rate * (grad * lax.rsqrt(row_new * col_new / row_mean))


def tie(x, after):
    return lax.optimization_barrier((x, after))[0]


def exchange_kernel(n_dp, n, x_ref, o_ref, dp_buf, rows, part_buf, total, whole, sems):
    me_d, me = lax.axis_index("dp"), lax.axis_index("tensor")
    width = x_ref.shape[1] // n
    columns = lambda t: pl.ds(pl.multiple_of(t * width, width), width)
    dp_peers = [(k - 1, lax.rem(me_d + k, n_dp)) for k in range(1, n_dp)]
    peers = [(k - 1, lax.rem(me + k, n)) for k in range(1, n)]
    barrier = pltpu.get_barrier_semaphore()
    for _, d in dp_peers:
        pl.semaphore_signal(barrier, inc=1, device_id={"dp": d}, device_id_type=pl.DeviceIdType.MESH)
    for _, t in peers:
        pl.semaphore_signal(barrier, inc=1, device_id={"tensor": t}, device_id_type=pl.DeviceIdType.MESH)
    pl.semaphore_wait(barrier, n_dp + n - 2)

    def push(stage, src, dst, k, device):
        copy = pltpu.make_async_remote_copy(
            src_ref=src, dst_ref=dst, send_sem=sems.at[0, stage, k], recv_sem=sems.at[1, stage, k],
            device_id=device, device_id_type=pl.DeviceIdType.MESH,
        )
        copy.start()
        return copy

    first = [push(0, x_ref.at[pl.ds(0, 8)], dp_buf.at[me_d], k, {"dp": d}) for k, d in dp_peers]
    rows[...] = x_ref[...]
    dp_buf[me_d] = x_ref[0:8, :]
    for copy in first:
        copy.wait()
    rows[0:8, :] = sum(dp_buf[d] for d in range(n_dp))
    second = [push(1, rows.at[:, columns(t)], part_buf.at[me], k, {"tensor": t}) for k, t in peers]
    part_buf[me] = rows[:, columns(me)]
    for copy in second:
        copy.wait()
    total[...] = sum(part_buf[t] for t in range(n))
    third = [push(2, total, whole.at[me], k, {"tensor": t}) for k, t in peers]
    whole[me] = total[...]
    for copy in third:
        copy.wait()
    for t in range(n):
        o_ref[:, t * width : (t + 1) * width] = whole[t]


def exchange(x, n_dp, n):
    height, width = x.shape
    slots = pltpu.VMEM((n, height, width // n), F32)
    return pl.pallas_call(
        functools.partial(exchange_kernel, n_dp, n),
        out_shape=jax.ShapeDtypeStruct(x.shape, F32),
        in_specs=[pl.BlockSpec(memory_space=pltpu.VMEM)],
        out_specs=pl.BlockSpec(memory_space=pltpu.VMEM),
        scratch_shapes=[
            pltpu.VMEM((n_dp, 8, width), F32),
            pltpu.VMEM(x.shape, F32),
            slots,
            pltpu.VMEM((height, width // n), F32),
            slots,
            pltpu.SemaphoreType.DMA((2, 3, max(n, n_dp) - 1)),
        ],
        compiler_params=pltpu.CompilerParams(collective_id=0, has_side_effects=True),
    )(x)


def on_device(
    layer_in,
    cotangent,
    lengths,
    prefix,
    pad_mask,
    clusters,
    qkv_w,
    out_w,
    gate_up_w,
    down_w,
    ln_params,
    qkv_row,
    qkv_col,
    out_row,
    out_col,
    gu_row,
    gu_col,
    down_row,
    down_col,
    ln_second,
):
    n_data = lax.axis_size("dp")
    n_tensor = lax.axis_size("tensor")
    tensor_rank = lax.axis_index("tensor")
    data_rank = lax.axis_index("dp")
    rows_dev, width = layer_in.shape
    cols_dev = qkv_w.shape[2]
    heads_dev = cols_dev // HD
    ff_dev = gate_up_w.shape[2]
    ff_pad = -(-ff_dev // 128) * 128
    n_clusters = max(2, n_data // 2)
    decay_rate = 1.0 - STEP ** (-0.8)
    seq_length = lengths[0]
    seq_prefix = prefix[0]
    ring = Ring(n_tensor)
    chunk_order = list(range(n_tensor))

    onehot = (clusters[:, None] == jnp.arange(n_clusters, dtype=jnp.int32)[None, :]).astype(F32)
    counts = jnp.sum(onehot, axis=0)
    own_row = jnp.sum(
        jnp.where((jnp.arange(n_data, dtype=jnp.int32) == data_rank)[:, None], onehot, 0.0), axis=0
    )
    seq_weight = jnp.sum(own_row / jnp.maximum(counts, 1.0))
    own_pos = tensor_rank * rows_dev + jnp.arange(rows_dev, dtype=jnp.int32)
    live_rows = ((own_pos < seq_length) & (pad_mask == 1)).astype(F32)
    grad_out = cotangent.astype(F32) * (live_rows * seq_weight)[:, None]
    grad_low = grad_out.astype(BF)

    key_live = (own_pos == 0) | (own_pos < seq_length) & (pad_mask == 1)
    seen_from = jnp.where(key_live, jnp.where(own_pos < seq_prefix, 0, own_pos), 2 * SLOT)
    seen_parts = jnp.stack([seen_from // 8 * 8, seen_from % 8], axis=1).astype(BF)
    seen_parts = jnp.repeat(seen_parts, 128, axis=1)
    seen_all = lax.all_gather(seen_parts, "tensor", axis=0, tiled=True).astype(F32)
    thr = seen_all[:, :128] + seen_all[:, 128:]

    w_qkv = qkv_w.reshape(width, 3 * cols_dev)
    col_index = tensor_rank * ff_dev + jnp.arange(ff_pad, dtype=jnp.int32)
    ff_real = ((col_index < FF) & (jnp.arange(ff_pad) < ff_dev)).astype(F32)
    ff_mask = ff_real[:ff_dev]

    layer_own = layer_in.astype(F32)
    act_one = []
    query = key = value = jnp.zeros((SLOT, cols_dev), BF)
    for s, pair in enumerate(ring.gather(layer_in)):
        rows = jnp.concatenate(pair, axis=0).astype(F32)
        act = layer_norm(rows, ln_params[0], ln_params[1]).astype(BF)
        act_one.append(act)
        qkv = dot(act, w_qkv, ((1,), (0,))).astype(BF)
        query = ring.put(query, qkv[:, :cols_dev], s, rows_dev)
        key = ring.put(key, qkv[:, cols_dev : 2 * cols_dev], s, rows_dev)
        value = ring.put(value, qkv[:, 2 * cols_dev :], s, rows_dev)
    last_pair = pair
    pad = ((0, ff_pad - ff_dev), (0, 0))
    gate_up_late, down_late = tie((jnp.transpose(gate_up_w, (2, 1, 0)), down_w), last_pair)
    w_gu = jnp.concatenate([jnp.pad(gate_up_late[:, i], pad) for i in range(2)], axis=0)
    w_down = jnp.pad(down_late, pad)

    grad_chunks = [jnp.concatenate(p, axis=0) for p in ring.gather(tie(grad_low, last_pair))]
    context, lse = attn_forward(thr, query, key, value)
    context_chunks = [ring.take(context, s, rows_dev) for s in chunk_order]
    attn_own = ring.scatter(lambda s: dot(context_chunks[s], out_w, ((1,), (0,))))
    hidden_own = layer_own + attn_own
    norm_two = layer_norm(hidden_own, ln_params[2], ln_params[3]).astype(BF)

    act_two, inner, d_gu = [], [], []
    for s, pair in enumerate(ring.gather(norm_two)):
        act = jnp.concatenate(pair, axis=0)
        act_two.append(act)
        gate_up = dot(act, w_gu, ((1,), (1,)))
        gate, up = gate_up[:, :ff_pad], gate_up[:, ff_pad:]
        gelu_gate, gelu_back = jax.vjp(jax.nn.gelu, gate)
        inner.append((gelu_gate * up * ff_real).astype(BF))
        d_inner = dot(grad_chunks[s], w_down, ((1,), (1,))) * ff_real
        d_gate = gelu_back(d_inner * up)[0]
        d_gu.append(jnp.concatenate([d_gate, d_inner * gelu_gate], axis=1).astype(BF))
    d_norm_two = ring.scatter(lambda s: dot(d_gu[s], w_gu, ((1,), (0,))))
    d_hidden_ln, ln_two_part = layer_norm_back(hidden_own, ln_params[2], d_norm_two)
    d_hidden = grad_out + d_hidden_ln
    d_hidden_chunks = []
    d_context = jnp.zeros((SLOT, cols_dev), BF)
    gu_part = []
    for s, pair in enumerate(ring.gather(d_hidden.astype(BF))):
        chunk = jnp.concatenate(pair, axis=0)
        d_hidden_chunks.append(chunk)
        if s == 1:
            inner_all, grad_all = (jnp.concatenate(tie(x, pair), axis=0) for x in (inner, grad_chunks))
            down_part = dot(inner_all, grad_all, ((0,), (0,)))[:ff_dev].astype(BF)
            down_low = lax.psum(down_part, "dp")
        if s in (2, 3):
            at = (s - 2) * ff_pad
            halves = [d[:, at : at + ff_pad] for d in d_gu]
            d_half, act_two_all = (jnp.concatenate(tie(x, pair), axis=0) for x in (halves, act_two))
            gu_part.append(dot(d_half, act_two_all, ((0,), (0,)))[:ff_dev].astype(BF))
        d_context = ring.put(d_context, dot(chunk, out_w, ((1,), (1,))).astype(BF), s, rows_dev)
    out_part = dot(
        jnp.concatenate(context_chunks, axis=0),
        jnp.concatenate(d_hidden_chunks, axis=0),
        ((0,), (0,)),
    ).astype(BF)
    gu_low = lax.psum(tie(jnp.stack(gu_part, axis=1), down_low), "dp")
    out_low = lax.psum(tie(out_part, gu_low), "dp")

    ffn_own = ring.scatter(lambda s: dot(tie(inner[s], d_hidden_chunks[-1]), w_down, ((1,), (0,))))
    layer_out = (hidden_own + ffn_own).astype(BF)
    d_qkv = attn_backward(thr, query, key, value, d_context, lse)
    d_qkv_chunks = [
        jnp.concatenate([ring.take(d, s, rows_dev) for d in d_qkv], axis=1) for s in chunk_order
    ]
    act_one_all = jnp.concatenate(act_one, axis=0)
    qkv_part = dot(act_one_all, jnp.concatenate(d_qkv_chunks, axis=0), ((0,), (0,))).astype(BF)
    qkv_part = jnp.transpose(qkv_part.reshape(width, 3, cols_dev), (1, 0, 2))
    qkv_low = lax.psum(tie(qkv_part, out_low), "dp")
    d_norm_one = ring.scatter(lambda s: dot(d_qkv_chunks[s], w_qkv, ((1,), (1,))))
    d_input_ln, ln_one_part = layer_norm_back(layer_own, ln_params[0], d_norm_one)
    input_grad = (d_hidden + d_input_ln).astype(BF)

    qkv_sum, gu_sum = qkv_low.astype(F32), gu_low.astype(F32)
    out_sum, down_sum = out_low.astype(F32), down_low.astype(F32)
    gate_up_t, qkv_t, out_t, down_t = tie(
        (jnp.transpose(gate_up_w, (2, 1, 0)), jnp.transpose(qkv_w, (1, 0, 2)), out_w, down_w),
        d_qkv[0],
    )
    gu_col_t = jnp.transpose(gu_col)
    blend = lambda old, total: decay_rate * old + (1.0 - decay_rate) * total
    square = lambda grad: grad * grad + eps_one
    square_sum = lambda w: jnp.sum(jnp.square(w.astype(F32)))

    qkv_sq, gu_sq = square(qkv_sum), square(gu_sum) * ff_mask[:, None, None]
    out_sq, down_sq = square(out_sum), square(down_sum) * ff_mask[:, None]
    qkv_col_new = blend(qkv_col, jnp.sum(qkv_sq, axis=1) / width)
    gu_col_new = blend(gu_col_t, jnp.sum(gu_sq, axis=2) / width)
    out_row_new = blend(out_row, jnp.sum(out_sq, axis=1) / width)
    down_row_new = blend(down_row, jnp.sum(down_sq, axis=1) / width)
    clean = lambda grad: grad * grad
    scalars = jnp.stack(
        [
            square_sum(qkv_t),
            jnp.sum(jnp.square(gate_up_t.astype(F32)) * ff_mask[:, None, None]),
            square_sum(out_t),
            jnp.sum(jnp.square(down_t.astype(F32)) * ff_mask[:, None]),
            jnp.sum(out_row_new),
            jnp.sum(down_row_new * ff_mask),
        ]
    )
    packed = jnp.concatenate(
        [
            ln_one_part,
            ln_two_part,
            jnp.pad(scalars / n_data, (0, width - scalars.shape[0]))[None],
            jnp.zeros((3, width), F32),
            jnp.stack(
                [
                    jnp.sum(qkv_sq, axis=(0, 2)),
                    jnp.sum(clean(qkv_sum) / qkv_col_new[:, None, :], axis=(0, 2)),
                    jnp.sum(gu_sq, axis=(0, 1)),
                    jnp.sum(clean(gu_sum) * (ff_mask[:, None] / gu_col_new)[:, :, None], axis=(0, 1)),
                    jnp.sum(out_sq, axis=0),
                    jnp.sum(clean(out_sum) / out_row_new[:, None], axis=0),
                    jnp.sum(down_sq, axis=0),
                    jnp.sum(clean(down_sum) * (ff_mask / down_row_new)[:, None], axis=0),
                ]
            ),
        ],
        axis=0,
    )
    packed = exchange(packed, n_data, n_tensor)
    ln_tot = packed[:4]
    qkv_wtot, gu_wtot, out_wtot, down_wtot, out_rtot, down_rtot = (packed[4, i] for i in range(6))
    qkv_tot, qkv_usq, gu_tot, gu_usq, out_tot, out_usq, down_tot, down_usq = (
        packed[8 + i] for i in range(8)
    )

    qkv_cols_all = 3 * cols_dev * n_tensor
    out_rows_all = cols_dev * n_tensor
    qkv_row_new = blend(qkv_row, qkv_tot / qkv_cols_all)
    qkv_mean = jnp.sum(qkv_row_new) / width
    gu_row_new = blend(gu_row, gu_tot / (2 * FF))
    gu_mean = jnp.sum(gu_row_new) / width
    out_col_new = blend(out_col, out_tot / out_rows_all)
    out_mean = out_rtot / out_rows_all
    down_col_new = blend(down_col, down_tot / FF)
    down_mean = down_rtot / FF
    qkv_new = apply_step(
        qkv_t, qkv_sum, qkv_row_new[None, :, None], qkv_col_new[:, None, :], qkv_mean,
        jnp.sum(qkv_usq / qkv_row_new) * qkv_mean, qkv_wtot, width * qkv_cols_all,
    )
    gu_new = apply_step(
        gate_up_t, gu_sum, gu_row_new[None, None, :], gu_col_new[:, :, None], gu_mean,
        jnp.sum(gu_usq / gu_row_new) * gu_mean, gu_wtot, width * 2 * FF,
    )
    out_new = apply_step(
        out_w, out_sum, out_row_new[:, None], out_col_new[None, :], out_mean,
        jnp.sum(out_usq / out_col_new) * out_mean, out_wtot, out_rows_all * width,
    )
    down_new = apply_step(
        down_w, down_sum, down_row_new[:, None], down_col_new[None, :], down_mean,
        jnp.sum(down_usq / down_col_new) * down_mean, down_wtot, FF * width,
    )
    ln_second_new = blend(ln_second, ln_tot * ln_tot + eps_one)
    ln_update = ln_tot * lax.rsqrt(ln_second_new)
    ln_urms = jnp.sqrt(jnp.mean(ln_update * ln_update, axis=1, keepdims=True))
    ln_wrms = jnp.sqrt(jnp.mean(ln_params * ln_params, axis=1, keepdims=True))
    ln_new = ln_params - rate_base * jnp.maximum(eps_two, ln_wrms) * ln_update / jnp.maximum(
        1.0, ln_urms / clip_bound
    )
    qkv_back = lambda x: jnp.transpose(x, (1, 0, 2))
    gu_back = lambda x: jnp.transpose(x, (2, 1, 0))
    return (
        layer_out,
        input_grad,
        qkv_back(qkv_sum),
        qkv_back(qkv_new),
        qkv_row_new,
        qkv_col_new,
        out_sum,
        out_new,
        out_row_new,
        out_col_new,
        gu_back(gu_sum),
        gu_back(gu_new),
        gu_row_new,
        jnp.transpose(gu_col_new),
        down_sum,
        down_new,
        down_row_new,
        down_col_new,
        ln_tot,
        ln_second_new,
        ln_new,
    )


def solution(mesh):
    in_specs = (
        P(("dp", "tensor"), None),
        P(("dp", "tensor"), None),
        P("dp"),
        P("dp"),
        P(("dp", "tensor")),
        P(),
        P(None, None, "tensor"),
        P("tensor", None),
        P(None, None, "tensor"),
        P("tensor", None),
        P(),
        P(),
        P(None, "tensor"),
        P("tensor"),
        P(),
        P(),
        P(None, "tensor"),
        P("tensor"),
        P(),
        P(),
    )
    out_specs = (
        P(("dp", "tensor"), None),
        P(("dp", "tensor"), None),
        P(None, None, "tensor"),
        P(None, None, "tensor"),
        P(),
        P(None, "tensor"),
        P("tensor", None),
        P("tensor", None),
        P("tensor"),
        P(),
        P(None, None, "tensor"),
        P(None, None, "tensor"),
        P(),
        P(None, "tensor"),
        P("tensor", None),
        P("tensor", None),
        P("tensor"),
        P(),
        P(),
        P(),
        P(),
    )
    return jax.shard_map(
        on_device, mesh=mesh, in_specs=in_specs, out_specs=out_specs, check_vma=False
    )
```

```python
import functools

import jax
import jax.numpy as jnp
from jax import lax
from jax.experimental import pallas as pl
from jax.experimental.pallas import tpu as pltpu
from jax.sharding import PartitionSpec as P

HD = 128
FF = 5461
SLOT = 2048
STEP = 10
PREFIX_MAX = SLOT // 2
Q_BLOCK = 512

ln_eps = 1e-05
eps_one = 1e-30
eps_two = 0.001
clip_bound = 1.0
rate_base = 1.0
masked_score = -1e30
LOG2E = 1.4426950408889634
BF = jnp.bfloat16
F32 = jnp.float32


def dot(a, b, dims):
    return lax.dot_general(a, b, (dims, ((), ())), preferred_element_type=F32)


def ring_order(n):
    b_size = 2 if n <= 8 else 4
    a_size = n // b_size
    order = []
    for a in range(a_size):
        cols = list(range(1, b_size))
        order += [a * b_size + c for c in (cols[::-1] if a % 2 else cols)]
    for a in range(a_size - 1, -1, -1):
        order.append(a * b_size)
    return order


class Ring:
    def __init__(self, n):
        self.n = n
        order = ring_order(n)
        self.fw = [(order[i], order[(i + 1) % n]) for i in range(n)]
        self.bw = [(order[i], order[(i - 1) % n]) for i in range(n)]
        place = [0] * n
        for p, t in enumerate(order):
            place[t] = p
        self.place = jnp.array(place, jnp.int32)
        self.pos = self.place[lax.axis_index("tensor")]

    def step(self, a, b):
        return lax.ppermute(a, "tensor", self.fw), lax.ppermute(b, "tensor", self.bw)

    def gather(self, x):
        half = x.shape[0] // 2
        a, b = x[:half], x[half:]
        yield a, b
        for _ in range(self.n - 1):
            a, b = self.step(a, b)
            yield a, b

    def scatter(self, part):
        acc = None
        for s in list(range(1, self.n)) + [0]:
            term = lax.optimization_barrier(part(s))
            half = term.shape[0] // 2
            ta, tb = term[:half], term[half:]
            if acc is not None:
                ra, rb = self.step(*acc)
                ta, tb = ra.astype(F32) + ta, rb.astype(F32) + tb
            acc = (ta.astype(BF), tb.astype(BF))
        return jnp.concatenate([ta, tb], axis=0)

    def places(self, rows):
        t = jnp.arange(self.n, dtype=jnp.int32)
        step = self.place[t] - self.pos
        first = lax.rem(2 * self.n - step, self.n) * rows
        second = lax.rem(step + self.n, self.n) * rows + rows // 2
        return jnp.stack([first, second], axis=1).reshape(-1)


PUSH = pl.DeviceIdType.MESH


def pick(index, table):
    out = jnp.int32(table[0])
    for k in range(1, len(table)):
        out = jnp.where(index == k, jnp.int32(table[k]), out)
    return out


def ring_gather(n, x_ref, land, send_sem, recv_sem, peers, work):
    order = ring_order(n)
    pos = pick(lax.axis_index("tensor"), [order.index(t) for t in range(n)])
    ahead = pick(lax.rem(pos + 1, n), order)
    behind = pick(lax.rem(pos + n - 1, n), order)
    barrier = pltpu.get_barrier_semaphore()
    greet = [ahead, behind] if peers is None else peers
    for t in greet:
        pl.semaphore_signal(barrier, inc=1, device_id={"tensor": t}, device_id_type=PUSH)
    half = x_ref.shape[0] // 2
    land[0, 0] = x_ref[:half, :]
    land[1, 0] = x_ref[half:, :]
    pl.semaphore_wait(barrier, len(greet))

    def copy(d, s):
        return pltpu.make_async_remote_copy(
            src_ref=land.at[d, s],
            dst_ref=land.at[d, s + 1],
            send_sem=send_sem.at[d, s],
            recv_sem=recv_sem.at[d, s],
            device_id={"tensor": (ahead, behind)[d]},
            device_id_type=PUSH,
        )

    def step(s, carry):
        for d in range(2):

            @pl.when(s > 0)
            def _():
                copy(d, s - 1).wait_recv()

            @pl.when(s < n - 1)
            def _():
                copy(d, s).start()

        work(s)
        return carry

    lax.fori_loop(0, n, step, 0)

    def sent(s, carry):
        for d in range(2):
            copy(d, s).wait_send()
        return carry

    lax.fori_loop(0, n - 1, sent, 0)


def first_kernel(
    n, x_ref, seen_ref, ln_ref, w_ref, act_ref, qkv_ref, seen_all,
    land, act_buf, seen_buf, send_sem, recv_sem, act_sem, seen_sem,
):
    rows, cols = x_ref.shape[0], w_ref.shape[2]
    me = lax.axis_index("tensor")
    peers = [lax.rem(me + k, n) for k in range(1, n)]

    def seen_copy(k):
        return pltpu.make_async_remote_copy(
            src_ref=seen_ref, dst_ref=seen_buf.at[me], send_sem=seen_sem.at[0, k],
            recv_sem=seen_sem.at[1, k], device_id={"tensor": peers[k]}, device_id_type=PUSH,
        )

    def act_copy(s):
        place = pl.ds(pl.multiple_of(s * rows, rows), rows)
        return pltpu.make_async_copy(act_buf.at[s], act_ref.at[place], act_sem.at[s])

    def work(s):
        @pl.when(s == 0)
        def _():
            for k in range(n - 1):
                seen_copy(k).start()

        chunk = jnp.concatenate([land[0, s], land[1, s]], axis=0).astype(F32)
        act = layer_norm(chunk, ln_ref[0:1, :], ln_ref[1:2, :]).astype(BF)
        act_buf[s] = act
        act_copy(s).start()
        place = pl.ds(pl.multiple_of(s * rows, rows), rows)
        for k in range(3):
            qkv_ref[place, k * cols : (k + 1) * cols] = dot(act, w_ref[k], ((1,), (0,))).astype(BF)

    ring_gather(n, x_ref, land, send_sem, recv_sem, peers, work)
    seen_buf[me] = seen_ref[...]
    for k in range(n - 1):
        seen_copy(k).wait()
    seen_all[...] = seen_buf[...]

    def written(s, carry):
        act_copy(s).wait()
        return carry

    lax.fori_loop(0, n, written, 0)


def ring_scratch(n, rows, width):
    return [pltpu.VMEM((2, n, rows // 2, width), BF)], [
        pltpu.SemaphoreType.DMA((2, n - 1)),
        pltpu.SemaphoreType.DMA((2, n - 1)),
    ]


VMEM_SPEC = pl.BlockSpec(memory_space=pltpu.VMEM)
ANY_SPEC = pl.BlockSpec(memory_space=pl.ANY)


def first_gather(n, x, seen, ln_params, w):
    rows, width = x.shape
    cols = w.shape[2]
    buf, sems = ring_scratch(n, rows, width)
    return pl.pallas_call(
        functools.partial(first_kernel, n),
        in_specs=[VMEM_SPEC] * 4,
        out_specs=[ANY_SPEC, VMEM_SPEC, VMEM_SPEC],
        out_shape=[
            jax.ShapeDtypeStruct((n * rows, width), BF),
            jax.ShapeDtypeStruct((n * rows, 3 * cols), BF),
            jax.ShapeDtypeStruct((n,) + seen.shape, F32),
        ],
        scratch_shapes=buf
        + [pltpu.VMEM((n, rows, width), BF), pltpu.VMEM((n,) + seen.shape, F32)]
        + sems
        + [pltpu.SemaphoreType.DMA((n,)), pltpu.SemaphoreType.DMA((2, n - 1))],
        compiler_params=pltpu.CompilerParams(
            collective_id=1, has_side_effects=True, vmem_limit_bytes=56 << 20
        ),
        cost_estimate=pl.CostEstimate(
            flops=6 * n * rows * width * cols, transcendentals=0, bytes_accessed=40 << 20
        ),
    )(x, seen, ln_params, w)


def back_kernel(n, x_ref, w_ref, all_ref, out_ref, land, send_sem, recv_sem, all_sem):
    rows = x_ref.shape[0]
    half = rows // 2

    def all_copy(d, s):
        place = pl.ds(pl.multiple_of(s * rows + d * half, half), half)
        return pltpu.make_async_copy(land.at[d, s], all_ref.at[place], all_sem.at[d, s])

    def work(s):
        for d in range(2):
            all_copy(d, s).start()
        chunk = jnp.concatenate([land[0, s], land[1, s]], axis=0)
        place = pl.ds(pl.multiple_of(s * rows, rows), rows)
        out_ref[place, :] = dot(chunk, w_ref[...], ((1,), (1,))).astype(BF)

    ring_gather(n, x_ref, land, send_sem, recv_sem, None, work)

    def written(s, carry):
        for d in range(2):
            all_copy(d, s).wait()
        return carry

    lax.fori_loop(0, n, written, 0)


def back_gather(n, x, w):
    rows, width = x.shape
    buf, sems = ring_scratch(n, rows, width)
    return pl.pallas_call(
        functools.partial(back_kernel, n),
        in_specs=[VMEM_SPEC] * 2,
        out_specs=[ANY_SPEC, VMEM_SPEC],
        out_shape=[
            jax.ShapeDtypeStruct((n * rows, width), BF),
            jax.ShapeDtypeStruct((n * rows, w.shape[0]), BF),
        ],
        scratch_shapes=buf + sems + [pltpu.SemaphoreType.DMA((2, n))],
        compiler_params=pltpu.CompilerParams(
            collective_id=2, has_side_effects=True, vmem_limit_bytes=40 << 20
        ),
        cost_estimate=pl.CostEstimate(
            flops=2 * n * rows * width * w.shape[0], transcendentals=0, bytes_accessed=40 << 20
        ),
    )(x, w)


def dp_sum(x, n_dp, axis):
    swap = lambda y, bit: lax.ppermute(y, "dp", [(i, i ^ bit) for i in range(n_dp)])
    core = lax.rem(lax.axis_index("dp"), 2)
    half = x.shape[axis] // 2
    part = lambda c: lax.dynamic_slice_in_dim(x, c * half, half, axis)
    mine = (part(core).astype(F32) + swap(part(1 - core), 1).astype(F32)).astype(BF)
    bit = 2
    while bit < n_dp:
        mine = (mine.astype(F32) + swap(mine, bit).astype(F32)).astype(BF)
        bit *= 2
    other = swap(mine, 1)
    first = jnp.where(core == 0, mine, other)
    second = jnp.where(core == 0, other, mine)
    return jnp.concatenate([first, second], axis=axis)


def norm_stats(rows):
    mean_row = jnp.mean(rows, axis=-1, keepdims=True)
    centered = rows - mean_row
    variance = jnp.mean(centered * centered, axis=-1, keepdims=True)
    scale = lax.rsqrt(variance + ln_eps)
    return centered * scale, scale


def layer_norm(rows, gain, shift):
    return norm_stats(rows)[0] * gain + shift


def layer_norm_back(rows, gain, e):
    n, scale = norm_stats(rows)
    eg = e * gain
    dv = scale * (
        eg - jnp.mean(eg, axis=-1, keepdims=True) - n * jnp.mean(eg * n, axis=-1, keepdims=True)
    )
    return dv, jnp.stack([jnp.sum(e * n, axis=0), jnp.sum(e, axis=0)])


def seen_mask(thr_ref, q0, shape):
    thr = thr_ref[: shape[0], :]
    thr = jnp.concatenate([thr] * (shape[1] // thr.shape[1]), axis=1)
    q_pos = (q0 + lax.broadcasted_iota(jnp.int32, shape, 1)).astype(F32)
    return q_pos >= thr


def q_blocks():
    return [(q0, max(PREFIX_MAX, q0 + Q_BLOCK)) for q0 in range(0, SLOT, Q_BLOCK)]


def to_order(places, src_ref, dst_ref):
    half = SLOT // places.shape[0]
    for j in range(places.shape[0]):
        place = pl.ds(pl.multiple_of(places[j], half), half)
        dst_ref[j * half : (j + 1) * half, :] = src_ref[place, :]


def from_order(places, q0, value, dst_ref, columns):
    half = SLOT // places.shape[0]
    for i in range(value.shape[0] // half):
        place = pl.ds(pl.multiple_of(places[q0 // half + i], half), half)
        dst_ref[place, columns] = value[i * half : (i + 1) * half, :]


def attn_forward_kernel(places, thr_ref, q_in, k_in, v_in, o_ref, lse_ref, q_ref, k_ref, v_ref):
    c = HD**-0.5 * LOG2E
    for src, dst in ((q_in, q_ref), (k_in, k_ref), (v_in, v_ref)):
        to_order(places, src, dst)
    for q0, klim in q_blocks():
        raw = dot(k_ref[:klim, :], q_ref[q0 : q0 + Q_BLOCK, :], ((1,), (1,)))
        raw = jnp.where(seen_mask(thr_ref, q0, raw.shape), raw, masked_score)
        top = jnp.max(raw, axis=0, keepdims=True)
        p = jnp.exp2((raw - top) * c)
        total = jnp.sum(p, axis=0, keepdims=True)
        out = dot(v_ref[:klim, :], p.astype(BF), ((0,), (0,))) / total
        from_order(places, q0, out.T.astype(BF), o_ref, slice(None))
        lse_ref[0, :, q0 : q0 + Q_BLOCK] = top * c + jnp.log2(total)


def attn_backward_kernel(
    places, thr_ref, q_in, k_in, v_in, do_in, lse_ref, d_ref,
    q_ref, k_ref, v_ref, do_ref, dk_sum, dv_sum,
):
    scale = HD**-0.5
    head, heads = pl.program_id(0), d_ref.shape[1] // (3 * HD)
    columns = lambda i: pl.ds(pl.multiple_of((i * heads + head) * HD, HD), HD)
    for src, dst in ((q_in, q_ref), (k_in, k_ref), (v_in, v_ref), (do_in, do_ref)):
        to_order(places, src, dst)
    dk_sum[...] = jnp.zeros_like(dk_sum)
    dv_sum[...] = jnp.zeros_like(dv_sum)
    for q0, klim in q_blocks():
        rows = slice(q0, q0 + Q_BLOCK)
        k, q, do = k_ref[:klim, :], q_ref[rows, :], do_ref[rows, :]
        raw = dot(k, q, ((1,), (1,)))
        p = jnp.exp2(raw * (scale * LOG2E) - lse_ref[0, :, rows])
        p = jnp.where(seen_mask(thr_ref, q0, raw.shape), p, 0.0)
        dv_sum[:klim, :] += dot(p.astype(BF), do, ((1,), (0,)))
        dp = dot(v_ref[:klim, :], do, ((1,), (1,)))
        delta = jnp.sum(p * dp, axis=0, keepdims=True)
        ds = (p * (dp - delta) * scale).astype(BF)
        dk_sum[:klim, :] += dot(ds, q, ((1,), (0,)))
        dq = dot(k, ds, ((0,), (0,))).T.astype(BF)
        from_order(places, q0, dq, d_ref, columns(0))
    from_order(places, 0, dk_sum[...].astype(BF), d_ref, columns(1))
    from_order(places, 0, dv_sum[...].astype(BF), d_ref, columns(2))


def cost(products, heads):
    cells = sum(Q_BLOCK * klim for _, klim in q_blocks()) * heads
    return pl.CostEstimate(
        flops=products * 2 * cells * HD, transcendentals=cells, bytes_accessed=8 * SLOT * HD * heads
    )


SMEM_SPEC = pl.BlockSpec(memory_space=pltpu.SMEM)
ATTN_PARAMS = pltpu.CompilerParams(vmem_limit_bytes=56 << 20)


def head_spec(k, heads):
    return pl.BlockSpec((SLOT, HD), lambda h: (0, k * heads + h))


def attn_forward(places, thr, qkv):
    heads = qkv.shape[1] // (3 * HD)
    lse = pl.BlockSpec((1, 1, SLOT), lambda h: (h, 0, 0))
    return pl.pallas_call(
        attn_forward_kernel,
        grid=(heads,),
        in_specs=[SMEM_SPEC, pl.BlockSpec((SLOT, 128), lambda h: (0, 0))]
        + [head_spec(k, heads) for k in range(3)],
        out_specs=[head_spec(0, heads), lse],
        out_shape=[
            jax.ShapeDtypeStruct((SLOT, heads * HD), BF),
            jax.ShapeDtypeStruct((heads, 1, SLOT), F32),
        ],
        scratch_shapes=[pltpu.VMEM((SLOT, HD), BF)] * 3,
        compiler_params=ATTN_PARAMS,
        cost_estimate=cost(2, heads),
    )(places, thr, qkv, qkv, qkv)


def attn_backward(places, thr, qkv, d_context, lse):
    heads = qkv.shape[1] // (3 * HD)
    return pl.pallas_call(
        attn_backward_kernel,
        grid=(heads,),
        in_specs=[SMEM_SPEC, pl.BlockSpec((SLOT, 128), lambda h: (0, 0))]
        + [head_spec(k, heads) for k in range(3)]
        + [head_spec(0, heads), pl.BlockSpec((1, 1, SLOT), lambda h: (h, 0, 0))],
        out_specs=pl.BlockSpec(qkv.shape, lambda h: (0, 0)),
        out_shape=jax.ShapeDtypeStruct(qkv.shape, BF),
        scratch_shapes=[pltpu.VMEM((SLOT, HD), BF)] * 4 + [pltpu.VMEM((SLOT, HD), F32)] * 2,
        compiler_params=ATTN_PARAMS,
        cost_estimate=cost(5, heads),
    )(places, thr, qkv, qkv, qkv, d_context, lse)


def step_rate(update_sq, weight_sq, n_real):
    update_rms = jnp.sqrt(update_sq / n_real)
    weight_rms = jnp.sqrt(weight_sq / n_real)
    return rate_base * jnp.maximum(eps_two, weight_rms) / jnp.maximum(1.0, update_rms / clip_bound)


def apply_step(weight, grad, row_new, col_new, row_mean, rate):
    row = lax.rsqrt(row_new) * (rate * jnp.sqrt(row_mean))
    return weight.astype(F32) - grad * (row[:, None] * lax.rsqrt(col_new)[None, :])


def pair_kernel(factors, *refs):
    g_ref, u_ref = refs[:2]
    o_ref = refs[-1]
    g, u = g_ref[...].astype(F32), u_ref[...].astype(F32)
    if factors:
        wg_ref, wu_ref, row_ref, cg_ref, cu_ref = refs[2:7]
        row = row_ref[...]
        g = wg_ref[...].astype(F32) - g * (row * cg_ref[...])
        u = wu_ref[...].astype(F32) - u * (row * cu_ref[...])
    o_ref[:, 0, :] = g
    o_ref[:, 1, :] = u


def pair_rows(gate, up, step=None):
    ff, width = gate.shape
    block = 96
    grid = (-(-ff // block),)
    wide = pl.BlockSpec((block, width), lambda i: (i, 0))
    args, specs = [gate, up], [wide, wide]
    if step is not None:
        w_gu, row, col_gate, col_up = step
        shift = w_gu.shape[0] // 2 // block
        column = pl.BlockSpec((block, 1), lambda i: (i, 0))
        args += [w_gu, w_gu, row[None, :], col_gate[:, None], col_up[:, None]]
        specs += [
            wide,
            pl.BlockSpec((block, width), lambda i: (i + shift, 0)),
            pl.BlockSpec((1, width), lambda i: (0, 0)),
            column,
            column,
        ]
    return pl.pallas_call(
        functools.partial(pair_kernel, step is not None),
        grid=grid,
        in_specs=specs,
        out_specs=pl.BlockSpec((block, 2, width), lambda i: (i, 0, 0)),
        out_shape=jax.ShapeDtypeStruct((ff, 2, width), F32),
        compiler_params=pltpu.CompilerParams(vmem_limit_bytes=40 << 20),
        cost_estimate=pl.CostEstimate(flops=8 * ff * width, transcendentals=0, bytes_accessed=16 * ff * width),
    )(*args)


def tie(x, after):
    return lax.optimization_barrier((x, after))[0]


def exchange_kernel(n_dp, n, x_ref, o_ref, dp_buf, rows, part_buf, total, whole, sems):
    me_d, me = lax.axis_index("dp"), lax.axis_index("tensor")
    width = x_ref.shape[1] // n
    columns = lambda t: pl.ds(pl.multiple_of(t * width, width), width)
    dp_peers = [(k - 1, lax.rem(me_d + k, n_dp)) for k in range(1, n_dp)]
    peers = [(k - 1, lax.rem(me + k, n)) for k in range(1, n)]
    barrier = pltpu.get_barrier_semaphore()
    for _, d in dp_peers:
        pl.semaphore_signal(barrier, inc=1, device_id={"dp": d}, device_id_type=pl.DeviceIdType.MESH)
    for _, t in peers:
        pl.semaphore_signal(barrier, inc=1, device_id={"tensor": t}, device_id_type=pl.DeviceIdType.MESH)
    pl.semaphore_wait(barrier, n_dp + n - 2)

    def push(stage, src, dst, k, device):
        copy = pltpu.make_async_remote_copy(
            src_ref=src, dst_ref=dst, send_sem=sems.at[0, stage, k], recv_sem=sems.at[1, stage, k],
            device_id=device, device_id_type=pl.DeviceIdType.MESH,
        )
        copy.start()
        return copy

    first = [push(0, x_ref.at[pl.ds(0, 8)], dp_buf.at[me_d], k, {"dp": d}) for k, d in dp_peers]
    rows[...] = x_ref[...]
    dp_buf[me_d] = x_ref[0:8, :]
    for copy in first:
        copy.wait()
    rows[0:8, :] = sum(dp_buf[d] for d in range(n_dp))
    second = [push(1, rows.at[:, columns(t)], part_buf.at[me], k, {"tensor": t}) for k, t in peers]
    part_buf[me] = rows[:, columns(me)]
    for copy in second:
        copy.wait()
    total[...] = sum(part_buf[t] for t in range(n))
    third = [push(2, total, whole.at[me], k, {"tensor": t}) for k, t in peers]
    whole[me] = total[...]
    for copy in third:
        copy.wait()
    for t in range(n):
        o_ref[:, t * width : (t + 1) * width] = whole[t]


def exchange(x, n_dp, n):
    height, width = x.shape
    slots = pltpu.VMEM((n, height, width // n), F32)
    return pl.pallas_call(
        functools.partial(exchange_kernel, n_dp, n),
        out_shape=jax.ShapeDtypeStruct(x.shape, F32),
        in_specs=[pl.BlockSpec(memory_space=pltpu.VMEM)],
        out_specs=pl.BlockSpec(memory_space=pltpu.VMEM),
        scratch_shapes=[
            pltpu.VMEM((n_dp, 8, width), F32),
            pltpu.VMEM(x.shape, F32),
            slots,
            pltpu.VMEM((height, width // n), F32),
            slots,
            pltpu.SemaphoreType.DMA((2, 3, max(n, n_dp) - 1)),
        ],
        compiler_params=pltpu.CompilerParams(collective_id=0, has_side_effects=True),
    )(x)


def on_device(
    layer_in,
    cotangent,
    lengths,
    prefix,
    pad_mask,
    clusters,
    qkv_w,
    out_w,
    gate_up_w,
    down_w,
    ln_params,
    qkv_row,
    qkv_col,
    out_row,
    out_col,
    gu_row,
    gu_col,
    down_row,
    down_col,
    ln_second,
):
    n_data = lax.axis_size("dp")
    n_tensor = lax.axis_size("tensor")
    tensor_rank = lax.axis_index("tensor")
    data_rank = lax.axis_index("dp")
    rows_dev, width = layer_in.shape
    cols_dev = qkv_w.shape[2]
    heads_dev = cols_dev // HD
    ff_dev = gate_up_w.shape[2]
    ff_pad = -(-ff_dev // 128) * 128
    n_clusters = max(2, n_data // 2)
    decay_rate = 1.0 - STEP ** (-0.8)
    seq_length = lengths[0]
    seq_prefix = prefix[0]
    ring = Ring(n_tensor)

    onehot = (clusters[:, None] == jnp.arange(n_clusters, dtype=jnp.int32)[None, :]).astype(F32)
    counts = jnp.sum(onehot, axis=0)
    own_row = jnp.sum(
        jnp.where((jnp.arange(n_data, dtype=jnp.int32) == data_rank)[:, None], onehot, 0.0), axis=0
    )
    seq_weight = jnp.sum(own_row / jnp.maximum(counts, 1.0))
    own_pos = tensor_rank * rows_dev + jnp.arange(rows_dev, dtype=jnp.int32)
    live_rows = ((own_pos < seq_length) & (pad_mask == 1)).astype(F32)
    grad_out = cotangent.astype(F32) * (live_rows * seq_weight)[:, None]
    grad_low = grad_out.astype(BF)

    key_live = (own_pos == 0) | (own_pos < seq_length) & (pad_mask == 1)
    seen_from = jnp.where(key_live, jnp.where(own_pos < seq_prefix, 0, own_pos), 2 * SLOT)
    seen = jnp.broadcast_to(seen_from.astype(F32)[None], (8, rows_dev))

    col_index = tensor_rank * ff_dev + jnp.arange(ff_pad, dtype=jnp.int32)
    ff_real = ((col_index < FF) & (jnp.arange(ff_pad) < ff_dev)).astype(F32)
    ff_mask = ff_real[:ff_dev]

    layer_own = layer_in.astype(F32)
    places = ring.places(rows_dev)
    act_one_all, qkv, seen_all = first_gather(
        n_tensor, layer_in, seen, ln_params, jnp.transpose(qkv_w, (1, 0, 2))
    )
    thr = jnp.broadcast_to(seen_all[:, 0].reshape(SLOT, 1), (SLOT, 128))

    grad_chunks = [jnp.concatenate(p, axis=0) for p in ring.gather(tie(grad_low, qkv))]
    pad = ((0, ff_pad - ff_dev), (0, 0))
    gate_up_late, down_late = tie(
        (jnp.transpose(gate_up_w, (2, 1, 0)), down_w), grad_chunks[min(3, n_tensor - 1)]
    )
    w_gu = jnp.concatenate([jnp.pad(gate_up_late[:, i], pad) for i in range(2)], axis=0)
    w_down = jnp.pad(down_late, pad)
    context, lse = attn_forward(places, thr, qkv)
    part_of = lambda x, s: x[s * rows_dev : (s + 1) * rows_dev]
    attn_own = ring.scatter(lambda s: dot(part_of(context, s), out_w, ((1,), (0,))))
    hidden_own = layer_own + attn_own
    norm_two = layer_norm(hidden_own, ln_params[2], ln_params[3]).astype(BF)

    act_two, inner, d_gu = [], [], []
    for s, pair in enumerate(ring.gather(norm_two)):
        act = jnp.concatenate(pair, axis=0)
        act_two.append(act)
        gate_up = dot(act, w_gu, ((1,), (1,)))
        gate, up = gate_up[:, :ff_pad], gate_up[:, ff_pad:]
        gelu_gate, gelu_back = jax.vjp(jax.nn.gelu, gate)
        inner.append((gelu_gate * up * ff_real).astype(BF))
        d_inner = dot(grad_chunks[s], w_down, ((1,), (1,))) * ff_real
        d_gate = gelu_back(d_inner * up)[0]
        d_gu.append(jnp.concatenate([d_gate, d_inner * gelu_gate], axis=1).astype(BF))
    d_norm_two = ring.scatter(lambda s: dot(d_gu[s], w_gu, ((1,), (0,))))
    d_hidden_ln, ln_two_part = layer_norm_back(hidden_own, ln_params[2], d_norm_two)
    d_hidden = grad_out + d_hidden_ln
    d_hidden_all, d_context = back_gather(n_tensor, d_hidden.astype(BF), out_w)

    ffn_own = ring.scatter(lambda s: dot(tie(inner[s], d_context), w_down, ((1,), (0,))))
    layer_out = (hidden_own + ffn_own).astype(BF)
    rows_of = lambda chunks: jnp.concatenate(tie(chunks, d_context), axis=0)
    inner_all, grad_all, d_gu_all, act_two_all = map(rows_of, (inner, grad_chunks, d_gu, act_two))
    across = lambda a, b: dot(a, b, ((0,), (0,)))
    down_part = across(inner_all, grad_all)[:ff_dev].astype(BF)
    gate_part = across(d_gu_all[:, :ff_pad], tie(act_two_all, down_part))[:ff_dev].astype(BF)
    up_part = across(d_gu_all[:, ff_pad:], tie(act_two_all, gate_part))[:ff_dev].astype(BF)
    d_qkv = attn_backward(places, thr, qkv, tie(d_context, up_part), lse)
    qkv_part = across(act_one_all, d_qkv).astype(BF)
    out_part = across(context, tie(d_hidden_all, qkv_part)).astype(BF)
    down_low = dp_sum(down_part, n_data, 1)
    gate_low = dp_sum(gate_part, n_data, 1)
    up_low = dp_sum(up_part, n_data, 1)
    qkv_low = dp_sum(qkv_part, n_data, 0)
    out_low = dp_sum(out_part, n_data, 1)
    w_qkv = tie(qkv_w, d_context).reshape(width, 3 * cols_dev)
    d_norm_one = ring.scatter(lambda s: dot(part_of(d_qkv, s), w_qkv, ((1,), (1,))))
    d_input_ln, ln_one_part = layer_norm_back(layer_own, ln_params[0], d_norm_one)
    input_grad = (d_hidden + d_input_ln).astype(BF)

    qkv_sum, out_sum, down_sum = qkv_low.astype(F32), out_low.astype(F32), down_low.astype(F32)
    gu_sum = (gate_low.astype(F32), up_low.astype(F32))
    gu_weights = (w_gu[:ff_dev], w_gu[ff_pad : ff_pad + ff_dev])
    gu_grad = pair_rows(gate_low, up_low)
    out_t, down_t, gu_t, qkv_t = tie((out_w, down_w, gu_weights, w_qkv), d_qkv)
    ff_col = ff_mask[:, None]
    blend = lambda old, total: decay_rate * old + (1.0 - decay_rate) * total
    square = lambda grad: grad * grad + eps_one
    square_sum = lambda w: jnp.sum(jnp.square(w.astype(F32)))

    qkv_sq, gu_sq = square(qkv_sum), [square(g) * ff_col for g in gu_sum]
    out_sq, down_sq = square(out_sum), square(down_sum) * ff_col
    qkv_col_new = blend(qkv_col.reshape(-1), jnp.sum(qkv_sq, axis=0) / width)
    gu_col_new = [blend(gu_col[i], jnp.sum(gu_sq[i], axis=1) / width) for i in range(2)]
    out_row_new = blend(out_row, jnp.sum(out_sq, axis=1) / width)
    down_row_new = blend(down_row, jnp.sum(down_sq, axis=1) / width)
    clean = lambda grad: grad * grad
    scalars = jnp.stack(
        [
            square_sum(qkv_t),
            sum(jnp.sum(jnp.square(w.astype(F32)) * ff_col) for w in gu_t),
            square_sum(out_t),
            jnp.sum(jnp.square(down_t.astype(F32)) * ff_col),
            jnp.sum(out_row_new),
            jnp.sum(down_row_new * ff_mask),
        ]
    )
    packed = jnp.concatenate(
        [
            ln_one_part,
            ln_two_part,
            jnp.pad(scalars / n_data, (0, width - scalars.shape[0]))[None],
            jnp.zeros((3, width), F32),
            jnp.stack(
                [
                    jnp.sum(qkv_sq, axis=1),
                    jnp.sum(clean(qkv_sum) / qkv_col_new[None, :], axis=1),
                    sum(jnp.sum(sq, axis=0) for sq in gu_sq),
                    sum(
                        jnp.sum(clean(g) * (ff_mask / col)[:, None], axis=0)
                        for g, col in zip(gu_sum, gu_col_new)
                    ),
                    jnp.sum(out_sq, axis=0),
                    jnp.sum(clean(out_sum) / out_row_new[:, None], axis=0),
                    jnp.sum(down_sq, axis=0),
                    jnp.sum(clean(down_sum) * (ff_mask / down_row_new)[:, None], axis=0),
                ]
            ),
        ],
        axis=0,
    )
    packed = exchange(packed, n_data, n_tensor)
    ln_tot = packed[:4]
    qkv_wtot, gu_wtot, out_wtot, down_wtot, out_rtot, down_rtot = (packed[4, i] for i in range(6))
    qkv_tot, qkv_usq, gu_tot, gu_usq, out_tot, out_usq, down_tot, down_usq = (
        packed[8 + i] for i in range(8)
    )

    qkv_cols_all = 3 * cols_dev * n_tensor
    out_rows_all = cols_dev * n_tensor
    qkv_row_new = blend(qkv_row, qkv_tot / qkv_cols_all)
    qkv_mean = jnp.sum(qkv_row_new) / width
    gu_row_new = blend(gu_row, gu_tot / (2 * FF))
    gu_mean = jnp.sum(gu_row_new) / width
    out_col_new = blend(out_col, out_tot / out_rows_all)
    out_mean = out_rtot / out_rows_all
    down_col_new = blend(down_col, down_tot / FF)
    down_mean = down_rtot / FF
    qkv_rate = step_rate(jnp.sum(qkv_usq / qkv_row_new) * qkv_mean, qkv_wtot, width * qkv_cols_all)
    gu_rate = step_rate(jnp.sum(gu_usq / gu_row_new) * gu_mean, gu_wtot, width * 2 * FF)
    out_rate = step_rate(jnp.sum(out_usq / out_col_new) * out_mean, out_wtot, out_rows_all * width)
    down_rate = step_rate(jnp.sum(down_usq / down_col_new) * down_mean, down_wtot, FF * width)
    qkv_new = apply_step(w_qkv, qkv_sum, qkv_row_new, qkv_col_new, qkv_mean, qkv_rate)
    out_new = apply_step(out_w, out_sum, out_row_new, out_col_new, out_mean, out_rate)
    down_new = apply_step(down_w, down_sum, down_row_new, down_col_new, down_mean, down_rate)
    gu_scale = lax.rsqrt(gu_row_new) * (gu_rate * jnp.sqrt(gu_mean))
    gu_new = pair_rows(gate_low, up_low, (w_gu, gu_scale, *map(lax.rsqrt, gu_col_new)))
    ln_second_new = blend(ln_second, ln_tot * ln_tot + eps_one)
    ln_update = ln_tot * lax.rsqrt(ln_second_new)
    ln_urms = jnp.sqrt(jnp.mean(ln_update * ln_update, axis=1, keepdims=True))
    ln_wrms = jnp.sqrt(jnp.mean(ln_params * ln_params, axis=1, keepdims=True))
    ln_new = ln_params - rate_base * jnp.maximum(eps_two, ln_wrms) * ln_update / jnp.maximum(
        1.0, ln_urms / clip_bound
    )
    qkv_back = lambda x: x.reshape(qkv_w.shape)
    return (
        layer_out,
        input_grad,
        qkv_back(qkv_sum),
        qkv_back(qkv_new),
        qkv_row_new,
        qkv_col_new.reshape(3, -1),
        out_sum,
        out_new,
        out_row_new,
        out_col_new,
        jnp.transpose(gu_grad, (2, 1, 0)),
        jnp.transpose(gu_new, (2, 1, 0)),
        gu_row_new,
        jnp.stack(gu_col_new),
        down_sum,
        down_new,
        down_row_new,
        down_col_new,
        ln_tot,
        ln_second_new,
        ln_new,
    )


def solution(mesh):
    in_specs = (
        P(("dp", "tensor"), None),
        P(("dp", "tensor"), None),
        P("dp"),
        P("dp"),
        P(("dp", "tensor")),
        P(),
        P(None, None, "tensor"),
        P("tensor", None),
        P(None, None, "tensor"),
        P("tensor", None),
        P(),
        P(),
        P(None, "tensor"),
        P("tensor"),
        P(),
        P(),
        P(None, "tensor"),
        P("tensor"),
        P(),
        P(),
    )
    out_specs = (
        P(("dp", "tensor"), None),
        P(("dp", "tensor"), None),
        P(None, None, "tensor"),
        P(None, None, "tensor"),
        P(),
        P(None, "tensor"),
        P("tensor", None),
        P("tensor", None),
        P("tensor"),
        P(),
        P(None, None, "tensor"),
        P(None, None, "tensor"),
        P(),
        P(None, "tensor"),
        P("tensor", None),
        P("tensor", None),
        P("tensor"),
        P(),
        P(),
        P(),
        P(),
    )
    return jax.shard_map(
        on_device, mesh=mesh, in_specs=in_specs, out_specs=out_specs, check_vma=False
    )
```

```python
import functools

import jax
import jax.numpy as jnp
from jax import lax
from jax.experimental import pallas as pl
from jax.experimental.pallas import tpu as pltpu
from jax.sharding import PartitionSpec as P

HD = 128
FF = 5461
SLOT = 2048
STEP = 10
PREFIX_MAX = SLOT // 2
Q_BLOCK = 512

ln_eps = 1e-05
eps_one = 1e-30
eps_two = 0.001
clip_bound = 1.0
rate_base = 1.0
masked_score = -1e30
LOG2E = 1.4426950408889634
BF = jnp.bfloat16
F32 = jnp.float32


def dot(a, b, dims):
    return lax.dot_general(a, b, (dims, ((), ())), preferred_element_type=F32)


def ring_order(n):
    b_size = 2 if n <= 8 else 4
    a_size = n // b_size
    order = []
    for a in range(a_size):
        cols = list(range(1, b_size))
        order += [a * b_size + c for c in (cols[::-1] if a % 2 else cols)]
    for a in range(a_size - 1, -1, -1):
        order.append(a * b_size)
    return order


class Ring:
    def __init__(self, n):
        self.n = n
        order = ring_order(n)
        self.fw = [(order[i], order[(i + 1) % n]) for i in range(n)]
        self.bw = [(order[i], order[(i - 1) % n]) for i in range(n)]
        place = [0] * n
        for p, t in enumerate(order):
            place[t] = p
        self.place = jnp.array(place, jnp.int32)
        self.pos = self.place[lax.axis_index("tensor")]

    def step(self, a, b):
        return lax.ppermute(a, "tensor", self.fw), lax.ppermute(b, "tensor", self.bw)

    def halves(self, x):
        half = x.shape[0] // 2
        return x[:half], x[half:]

    def scatter_order(self):
        return list(range(1, self.n)) + [0]

    def add(self, received, term, after=()):
        term = lax.optimization_barrier((term, after))[0]
        parts = self.halves(term)
        if received is not None:
            parts = tuple(r.astype(F32) + t for r, t in zip(received, parts))
        return parts

    def low(self, parts):
        return tuple(p.astype(BF) for p in parts)

    def send(self, parts):
        return self.step(*self.low(parts))

    def places(self, rows):
        t = jnp.arange(self.n, dtype=jnp.int32)
        step = self.place[t] - self.pos
        first = lax.rem(2 * self.n - step, self.n) * rows
        second = lax.rem(step + self.n, self.n) * rows + rows // 2
        return jnp.stack([first, second], axis=1).reshape(-1)


PUSH = pl.DeviceIdType.MESH


def pick(index, table):
    out = jnp.int32(table[0])
    for k in range(1, len(table)):
        out = jnp.where(index == k, jnp.int32(table[k]), out)
    return out


def ring_gather(n, x_ref, land, send_sem, recv_sem, peers, work):
    order = ring_order(n)
    pos = pick(lax.axis_index("tensor"), [order.index(t) for t in range(n)])
    ahead = pick(lax.rem(pos + 1, n), order)
    behind = pick(lax.rem(pos + n - 1, n), order)
    barrier = pltpu.get_barrier_semaphore()
    greet = [ahead, behind] if peers is None else peers
    for t in greet:
        pl.semaphore_signal(barrier, inc=1, device_id={"tensor": t}, device_id_type=PUSH)
    half = x_ref.shape[0] // 2
    land[0, 0] = x_ref[:half, :]
    land[1, 0] = x_ref[half:, :]
    pl.semaphore_wait(barrier, len(greet))

    def copy(d, s):
        return pltpu.make_async_remote_copy(
            src_ref=land.at[d, s],
            dst_ref=land.at[d, s + 1],
            send_sem=send_sem.at[d, s],
            recv_sem=recv_sem.at[d, s],
            device_id={"tensor": (ahead, behind)[d]},
            device_id_type=PUSH,
        )

    def step(s, carry):
        for d in range(2):

            @pl.when(s > 0)
            def _():
                copy(d, s - 1).wait_recv()

            @pl.when(s < n - 1)
            def _():
                copy(d, s).start()

        work(s)
        return carry

    lax.fori_loop(0, n, step, 0)

    def sent(s, carry):
        for d in range(2):
            copy(d, s).wait_send()
        return carry

    lax.fori_loop(0, n - 1, sent, 0)


def first_kernel(
    n, x_ref, seen_ref, ln_ref, w_ref, act_ref, qkv_ref, seen_all,
    land, act_buf, seen_buf, send_sem, recv_sem, act_sem, seen_sem,
):
    rows, cols = x_ref.shape[0], w_ref.shape[2]
    me = lax.axis_index("tensor")
    peers = [lax.rem(me + k, n) for k in range(1, n)]

    def seen_copy(k):
        return pltpu.make_async_remote_copy(
            src_ref=seen_ref, dst_ref=seen_buf.at[me], send_sem=seen_sem.at[0, k],
            recv_sem=seen_sem.at[1, k], device_id={"tensor": peers[k]}, device_id_type=PUSH,
        )

    def act_copy(s):
        place = pl.ds(pl.multiple_of(s * rows, rows), rows)
        return pltpu.make_async_copy(act_buf.at[s], act_ref.at[place], act_sem.at[s])

    def work(s):
        @pl.when(s == 0)
        def _():
            for k in range(n - 1):
                seen_copy(k).start()

        chunk = jnp.concatenate([land[0, s], land[1, s]], axis=0).astype(F32)
        act = layer_norm(chunk, ln_ref[0:1, :], ln_ref[1:2, :]).astype(BF)
        act_buf[s] = act
        act_copy(s).start()
        place = pl.ds(pl.multiple_of(s * rows, rows), rows)
        for k in range(3):
            qkv_ref[place, k * cols : (k + 1) * cols] = dot(act, w_ref[k], ((1,), (0,))).astype(BF)

    ring_gather(n, x_ref, land, send_sem, recv_sem, peers, work)
    seen_buf[me] = seen_ref[...]
    for k in range(n - 1):
        seen_copy(k).wait()
    seen_all[...] = seen_buf[...]

    def written(s, carry):
        act_copy(s).wait()
        return carry

    lax.fori_loop(0, n, written, 0)


def ring_scratch(n, rows, width):
    return [pltpu.VMEM((2, n, rows // 2, width), BF)], [
        pltpu.SemaphoreType.DMA((2, n - 1)),
        pltpu.SemaphoreType.DMA((2, n - 1)),
    ]


VMEM_SPEC = pl.BlockSpec(memory_space=pltpu.VMEM)
ANY_SPEC = pl.BlockSpec(memory_space=pl.ANY)


def first_gather(n, x, seen, ln_params, w):
    rows, width = x.shape
    cols = w.shape[2]
    buf, sems = ring_scratch(n, rows, width)
    return pl.pallas_call(
        functools.partial(first_kernel, n),
        in_specs=[VMEM_SPEC] * 4,
        out_specs=[ANY_SPEC, VMEM_SPEC, VMEM_SPEC],
        out_shape=[
            jax.ShapeDtypeStruct((n * rows, width), BF),
            jax.ShapeDtypeStruct((n * rows, 3 * cols), BF),
            jax.ShapeDtypeStruct((n,) + seen.shape, F32),
        ],
        scratch_shapes=buf
        + [pltpu.VMEM((n, rows, width), BF), pltpu.VMEM((n,) + seen.shape, F32)]
        + sems
        + [pltpu.SemaphoreType.DMA((n,)), pltpu.SemaphoreType.DMA((2, n - 1))],
        compiler_params=pltpu.CompilerParams(
            collective_id=1, has_side_effects=True, vmem_limit_bytes=56 << 20
        ),
        cost_estimate=pl.CostEstimate(
            flops=6 * n * rows * width * cols, transcendentals=0, bytes_accessed=40 << 20
        ),
    )(x, seen, ln_params, w)


class DpSum:
    def __init__(self, n_dp, axis):
        self.n_dp, self.axis = n_dp, axis
        self.core = lax.rem(lax.axis_index("dp"), 2)

    def swap(self, y, bit):
        return lax.ppermute(y, "dp", [(i, i ^ bit) for i in range(self.n_dp)])

    def cores(self, x):
        half = x.shape[self.axis] // 2
        part = lambda c: lax.dynamic_slice_in_dim(x, c * half, half, self.axis)
        return (part(self.core).astype(F32) + self.swap(part(1 - self.core), 1).astype(F32)).astype(BF)

    def chips(self, mine):
        bit = 2
        while bit < self.n_dp:
            mine = (mine.astype(F32) + self.swap(mine, bit).astype(F32)).astype(BF)
            bit *= 2
        return mine

    def join(self, mine):
        other = self.swap(mine, 1)
        first = jnp.where(self.core == 0, mine, other)
        second = jnp.where(self.core == 0, other, mine)
        return jnp.concatenate([first, second], axis=self.axis)


def norm_stats(rows):
    mean_row = jnp.mean(rows, axis=-1, keepdims=True)
    centered = rows - mean_row
    variance = jnp.mean(centered * centered, axis=-1, keepdims=True)
    scale = lax.rsqrt(variance + ln_eps)
    return centered * scale, scale


def layer_norm(rows, gain, shift):
    return norm_stats(rows)[0] * gain + shift


def layer_norm_back(rows, gain, e):
    n, scale = norm_stats(rows)
    eg = e * gain
    dv = scale * (
        eg - jnp.mean(eg, axis=-1, keepdims=True) - n * jnp.mean(eg * n, axis=-1, keepdims=True)
    )
    return dv, jnp.stack([jnp.sum(e * n, axis=0), jnp.sum(e, axis=0)])


def seen_mask(thr_ref, q0, shape):
    thr = thr_ref[: shape[0], :]
    thr = jnp.concatenate([thr] * (shape[1] // thr.shape[1]), axis=1)
    q_pos = (q0 + lax.broadcasted_iota(jnp.int32, shape, 1)).astype(F32)
    return q_pos >= thr


def q_blocks():
    return [(q0, max(PREFIX_MAX, q0 + Q_BLOCK)) for q0 in range(0, SLOT, Q_BLOCK)]


def to_order(places, src_ref, dst_ref):
    half = SLOT // places.shape[0]
    for j in range(places.shape[0]):
        place = pl.ds(pl.multiple_of(places[j], half), half)
        dst_ref[j * half : (j + 1) * half, :] = src_ref[place, :]


def from_order(places, q0, value, dst_ref, columns):
    half = SLOT // places.shape[0]
    for i in range(value.shape[0] // half):
        place = pl.ds(pl.multiple_of(places[q0 // half + i], half), half)
        dst_ref[place, columns] = value[i * half : (i + 1) * half, :]


def attn_forward_kernel(places, thr_ref, q_in, k_in, v_in, o_ref, lse_ref, q_ref, k_ref, v_ref):
    c = HD**-0.5 * LOG2E
    for src, dst in ((q_in, q_ref), (k_in, k_ref), (v_in, v_ref)):
        to_order(places, src, dst)
    for q0, klim in q_blocks():
        raw = dot(k_ref[:klim, :], q_ref[q0 : q0 + Q_BLOCK, :], ((1,), (1,)))
        raw = jnp.where(seen_mask(thr_ref, q0, raw.shape), raw, masked_score)
        top = jnp.max(raw, axis=0, keepdims=True)
        p = jnp.exp2((raw - top) * c)
        total = jnp.sum(p, axis=0, keepdims=True)
        out = dot(v_ref[:klim, :], p.astype(BF), ((0,), (0,))) / total
        from_order(places, q0, out.T.astype(BF), o_ref, slice(None))
        lse_ref[0, :, q0 : q0 + Q_BLOCK] = top * c + jnp.log2(total)


def attn_backward_kernel(
    places, thr_ref, q_in, k_in, v_in, do_in, lse_ref, d_ref,
    q_ref, k_ref, v_ref, do_ref, dk_sum, dv_sum,
):
    scale = HD**-0.5
    columns = lambda i: slice(i * HD, (i + 1) * HD)
    for src, dst in ((q_in, q_ref), (k_in, k_ref), (v_in, v_ref), (do_in, do_ref)):
        to_order(places, src, dst)
    dk_sum[...] = jnp.zeros_like(dk_sum)
    dv_sum[...] = jnp.zeros_like(dv_sum)
    for q0, klim in q_blocks():
        rows = slice(q0, q0 + Q_BLOCK)
        k, q, do = k_ref[:klim, :], q_ref[rows, :], do_ref[rows, :]
        raw = dot(k, q, ((1,), (1,)))
        p = jnp.exp2(raw * (scale * LOG2E) - lse_ref[0, :, rows])
        p = jnp.where(seen_mask(thr_ref, q0, raw.shape), p, 0.0)
        dv_sum[:klim, :] += dot(p.astype(BF), do, ((1,), (0,)))
        dp = dot(v_ref[:klim, :], do, ((1,), (1,)))
        delta = jnp.sum(p * dp, axis=0, keepdims=True)
        ds = (p * (dp - delta) * scale).astype(BF)
        dk_sum[:klim, :] += dot(ds, q, ((1,), (0,)))
        dq = dot(k, ds, ((0,), (0,))).T.astype(BF)
        from_order(places, q0, dq, d_ref, columns(0))
    from_order(places, 0, dk_sum[...].astype(BF), d_ref, columns(1))
    from_order(places, 0, dv_sum[...].astype(BF), d_ref, columns(2))


def cost(micros):
    return pl.CostEstimate(flops=int(micros * 1e9), transcendentals=0, bytes_accessed=4 << 20)


SMEM_SPEC = pl.BlockSpec(memory_space=pltpu.SMEM)
ATTN_PARAMS = pltpu.CompilerParams(vmem_limit_bytes=56 << 20)


def head_spec(k, heads):
    return pl.BlockSpec((SLOT, HD), lambda h: (0, k * heads + h))


def attn_forward(places, thr, qkv):
    heads = qkv.shape[1] // (3 * HD)
    lse = pl.BlockSpec((1, 1, SLOT), lambda h: (h, 0, 0))
    return pl.pallas_call(
        attn_forward_kernel,
        grid=(heads,),
        in_specs=[SMEM_SPEC, pl.BlockSpec((SLOT, 128), lambda h: (0, 0))]
        + [head_spec(k, heads) for k in range(3)],
        out_specs=[head_spec(0, heads), lse],
        out_shape=[
            jax.ShapeDtypeStruct((SLOT, heads * HD), BF),
            jax.ShapeDtypeStruct((heads, 1, SLOT), F32),
        ],
        scratch_shapes=[pltpu.VMEM((SLOT, HD), BF)] * 3,
        compiler_params=ATTN_PARAMS,
        cost_estimate=cost(6.5 * heads),
    )(places, thr, qkv, qkv, qkv)


def attn_backward(head, places, thr, qkv, d_context, lse):
    heads = qkv.shape[1] // (3 * HD)
    spec = lambda k: pl.BlockSpec((SLOT, HD), lambda i: (0, k))
    return pl.pallas_call(
        attn_backward_kernel,
        grid=(1,),
        in_specs=[SMEM_SPEC, pl.BlockSpec((SLOT, 128), lambda i: (0, 0))]
        + [spec(k * heads + head) for k in range(3)]
        + [spec(head), pl.BlockSpec((1, 1, SLOT), lambda i: (head, 0, 0))],
        out_specs=pl.BlockSpec((SLOT, 3 * HD), lambda i: (0, 0)),
        out_shape=jax.ShapeDtypeStruct((SLOT, 3 * HD), BF),
        scratch_shapes=[pltpu.VMEM((SLOT, HD), BF)] * 4 + [pltpu.VMEM((SLOT, HD), F32)] * 2,
        compiler_params=ATTN_PARAMS,
        cost_estimate=cost(11.5),
    )(places, thr, qkv, qkv, qkv, d_context, lse)


def step_rate(update_sq, weight_sq, n_real):
    update_rms = jnp.sqrt(update_sq / n_real)
    weight_rms = jnp.sqrt(weight_sq / n_real)
    return rate_base * jnp.maximum(eps_two, weight_rms) / jnp.maximum(1.0, update_rms / clip_bound)


def apply_step(weight, grad, row_new, col_new, row_mean, rate):
    row = lax.rsqrt(row_new) * (rate * jnp.sqrt(row_mean))
    return weight.astype(F32) - grad * (row[:, None] * lax.rsqrt(col_new)[None, :])


def pair_kernel(factors, *refs):
    g_ref, u_ref = refs[:2]
    o_ref = refs[-1]
    g, u = g_ref[...].astype(F32), u_ref[...].astype(F32)
    if factors:
        wg_ref, wu_ref, row_ref, cg_ref, cu_ref = refs[2:7]
        row = row_ref[...]
        g = wg_ref[...].astype(F32) - g * (row * cg_ref[...])
        u = wu_ref[...].astype(F32) - u * (row * cu_ref[...])
    o_ref[:, 0, :] = g
    o_ref[:, 1, :] = u


def pair_rows(gate, up, step=None):
    ff, width = gate.shape
    block = 96
    grid = (-(-ff // block),)
    wide = pl.BlockSpec((block, width), lambda i: (i, 0))
    args, specs = [gate, up], [wide, wide]
    if step is not None:
        w_gu, row, col_gate, col_up = step
        shift = w_gu.shape[0] // 2 // block
        column = pl.BlockSpec((block, 1), lambda i: (i, 0))
        args += [w_gu, w_gu, row[None, :], col_gate[:, None], col_up[:, None]]
        specs += [
            wide,
            pl.BlockSpec((block, width), lambda i: (i + shift, 0)),
            pl.BlockSpec((1, width), lambda i: (0, 0)),
            column,
            column,
        ]
    return pl.pallas_call(
        functools.partial(pair_kernel, step is not None),
        grid=grid,
        in_specs=specs,
        out_specs=pl.BlockSpec((block, 2, width), lambda i: (i, 0, 0)),
        out_shape=jax.ShapeDtypeStruct((ff, 2, width), F32),
        compiler_params=pltpu.CompilerParams(vmem_limit_bytes=40 << 20),
        cost_estimate=pl.CostEstimate(flops=8 * ff * width, transcendentals=0, bytes_accessed=16 * ff * width),
    )(*args)


def tie(x, after):
    return lax.optimization_barrier((x, after))[0]


def exchange_kernel(n_dp, n, x_ref, o_ref, dp_buf, rows, part_buf, total, whole, sems):
    me_d, me = lax.axis_index("dp"), lax.axis_index("tensor")
    width = x_ref.shape[1] // n
    columns = lambda t: pl.ds(pl.multiple_of(t * width, width), width)
    dp_peers = [(k - 1, lax.rem(me_d + k, n_dp)) for k in range(1, n_dp)]
    peers = [(k - 1, lax.rem(me + k, n)) for k in range(1, n)]
    barrier = pltpu.get_barrier_semaphore()
    for _, d in dp_peers:
        pl.semaphore_signal(barrier, inc=1, device_id={"dp": d}, device_id_type=pl.DeviceIdType.MESH)
    for _, t in peers:
        pl.semaphore_signal(barrier, inc=1, device_id={"tensor": t}, device_id_type=pl.DeviceIdType.MESH)
    pl.semaphore_wait(barrier, n_dp + n - 2)

    def push(stage, src, dst, k, device):
        copy = pltpu.make_async_remote_copy(
            src_ref=src, dst_ref=dst, send_sem=sems.at[0, stage, k], recv_sem=sems.at[1, stage, k],
            device_id=device, device_id_type=pl.DeviceIdType.MESH,
        )
        copy.start()
        return copy

    first = [push(0, x_ref.at[pl.ds(0, 8)], dp_buf.at[me_d], k, {"dp": d}) for k, d in dp_peers]
    rows[...] = x_ref[...]
    dp_buf[me_d] = x_ref[0:8, :]
    for copy in first:
        copy.wait()
    rows[0:8, :] = sum(dp_buf[d] for d in range(n_dp))
    second = [push(1, rows.at[:, columns(t)], part_buf.at[me], k, {"tensor": t}) for k, t in peers]
    part_buf[me] = rows[:, columns(me)]
    for copy in second:
        copy.wait()
    total[...] = sum(part_buf[t] for t in range(n))
    third = [push(2, total, whole.at[me], k, {"tensor": t}) for k, t in peers]
    whole[me] = total[...]
    for copy in third:
        copy.wait()
    for t in range(n):
        o_ref[:, t * width : (t + 1) * width] = whole[t]


def small_kernel(n_dp, n, x_ref, o_ref, dp_buf, total, t_buf, sems):
    me_d, me = lax.axis_index("dp"), lax.axis_index("tensor")
    dp_peers = [(k - 1, lax.rem(me_d + k, n_dp)) for k in range(1, n_dp)]
    peers = [(k - 1, lax.rem(me + k, n)) for k in range(1, n)]
    barrier = pltpu.get_barrier_semaphore()
    for _, d in dp_peers:
        pl.semaphore_signal(barrier, inc=1, device_id={"dp": d}, device_id_type=PUSH)
    for _, t in peers:
        pl.semaphore_signal(barrier, inc=1, device_id={"tensor": t}, device_id_type=PUSH)
    pl.semaphore_wait(barrier, n_dp + n - 2)

    def push(stage, src, dst, k, device):
        copy = pltpu.make_async_remote_copy(
            src_ref=src, dst_ref=dst, send_sem=sems.at[0, stage, k], recv_sem=sems.at[1, stage, k],
            device_id=device, device_id_type=PUSH,
        )
        copy.start()
        return copy

    first = [push(0, x_ref, dp_buf.at[me_d], k, {"dp": d}) for k, d in dp_peers]
    dp_buf[me_d] = x_ref[...]
    for copy in first:
        copy.wait()
    total[...] = sum(dp_buf[d] for d in range(n_dp))
    second = [push(1, total, t_buf.at[me], k, {"tensor": t}) for k, t in peers]
    t_buf[me] = total[...]
    for copy in second:
        copy.wait()
    o_ref[...] = sum(t_buf[t] for t in range(n))


def small_sum(x, n_dp, n):
    return pl.pallas_call(
        functools.partial(small_kernel, n_dp, n),
        out_shape=jax.ShapeDtypeStruct(x.shape, F32),
        in_specs=[VMEM_SPEC],
        out_specs=VMEM_SPEC,
        scratch_shapes=[
            pltpu.VMEM((n_dp,) + x.shape, F32),
            pltpu.VMEM(x.shape, F32),
            pltpu.VMEM((n,) + x.shape, F32),
            pltpu.SemaphoreType.DMA((2, 2, max(n, n_dp) - 1)),
        ],
        compiler_params=pltpu.CompilerParams(collective_id=2, has_side_effects=True),
        cost_estimate=cost(8),
    )(x)


def exchange(x, n_dp, n):
    height, width = x.shape
    slots = pltpu.VMEM((n, height, width // n), F32)
    return pl.pallas_call(
        functools.partial(exchange_kernel, n_dp, n),
        out_shape=jax.ShapeDtypeStruct(x.shape, F32),
        in_specs=[pl.BlockSpec(memory_space=pltpu.VMEM)],
        out_specs=pl.BlockSpec(memory_space=pltpu.VMEM),
        scratch_shapes=[
            pltpu.VMEM((n_dp, 8, width), F32),
            pltpu.VMEM(x.shape, F32),
            slots,
            pltpu.VMEM((height, width // n), F32),
            slots,
            pltpu.SemaphoreType.DMA((2, 3, max(n, n_dp) - 1)),
        ],
        compiler_params=pltpu.CompilerParams(collective_id=0, has_side_effects=True),
        cost_estimate=cost(16),
    )(x)


def on_device(
    layer_in,
    cotangent,
    lengths,
    prefix,
    pad_mask,
    clusters,
    qkv_w,
    out_w,
    gate_up_w,
    down_w,
    ln_params,
    qkv_row,
    qkv_col,
    out_row,
    out_col,
    gu_row,
    gu_col,
    down_row,
    down_col,
    ln_second,
):
    n_data = lax.axis_size("dp")
    n_tensor = lax.axis_size("tensor")
    tensor_rank = lax.axis_index("tensor")
    data_rank = lax.axis_index("dp")
    rows_dev, width = layer_in.shape
    cols_dev = qkv_w.shape[2]
    heads_dev = cols_dev // HD
    ff_dev = gate_up_w.shape[2]
    ff_pad = -(-ff_dev // 128) * 128
    n_clusters = max(2, n_data // 2)
    decay_rate = 1.0 - STEP ** (-0.8)
    seq_length = lengths[0]
    seq_prefix = prefix[0]
    ring = Ring(n_tensor)

    onehot = (clusters[:, None] == jnp.arange(n_clusters, dtype=jnp.int32)[None, :]).astype(F32)
    counts = jnp.sum(onehot, axis=0)
    own_row = jnp.sum(
        jnp.where((jnp.arange(n_data, dtype=jnp.int32) == data_rank)[:, None], onehot, 0.0), axis=0
    )
    seq_weight = jnp.sum(own_row / jnp.maximum(counts, 1.0))
    own_pos = tensor_rank * rows_dev + jnp.arange(rows_dev, dtype=jnp.int32)
    live_rows = ((own_pos < seq_length) & (pad_mask == 1)).astype(F32)
    grad_out = cotangent.astype(F32) * (live_rows * seq_weight)[:, None]
    grad_low = grad_out.astype(BF)

    key_live = (own_pos == 0) | (own_pos < seq_length) & (pad_mask == 1)
    seen_from = jnp.where(key_live, jnp.where(own_pos < seq_prefix, 0, own_pos), 2 * SLOT)
    seen = jnp.broadcast_to(seen_from.astype(F32)[None], (8, rows_dev))

    col_index = tensor_rank * ff_dev + jnp.arange(ff_pad, dtype=jnp.int32)
    ff_real = ((col_index < FF) & (jnp.arange(ff_pad) < ff_dev)).astype(F32)
    ff_mask = ff_real[:ff_dev]

    layer_own = layer_in.astype(F32)
    places = ring.places(rows_dev)
    act_one_all, qkv, seen_all = first_gather(
        n_tensor, layer_in, seen, ln_params, jnp.transpose(qkv_w, (1, 0, 2))
    )
    thr = jnp.broadcast_to(seen_all[:, 0].reshape(SLOT, 1), (SLOT, 128))

    pair = ring.halves(tie(grad_low, qkv))
    grad_pairs = [pair, ring.step(*pair)]
    context, lse = attn_forward(places, thr, qkv)
    pair = tie(grad_pairs[1], context)
    for s in range(2, n_tensor):
        pair = ring.step(*pair)
        grad_pairs.append(pair)
    grad_chunks = [jnp.concatenate(p, axis=0) for p in grad_pairs]
    pad = ((0, ff_pad - ff_dev), (0, 0))
    gate_up_late, down_late = tie(
        (jnp.transpose(gate_up_w, (2, 1, 0)), down_w), grad_chunks[min(3, n_tensor - 1)]
    )
    w_gu = jnp.concatenate([jnp.pad(gate_up_late[:, i], pad) for i in range(2)], axis=0)
    w_down = jnp.pad(down_late, pad)
    part_of = lambda x, s: x[s * rows_dev : (s + 1) * rows_dev]
    acc = None
    for s in ring.scatter_order():
        received = None if acc is None else ring.send(acc)
        acc = ring.add(received, dot(part_of(context, s), out_w, ((1,), (0,))))
    attn_own = jnp.concatenate(acc, axis=0)
    hidden_own = layer_own + attn_own
    norm_two = layer_norm(hidden_own, ln_params[2], ln_params[3]).astype(BF)

    act_two, inner, d_gu = [], [], []
    pair = ring.halves(norm_two)
    for s in range(n_tensor):
        pair = ring.step(*pair) if s else pair
        act = jnp.concatenate(pair, axis=0)
        act_two.append(act)
        gate_up = dot(act, w_gu, ((1,), (1,)))
        gate, up = gate_up[:, :ff_pad], gate_up[:, ff_pad:]
        gelu_gate, gelu_back = jax.vjp(jax.nn.gelu, gate)
        inner.append((gelu_gate * up * ff_real).astype(BF))
        d_inner = dot(grad_chunks[s], w_down, ((1,), (1,))) * ff_real
        d_gate = gelu_back(d_inner * up)[0]
        d_gu.append(jnp.concatenate([d_gate, d_inner * gelu_gate], axis=1).astype(BF))
    acc = None
    for s in ring.scatter_order():
        received = None if acc is None else ring.send(acc)
        acc = ring.add(received, dot(d_gu[s], w_gu, ((1,), (0,))))
    d_norm_two = jnp.concatenate(acc, axis=0)

    d_hidden_ln, ln_two_part = layer_norm_back(hidden_own, ln_params[2], d_norm_two)
    d_hidden = grad_out + d_hidden_ln
    dp_wide, dp_tall = DpSum(n_data, 1), DpSum(n_data, 0)
    across = lambda a, b: dot(a, b, ((0,), (0,)))
    rows_of = lambda chunks, after: jnp.concatenate(tie(chunks, after), axis=0)
    products = [
        lambda after: across(rows_of(inner, after), rows_of(grad_chunks, after)),
        lambda after: across(rows_of([d[:, :ff_pad] for d in d_gu], after), rows_of(act_two, after)),
        lambda after: across(rows_of([d[:, ff_pad:] for d in d_gu], after), rows_of(act_two, after)),
    ]
    lag = 2
    order = ring.scatter_order()
    ffn_term = lambda i, after: dot(tie(inner[order[i]], after), w_down, ((1,), (0,)))
    pair = ring.halves(d_hidden.astype(BF))
    hidden_pairs = [pair]
    acc, sums, done = None, [], 0
    held = {s: () for s in range(n_tensor)}
    for s in range(1, n_tensor):
        arriving = ring.step(*pair)
        work = ()
        if s <= len(products):
            work = products[s - 1](pair)[:ff_dev].astype(BF)
            mine = dp_wide.cores(work)
            sums.append(mine)
        if s >= lag:
            received = None if acc is None else ring.send(acc)
            acc = ring.add(received, ffn_term(done, pair), work)
            done += 1
        held[s] = (work, () if acc is None else ring.low(acc))
        extra = ()
        if 3 <= s < 3 + len(products):
            extra = sums[s - 3]
            sums[s - 3] = dp_wide.chips(extra)
        hidden_pairs.append(arriving)
        pair = tie(arriving, (held[s - 1], extra))
    hidden_chunks = [jnp.concatenate(p, axis=0) for p in hidden_pairs]
    d_context = jnp.concatenate(
        [dot(chunk, out_w, ((1,), (1,))).astype(BF) for chunk in hidden_chunks], axis=0
    )
    out_part = across(context, jnp.concatenate(hidden_chunks, axis=0)).astype(BF)
    out_mine = dp_wide.cores(out_part)

    heads = list(range(heads_dev))
    d_heads = []
    while done < n_tensor:
        received = ring.send(acc)
        work = ()
        if heads:
            head = heads.pop(0)
            d_in = tie(d_context, (ring.low(acc), out_part if head == 0 else d_heads[-1]))
            work = attn_backward(head, places, thr, qkv, d_in, lse)
            d_heads.append(work)
        acc = ring.add(received, ffn_term(done, d_context), (work, sums[0]))
        done += 1
    for head in heads:
        d_heads.append(attn_backward(head, places, thr, qkv, d_context, lse))
    layer_out = (hidden_own + jnp.concatenate(acc, axis=0)).astype(BF)
    ffn_done = layer_out

    by_head = lambda x: jnp.swapaxes(
        x.reshape(x.shape[:-2] + (3, heads_dev, HD)), -3, -2
    ).reshape(x.shape[:-2] + (3 * cols_dev,))
    by_kind = lambda x: jnp.swapaxes(
        x.reshape(x.shape[:-1] + (heads_dev, 3, HD)), -3, -2
    ).reshape(x.shape[:-1] + (3, cols_dev))
    w_qkv = by_head(tie(qkv_w, pair))
    d_qkv = tie(jnp.concatenate(d_heads, axis=1), ffn_done)
    out_mine = dp_wide.chips(out_mine)
    qkv_part = across(act_one_all, d_qkv).astype(BF)
    qkv_mine = dp_tall.cores(qkv_part)
    qkv_mid = dp_tall.chips(qkv_mine)
    down_low, gate_low, up_low = (dp_wide.join(x) for x in sums)
    out_low, qkv_low = dp_wide.join(out_mine), dp_tall.join(qkv_mid)

    qkv_sum, out_sum, down_sum = qkv_low.astype(F32), out_low.astype(F32), down_low.astype(F32)
    gu_sum = (gate_low.astype(F32), up_low.astype(F32))
    gu_weights = (w_gu[:ff_dev], w_gu[ff_pad : ff_pad + ff_dev])
    gu_grad = pair_rows(gate_low, up_low)
    out_t, down_t, gu_t, qkv_t = tie((out_w, down_w, gu_weights, w_qkv), d_qkv)
    ff_col = ff_mask[:, None]
    blend = lambda old, total: decay_rate * old + (1.0 - decay_rate) * total
    square = lambda grad: grad * grad + eps_one
    square_sum = lambda w: jnp.sum(jnp.square(w.astype(F32)))

    qkv_sq, gu_sq = square(qkv_sum), [square(g) * ff_col for g in gu_sum]
    out_sq, down_sq = square(out_sum), square(down_sum) * ff_col
    qkv_col_new = blend(by_head(qkv_col), jnp.sum(qkv_sq, axis=0) / width)
    gu_col_new = [blend(gu_col[i], jnp.sum(gu_sq[i], axis=1) / width) for i in range(2)]
    out_row_new = blend(out_row, jnp.sum(out_sq, axis=1) / width)
    down_row_new = blend(down_row, jnp.sum(down_sq, axis=1) / width)
    clean = lambda grad: grad * grad
    scalars = jnp.stack(
        [
            square_sum(qkv_t),
            sum(jnp.sum(jnp.square(w.astype(F32)) * ff_col) for w in gu_t),
            square_sum(out_t),
            jnp.sum(jnp.square(down_t.astype(F32)) * ff_col),
            jnp.sum(out_row_new),
            jnp.sum(down_row_new * ff_mask),
        ]
    )
    packed = jnp.concatenate(
        [
            ln_two_part,
            jnp.pad(scalars / n_data, (0, width - scalars.shape[0]))[None],
            jnp.zeros((5, width), F32),
            jnp.stack(
                [
                    jnp.sum(qkv_sq, axis=1),
                    jnp.sum(clean(qkv_sum) / qkv_col_new[None, :], axis=1),
                    sum(jnp.sum(sq, axis=0) for sq in gu_sq),
                    sum(
                        jnp.sum(clean(g) * (ff_mask / col)[:, None], axis=0)
                        for g, col in zip(gu_sum, gu_col_new)
                    ),
                    jnp.sum(out_sq, axis=0),
                    jnp.sum(clean(out_sum) / out_row_new[:, None], axis=0),
                    jnp.sum(down_sq, axis=0),
                    jnp.sum(clean(down_sum) * (ff_mask / down_row_new)[:, None], axis=0),
                ]
            ),
        ],
        axis=0,
    )
    packed = exchange(packed, n_data, n_tensor)
    ln_two_tot = packed[:2]
    qkv_wtot, gu_wtot, out_wtot, down_wtot, out_rtot, down_rtot = (packed[2, i] for i in range(6))
    qkv_tot, qkv_usq, gu_tot, gu_usq, out_tot, out_usq, down_tot, down_usq = (
        packed[8 + i] for i in range(8)
    )

    qkv_cols_all = 3 * cols_dev * n_tensor
    out_rows_all = cols_dev * n_tensor
    qkv_row_new = blend(qkv_row, qkv_tot / qkv_cols_all)
    qkv_mean = jnp.sum(qkv_row_new) / width
    gu_row_new = blend(gu_row, gu_tot / (2 * FF))
    gu_mean = jnp.sum(gu_row_new) / width
    out_col_new = blend(out_col, out_tot / out_rows_all)
    out_mean = out_rtot / out_rows_all
    down_col_new = blend(down_col, down_tot / FF)
    down_mean = down_rtot / FF
    qkv_rate = step_rate(jnp.sum(qkv_usq / qkv_row_new) * qkv_mean, qkv_wtot, width * qkv_cols_all)
    gu_rate = step_rate(jnp.sum(gu_usq / gu_row_new) * gu_mean, gu_wtot, width * 2 * FF)
    out_rate = step_rate(jnp.sum(out_usq / out_col_new) * out_mean, out_wtot, out_rows_all * width)
    down_rate = step_rate(jnp.sum(down_usq / down_col_new) * down_mean, down_wtot, FF * width)
    pace = {1: qkv_part, 2: (qkv_mine, out_mine, down_low), 3: gate_low, 4: up_low, 5: out_low}
    acc = None
    for i, s in enumerate(order):
        received = None if acc is None else ring.send(acc)
        after = pace.get(i, ())
        if i == n_tensor - 1:
            after = (qkv_row_new, gu_row_new, out_col_new, down_col_new)
        acc = ring.add(received, dot(part_of(d_qkv, s), w_qkv, ((1,), (1,))), after)
    d_norm_one = jnp.concatenate(acc, axis=0)
    d_input_ln, ln_one_part = layer_norm_back(layer_own, ln_params[0], d_norm_one)
    input_grad = (d_hidden + d_input_ln).astype(BF)

    qkv_new = apply_step(w_qkv, qkv_sum, qkv_row_new, qkv_col_new, qkv_mean, qkv_rate)
    out_new = apply_step(out_w, out_sum, out_row_new, out_col_new, out_mean, out_rate)
    down_new = apply_step(down_w, down_sum, down_row_new, down_col_new, down_mean, down_rate)
    gu_scale = lax.rsqrt(gu_row_new) * (gu_rate * jnp.sqrt(gu_mean))
    gu_new = pair_rows(gate_low, up_low, (w_gu, gu_scale, *map(lax.rsqrt, gu_col_new)))
    ln_one_part = tie(ln_one_part, (qkv_new, out_new, down_new, gu_new))
    ln_one_tot = small_sum(ln_one_part.reshape(8, -1), n_data, n_tensor).reshape(2, width)
    ln_tot = jnp.concatenate([ln_one_tot, ln_two_tot], axis=0)
    ln_second_new = blend(ln_second, ln_tot * ln_tot + eps_one)
    ln_update = ln_tot * lax.rsqrt(ln_second_new)
    ln_urms = jnp.sqrt(jnp.mean(ln_update * ln_update, axis=1, keepdims=True))
    ln_wrms = jnp.sqrt(jnp.mean(ln_params * ln_params, axis=1, keepdims=True))
    ln_new = ln_params - rate_base * jnp.maximum(eps_two, ln_wrms) * ln_update / jnp.maximum(
        1.0, ln_urms / clip_bound
    )
    return (
        layer_out,
        input_grad,
        by_kind(qkv_sum),
        by_kind(qkv_new),
        qkv_row_new,
        by_kind(qkv_col_new),
        out_sum,
        out_new,
        out_row_new,
        out_col_new,
        jnp.transpose(gu_grad, (2, 1, 0)),
        jnp.transpose(gu_new, (2, 1, 0)),
        gu_row_new,
        jnp.stack(gu_col_new),
        down_sum,
        down_new,
        down_row_new,
        down_col_new,
        ln_tot,
        ln_second_new,
        ln_new,
    )


def solution(mesh):
    in_specs = (
        P(("dp", "tensor"), None),
        P(("dp", "tensor"), None),
        P("dp"),
        P("dp"),
        P(("dp", "tensor")),
        P(),
        P(None, None, "tensor"),
        P("tensor", None),
        P(None, None, "tensor"),
        P("tensor", None),
        P(),
        P(),
        P(None, "tensor"),
        P("tensor"),
        P(),
        P(),
        P(None, "tensor"),
        P("tensor"),
        P(),
        P(),
    )
    out_specs = (
        P(("dp", "tensor"), None),
        P(("dp", "tensor"), None),
        P(None, None, "tensor"),
        P(None, None, "tensor"),
        P(),
        P(None, "tensor"),
        P("tensor", None),
        P("tensor", None),
        P("tensor"),
        P(),
        P(None, None, "tensor"),
        P(None, None, "tensor"),
        P(),
        P(None, "tensor"),
        P("tensor", None),
        P("tensor", None),
        P("tensor"),
        P(),
        P(),
        P(),
        P(),
    )
    return jax.shard_map(
        on_device, mesh=mesh, in_specs=in_specs, out_specs=out_specs, check_vma=False
    )
```

```python
import functools

import jax
import jax.numpy as jnp
from jax import lax
from jax.experimental import pallas as pl
from jax.experimental.pallas import tpu as pltpu
from jax.sharding import PartitionSpec as P

HD = 128
FF = 5461
SLOT = 2048
STEP = 10
PREFIX_MAX = SLOT // 2
Q_BLOCK = 512

ln_eps = 1e-05
eps_one = 1e-30
eps_two = 0.001
clip_bound = 1.0
rate_base = 1.0
masked_score = -1e30
LOG2E = 1.4426950408889634
BF = jnp.bfloat16
F32 = jnp.float32


def dot(a, b, dims):
    return lax.dot_general(a, b, (dims, ((), ())), preferred_element_type=F32)


def ring_order(n):
    b_size = 2 if n <= 8 else 4
    a_size = n // b_size
    order = []
    for a in range(a_size):
        cols = list(range(1, b_size))
        order += [a * b_size + c for c in (cols[::-1] if a % 2 else cols)]
    for a in range(a_size - 1, -1, -1):
        order.append(a * b_size)
    return order


class Ring:
    def __init__(self, n):
        self.n = n
        order = ring_order(n)
        self.fw = [(order[i], order[(i + 1) % n]) for i in range(n)]
        self.bw = [(order[i], order[(i - 1) % n]) for i in range(n)]
        place = [0] * n
        for p, t in enumerate(order):
            place[t] = p
        self.place = jnp.array(place, jnp.int32)
        self.pos = self.place[lax.axis_index("tensor")]

    def step(self, a, b):
        return lax.ppermute(a, "tensor", self.fw), lax.ppermute(b, "tensor", self.bw)

    def halves(self, x):
        half = x.shape[0] // 2
        return x[:half], x[half:]

    def scatter_order(self):
        return list(range(1, self.n)) + [0]

    def add(self, received, term, after=()):
        term = lax.optimization_barrier((term, after))[0]
        parts = self.halves(term)
        if received is not None:
            parts = tuple(r.astype(F32) + t for r, t in zip(received, parts))
        return parts

    def low(self, parts):
        return tuple(p.astype(BF) for p in parts)

    def send(self, parts):
        return self.step(*self.low(parts))

    def places(self, rows):
        t = jnp.arange(self.n, dtype=jnp.int32)
        step = self.place[t] - self.pos
        first = lax.rem(2 * self.n - step, self.n) * rows
        second = lax.rem(step + self.n, self.n) * rows + rows // 2
        return jnp.stack([first, second], axis=1).reshape(-1)


def cost(micros):
    return pl.CostEstimate(flops=int(micros * 1e9), transcendentals=0, bytes_accessed=4 << 20)


PUSH = pl.DeviceIdType.MESH


def pick(index, table):
    out = jnp.int32(table[0])
    for k in range(1, len(table)):
        out = jnp.where(index == k, jnp.int32(table[k]), out)
    return out


def neighbours(n):
    order = ring_order(n)
    pos = pick(lax.axis_index("tensor"), [order.index(t) for t in range(n)])
    ahead = pick(lax.rem(pos + 1, n), order)
    behind = pick(lax.rem(pos + n - 1, n), order)
    return pos, [{"tensor": ahead}, {"tensor": behind}]


def other_core():
    me = lax.axis_index("dp")
    return {"dp": me + 1 - 2 * lax.rem(me, 2)}


def greet(devices):
    barrier = pltpu.get_barrier_semaphore()
    for device in devices:
        pl.semaphore_signal(barrier, inc=1, device_id=device, device_id_type=PUSH)
    pl.semaphore_wait(barrier, len(devices))


def ring_copy(land, send_sem, recv_sem, sides, d, s):
    return pltpu.make_async_remote_copy(
        src_ref=land.at[d, s],
        dst_ref=land.at[d, s + 1],
        send_sem=send_sem.at[d, s],
        recv_sem=recv_sem.at[d, s],
        device_id=sides[d],
        device_id_type=PUSH,
    )


def ring_sent(n, copy):
    def sent(s, carry):
        for d in range(2):
            copy(d, s).wait_send()
        return carry

    lax.fori_loop(0, n - 1, sent, 0)


def ring_gather(n, x_ref, land, send_sem, recv_sem, sides, work):
    copy = functools.partial(ring_copy, land, send_sem, recv_sem, sides)
    half = x_ref.shape[0] // 2
    land[0, 0] = x_ref[:half, :]
    land[1, 0] = x_ref[half:, :]

    def step(s, carry):
        for d in range(2):

            @pl.when(s > 0)
            def _():
                copy(d, s - 1).wait_recv()

            @pl.when(s < n - 1)
            def _():
                copy(d, s).start()

        work(s)
        return carry

    lax.fori_loop(0, n, step, 0)
    ring_sent(n, copy)


def ring_scatter(n, land, send_sem, recv_sem, sides, term_buf, term, work, finish):
    copy = functools.partial(ring_copy, land, send_sem, recv_sem, sides)
    half = term_buf.shape[0] // 2
    for d in range(2):
        land[d, 0] = jnp.zeros(land.shape[2:], land.dtype)

    def step(s, carry):
        term(lax.rem(s + 1, n))
        for d in range(2):
            rows = slice(d * half, (d + 1) * half)

            @pl.when(s > 0)
            def _():
                copy(d, s - 1).wait_recv()

            total = land[d, s].astype(F32) + term_buf[rows, :]

            @pl.when(s < n - 1)
            def _():
                land[d, s] = total.astype(BF)
                copy(d, s).start()

            @pl.when(s == n - 1)
            def _():
                finish(rows, total)

        work(s)
        return carry

    lax.fori_loop(0, n, step, 0)
    ring_sent(n, copy)


def dot_columns(out, a, b, dims, block=512):
    width = b.shape[1]

    def columns(j, carry):
        at = pl.ds(pl.multiple_of(j * block, block), block)
        out(at, dot(a, b[:, at], dims))
        return carry

    lax.fori_loop(0, width // block, columns, 0)


def first_kernel(
    n, x_ref, seen_ref, ln_ref, w_ref, act_ref, qkv_ref, seen_all,
    land, act_buf, seen_buf, send_sem, recv_sem, act_sem, seen_sem,
):
    rows, cols = x_ref.shape[0], w_ref.shape[2]
    me = lax.axis_index("tensor")
    peers = [lax.rem(me + k, n) for k in range(1, n)]
    sides = neighbours(n)[1]
    greet([{"tensor": t} for t in peers])

    def seen_copy(k):
        return pltpu.make_async_remote_copy(
            src_ref=seen_ref, dst_ref=seen_buf.at[me], send_sem=seen_sem.at[0, k],
            recv_sem=seen_sem.at[1, k], device_id={"tensor": peers[k]}, device_id_type=PUSH,
        )

    def act_copy(s):
        place = pl.ds(pl.multiple_of(s * rows, rows), rows)
        return pltpu.make_async_copy(act_buf.at[s], act_ref.at[place], act_sem.at[s])

    def work(s):
        @pl.when(s == 0)
        def _():
            for k in range(n - 1):
                seen_copy(k).start()

        chunk = jnp.concatenate([land[0, s], land[1, s]], axis=0).astype(F32)
        act = layer_norm(chunk, ln_ref[0:1, :], ln_ref[1:2, :]).astype(BF)
        act_buf[s] = act
        act_copy(s).start()
        place = pl.ds(pl.multiple_of(s * rows, rows), rows)
        for k in range(3):
            qkv_ref[place, k * cols : (k + 1) * cols] = dot(act, w_ref[k], ((1,), (0,))).astype(BF)

    ring_gather(n, x_ref, land, send_sem, recv_sem, sides, work)
    seen_buf[me] = seen_ref[...]
    for k in range(n - 1):
        seen_copy(k).wait()
    seen_all[...] = seen_buf[...]

    def written(s, carry):
        act_copy(s).wait()
        return carry

    lax.fori_loop(0, n, written, 0)


def ring_scratch(n, rows, width):
    return [pltpu.VMEM((2, n, rows // 2, width), BF)], [
        pltpu.SemaphoreType.DMA((2, n - 1)),
        pltpu.SemaphoreType.DMA((2, n - 1)),
    ]


VMEM_SPEC = pl.BlockSpec(memory_space=pltpu.VMEM)
ANY_SPEC = pl.BlockSpec(memory_space=pl.ANY)


def first_gather(n, x, seen, ln_params, w):
    rows, width = x.shape
    cols = w.shape[2]
    buf, sems = ring_scratch(n, rows, width)
    return pl.pallas_call(
        functools.partial(first_kernel, n),
        in_specs=[VMEM_SPEC] * 4,
        out_specs=[ANY_SPEC, VMEM_SPEC, VMEM_SPEC],
        out_shape=[
            jax.ShapeDtypeStruct((n * rows, width), BF),
            jax.ShapeDtypeStruct((n * rows, 3 * cols), BF),
            jax.ShapeDtypeStruct((n,) + seen.shape, F32),
        ],
        scratch_shapes=buf
        + [pltpu.VMEM((n, rows, width), BF), pltpu.VMEM((n,) + seen.shape, F32)]
        + sems
        + [pltpu.SemaphoreType.DMA((n,)), pltpu.SemaphoreType.DMA((2, n - 1))],
        compiler_params=pltpu.CompilerParams(
            collective_id=1, has_side_effects=True, vmem_limit_bytes=56 << 20
        ),
        cost_estimate=pl.CostEstimate(
            flops=6 * n * rows * width * cols, transcendentals=0, bytes_accessed=40 << 20
        ),
    )(x, seen, ln_params, w)


def back_kernel(
    n, x_ref, w_ref, ctx_ref, inner_hbm, d_gu_hbm, grad_hbm, act_hbm,
    d_ctx_ref, out_ref, mine_ref,
    land, lhs, rhs, part, core_land, out_sum, send_sem, recv_sem, load_sem, core_sem,
):
    rows, ff_pad = x_ref.shape[0], lhs.shape[2]
    ff_rows, half = core_land.shape[1:]
    sides, partner = neighbours(n)[1], other_core()
    core = lax.rem(lax.axis_index("dp"), 2)
    of_core = lambda c: pl.ds(pl.multiple_of(c * half, half), half)
    loads = [
        pltpu.make_async_copy(src, dst, load_sem.at[i])
        for i, (src, dst) in enumerate(
            (
                (inner_hbm, lhs.at[0]),
                (grad_hbm, rhs.at[0]),
                (d_gu_hbm.at[:, pl.ds(0, ff_pad)], lhs.at[1]),
                (act_hbm, rhs.at[1]),
                (d_gu_hbm.at[:, pl.ds(ff_pad, ff_pad)], lhs.at[2]),
            )
        )
    ]
    for load in loads:
        load.start()
    out_sum[...] = jnp.zeros_like(out_sum)
    greet(sides + [partner])

    def core_copy(i):
        return pltpu.make_async_remote_copy(
            src_ref=part.at[i, :, of_core(1 - core)],
            dst_ref=core_land.at[i],
            send_sem=core_sem.at[0, i],
            recv_sem=core_sem.at[1, i],
            device_id=partner,
            device_id_type=PUSH,
        )

    def work(s):
        chunk = jnp.concatenate([land[0, s], land[1, s]], axis=0)
        place = pl.ds(pl.multiple_of(s * rows, rows), rows)
        d_ctx_ref[place, :] = dot(chunk, w_ref[...], ((1,), (1,))).astype(BF)
        out_sum[...] += dot(ctx_ref[place, :], chunk, ((0,), (0,)))
        for i in range(3):

            @pl.when(s == i + 1)
            def _():
                for load in (loads[:2], loads[2:4], loads[4:])[i]:
                    load.wait()

                def put(at, value):
                    part[i, :, at] = value[:ff_rows].astype(BF)

                dot_columns(put, lhs[i], rhs.at[min(i, 1)], ((0,), (0,)))
                core_copy(i).start()

            @pl.when(s == i + 3)
            def _():
                core_copy(i).wait()
                total = part[i, :, of_core(core)].astype(F32) + core_land[i].astype(F32)
                mine_ref[i] = total.astype(BF)

    ring_gather(n, x_ref, land, send_sem, recv_sem, sides, work)
    out_ref[...] = out_sum[...].astype(BF)


def back_gather(n, ff_dev, x, w, context, inner, d_gu, grad, act):
    rows, width = x.shape
    ff_pad = inner.shape[1]
    ff_rows = -(-ff_dev // 16) * 16
    buf, sems = ring_scratch(n, rows, width)
    return pl.pallas_call(
        functools.partial(back_kernel, n),
        in_specs=[VMEM_SPEC] * 3 + [ANY_SPEC] * 4,
        out_specs=[VMEM_SPEC] * 3,
        out_shape=[
            jax.ShapeDtypeStruct((n * rows, w.shape[0]), BF),
            jax.ShapeDtypeStruct(w.shape, BF),
            jax.ShapeDtypeStruct((3, ff_rows, width // 2), BF),
        ],
        scratch_shapes=buf
        + [
            pltpu.VMEM((3, n * rows, ff_pad), BF),
            pltpu.VMEM((2, n * rows, width), BF),
            pltpu.VMEM((3, ff_rows, width), BF),
            pltpu.VMEM((3, ff_rows, width // 2), BF),
            pltpu.VMEM(w.shape, F32),
        ]
        + sems
        + [pltpu.SemaphoreType.DMA((5,)), pltpu.SemaphoreType.DMA((2, 3))],
        compiler_params=pltpu.CompilerParams(
            collective_id=3, has_side_effects=True, vmem_limit_bytes=60 << 20
        ),
        cost_estimate=cost(80),
    )(x, w, context, inner, d_gu, grad, act)


def ffn_kernel(
    n, heads, inner_ref, w_ref, hidden_ref, thr_ref, qkv_ref, d_ctx_ref, lse_ref,
    out_ref, d_qkv_ref,
    land, term_buf, q_ref, k_ref, v_ref, do_ref, dk_sum, dv_sum, send_sem, recv_sem,
):
    rows = hidden_ref.shape[0]
    pos, sides = neighbours(n)
    greet(sides)
    places = []
    place_of = [ring_order(n).index(t) for t in range(n)]
    for t in range(n):
        places.append(lax.rem(pos + (n - place_of[t]), n) * rows)
        places.append(lax.rem(place_of[t] - pos + n, n) * rows + rows // 2)

    def term(c):
        place = pl.ds(pl.multiple_of(c * rows, rows), rows)

        def put(at, value):
            term_buf[:, at] = value

        dot_columns(put, inner_ref[place, :], w_ref, ((1,), (0,)))

    def work(s):
        for h in range(heads):

            @pl.when(s == h + 1)
            def _():
                columns = lambda i: slice((i * heads + h) * HD, (i * heads + h + 1) * HD)
                for i, dst in enumerate((q_ref, k_ref, v_ref)):
                    to_order(places, qkv_ref, columns(i), dst)
                to_order(places, d_ctx_ref, columns(0), do_ref)
                attn_backward_head(
                    places, thr_ref, lse_ref.at[h], q_ref, k_ref, v_ref, do_ref, dk_sum, dv_sum,
                    d_qkv_ref, columns,
                )

    def finish(at, total):
        out_ref[at, :] = (hidden_ref[at, :] + total).astype(BF)

    ring_scatter(n, land, send_sem, recv_sem, sides, term_buf, term, work, finish)


def ffn_scatter(n, inner, w, hidden, thr, qkv, d_context, lse):
    rows, width = hidden.shape
    heads = d_context.shape[1] // HD
    buf, sems = ring_scratch(n, rows, width)
    return pl.pallas_call(
        functools.partial(ffn_kernel, n, heads),
        in_specs=[VMEM_SPEC] * 7,
        out_specs=[VMEM_SPEC] * 2,
        out_shape=[
            jax.ShapeDtypeStruct((rows, width), BF),
            jax.ShapeDtypeStruct(qkv.shape, BF),
        ],
        scratch_shapes=buf
        + [pltpu.VMEM((rows, width), F32)]
        + [pltpu.VMEM((SLOT, HD), BF)] * 4
        + [pltpu.VMEM((SLOT, HD), F32)] * 2
        + sems,
        compiler_params=pltpu.CompilerParams(
            collective_id=4, has_side_effects=True, vmem_limit_bytes=60 << 20
        ),
        cost_estimate=cost(85),
    )(inner, w, hidden, thr, qkv, d_context, lse)


class DpSum:
    def __init__(self, n_dp, axis):
        self.n_dp, self.axis = n_dp, axis
        self.core = lax.rem(lax.axis_index("dp"), 2)

    def swap(self, y, bit):
        return lax.ppermute(y, "dp", [(i, i ^ bit) for i in range(self.n_dp)])

    def cores(self, x):
        half = x.shape[self.axis] // 2
        part = lambda c: lax.dynamic_slice_in_dim(x, c * half, half, self.axis)
        return (part(self.core).astype(F32) + self.swap(part(1 - self.core), 1).astype(F32)).astype(BF)

    def chips(self, mine):
        bit = 2
        while bit < self.n_dp:
            mine = (mine.astype(F32) + self.swap(mine, bit).astype(F32)).astype(BF)
            bit *= 2
        return mine

    def join(self, mine):
        other = self.swap(mine, 1)
        first = jnp.where(self.core == 0, mine, other)
        second = jnp.where(self.core == 0, other, mine)
        return jnp.concatenate([first, second], axis=self.axis)


def norm_stats(rows):
    mean_row = jnp.mean(rows, axis=-1, keepdims=True)
    centered = rows - mean_row
    variance = jnp.mean(centered * centered, axis=-1, keepdims=True)
    scale = lax.rsqrt(variance + ln_eps)
    return centered * scale, scale


def layer_norm(rows, gain, shift):
    return norm_stats(rows)[0] * gain + shift


def layer_norm_back(rows, gain, e):
    n, scale = norm_stats(rows)
    eg = e * gain
    dv = scale * (
        eg - jnp.mean(eg, axis=-1, keepdims=True) - n * jnp.mean(eg * n, axis=-1, keepdims=True)
    )
    return dv, jnp.stack([jnp.sum(e * n, axis=0), jnp.sum(e, axis=0)])


def seen_mask(thr_ref, q0, shape):
    thr = thr_ref[: shape[0], :]
    thr = jnp.concatenate([thr] * (shape[1] // thr.shape[1]), axis=1)
    q_pos = (q0 + lax.broadcasted_iota(jnp.int32, shape, 1)).astype(F32)
    return q_pos >= thr


def q_blocks():
    return [(q0, max(PREFIX_MAX, q0 + Q_BLOCK)) for q0 in range(0, SLOT, Q_BLOCK)]


def to_order(places, src_ref, columns, dst_ref):
    half = SLOT // len(places)
    for j, start in enumerate(places):
        place = pl.ds(pl.multiple_of(start, half), half)
        dst_ref[j * half : (j + 1) * half, :] = src_ref[place, columns]


def from_order(places, q0, value, dst_ref, columns):
    half = SLOT // len(places)
    for i in range(value.shape[0] // half):
        place = pl.ds(pl.multiple_of(places[q0 // half + i], half), half)
        dst_ref[place, columns] = value[i * half : (i + 1) * half, :]


def attn_forward_kernel(places, thr_ref, q_in, k_in, v_in, o_ref, lse_ref, q_ref, k_ref, v_ref):
    c = HD**-0.5 * LOG2E
    places = [places[j] for j in range(places.shape[0])]
    for src, dst in ((q_in, q_ref), (k_in, k_ref), (v_in, v_ref)):
        to_order(places, src, slice(None), dst)
    for q0, klim in q_blocks():
        raw = dot(k_ref[:klim, :], q_ref[q0 : q0 + Q_BLOCK, :], ((1,), (1,)))
        raw = jnp.where(seen_mask(thr_ref, q0, raw.shape), raw, masked_score)
        top = jnp.max(raw, axis=0, keepdims=True)
        p = jnp.exp2((raw - top) * c)
        total = jnp.sum(p, axis=0, keepdims=True)
        out = dot(v_ref[:klim, :], p.astype(BF), ((0,), (0,))) / total
        from_order(places, q0, out.T.astype(BF), o_ref, slice(None))
        lse_ref[0, :, q0 : q0 + Q_BLOCK] = top * c + jnp.log2(total)


def attn_backward_head(
    places, thr_ref, lse_ref, q_ref, k_ref, v_ref, do_ref, dk_sum, dv_sum, d_ref, columns
):
    scale = HD**-0.5
    dk_sum[...] = jnp.zeros_like(dk_sum)
    dv_sum[...] = jnp.zeros_like(dv_sum)
    for q0, klim in q_blocks():
        rows = slice(q0, q0 + Q_BLOCK)
        k, q, do = k_ref[:klim, :], q_ref[rows, :], do_ref[rows, :]
        raw = dot(k, q, ((1,), (1,)))
        p = jnp.exp2(raw * (scale * LOG2E) - lse_ref[:, rows])
        p = jnp.where(seen_mask(thr_ref, q0, raw.shape), p, 0.0)
        dv_sum[:klim, :] += dot(p.astype(BF), do, ((1,), (0,)))
        dp = dot(v_ref[:klim, :], do, ((1,), (1,)))
        delta = jnp.sum(p * dp, axis=0, keepdims=True)
        ds = (p * (dp - delta) * scale).astype(BF)
        dk_sum[:klim, :] += dot(ds, q, ((1,), (0,)))
        dq = dot(k, ds, ((0,), (0,))).T.astype(BF)
        from_order(places, q0, dq, d_ref, columns(0))
    from_order(places, 0, dk_sum[...].astype(BF), d_ref, columns(1))
    from_order(places, 0, dv_sum[...].astype(BF), d_ref, columns(2))


SMEM_SPEC = pl.BlockSpec(memory_space=pltpu.SMEM)
ATTN_PARAMS = pltpu.CompilerParams(vmem_limit_bytes=56 << 20)


def head_spec(k, heads):
    return pl.BlockSpec((SLOT, HD), lambda h: (0, k * heads + h))


def attn_forward(places, thr, qkv):
    heads = qkv.shape[1] // (3 * HD)
    lse = pl.BlockSpec((1, 1, SLOT), lambda h: (h, 0, 0))
    return pl.pallas_call(
        attn_forward_kernel,
        grid=(heads,),
        in_specs=[SMEM_SPEC, pl.BlockSpec((SLOT, 128), lambda h: (0, 0))]
        + [head_spec(k, heads) for k in range(3)],
        out_specs=[head_spec(0, heads), lse],
        out_shape=[
            jax.ShapeDtypeStruct((SLOT, heads * HD), BF),
            jax.ShapeDtypeStruct((heads, 1, SLOT), F32),
        ],
        scratch_shapes=[pltpu.VMEM((SLOT, HD), BF)] * 3,
        compiler_params=ATTN_PARAMS,
        cost_estimate=cost(6.5 * heads),
    )(places, thr, qkv, qkv, qkv)


def step_rate(update_sq, weight_sq, n_real):
    update_rms = jnp.sqrt(update_sq / n_real)
    weight_rms = jnp.sqrt(weight_sq / n_real)
    return rate_base * jnp.maximum(eps_two, weight_rms) / jnp.maximum(1.0, update_rms / clip_bound)


def apply_step(weight, grad, row_new, col_new, row_mean, rate):
    row = lax.rsqrt(row_new) * (rate * jnp.sqrt(row_mean))
    return weight.astype(F32) - grad * (row[:, None] * lax.rsqrt(col_new)[None, :])


def pair_kernel(factors, *refs):
    g_ref, u_ref = refs[:2]
    o_ref = refs[-1]
    g, u = g_ref[...].astype(F32), u_ref[...].astype(F32)
    if factors:
        wg_ref, wu_ref, row_ref, cg_ref, cu_ref = refs[2:7]
        row = row_ref[...]
        g = wg_ref[...].astype(F32) - g * (row * cg_ref[...])
        u = wu_ref[...].astype(F32) - u * (row * cu_ref[...])
    o_ref[:, 0, :] = g
    o_ref[:, 1, :] = u


def pair_rows(gate, up, step=None):
    ff, width = gate.shape
    block = 96
    grid = (-(-ff // block),)
    wide = pl.BlockSpec((block, width), lambda i: (i, 0))
    args, specs = [gate, up], [wide, wide]
    if step is not None:
        w_gu, row, col_gate, col_up = step
        shift = w_gu.shape[0] // 2 // block
        column = pl.BlockSpec((block, 1), lambda i: (i, 0))
        args += [w_gu, w_gu, row[None, :], col_gate[:, None], col_up[:, None]]
        specs += [
            wide,
            pl.BlockSpec((block, width), lambda i: (i + shift, 0)),
            pl.BlockSpec((1, width), lambda i: (0, 0)),
            column,
            column,
        ]
    return pl.pallas_call(
        functools.partial(pair_kernel, step is not None),
        grid=grid,
        in_specs=specs,
        out_specs=pl.BlockSpec((block, 2, width), lambda i: (i, 0, 0)),
        out_shape=jax.ShapeDtypeStruct((ff, 2, width), F32),
        compiler_params=pltpu.CompilerParams(vmem_limit_bytes=40 << 20),
        cost_estimate=pl.CostEstimate(flops=8 * ff * width, transcendentals=0, bytes_accessed=16 * ff * width),
    )(*args)


def tie(x, after):
    return lax.optimization_barrier((x, after))[0]


def exchange_kernel(n_dp, n, x_ref, o_ref, dp_buf, rows, part_buf, total, whole, sems):
    me_d, me = lax.axis_index("dp"), lax.axis_index("tensor")
    width = x_ref.shape[1] // n
    columns = lambda t: pl.ds(pl.multiple_of(t * width, width), width)
    dp_peers = [(k - 1, lax.rem(me_d + k, n_dp)) for k in range(1, n_dp)]
    peers = [(k - 1, lax.rem(me + k, n)) for k in range(1, n)]
    barrier = pltpu.get_barrier_semaphore()
    for _, d in dp_peers:
        pl.semaphore_signal(barrier, inc=1, device_id={"dp": d}, device_id_type=pl.DeviceIdType.MESH)
    for _, t in peers:
        pl.semaphore_signal(barrier, inc=1, device_id={"tensor": t}, device_id_type=pl.DeviceIdType.MESH)
    pl.semaphore_wait(barrier, n_dp + n - 2)

    def push(stage, src, dst, k, device):
        copy = pltpu.make_async_remote_copy(
            src_ref=src, dst_ref=dst, send_sem=sems.at[0, stage, k], recv_sem=sems.at[1, stage, k],
            device_id=device, device_id_type=pl.DeviceIdType.MESH,
        )
        copy.start()
        return copy

    first = [push(0, x_ref.at[pl.ds(0, 8)], dp_buf.at[me_d], k, {"dp": d}) for k, d in dp_peers]
    rows[...] = x_ref[...]
    dp_buf[me_d] = x_ref[0:8, :]
    for copy in first:
        copy.wait()
    rows[0:8, :] = sum(dp_buf[d] for d in range(n_dp))
    second = [push(1, rows.at[:, columns(t)], part_buf.at[me], k, {"tensor": t}) for k, t in peers]
    part_buf[me] = rows[:, columns(me)]
    for copy in second:
        copy.wait()
    total[...] = sum(part_buf[t] for t in range(n))
    third = [push(2, total, whole.at[me], k, {"tensor": t}) for k, t in peers]
    whole[me] = total[...]
    for copy in third:
        copy.wait()
    for t in range(n):
        o_ref[:, t * width : (t + 1) * width] = whole[t]


def small_kernel(n_dp, n, x_ref, o_ref, dp_buf, total, t_buf, sems):
    me_d, me = lax.axis_index("dp"), lax.axis_index("tensor")
    dp_peers = [(k - 1, lax.rem(me_d + k, n_dp)) for k in range(1, n_dp)]
    peers = [(k - 1, lax.rem(me + k, n)) for k in range(1, n)]
    barrier = pltpu.get_barrier_semaphore()
    for _, d in dp_peers:
        pl.semaphore_signal(barrier, inc=1, device_id={"dp": d}, device_id_type=PUSH)
    for _, t in peers:
        pl.semaphore_signal(barrier, inc=1, device_id={"tensor": t}, device_id_type=PUSH)
    pl.semaphore_wait(barrier, n_dp + n - 2)

    def push(stage, src, dst, k, device):
        copy = pltpu.make_async_remote_copy(
            src_ref=src, dst_ref=dst, send_sem=sems.at[0, stage, k], recv_sem=sems.at[1, stage, k],
            device_id=device, device_id_type=PUSH,
        )
        copy.start()
        return copy

    first = [push(0, x_ref, dp_buf.at[me_d], k, {"dp": d}) for k, d in dp_peers]
    dp_buf[me_d] = x_ref[...]
    for copy in first:
        copy.wait()
    total[...] = sum(dp_buf[d] for d in range(n_dp))
    second = [push(1, total, t_buf.at[me], k, {"tensor": t}) for k, t in peers]
    t_buf[me] = total[...]
    for copy in second:
        copy.wait()
    o_ref[...] = sum(t_buf[t] for t in range(n))


def small_sum(x, n_dp, n):
    return pl.pallas_call(
        functools.partial(small_kernel, n_dp, n),
        out_shape=jax.ShapeDtypeStruct(x.shape, F32),
        in_specs=[VMEM_SPEC],
        out_specs=VMEM_SPEC,
        scratch_shapes=[
            pltpu.VMEM((n_dp,) + x.shape, F32),
            pltpu.VMEM(x.shape, F32),
            pltpu.VMEM((n,) + x.shape, F32),
            pltpu.SemaphoreType.DMA((2, 2, max(n, n_dp) - 1)),
        ],
        compiler_params=pltpu.CompilerParams(collective_id=2, has_side_effects=True),
        cost_estimate=cost(8),
    )(x)


def exchange(x, n_dp, n):
    height, width = x.shape
    slots = pltpu.VMEM((n, height, width // n), F32)
    return pl.pallas_call(
        functools.partial(exchange_kernel, n_dp, n),
        out_shape=jax.ShapeDtypeStruct(x.shape, F32),
        in_specs=[pl.BlockSpec(memory_space=pltpu.VMEM)],
        out_specs=pl.BlockSpec(memory_space=pltpu.VMEM),
        scratch_shapes=[
            pltpu.VMEM((n_dp, 8, width), F32),
            pltpu.VMEM(x.shape, F32),
            slots,
            pltpu.VMEM((height, width // n), F32),
            slots,
            pltpu.SemaphoreType.DMA((2, 3, max(n, n_dp) - 1)),
        ],
        compiler_params=pltpu.CompilerParams(collective_id=0, has_side_effects=True),
        cost_estimate=cost(16),
    )(x)


def on_device(
    layer_in,
    cotangent,
    lengths,
    prefix,
    pad_mask,
    clusters,
    qkv_w,
    out_w,
    gate_up_w,
    down_w,
    ln_params,
    qkv_row,
    qkv_col,
    out_row,
    out_col,
    gu_row,
    gu_col,
    down_row,
    down_col,
    ln_second,
):
    n_data = lax.axis_size("dp")
    n_tensor = lax.axis_size("tensor")
    tensor_rank = lax.axis_index("tensor")
    data_rank = lax.axis_index("dp")
    rows_dev, width = layer_in.shape
    cols_dev = qkv_w.shape[2]
    heads_dev = cols_dev // HD
    ff_dev = gate_up_w.shape[2]
    ff_pad = -(-ff_dev // 128) * 128
    n_clusters = max(2, n_data // 2)
    decay_rate = 1.0 - STEP ** (-0.8)
    seq_length = lengths[0]
    seq_prefix = prefix[0]
    ring = Ring(n_tensor)

    onehot = (clusters[:, None] == jnp.arange(n_clusters, dtype=jnp.int32)[None, :]).astype(F32)
    counts = jnp.sum(onehot, axis=0)
    own_row = jnp.sum(
        jnp.where((jnp.arange(n_data, dtype=jnp.int32) == data_rank)[:, None], onehot, 0.0), axis=0
    )
    seq_weight = jnp.sum(own_row / jnp.maximum(counts, 1.0))
    own_pos = tensor_rank * rows_dev + jnp.arange(rows_dev, dtype=jnp.int32)
    live_rows = ((own_pos < seq_length) & (pad_mask == 1)).astype(F32)
    grad_out = cotangent.astype(F32) * (live_rows * seq_weight)[:, None]
    grad_low = grad_out.astype(BF)

    key_live = (own_pos == 0) | (own_pos < seq_length) & (pad_mask == 1)
    seen_from = jnp.where(key_live, jnp.where(own_pos < seq_prefix, 0, own_pos), 2 * SLOT)
    seen = jnp.broadcast_to(seen_from.astype(F32)[None], (8, rows_dev))

    col_index = tensor_rank * ff_dev + jnp.arange(ff_pad, dtype=jnp.int32)
    ff_real = ((col_index < FF) & (jnp.arange(ff_pad) < ff_dev)).astype(F32)
    ff_mask = ff_real[:ff_dev]

    layer_own = layer_in.astype(F32)
    places = ring.places(rows_dev)
    act_one_all, qkv, seen_all = first_gather(
        n_tensor, layer_in, seen, ln_params, jnp.transpose(qkv_w, (1, 0, 2))
    )
    thr = jnp.broadcast_to(seen_all[:, 0].reshape(SLOT, 1), (SLOT, 128))

    pair = ring.halves(tie(grad_low, qkv))
    grad_pairs = [pair, ring.step(*pair)]
    context, lse = attn_forward(places, thr, qkv)
    pair = tie(grad_pairs[1], context)
    for s in range(2, n_tensor):
        pair = ring.step(*pair)
        grad_pairs.append(pair)
    grad_chunks = [jnp.concatenate(p, axis=0) for p in grad_pairs]
    pad = ((0, ff_pad - ff_dev), (0, 0))
    gate_up_late, down_late = tie(
        (jnp.transpose(gate_up_w, (2, 1, 0)), down_w), grad_chunks[min(3, n_tensor - 1)]
    )
    w_gu = jnp.concatenate([jnp.pad(gate_up_late[:, i], pad) for i in range(2)], axis=0)
    w_down = jnp.pad(down_late, pad)
    part_of = lambda x, s: x[s * rows_dev : (s + 1) * rows_dev]
    acc = None
    for s in ring.scatter_order():
        received = None if acc is None else ring.send(acc)
        acc = ring.add(received, dot(part_of(context, s), out_w, ((1,), (0,))))
    attn_own = jnp.concatenate(acc, axis=0)
    hidden_own = layer_own + attn_own
    norm_two = layer_norm(hidden_own, ln_params[2], ln_params[3]).astype(BF)

    act_two, inner, d_gu = [], [], []
    pair = ring.halves(norm_two)
    for s in range(n_tensor):
        pair = ring.step(*pair) if s else pair
        act = jnp.concatenate(pair, axis=0)
        act_two.append(act)
        gate_up = dot(act, w_gu, ((1,), (1,)))
        gate, up = gate_up[:, :ff_pad], gate_up[:, ff_pad:]
        gelu_gate, gelu_back = jax.vjp(jax.nn.gelu, gate)
        inner.append((gelu_gate * up * ff_real).astype(BF))
        d_inner = dot(grad_chunks[s], w_down, ((1,), (1,))) * ff_real
        d_gate = gelu_back(d_inner * up)[0]
        d_gu.append(jnp.concatenate([d_gate, d_inner * gelu_gate], axis=1).astype(BF))
    acc = None
    for s in ring.scatter_order():
        received = None if acc is None else ring.send(acc)
        acc = ring.add(received, dot(d_gu[s], w_gu, ((1,), (0,))))
    d_norm_two = jnp.concatenate(acc, axis=0)

    d_hidden_ln, ln_two_part = layer_norm_back(hidden_own, ln_params[2], d_norm_two)
    d_hidden = grad_out + d_hidden_ln
    whole = lambda chunks: jnp.concatenate(chunks, axis=0)
    inner_all = whole(inner)
    d_context, out_part, ff_mine = back_gather(
        n_tensor, ff_dev, d_hidden.astype(BF), out_w, context,
        inner_all, whole(d_gu), whole(grad_chunks), whole(act_two),
    )
    dp_wide, dp_tall = DpSum(n_data, 1), DpSum(n_data, 0)
    ff_mine = DpSum(n_data, 2).chips(ff_mine)
    out_mine = dp_wide.cores(out_part)

    layer_out, d_qkv = ffn_scatter(
        n_tensor, inner_all, w_down, hidden_own, thr, qkv, d_context, lse
    )

    w_qkv = tie(qkv_w, d_context).reshape(width, 3 * cols_dev)
    out_mine = dp_wide.chips(out_mine)
    qkv_part = dot(act_one_all, d_qkv, ((0,), (0,))).astype(BF)
    qkv_mine = dp_tall.cores(qkv_part)
    qkv_mid = dp_tall.chips(qkv_mine)
    ff_low = DpSum(n_data, 2).join(ff_mine)[:, :ff_dev]
    down_low, gate_low, up_low = (ff_low[i] for i in range(3))
    out_low, qkv_low = dp_wide.join(out_mine), dp_tall.join(qkv_mid)

    qkv_sum, out_sum, down_sum = qkv_low.astype(F32), out_low.astype(F32), down_low.astype(F32)
    gu_sum = (gate_low.astype(F32), up_low.astype(F32))
    gu_weights = (w_gu[:ff_dev], w_gu[ff_pad : ff_pad + ff_dev])
    gu_grad = pair_rows(gate_low, up_low)
    out_t, down_t, gu_t, qkv_t = tie((out_w, down_w, gu_weights, w_qkv), d_qkv)
    ff_col = ff_mask[:, None]
    blend = lambda old, total: decay_rate * old + (1.0 - decay_rate) * total
    square = lambda grad: grad * grad + eps_one
    square_sum = lambda w: jnp.sum(jnp.square(w.astype(F32)))

    qkv_sq, gu_sq = square(qkv_sum), [square(g) * ff_col for g in gu_sum]
    out_sq, down_sq = square(out_sum), square(down_sum) * ff_col
    qkv_col_new = blend(qkv_col.reshape(-1), jnp.sum(qkv_sq, axis=0) / width)
    gu_col_new = [blend(gu_col[i], jnp.sum(gu_sq[i], axis=1) / width) for i in range(2)]
    out_row_new = blend(out_row, jnp.sum(out_sq, axis=1) / width)
    down_row_new = blend(down_row, jnp.sum(down_sq, axis=1) / width)
    clean = lambda grad: grad * grad
    scalars = jnp.stack(
        [
            square_sum(qkv_t),
            sum(jnp.sum(jnp.square(w.astype(F32)) * ff_col) for w in gu_t),
            square_sum(out_t),
            jnp.sum(jnp.square(down_t.astype(F32)) * ff_col),
            jnp.sum(out_row_new),
            jnp.sum(down_row_new * ff_mask),
        ]
    )
    packed = jnp.concatenate(
        [
            ln_two_part,
            jnp.pad(scalars / n_data, (0, width - scalars.shape[0]))[None],
            jnp.zeros((5, width), F32),
            jnp.stack(
                [
                    jnp.sum(qkv_sq, axis=1),
                    jnp.sum(clean(qkv_sum) / qkv_col_new[None, :], axis=1),
                    sum(jnp.sum(sq, axis=0) for sq in gu_sq),
                    sum(
                        jnp.sum(clean(g) * (ff_mask / col)[:, None], axis=0)
                        for g, col in zip(gu_sum, gu_col_new)
                    ),
                    jnp.sum(out_sq, axis=0),
                    jnp.sum(clean(out_sum) / out_row_new[:, None], axis=0),
                    jnp.sum(down_sq, axis=0),
                    jnp.sum(clean(down_sum) * (ff_mask / down_row_new)[:, None], axis=0),
                ]
            ),
        ],
        axis=0,
    )
    packed = exchange(packed, n_data, n_tensor)
    ln_two_tot = packed[:2]
    qkv_wtot, gu_wtot, out_wtot, down_wtot, out_rtot, down_rtot = (packed[2, i] for i in range(6))
    qkv_tot, qkv_usq, gu_tot, gu_usq, out_tot, out_usq, down_tot, down_usq = (
        packed[8 + i] for i in range(8)
    )

    qkv_cols_all = 3 * cols_dev * n_tensor
    out_rows_all = cols_dev * n_tensor
    qkv_row_new = blend(qkv_row, qkv_tot / qkv_cols_all)
    qkv_mean = jnp.sum(qkv_row_new) / width
    gu_row_new = blend(gu_row, gu_tot / (2 * FF))
    gu_mean = jnp.sum(gu_row_new) / width
    out_col_new = blend(out_col, out_tot / out_rows_all)
    out_mean = out_rtot / out_rows_all
    down_col_new = blend(down_col, down_tot / FF)
    down_mean = down_rtot / FF
    qkv_rate = step_rate(jnp.sum(qkv_usq / qkv_row_new) * qkv_mean, qkv_wtot, width * qkv_cols_all)
    gu_rate = step_rate(jnp.sum(gu_usq / gu_row_new) * gu_mean, gu_wtot, width * 2 * FF)
    out_rate = step_rate(jnp.sum(out_usq / out_col_new) * out_mean, out_wtot, out_rows_all * width)
    down_rate = step_rate(jnp.sum(down_usq / down_col_new) * down_mean, down_wtot, FF * width)
    order = ring.scatter_order()
    pace = {1: qkv_part, 2: (qkv_mine, ff_mine), 3: ff_low, 4: out_mine, 5: qkv_mid}
    acc = None
    for i, s in enumerate(order):
        received = None if acc is None else ring.send(acc)
        after = pace.get(i, ())
        acc = ring.add(received, dot(part_of(d_qkv, s), w_qkv, ((1,), (1,))), after)
    d_norm_one = jnp.concatenate(acc, axis=0)
    d_input_ln, ln_one_part = layer_norm_back(layer_own, ln_params[0], d_norm_one)
    input_grad = (d_hidden + d_input_ln).astype(BF)

    qkv_new = apply_step(w_qkv, qkv_sum, qkv_row_new, qkv_col_new, qkv_mean, qkv_rate)
    out_new = apply_step(out_w, out_sum, out_row_new, out_col_new, out_mean, out_rate)
    down_new = apply_step(down_w, down_sum, down_row_new, down_col_new, down_mean, down_rate)
    gu_scale = lax.rsqrt(gu_row_new) * (gu_rate * jnp.sqrt(gu_mean))
    gu_new = pair_rows(gate_low, up_low, (w_gu, gu_scale, *map(lax.rsqrt, gu_col_new)))
    ln_one_part = tie(ln_one_part, (qkv_new, out_new, down_new, gu_new))
    ln_one_tot = small_sum(ln_one_part.reshape(8, -1), n_data, n_tensor).reshape(2, width)
    ln_tot = jnp.concatenate([ln_one_tot, ln_two_tot], axis=0)
    ln_second_new = blend(ln_second, ln_tot * ln_tot + eps_one)
    ln_update = ln_tot * lax.rsqrt(ln_second_new)
    ln_urms = jnp.sqrt(jnp.mean(ln_update * ln_update, axis=1, keepdims=True))
    ln_wrms = jnp.sqrt(jnp.mean(ln_params * ln_params, axis=1, keepdims=True))
    ln_new = ln_params - rate_base * jnp.maximum(eps_two, ln_wrms) * ln_update / jnp.maximum(
        1.0, ln_urms / clip_bound
    )
    return (
        layer_out,
        input_grad,
        qkv_sum.reshape(qkv_w.shape),
        qkv_new.reshape(qkv_w.shape),
        qkv_row_new,
        qkv_col_new.reshape(3, -1),
        out_sum,
        out_new,
        out_row_new,
        out_col_new,
        jnp.transpose(gu_grad, (2, 1, 0)),
        jnp.transpose(gu_new, (2, 1, 0)),
        gu_row_new,
        jnp.stack(gu_col_new),
        down_sum,
        down_new,
        down_row_new,
        down_col_new,
        ln_tot,
        ln_second_new,
        ln_new,
    )


def solution(mesh):
    in_specs = (
        P(("dp", "tensor"), None),
        P(("dp", "tensor"), None),
        P("dp"),
        P("dp"),
        P(("dp", "tensor")),
        P(),
        P(None, None, "tensor"),
        P("tensor", None),
        P(None, None, "tensor"),
        P("tensor", None),
        P(),
        P(),
        P(None, "tensor"),
        P("tensor"),
        P(),
        P(),
        P(None, "tensor"),
        P("tensor"),
        P(),
        P(),
    )
    out_specs = (
        P(("dp", "tensor"), None),
        P(("dp", "tensor"), None),
        P(None, None, "tensor"),
        P(None, None, "tensor"),
        P(),
        P(None, "tensor"),
        P("tensor", None),
        P("tensor", None),
        P("tensor"),
        P(),
        P(None, None, "tensor"),
        P(None, None, "tensor"),
        P(),
        P(None, "tensor"),
        P("tensor", None),
        P("tensor", None),
        P("tensor"),
        P(),
        P(),
        P(),
        P(),
    )
    return jax.shard_map(
        on_device, mesh=mesh, in_specs=in_specs, out_specs=out_specs, check_vma=False
    )
```

```python
import functools

import jax
import jax.numpy as jnp
from jax import lax
from jax.experimental import pallas as pl
from jax.experimental.pallas import tpu as pltpu
from jax.sharding import PartitionSpec as P

HD = 128
FF = 5461
SLOT = 2048
STEP = 10
PREFIX_MAX = SLOT // 2
Q_BLOCK = 512

ln_eps = 1e-05
eps_one = 1e-30
eps_two = 0.001
clip_bound = 1.0
rate_base = 1.0
masked_score = -1e30
LOG2E = 1.4426950408889634
BF = jnp.bfloat16
F32 = jnp.float32


def dot(a, b, dims):
    return lax.dot_general(a, b, (dims, ((), ())), preferred_element_type=F32)


def ring_order(n):
    b_size = 2 if n <= 8 else 4
    a_size = n // b_size
    order = []
    for a in range(a_size):
        cols = list(range(1, b_size))
        order += [a * b_size + c for c in (cols[::-1] if a % 2 else cols)]
    for a in range(a_size - 1, -1, -1):
        order.append(a * b_size)
    return order


class Ring:
    def __init__(self, n):
        self.n = n
        order = ring_order(n)
        self.fw = [(order[i], order[(i + 1) % n]) for i in range(n)]
        self.bw = [(order[i], order[(i - 1) % n]) for i in range(n)]
        place = [0] * n
        for p, t in enumerate(order):
            place[t] = p
        self.place = jnp.array(place, jnp.int32)
        self.pos = self.place[lax.axis_index("tensor")]

    def step(self, a, b):
        return lax.ppermute(a, "tensor", self.fw), lax.ppermute(b, "tensor", self.bw)

    def halves(self, x):
        half = x.shape[0] // 2
        return x[:half], x[half:]

    def scatter_order(self):
        return list(range(1, self.n)) + [0]

    def add(self, received, term, after=()):
        term = lax.optimization_barrier((term, after))[0]
        parts = self.halves(term)
        if received is not None:
            parts = tuple(r.astype(F32) + t for r, t in zip(received, parts))
        return parts

    def low(self, parts):
        return tuple(p.astype(BF) for p in parts)

    def send(self, parts):
        return self.step(*self.low(parts))

    def places(self, rows):
        t = jnp.arange(self.n, dtype=jnp.int32)
        step = self.place[t] - self.pos
        first = lax.rem(2 * self.n - step, self.n) * rows
        second = lax.rem(step + self.n, self.n) * rows + rows // 2
        return jnp.stack([first, second], axis=1).reshape(-1)


def cost(micros):
    return pl.CostEstimate(flops=int(micros * 1e9), transcendentals=0, bytes_accessed=4 << 20)


PUSH = pl.DeviceIdType.MESH


def pick(index, table):
    out = jnp.int32(table[0])
    for k in range(1, len(table)):
        out = jnp.where(index == k, jnp.int32(table[k]), out)
    return out


def neighbours(n):
    order = ring_order(n)
    pos = pick(lax.axis_index("tensor"), [order.index(t) for t in range(n)])
    ahead = pick(lax.rem(pos + 1, n), order)
    behind = pick(lax.rem(pos + n - 1, n), order)
    return pos, [{"tensor": ahead}, {"tensor": behind}]


def other_core():
    me = lax.axis_index("dp")
    return {"dp": me + 1 - 2 * lax.rem(me, 2)}


def greet(devices):
    barrier = pltpu.get_barrier_semaphore()
    for device in devices:
        pl.semaphore_signal(barrier, inc=1, device_id=device, device_id_type=PUSH)
    pl.semaphore_wait(barrier, len(devices))


def ring_copy(land, send_sem, recv_sem, sides, d, s):
    return pltpu.make_async_remote_copy(
        src_ref=land.at[d, s],
        dst_ref=land.at[d, s + 1],
        send_sem=send_sem.at[d, s],
        recv_sem=recv_sem.at[d, s],
        device_id=sides[d],
        device_id_type=PUSH,
    )


def ring_sent(n, copy):
    def sent(s, carry):
        for d in range(2):
            copy(d, s).wait_send()
        return carry

    lax.fori_loop(0, n - 1, sent, 0)


def ring_gather(n, x_ref, land, send_sem, recv_sem, sides, work):
    copy = functools.partial(ring_copy, land, send_sem, recv_sem, sides)
    half = x_ref.shape[0] // 2
    land[0, 0] = x_ref[:half, :]
    land[1, 0] = x_ref[half:, :]

    def step(s, carry):
        for d in range(2):

            @pl.when(s > 0)
            def _():
                copy(d, s - 1).wait_recv()

            @pl.when(s < n - 1)
            def _():
                copy(d, s).start()

        work(s)
        return carry

    lax.fori_loop(0, n, step, 0)
    ring_sent(n, copy)


def ring_scatter(n, land, send_sem, recv_sem, sides, term_buf, term, work, finish):
    copy = functools.partial(ring_copy, land, send_sem, recv_sem, sides)
    half = term_buf.shape[0] // 2
    for d in range(2):
        land[d, 0] = jnp.zeros(land.shape[2:], land.dtype)

    def step(s, carry):
        term(lax.rem(s + 1, n))
        for d in range(2):
            rows = slice(d * half, (d + 1) * half)

            @pl.when(s > 0)
            def _():
                copy(d, s - 1).wait_recv()

            total = land[d, s].astype(F32) + term_buf[rows, :]

            @pl.when(s < n - 1)
            def _():
                land[d, s] = total.astype(BF)
                copy(d, s).start()

            @pl.when(s == n - 1)
            def _():
                finish(rows, total)

        work(s)
        return carry

    lax.fori_loop(0, n, step, 0)
    ring_sent(n, copy)


def dot_columns(out, a, b, dims, block=512):
    width = b.shape[1]

    def columns(j, carry):
        at = pl.ds(pl.multiple_of(j * block, block), block)
        out(at, dot(a, b[:, at], dims))
        return carry

    lax.fori_loop(0, width // block, columns, 0)


def first_kernel(
    n, x_ref, seen_ref, ln_ref, w_ref, act_ref, qkv_ref, seen_all,
    land, act_buf, seen_buf, send_sem, recv_sem, act_sem, seen_sem,
):
    rows, cols = x_ref.shape[0], w_ref.shape[2]
    me = lax.axis_index("tensor")
    peers = [lax.rem(me + k, n) for k in range(1, n)]
    sides = neighbours(n)[1]
    greet([{"tensor": t} for t in peers])

    def seen_copy(k):
        return pltpu.make_async_remote_copy(
            src_ref=seen_ref, dst_ref=seen_buf.at[me], send_sem=seen_sem.at[0, k],
            recv_sem=seen_sem.at[1, k], device_id={"tensor": peers[k]}, device_id_type=PUSH,
        )

    def act_copy(s):
        place = pl.ds(pl.multiple_of(s * rows, rows), rows)
        return pltpu.make_async_copy(act_buf.at[s], act_ref.at[place], act_sem.at[s])

    def work(s):
        @pl.when(s == 0)
        def _():
            for k in range(n - 1):
                seen_copy(k).start()

        chunk = jnp.concatenate([land[0, s], land[1, s]], axis=0).astype(F32)
        act = layer_norm(chunk, ln_ref[0:1, :], ln_ref[1:2, :]).astype(BF)
        act_buf[s] = act
        act_copy(s).start()
        place = pl.ds(pl.multiple_of(s * rows, rows), rows)
        for k in range(3):
            qkv_ref[place, k * cols : (k + 1) * cols] = dot(act, w_ref[k], ((1,), (0,))).astype(BF)

    ring_gather(n, x_ref, land, send_sem, recv_sem, sides, work)
    seen_buf[me] = seen_ref[...]
    for k in range(n - 1):
        seen_copy(k).wait()
    seen_all[...] = seen_buf[...]

    def written(s, carry):
        act_copy(s).wait()
        return carry

    lax.fori_loop(0, n, written, 0)


def ring_scratch(n, rows, width):
    return [pltpu.VMEM((2, n, rows // 2, width), BF)], [
        pltpu.SemaphoreType.DMA((2, n - 1)),
        pltpu.SemaphoreType.DMA((2, n - 1)),
    ]


VMEM_SPEC = pl.BlockSpec(memory_space=pltpu.VMEM)
ANY_SPEC = pl.BlockSpec(memory_space=pl.ANY)


def first_gather(n, x, seen, ln_params, w):
    rows, width = x.shape
    cols = w.shape[2]
    buf, sems = ring_scratch(n, rows, width)
    return pl.pallas_call(
        functools.partial(first_kernel, n),
        in_specs=[VMEM_SPEC] * 4,
        out_specs=[ANY_SPEC, VMEM_SPEC, VMEM_SPEC],
        out_shape=[
            jax.ShapeDtypeStruct((n * rows, width), BF),
            jax.ShapeDtypeStruct((n * rows, 3 * cols), BF),
            jax.ShapeDtypeStruct((n,) + seen.shape, F32),
        ],
        scratch_shapes=buf
        + [pltpu.VMEM((n, rows, width), BF), pltpu.VMEM((n,) + seen.shape, F32)]
        + sems
        + [pltpu.SemaphoreType.DMA((n,)), pltpu.SemaphoreType.DMA((2, n - 1))],
        compiler_params=pltpu.CompilerParams(
            collective_id=1, has_side_effects=True, vmem_limit_bytes=56 << 20
        ),
        cost_estimate=pl.CostEstimate(
            flops=6 * n * rows * width * cols, transcendentals=0, bytes_accessed=40 << 20
        ),
    )(x, seen, ln_params, w)


def back_kernel(
    n, x_ref, w_ref, ctx_ref, inner_hbm, d_gu_hbm, grad_hbm, act_hbm,
    d_ctx_ref, out_ref, mine_ref,
    land, lhs, rhs, part, core_land, out_sum, send_sem, recv_sem, load_sem, core_sem,
):
    rows, ff_pad = x_ref.shape[0], lhs.shape[2]
    ff_rows, half = core_land.shape[1:]
    sides, partner = neighbours(n)[1], other_core()
    core = lax.rem(lax.axis_index("dp"), 2)
    of_core = lambda c: pl.ds(pl.multiple_of(c * half, half), half)
    loads = [
        pltpu.make_async_copy(src, dst, load_sem.at[i])
        for i, (src, dst) in enumerate(
            (
                (inner_hbm, lhs.at[0]),
                (grad_hbm, rhs.at[0]),
                (d_gu_hbm.at[:, pl.ds(0, ff_pad)], lhs.at[1]),
                (act_hbm, rhs.at[1]),
                (d_gu_hbm.at[:, pl.ds(ff_pad, ff_pad)], lhs.at[2]),
            )
        )
    ]
    for load in loads:
        load.start()
    out_sum[...] = jnp.zeros_like(out_sum)
    greet(sides + [partner])

    def core_copy(i):
        return pltpu.make_async_remote_copy(
            src_ref=part.at[i, :, of_core(1 - core)],
            dst_ref=core_land.at[i],
            send_sem=core_sem.at[0, i],
            recv_sem=core_sem.at[1, i],
            device_id=partner,
            device_id_type=PUSH,
        )

    def work(s):
        chunk = jnp.concatenate([land[0, s], land[1, s]], axis=0)
        place = pl.ds(pl.multiple_of(s * rows, rows), rows)
        d_ctx_ref[place, :] = dot(chunk, w_ref[...], ((1,), (1,))).astype(BF)
        out_sum[...] += dot(ctx_ref[place, :], chunk, ((0,), (0,)))
        for i in range(3):

            @pl.when(s == i + 1)
            def _():
                for load in (loads[:2], loads[2:4], loads[4:])[i]:
                    load.wait()

                def put(at, value):
                    part[i, :, at] = value[:ff_rows].astype(BF)

                dot_columns(put, lhs[i], rhs.at[min(i, 1)], ((0,), (0,)))
                core_copy(i).start()

            @pl.when(s == i + 3)
            def _():
                core_copy(i).wait()
                total = part[i, :, of_core(core)].astype(F32) + core_land[i].astype(F32)
                mine_ref[i] = total.astype(BF)

    ring_gather(n, x_ref, land, send_sem, recv_sem, sides, work)
    out_ref[...] = out_sum[...].astype(BF)


def back_gather(n, ff_dev, x, w, context, inner, d_gu, grad, act):
    rows, width = x.shape
    ff_pad = inner.shape[1]
    ff_rows = -(-ff_dev // 16) * 16
    buf, sems = ring_scratch(n, rows, width)
    return pl.pallas_call(
        functools.partial(back_kernel, n),
        in_specs=[VMEM_SPEC] * 3 + [ANY_SPEC] * 4,
        out_specs=[VMEM_SPEC] * 3,
        out_shape=[
            jax.ShapeDtypeStruct((n * rows, w.shape[0]), BF),
            jax.ShapeDtypeStruct(w.shape, BF),
            jax.ShapeDtypeStruct((3, ff_rows, width // 2), BF),
        ],
        scratch_shapes=buf
        + [
            pltpu.VMEM((3, n * rows, ff_pad), BF),
            pltpu.VMEM((2, n * rows, width), BF),
            pltpu.VMEM((3, ff_rows, width), BF),
            pltpu.VMEM((3, ff_rows, width // 2), BF),
            pltpu.VMEM(w.shape, F32),
        ]
        + sems
        + [pltpu.SemaphoreType.DMA((5,)), pltpu.SemaphoreType.DMA((2, 3))],
        compiler_params=pltpu.CompilerParams(
            collective_id=3, has_side_effects=True, vmem_limit_bytes=60 << 20
        ),
        cost_estimate=cost(80),
    )(x, w, context, inner, d_gu, grad, act)


def ffn_kernel(
    n, n_x, heads, inner_ref, w_ref, hidden_ref, thr_ref, qkv_ref, d_ctx_ref, lse_ref,
    out_part_ref, act_hbm, mine_hbm,
    out_ref, d_qkv_ref, slots_hbm, qkv_mine_ref, out_mine_ref,
    land, term_buf, q_ref, k_ref, v_ref, do_ref, dk_sum, dv_sum,
    act_buf, part, qkv_land, out_land,
    send_sem, recv_sem, act_sem, core_sem, slot_sem, own_sem,
):
    rows = hidden_ref.shape[0]
    pos, sides = neighbours(n)
    partner = other_core()
    core, chip = lax.rem(lax.axis_index("dp"), 2), lax.axis_index("dp") // 2
    chips = [{"dp": 2 * lax.rem(chip + k, n_x) + core} for k in range(1, n_x)]
    block = act_buf.shape[2]
    blocks = act_hbm.shape[1] // block
    tall, wide = qkv_land.shape[0], out_land.shape[1]
    tall_of = lambda c: pl.ds(pl.multiple_of(c * tall, tall), tall)
    wide_of = lambda c: pl.ds(pl.multiple_of(c * wide, wide), wide)

    def act_load(j):
        return pltpu.make_async_copy(
            act_hbm.at[:, pl.ds(j * block, block)], act_buf.at[j % 2], act_sem.at[j]
        )

    def core_copy(i):
        src, dst = (
            (part.at[tall_of(1 - core)], qkv_land),
            (out_part_ref.at[:, wide_of(1 - core)], out_land),
        )[i]
        return pltpu.make_async_remote_copy(
            src_ref=src, dst_ref=dst, send_sem=core_sem.at[0, i], recv_sem=core_sem.at[1, i],
            device_id=partner, device_id_type=PUSH,
        )

    def slot_copy(k):
        return pltpu.make_async_remote_copy(
            src_ref=mine_hbm, dst_ref=slots_hbm.at[chip], send_sem=slot_sem.at[0, k],
            recv_sem=slot_sem.at[1, k], device_id=chips[k], device_id_type=PUSH,
        )

    own_copy = pltpu.make_async_copy(mine_hbm, slots_hbm.at[chip], own_sem)
    for j in range(2):
        act_load(j).start()
    greet(sides + [partner] + chips)
    core_copy(1).start()
    for k in range(n_x - 1):
        slot_copy(k).start()
    own_copy.start()
    places = []
    place_of = [ring_order(n).index(t) for t in range(n)]
    for t in range(n):
        places.append(lax.rem(pos + (n - place_of[t]), n) * rows)
        places.append(lax.rem(place_of[t] - pos + n, n) * rows + rows // 2)

    def term(c):
        place = pl.ds(pl.multiple_of(c * rows, rows), rows)

        def put(at, value):
            term_buf[:, at] = value

        dot_columns(put, inner_ref[place, :], w_ref, ((1,), (0,)))

    def work(s):
        for h in range(heads):

            @pl.when(s == h + 1)
            def _():
                columns = lambda i: slice((i * heads + h) * HD, (i * heads + h + 1) * HD)
                for i, dst in enumerate((q_ref, k_ref, v_ref)):
                    to_order(places, qkv_ref, columns(i), dst)
                to_order(places, d_ctx_ref, columns(0), do_ref)
                attn_backward_head(
                    places, thr_ref, lse_ref.at[h], q_ref, k_ref, v_ref, do_ref, dk_sum, dv_sum,
                    d_qkv_ref, columns,
                )

        @pl.when(s == 1)
        def _():
            core_copy(1).wait()
            total = out_part_ref[:, wide_of(core)].astype(F32) + out_land[...].astype(F32)
            out_mine_ref[...] = total.astype(BF)

        for turn in range(blocks // 2):

            @pl.when(s == heads + 1 + turn)
            def _():
                for j in (2 * turn, 2 * turn + 1):
                    act_load(j).wait()
                    grad = dot(d_qkv_ref[...], act_buf[j % 2], ((0,), (0,)))
                    part[j * block : (j + 1) * block, :] = grad.T.astype(BF)
                for j in (2 * turn + 2, 2 * turn + 3):
                    if j < blocks:
                        act_load(j).start()
                if turn == blocks // 2 - 1:
                    core_copy(0).start()

        @pl.when(s == heads + 2 + blocks // 2)
        def _():
            core_copy(0).wait()
            total = part[tall_of(core), :].astype(F32) + qkv_land[...].astype(F32)
            qkv_mine_ref[...] = total.astype(BF)

    def finish(at, total):
        out_ref[at, :] = (hidden_ref[at, :] + total).astype(BF)

    ring_scatter(n, land, send_sem, recv_sem, sides, term_buf, term, work, finish)
    for k in range(n_x - 1):
        slot_copy(k).wait()
    own_copy.wait()


def ffn_scatter(n, n_x, inner, w, hidden, thr, qkv, d_context, lse, out_part, act, mine):
    rows, width = hidden.shape
    cols, block = d_context.shape[1], 512
    heads = d_context.shape[1] // HD
    buf, sems = ring_scratch(n, rows, width)
    return pl.pallas_call(
        functools.partial(ffn_kernel, n, n_x, heads),
        in_specs=[VMEM_SPEC] * 8 + [ANY_SPEC] * 2,
        out_specs=[VMEM_SPEC] * 2 + [ANY_SPEC] + [VMEM_SPEC] * 2,
        out_shape=[
            jax.ShapeDtypeStruct((rows, width), BF),
            jax.ShapeDtypeStruct(qkv.shape, BF),
            jax.ShapeDtypeStruct((n_x,) + mine.shape, BF),
            jax.ShapeDtypeStruct((width // 2, 3 * cols), BF),
            jax.ShapeDtypeStruct((cols, width // 2), BF),
        ],
        scratch_shapes=buf
        + [pltpu.VMEM((rows, width), F32)]
        + [pltpu.VMEM((SLOT, HD), BF)] * 4
        + [pltpu.VMEM((SLOT, HD), F32)] * 2
        + [
            pltpu.VMEM((2, n * rows, block), BF),
            pltpu.VMEM((width, 3 * cols), BF),
            pltpu.VMEM((width // 2, 3 * cols), BF),
            pltpu.VMEM((cols, width // 2), BF),
        ]
        + sems
        + [
            pltpu.SemaphoreType.DMA((width // block,)),
            pltpu.SemaphoreType.DMA((2, 2)),
            pltpu.SemaphoreType.DMA((2, n_x - 1)),
            pltpu.SemaphoreType.DMA,
        ],
        compiler_params=pltpu.CompilerParams(
            collective_id=4, has_side_effects=True, vmem_limit_bytes=62 << 20
        ),
        cost_estimate=cost(95),
    )(inner, w, hidden, thr, qkv, d_context, lse, out_part, act, mine)


class DpSum:
    def __init__(self, n_dp, axis):
        self.n_dp, self.axis = n_dp, axis
        self.core = lax.rem(lax.axis_index("dp"), 2)

    def swap(self, y, bit):
        return lax.ppermute(y, "dp", [(i, i ^ bit) for i in range(self.n_dp)])

    def cores(self, x):
        half = x.shape[self.axis] // 2
        part = lambda c: lax.dynamic_slice_in_dim(x, c * half, half, self.axis)
        return (part(self.core).astype(F32) + self.swap(part(1 - self.core), 1).astype(F32)).astype(BF)

    def chips(self, mine):
        bit = 2
        while bit < self.n_dp:
            mine = (mine.astype(F32) + self.swap(mine, bit).astype(F32)).astype(BF)
            bit *= 2
        return mine

    def join(self, mine):
        other = self.swap(mine, 1)
        first = jnp.where(self.core == 0, mine, other)
        second = jnp.where(self.core == 0, other, mine)
        return jnp.concatenate([first, second], axis=self.axis)


def norm_stats(rows):
    mean_row = jnp.mean(rows, axis=-1, keepdims=True)
    centered = rows - mean_row
    variance = jnp.mean(centered * centered, axis=-1, keepdims=True)
    scale = lax.rsqrt(variance + ln_eps)
    return centered * scale, scale


def layer_norm(rows, gain, shift):
    return norm_stats(rows)[0] * gain + shift


def layer_norm_back(rows, gain, e):
    n, scale = norm_stats(rows)
    eg = e * gain
    dv = scale * (
        eg - jnp.mean(eg, axis=-1, keepdims=True) - n * jnp.mean(eg * n, axis=-1, keepdims=True)
    )
    return dv, jnp.stack([jnp.sum(e * n, axis=0), jnp.sum(e, axis=0)])


def seen_mask(thr_ref, q0, shape):
    thr = thr_ref[: shape[0], :]
    thr = jnp.concatenate([thr] * (shape[1] // thr.shape[1]), axis=1)
    q_pos = (q0 + lax.broadcasted_iota(jnp.int32, shape, 1)).astype(F32)
    return q_pos >= thr


def q_blocks():
    return [(q0, max(PREFIX_MAX, q0 + Q_BLOCK)) for q0 in range(0, SLOT, Q_BLOCK)]


def to_order(places, src_ref, columns, dst_ref):
    half = SLOT // len(places)
    for j, start in enumerate(places):
        place = pl.ds(pl.multiple_of(start, half), half)
        dst_ref[j * half : (j + 1) * half, :] = src_ref[place, columns]


def from_order(places, q0, value, dst_ref, columns):
    half = SLOT // len(places)
    for i in range(value.shape[0] // half):
        place = pl.ds(pl.multiple_of(places[q0 // half + i], half), half)
        dst_ref[place, columns] = value[i * half : (i + 1) * half, :]


def attn_forward_kernel(places, thr_ref, q_in, k_in, v_in, o_ref, lse_ref, q_ref, k_ref, v_ref):
    c = HD**-0.5 * LOG2E
    places = [places[j] for j in range(places.shape[0])]
    for src, dst in ((q_in, q_ref), (k_in, k_ref), (v_in, v_ref)):
        to_order(places, src, slice(None), dst)
    for q0, klim in q_blocks():
        raw = dot(k_ref[:klim, :], q_ref[q0 : q0 + Q_BLOCK, :], ((1,), (1,)))
        raw = jnp.where(seen_mask(thr_ref, q0, raw.shape), raw, masked_score)
        top = jnp.max(raw, axis=0, keepdims=True)
        p = jnp.exp2((raw - top) * c)
        total = jnp.sum(p, axis=0, keepdims=True)
        out = dot(v_ref[:klim, :], p.astype(BF), ((0,), (0,))) / total
        from_order(places, q0, out.T.astype(BF), o_ref, slice(None))
        lse_ref[0, :, q0 : q0 + Q_BLOCK] = top * c + jnp.log2(total)


def attn_backward_head(
    places, thr_ref, lse_ref, q_ref, k_ref, v_ref, do_ref, dk_sum, dv_sum, d_ref, columns
):
    scale = HD**-0.5
    dk_sum[...] = jnp.zeros_like(dk_sum)
    dv_sum[...] = jnp.zeros_like(dv_sum)
    for q0, klim in q_blocks():
        rows = slice(q0, q0 + Q_BLOCK)
        k, q, do = k_ref[:klim, :], q_ref[rows, :], do_ref[rows, :]
        raw = dot(k, q, ((1,), (1,)))
        p = jnp.exp2(raw * (scale * LOG2E) - lse_ref[:, rows])
        p = jnp.where(seen_mask(thr_ref, q0, raw.shape), p, 0.0)
        dv_sum[:klim, :] += dot(p.astype(BF), do, ((1,), (0,)))
        dp = dot(v_ref[:klim, :], do, ((1,), (1,)))
        delta = jnp.sum(p * dp, axis=0, keepdims=True)
        ds = (p * (dp - delta) * scale).astype(BF)
        dk_sum[:klim, :] += dot(ds, q, ((1,), (0,)))
        dq = dot(k, ds, ((0,), (0,))).T.astype(BF)
        from_order(places, q0, dq, d_ref, columns(0))
    from_order(places, 0, dk_sum[...].astype(BF), d_ref, columns(1))
    from_order(places, 0, dv_sum[...].astype(BF), d_ref, columns(2))


SMEM_SPEC = pl.BlockSpec(memory_space=pltpu.SMEM)
ATTN_PARAMS = pltpu.CompilerParams(vmem_limit_bytes=56 << 20)


def head_spec(k, heads):
    return pl.BlockSpec((SLOT, HD), lambda h: (0, k * heads + h))


def attn_forward(places, thr, qkv):
    heads = qkv.shape[1] // (3 * HD)
    lse = pl.BlockSpec((1, 1, SLOT), lambda h: (h, 0, 0))
    return pl.pallas_call(
        attn_forward_kernel,
        grid=(heads,),
        in_specs=[SMEM_SPEC, pl.BlockSpec((SLOT, 128), lambda h: (0, 0))]
        + [head_spec(k, heads) for k in range(3)],
        out_specs=[head_spec(0, heads), lse],
        out_shape=[
            jax.ShapeDtypeStruct((SLOT, heads * HD), BF),
            jax.ShapeDtypeStruct((heads, 1, SLOT), F32),
        ],
        scratch_shapes=[pltpu.VMEM((SLOT, HD), BF)] * 3,
        compiler_params=ATTN_PARAMS,
        cost_estimate=cost(6.5 * heads),
    )(places, thr, qkv, qkv, qkv)


def step_rate(update_sq, weight_sq, n_real):
    update_rms = jnp.sqrt(update_sq / n_real)
    weight_rms = jnp.sqrt(weight_sq / n_real)
    return rate_base * jnp.maximum(eps_two, weight_rms) / jnp.maximum(1.0, update_rms / clip_bound)


def apply_step(weight, grad, row_new, col_new, row_mean, rate):
    row = lax.rsqrt(row_new) * (rate * jnp.sqrt(row_mean))
    return weight.astype(F32) - grad * (row[:, None] * lax.rsqrt(col_new)[None, :])


def pair_kernel(factors, *refs):
    g_ref, u_ref = refs[:2]
    o_ref = refs[-1]
    g, u = g_ref[...].astype(F32), u_ref[...].astype(F32)
    if factors:
        wg_ref, wu_ref, row_ref, cg_ref, cu_ref = refs[2:7]
        row = row_ref[...]
        g = wg_ref[...].astype(F32) - g * (row * cg_ref[...])
        u = wu_ref[...].astype(F32) - u * (row * cu_ref[...])
    o_ref[:, 0, :] = g
    o_ref[:, 1, :] = u


def pair_rows(gate, up, step=None):
    ff, width = gate.shape
    block = 96
    grid = (-(-ff // block),)
    wide = pl.BlockSpec((block, width), lambda i: (i, 0))
    args, specs = [gate, up], [wide, wide]
    if step is not None:
        w_gu, row, col_gate, col_up = step
        shift = w_gu.shape[0] // 2 // block
        column = pl.BlockSpec((block, 1), lambda i: (i, 0))
        args += [w_gu, w_gu, row[None, :], col_gate[:, None], col_up[:, None]]
        specs += [
            wide,
            pl.BlockSpec((block, width), lambda i: (i + shift, 0)),
            pl.BlockSpec((1, width), lambda i: (0, 0)),
            column,
            column,
        ]
    return pl.pallas_call(
        functools.partial(pair_kernel, step is not None),
        grid=grid,
        in_specs=specs,
        out_specs=pl.BlockSpec((block, 2, width), lambda i: (i, 0, 0)),
        out_shape=jax.ShapeDtypeStruct((ff, 2, width), F32),
        compiler_params=pltpu.CompilerParams(vmem_limit_bytes=40 << 20),
        cost_estimate=pl.CostEstimate(flops=8 * ff * width, transcendentals=0, bytes_accessed=16 * ff * width),
    )(*args)


def tie(x, after):
    return lax.optimization_barrier((x, after))[0]


def exchange_kernel(n_dp, n, x_ref, o_ref, dp_buf, rows, part_buf, total, whole, sems):
    me_d, me = lax.axis_index("dp"), lax.axis_index("tensor")
    width = x_ref.shape[1] // n
    columns = lambda t: pl.ds(pl.multiple_of(t * width, width), width)
    dp_peers = [(k - 1, lax.rem(me_d + k, n_dp)) for k in range(1, n_dp)]
    peers = [(k - 1, lax.rem(me + k, n)) for k in range(1, n)]
    barrier = pltpu.get_barrier_semaphore()
    for _, d in dp_peers:
        pl.semaphore_signal(barrier, inc=1, device_id={"dp": d}, device_id_type=pl.DeviceIdType.MESH)
    for _, t in peers:
        pl.semaphore_signal(barrier, inc=1, device_id={"tensor": t}, device_id_type=pl.DeviceIdType.MESH)
    pl.semaphore_wait(barrier, n_dp + n - 2)

    def push(stage, src, dst, k, device):
        copy = pltpu.make_async_remote_copy(
            src_ref=src, dst_ref=dst, send_sem=sems.at[0, stage, k], recv_sem=sems.at[1, stage, k],
            device_id=device, device_id_type=pl.DeviceIdType.MESH,
        )
        copy.start()
        return copy

    first = [push(0, x_ref.at[pl.ds(0, 8)], dp_buf.at[me_d], k, {"dp": d}) for k, d in dp_peers]
    rows[...] = x_ref[...]
    dp_buf[me_d] = x_ref[0:8, :]
    for copy in first:
        copy.wait()
    rows[0:8, :] = sum(dp_buf[d] for d in range(n_dp))
    second = [push(1, rows.at[:, columns(t)], part_buf.at[me], k, {"tensor": t}) for k, t in peers]
    part_buf[me] = rows[:, columns(me)]
    for copy in second:
        copy.wait()
    total[...] = sum(part_buf[t] for t in range(n))
    third = [push(2, total, whole.at[me], k, {"tensor": t}) for k, t in peers]
    whole[me] = total[...]
    for copy in third:
        copy.wait()
    for t in range(n):
        o_ref[:, t * width : (t + 1) * width] = whole[t]


def small_kernel(n_dp, n, x_ref, o_ref, dp_buf, total, t_buf, sems):
    me_d, me = lax.axis_index("dp"), lax.axis_index("tensor")
    dp_peers = [(k - 1, lax.rem(me_d + k, n_dp)) for k in range(1, n_dp)]
    peers = [(k - 1, lax.rem(me + k, n)) for k in range(1, n)]
    barrier = pltpu.get_barrier_semaphore()
    for _, d in dp_peers:
        pl.semaphore_signal(barrier, inc=1, device_id={"dp": d}, device_id_type=PUSH)
    for _, t in peers:
        pl.semaphore_signal(barrier, inc=1, device_id={"tensor": t}, device_id_type=PUSH)
    pl.semaphore_wait(barrier, n_dp + n - 2)

    def push(stage, src, dst, k, device):
        copy = pltpu.make_async_remote_copy(
            src_ref=src, dst_ref=dst, send_sem=sems.at[0, stage, k], recv_sem=sems.at[1, stage, k],
            device_id=device, device_id_type=PUSH,
        )
        copy.start()
        return copy

    first = [push(0, x_ref, dp_buf.at[me_d], k, {"dp": d}) for k, d in dp_peers]
    dp_buf[me_d] = x_ref[...]
    for copy in first:
        copy.wait()
    total[...] = sum(dp_buf[d] for d in range(n_dp))
    second = [push(1, total, t_buf.at[me], k, {"tensor": t}) for k, t in peers]
    t_buf[me] = total[...]
    for copy in second:
        copy.wait()
    o_ref[...] = sum(t_buf[t] for t in range(n))


def small_sum(x, n_dp, n):
    return pl.pallas_call(
        functools.partial(small_kernel, n_dp, n),
        out_shape=jax.ShapeDtypeStruct(x.shape, F32),
        in_specs=[VMEM_SPEC],
        out_specs=VMEM_SPEC,
        scratch_shapes=[
            pltpu.VMEM((n_dp,) + x.shape, F32),
            pltpu.VMEM(x.shape, F32),
            pltpu.VMEM((n,) + x.shape, F32),
            pltpu.SemaphoreType.DMA((2, 2, max(n, n_dp) - 1)),
        ],
        compiler_params=pltpu.CompilerParams(collective_id=2, has_side_effects=True),
        cost_estimate=cost(8),
    )(x)


def exchange(x, n_dp, n):
    height, width = x.shape
    slots = pltpu.VMEM((n, height, width // n), F32)
    return pl.pallas_call(
        functools.partial(exchange_kernel, n_dp, n),
        out_shape=jax.ShapeDtypeStruct(x.shape, F32),
        in_specs=[pl.BlockSpec(memory_space=pltpu.VMEM)],
        out_specs=pl.BlockSpec(memory_space=pltpu.VMEM),
        scratch_shapes=[
            pltpu.VMEM((n_dp, 8, width), F32),
            pltpu.VMEM(x.shape, F32),
            slots,
            pltpu.VMEM((height, width // n), F32),
            slots,
            pltpu.SemaphoreType.DMA((2, 3, max(n, n_dp) - 1)),
        ],
        compiler_params=pltpu.CompilerParams(collective_id=0, has_side_effects=True),
        cost_estimate=cost(16),
    )(x)


def on_device(
    layer_in,
    cotangent,
    lengths,
    prefix,
    pad_mask,
    clusters,
    qkv_w,
    out_w,
    gate_up_w,
    down_w,
    ln_params,
    qkv_row,
    qkv_col,
    out_row,
    out_col,
    gu_row,
    gu_col,
    down_row,
    down_col,
    ln_second,
):
    n_data = lax.axis_size("dp")
    n_tensor = lax.axis_size("tensor")
    tensor_rank = lax.axis_index("tensor")
    data_rank = lax.axis_index("dp")
    rows_dev, width = layer_in.shape
    cols_dev = qkv_w.shape[2]
    heads_dev = cols_dev // HD
    ff_dev = gate_up_w.shape[2]
    ff_pad = -(-ff_dev // 128) * 128
    n_clusters = max(2, n_data // 2)
    decay_rate = 1.0 - STEP ** (-0.8)
    seq_length = lengths[0]
    seq_prefix = prefix[0]
    ring = Ring(n_tensor)

    onehot = (clusters[:, None] == jnp.arange(n_clusters, dtype=jnp.int32)[None, :]).astype(F32)
    counts = jnp.sum(onehot, axis=0)
    own_row = jnp.sum(
        jnp.where((jnp.arange(n_data, dtype=jnp.int32) == data_rank)[:, None], onehot, 0.0), axis=0
    )
    seq_weight = jnp.sum(own_row / jnp.maximum(counts, 1.0))
    own_pos = tensor_rank * rows_dev + jnp.arange(rows_dev, dtype=jnp.int32)
    live_rows = ((own_pos < seq_length) & (pad_mask == 1)).astype(F32)
    grad_out = cotangent.astype(F32) * (live_rows * seq_weight)[:, None]
    grad_low = grad_out.astype(BF)

    key_live = (own_pos == 0) | (own_pos < seq_length) & (pad_mask == 1)
    seen_from = jnp.where(key_live, jnp.where(own_pos < seq_prefix, 0, own_pos), 2 * SLOT)
    seen = jnp.broadcast_to(seen_from.astype(F32)[None], (8, rows_dev))

    col_index = tensor_rank * ff_dev + jnp.arange(ff_pad, dtype=jnp.int32)
    ff_real = ((col_index < FF) & (jnp.arange(ff_pad) < ff_dev)).astype(F32)
    ff_mask = ff_real[:ff_dev]

    layer_own = layer_in.astype(F32)
    places = ring.places(rows_dev)
    act_one_all, qkv, seen_all = first_gather(
        n_tensor, layer_in, seen, ln_params, jnp.transpose(qkv_w, (1, 0, 2))
    )
    thr = jnp.broadcast_to(seen_all[:, 0].reshape(SLOT, 1), (SLOT, 128))

    pair = ring.halves(tie(grad_low, qkv))
    grad_pairs = [pair, ring.step(*pair)]
    context, lse = attn_forward(places, thr, qkv)
    pair = tie(grad_pairs[1], context)
    for s in range(2, n_tensor):
        pair = ring.step(*pair)
        grad_pairs.append(pair)
    grad_chunks = [jnp.concatenate(p, axis=0) for p in grad_pairs]
    pad = ((0, ff_pad - ff_dev), (0, 0))
    gate_up_late, down_late = tie(
        (jnp.transpose(gate_up_w, (2, 1, 0)), down_w), grad_chunks[min(3, n_tensor - 1)]
    )
    w_gu = jnp.concatenate([jnp.pad(gate_up_late[:, i], pad) for i in range(2)], axis=0)
    w_down = jnp.pad(down_late, pad)
    part_of = lambda x, s: x[s * rows_dev : (s + 1) * rows_dev]
    acc = None
    for s in ring.scatter_order():
        received = None if acc is None else ring.send(acc)
        acc = ring.add(received, dot(part_of(context, s), out_w, ((1,), (0,))))
    attn_own = jnp.concatenate(acc, axis=0)
    hidden_own = layer_own + attn_own
    norm_two = layer_norm(hidden_own, ln_params[2], ln_params[3]).astype(BF)

    act_two, inner, d_gu = [], [], []
    pair = ring.halves(norm_two)
    for s in range(n_tensor):
        pair = ring.step(*pair) if s else pair
        act = jnp.concatenate(pair, axis=0)
        act_two.append(act)
        gate_up = dot(act, w_gu, ((1,), (1,)))
        gate, up = gate_up[:, :ff_pad], gate_up[:, ff_pad:]
        gelu_gate, gelu_back = jax.vjp(jax.nn.gelu, gate)
        inner.append((gelu_gate * up * ff_real).astype(BF))
        d_inner = dot(grad_chunks[s], w_down, ((1,), (1,))) * ff_real
        d_gate = gelu_back(d_inner * up)[0]
        d_gu.append(jnp.concatenate([d_gate, d_inner * gelu_gate], axis=1).astype(BF))
    acc = None
    for s in ring.scatter_order():
        received = None if acc is None else ring.send(acc)
        acc = ring.add(received, dot(d_gu[s], w_gu, ((1,), (0,))))
    d_norm_two = jnp.concatenate(acc, axis=0)

    d_hidden_ln, ln_two_part = layer_norm_back(hidden_own, ln_params[2], d_norm_two)
    d_hidden = grad_out + d_hidden_ln
    whole = lambda chunks: jnp.concatenate(chunks, axis=0)
    inner_all = whole(inner)
    d_context, out_part, ff_mine = back_gather(
        n_tensor, ff_dev, d_hidden.astype(BF), out_w, context,
        inner_all, whole(d_gu), whole(grad_chunks), whole(act_two),
    )
    n_x = n_data // 2
    layer_out, d_qkv, ff_slots, qkv_mine, out_mine = ffn_scatter(
        n_tensor, n_x, inner_all, w_down, hidden_own, thr, qkv, d_context, lse,
        out_part, act_one_all, ff_mine,
    )

    dp_wide, dp_tall = DpSum(n_data, 1), DpSum(n_data, 0)
    w_qkv = tie(qkv_w, d_context).reshape(width, 3 * cols_dev)
    qkv_mid, out_mid = dp_tall.chips(qkv_mine), dp_wide.chips(out_mine)
    ff_mid = sum(ff_slots[x].astype(F32) for x in range(n_x)).astype(BF)
    ff_low = DpSum(n_data, 2).join(ff_mid)[:, :ff_dev]
    down_low, gate_low, up_low = (ff_low[i] for i in range(3))
    out_low, qkv_low = dp_wide.join(out_mid), dp_tall.join(qkv_mid)

    qkv_sum, out_sum, down_sum = qkv_low.astype(F32), out_low.astype(F32), down_low.astype(F32)
    gu_sum = (gate_low.astype(F32), up_low.astype(F32))
    gu_weights = (w_gu[:ff_dev], w_gu[ff_pad : ff_pad + ff_dev])
    gu_grad = pair_rows(gate_low, up_low)
    out_t, down_t, gu_t, qkv_t = tie((out_w, down_w, gu_weights, w_qkv), d_qkv)
    ff_col = ff_mask[:, None]
    blend = lambda old, total: decay_rate * old + (1.0 - decay_rate) * total
    square = lambda grad: grad * grad + eps_one
    square_sum = lambda w: jnp.sum(jnp.square(w.astype(F32)))

    qkv_sq, gu_sq = square(qkv_sum), [square(g) * ff_col for g in gu_sum]
    out_sq, down_sq = square(out_sum), square(down_sum) * ff_col
    qkv_col_new = blend(qkv_col.reshape(-1), jnp.sum(qkv_sq, axis=0) / width)
    gu_col_new = [blend(gu_col[i], jnp.sum(gu_sq[i], axis=1) / width) for i in range(2)]
    out_row_new = blend(out_row, jnp.sum(out_sq, axis=1) / width)
    down_row_new = blend(down_row, jnp.sum(down_sq, axis=1) / width)
    clean = lambda grad: grad * grad
    scalars = jnp.stack(
        [
            square_sum(qkv_t),
            sum(jnp.sum(jnp.square(w.astype(F32)) * ff_col) for w in gu_t),
            square_sum(out_t),
            jnp.sum(jnp.square(down_t.astype(F32)) * ff_col),
            jnp.sum(out_row_new),
            jnp.sum(down_row_new * ff_mask),
        ]
    )
    packed = jnp.concatenate(
        [
            ln_two_part,
            jnp.pad(scalars / n_data, (0, width - scalars.shape[0]))[None],
            jnp.zeros((5, width), F32),
            jnp.stack(
                [
                    jnp.sum(qkv_sq, axis=1),
                    jnp.sum(clean(qkv_sum) / qkv_col_new[None, :], axis=1),
                    sum(jnp.sum(sq, axis=0) for sq in gu_sq),
                    sum(
                        jnp.sum(clean(g) * (ff_mask / col)[:, None], axis=0)
                        for g, col in zip(gu_sum, gu_col_new)
                    ),
                    jnp.sum(out_sq, axis=0),
                    jnp.sum(clean(out_sum) / out_row_new[:, None], axis=0),
                    jnp.sum(down_sq, axis=0),
                    jnp.sum(clean(down_sum) * (ff_mask / down_row_new)[:, None], axis=0),
                ]
            ),
        ],
        axis=0,
    )
    packed = exchange(packed, n_data, n_tensor)
    ln_two_tot = packed[:2]
    qkv_wtot, gu_wtot, out_wtot, down_wtot, out_rtot, down_rtot = (packed[2, i] for i in range(6))
    qkv_tot, qkv_usq, gu_tot, gu_usq, out_tot, out_usq, down_tot, down_usq = (
        packed[8 + i] for i in range(8)
    )

    qkv_cols_all = 3 * cols_dev * n_tensor
    out_rows_all = cols_dev * n_tensor
    qkv_row_new = blend(qkv_row, qkv_tot / qkv_cols_all)
    qkv_mean = jnp.sum(qkv_row_new) / width
    gu_row_new = blend(gu_row, gu_tot / (2 * FF))
    gu_mean = jnp.sum(gu_row_new) / width
    out_col_new = blend(out_col, out_tot / out_rows_all)
    out_mean = out_rtot / out_rows_all
    down_col_new = blend(down_col, down_tot / FF)
    down_mean = down_rtot / FF
    qkv_rate = step_rate(jnp.sum(qkv_usq / qkv_row_new) * qkv_mean, qkv_wtot, width * qkv_cols_all)
    gu_rate = step_rate(jnp.sum(gu_usq / gu_row_new) * gu_mean, gu_wtot, width * 2 * FF)
    out_rate = step_rate(jnp.sum(out_usq / out_col_new) * out_mean, out_wtot, out_rows_all * width)
    down_rate = step_rate(jnp.sum(down_usq / down_col_new) * down_mean, down_wtot, FF * width)
    order = ring.scatter_order()
    pace = {3: ff_low, 5: (out_mid, qkv_mid), n_tensor - 1: (qkv_row_new, gu_row_new, out_col_new, down_col_new)}
    acc = None
    for i, s in enumerate(order):
        received = None if acc is None else ring.send(acc)
        after = pace.get(i, ())
        acc = ring.add(received, dot(part_of(d_qkv, s), w_qkv, ((1,), (1,))), after)
    d_norm_one = jnp.concatenate(acc, axis=0)
    d_input_ln, ln_one_part = layer_norm_back(layer_own, ln_params[0], d_norm_one)
    input_grad = (d_hidden + d_input_ln).astype(BF)

    qkv_new = apply_step(w_qkv, qkv_sum, qkv_row_new, qkv_col_new, qkv_mean, qkv_rate)
    out_new = apply_step(out_w, out_sum, out_row_new, out_col_new, out_mean, out_rate)
    down_new = apply_step(down_w, down_sum, down_row_new, down_col_new, down_mean, down_rate)
    gu_scale = lax.rsqrt(gu_row_new) * (gu_rate * jnp.sqrt(gu_mean))
    gu_new = pair_rows(gate_low, up_low, (w_gu, gu_scale, *map(lax.rsqrt, gu_col_new)))
    ln_one_part = tie(ln_one_part, (qkv_new, out_new, down_new, gu_new))
    ln_one_tot = small_sum(ln_one_part.reshape(8, -1), n_data, n_tensor).reshape(2, width)
    ln_tot = jnp.concatenate([ln_one_tot, ln_two_tot], axis=0)
    ln_second_new = blend(ln_second, ln_tot * ln_tot + eps_one)
    ln_update = ln_tot * lax.rsqrt(ln_second_new)
    ln_urms = jnp.sqrt(jnp.mean(ln_update * ln_update, axis=1, keepdims=True))
    ln_wrms = jnp.sqrt(jnp.mean(ln_params * ln_params, axis=1, keepdims=True))
    ln_new = ln_params - rate_base * jnp.maximum(eps_two, ln_wrms) * ln_update / jnp.maximum(
        1.0, ln_urms / clip_bound
    )
    return (
        layer_out,
        input_grad,
        qkv_sum.reshape(qkv_w.shape),
        qkv_new.reshape(qkv_w.shape),
        qkv_row_new,
        qkv_col_new.reshape(3, -1),
        out_sum,
        out_new,
        out_row_new,
        out_col_new,
        jnp.transpose(gu_grad, (2, 1, 0)),
        jnp.transpose(gu_new, (2, 1, 0)),
        gu_row_new,
        jnp.stack(gu_col_new),
        down_sum,
        down_new,
        down_row_new,
        down_col_new,
        ln_tot,
        ln_second_new,
        ln_new,
    )


def solution(mesh):
    in_specs = (
        P(("dp", "tensor"), None),
        P(("dp", "tensor"), None),
        P("dp"),
        P("dp"),
        P(("dp", "tensor")),
        P(),
        P(None, None, "tensor"),
        P("tensor", None),
        P(None, None, "tensor"),
        P("tensor", None),
        P(),
        P(),
        P(None, "tensor"),
        P("tensor"),
        P(),
        P(),
        P(None, "tensor"),
        P("tensor"),
        P(),
        P(),
    )
    out_specs = (
        P(("dp", "tensor"), None),
        P(("dp", "tensor"), None),
        P(None, None, "tensor"),
        P(None, None, "tensor"),
        P(),
        P(None, "tensor"),
        P("tensor", None),
        P("tensor", None),
        P("tensor"),
        P(),
        P(None, None, "tensor"),
        P(None, None, "tensor"),
        P(),
        P(None, "tensor"),
        P("tensor", None),
        P("tensor", None),
        P("tensor"),
        P(),
        P(),
        P(),
        P(),
    )
    return jax.shard_map(
        on_device, mesh=mesh, in_specs=in_specs, out_specs=out_specs, check_vma=False
    )
```

```python
import functools

import jax
import jax.numpy as jnp
from jax import lax
from jax.experimental import pallas as pl
from jax.experimental.pallas import tpu as pltpu
from jax.sharding import PartitionSpec as P

HD = 128
FF = 5461
SLOT = 2048
STEP = 10
PREFIX_MAX = SLOT // 2
Q_BLOCK = 512

ln_eps = 1e-05
eps_one = 1e-30
eps_two = 0.001
clip_bound = 1.0
rate_base = 1.0
masked_score = -1e30
LOG2E = 1.4426950408889634
BF = jnp.bfloat16
F32 = jnp.float32


def dot(a, b, dims):
    return lax.dot_general(a, b, (dims, ((), ())), preferred_element_type=F32)


def ring_order(n):
    b_size = 2 if n <= 8 else 4
    a_size = n // b_size
    order = []
    for a in range(a_size):
        cols = list(range(1, b_size))
        order += [a * b_size + c for c in (cols[::-1] if a % 2 else cols)]
    for a in range(a_size - 1, -1, -1):
        order.append(a * b_size)
    return order


class Ring:
    def __init__(self, n):
        self.n = n
        order = ring_order(n)
        self.fw = [(order[i], order[(i + 1) % n]) for i in range(n)]
        self.bw = [(order[i], order[(i - 1) % n]) for i in range(n)]
        place = [0] * n
        for p, t in enumerate(order):
            place[t] = p
        self.place = jnp.array(place, jnp.int32)
        self.pos = self.place[lax.axis_index("tensor")]

    def step(self, a, b):
        return lax.ppermute(a, "tensor", self.fw), lax.ppermute(b, "tensor", self.bw)

    def halves(self, x):
        half = x.shape[0] // 2
        return x[:half], x[half:]

    def scatter_order(self):
        return list(range(1, self.n)) + [0]

    def add(self, received, term, after=()):
        term = lax.optimization_barrier((term, after))[0]
        parts = self.halves(term)
        if received is not None:
            parts = tuple(r.astype(F32) + t for r, t in zip(received, parts))
        return parts

    def low(self, parts):
        return tuple(p.astype(BF) for p in parts)

    def send(self, parts):
        return self.step(*self.low(parts))

    def places(self, rows):
        t = jnp.arange(self.n, dtype=jnp.int32)
        step = self.place[t] - self.pos
        first = lax.rem(2 * self.n - step, self.n) * rows
        second = lax.rem(step + self.n, self.n) * rows + rows // 2
        return jnp.stack([first, second], axis=1).reshape(-1)


def cost(micros):
    return pl.CostEstimate(flops=int(micros * 1e9), transcendentals=0, bytes_accessed=4 << 20)


PUSH = pl.DeviceIdType.MESH
PIECES = 2


def pick(index, table):
    out = jnp.int32(table[0])
    for k in range(1, len(table)):
        out = jnp.where(index == k, jnp.int32(table[k]), out)
    return out


def neighbours(n):
    order = ring_order(n)
    pos = pick(lax.axis_index("tensor"), [order.index(t) for t in range(n)])
    ahead = pick(lax.rem(pos + 1, n), order)
    behind = pick(lax.rem(pos + n - 1, n), order)
    return pos, [{"tensor": ahead}, {"tensor": behind}]


def other_core():
    me = lax.axis_index("dp")
    return {"dp": me + 1 - 2 * lax.rem(me, 2)}


def other_chips(n_x):
    core, chip = lax.rem(lax.axis_index("dp"), 2), lax.axis_index("dp") // 2
    return chip, [{"dp": 2 * lax.rem(chip + k, n_x) + core} for k in range(1, n_x)]


def greet(devices):
    barrier = pltpu.get_barrier_semaphore()
    for device in devices:
        pl.semaphore_signal(barrier, inc=1, device_id=device, device_id_type=PUSH)
    pl.semaphore_wait(barrier, len(devices))


def ring_copy(land, send_sem, recv_sem, sides, d, s, piece=None):
    src, dst, sem = land.at[d, s], land.at[d, s + 1], d
    if piece is not None:
        size = land.shape[2] // PIECES
        rows = pl.ds(piece * size, size)
        src, dst, sem = land.at[d, s, rows], land.at[d, s + 1, rows], d * PIECES + piece
    return pltpu.make_async_remote_copy(
        src_ref=src,
        dst_ref=dst,
        send_sem=send_sem.at[sem, s],
        recv_sem=recv_sem.at[sem, s],
        device_id=sides[d],
        device_id_type=PUSH,
    )


def ring_sent(n, copy, pieces=(None,)):
    def sent(s, carry):
        for d in range(2):
            for piece in pieces:
                copy(d, s, piece).wait_send()
        return carry

    lax.fori_loop(0, n - 1, sent, 0)


def ring_gather(n, x_ref, land, send_sem, recv_sem, sides, work):
    copy = functools.partial(ring_copy, land, send_sem, recv_sem, sides)
    half = x_ref.shape[0] // 2
    land[0, 0] = x_ref[:half, :]
    land[1, 0] = x_ref[half:, :]

    def step(s, carry):
        for d in range(2):

            @pl.when(s > 0)
            def _():
                copy(d, s - 1).wait_recv()

            @pl.when(s < n - 1)
            def _():
                copy(d, s).start()

        work(s)
        return carry

    lax.fori_loop(0, n, step, 0)
    ring_sent(n, copy)


def ring_scatter(n, land, send_sem, recv_sem, sides, term_buf, term, work, finish):
    copy = functools.partial(ring_copy, land, send_sem, recv_sem, sides)
    half = term_buf.shape[0] // 2
    size = half // PIECES
    for d in range(2):
        land[d, 0] = jnp.zeros(land.shape[2:], land.dtype)

    def step(s, carry):
        term(lax.rem(s + 1, n))
        for piece in range(PIECES):
            for d in range(2):
                part = slice(piece * size, (piece + 1) * size)
                rows = slice(d * half + piece * size, d * half + (piece + 1) * size)

                @pl.when(s > 0)
                def _():
                    copy(d, s - 1, piece).wait_recv()

                total = land[d, s, part].astype(F32) + term_buf[rows, :]

                @pl.when(s < n - 1)
                def _():
                    land[d, s, part] = total.astype(BF)
                    copy(d, s, piece).start()

                @pl.when(s == n - 1)
                def _():
                    finish(rows, total)

        work(s)
        return carry

    lax.fori_loop(0, n, step, 0)
    ring_sent(n, copy, range(PIECES))


def dot_columns(out, a, b, dims, block=512):
    width = b.shape[1]

    def columns(j, carry):
        at = pl.ds(pl.multiple_of(j * block, block), block)
        out(at, dot(a, b[:, at], dims))
        return carry

    lax.fori_loop(0, width // block, columns, 0)


def first_kernel(
    n, x_ref, seen_ref, ln_ref, w_ref, act_ref, qkv_ref, seen_all,
    land, act_buf, seen_buf, send_sem, recv_sem, act_sem, seen_sem,
):
    rows, cols = x_ref.shape[0], w_ref.shape[2]
    me = lax.axis_index("tensor")
    peers = [lax.rem(me + k, n) for k in range(1, n)]
    sides = neighbours(n)[1]
    greet([{"tensor": t} for t in peers])

    def seen_copy(k):
        return pltpu.make_async_remote_copy(
            src_ref=seen_ref, dst_ref=seen_buf.at[me], send_sem=seen_sem.at[0, k],
            recv_sem=seen_sem.at[1, k], device_id={"tensor": peers[k]}, device_id_type=PUSH,
        )

    def act_copy(s):
        place = pl.ds(pl.multiple_of(s * rows, rows), rows)
        return pltpu.make_async_copy(act_buf.at[s], act_ref.at[place], act_sem.at[s])

    def work(s):
        @pl.when(s == 0)
        def _():
            for k in range(n - 1):
                seen_copy(k).start()

        chunk = jnp.concatenate([land[0, s], land[1, s]], axis=0).astype(F32)
        act = layer_norm(chunk, ln_ref[0:1, :], ln_ref[1:2, :]).astype(BF)
        act_buf[s] = act
        act_copy(s).start()
        place = pl.ds(pl.multiple_of(s * rows, rows), rows)
        for k in range(3):
            qkv_ref[place, k * cols : (k + 1) * cols] = dot(act, w_ref[k], ((1,), (0,))).astype(BF)

    ring_gather(n, x_ref, land, send_sem, recv_sem, sides, work)
    seen_buf[me] = seen_ref[...]
    for k in range(n - 1):
        seen_copy(k).wait()
    seen_all[...] = seen_buf[...]

    def written(s, carry):
        act_copy(s).wait()
        return carry

    lax.fori_loop(0, n, written, 0)


def ring_scratch(n, rows, width, pieces=1):
    return [pltpu.VMEM((2, n, rows // 2, width), BF)], [
        pltpu.SemaphoreType.DMA((2 * pieces, n - 1)),
        pltpu.SemaphoreType.DMA((2 * pieces, n - 1)),
    ]


VMEM_SPEC = pl.BlockSpec(memory_space=pltpu.VMEM)
ANY_SPEC = pl.BlockSpec(memory_space=pl.ANY)


def first_gather(n, x, seen, ln_params, w):
    rows, width = x.shape
    cols = w.shape[2]
    buf, sems = ring_scratch(n, rows, width)
    return pl.pallas_call(
        functools.partial(first_kernel, n),
        in_specs=[VMEM_SPEC] * 4,
        out_specs=[ANY_SPEC, VMEM_SPEC, VMEM_SPEC],
        out_shape=[
            jax.ShapeDtypeStruct((n * rows, width), BF),
            jax.ShapeDtypeStruct((n * rows, 3 * cols), BF),
            jax.ShapeDtypeStruct((n,) + seen.shape, F32),
        ],
        scratch_shapes=buf
        + [pltpu.VMEM((n, rows, width), BF), pltpu.VMEM((n,) + seen.shape, F32)]
        + sems
        + [pltpu.SemaphoreType.DMA((n,)), pltpu.SemaphoreType.DMA((2, n - 1))],
        compiler_params=pltpu.CompilerParams(
            collective_id=1, has_side_effects=True, vmem_limit_bytes=56 << 20
        ),
        cost_estimate=pl.CostEstimate(
            flops=6 * n * rows * width * cols, transcendentals=0, bytes_accessed=40 << 20
        ),
    )(x, seen, ln_params, w)


def back_kernel(
    n, n_x, x_ref, w_ref, ctx_ref, inner_hbm, d_gu_hbm, grad_hbm, act_hbm,
    d_ctx_ref, out_ref, mine_ref, slots_hbm,
    land, lhs, rhs, part, core_land, out_sum, send_sem, recv_sem, load_sem, core_sem, slot_sem,
):
    rows, ff_pad = x_ref.shape[0], lhs.shape[2]
    ff_rows, half = core_land.shape[1:]
    sides, partner = neighbours(n)[1], other_core()
    core = lax.rem(lax.axis_index("dp"), 2)
    of_core = lambda c: pl.ds(pl.multiple_of(c * half, half), half)
    loads = [
        pltpu.make_async_copy(src, dst, load_sem.at[i])
        for i, (src, dst) in enumerate(
            (
                (inner_hbm, lhs.at[0]),
                (grad_hbm, rhs.at[0]),
                (d_gu_hbm.at[:, pl.ds(0, ff_pad)], lhs.at[1]),
                (act_hbm, rhs.at[1]),
                (d_gu_hbm.at[:, pl.ds(ff_pad, ff_pad)], lhs.at[2]),
            )
        )
    ]
    for load in loads:
        load.start()
    out_sum[...] = jnp.zeros_like(out_sum)
    chip, chips = other_chips(n_x)
    greet(sides + [partner] + chips)

    def slot_copy(k):
        return pltpu.make_async_remote_copy(
            src_ref=mine_ref.at[0], dst_ref=slots_hbm.at[chip], send_sem=slot_sem.at[0, k],
            recv_sem=slot_sem.at[1, k], device_id=chips[k], device_id_type=PUSH,
        )

    def core_copy(i):
        return pltpu.make_async_remote_copy(
            src_ref=part.at[i, :, of_core(1 - core)],
            dst_ref=core_land.at[i],
            send_sem=core_sem.at[0, i],
            recv_sem=core_sem.at[1, i],
            device_id=partner,
            device_id_type=PUSH,
        )

    def work(s):
        chunk = jnp.concatenate([land[0, s], land[1, s]], axis=0)
        place = pl.ds(pl.multiple_of(s * rows, rows), rows)
        d_ctx_ref[place, :] = dot(chunk, w_ref[...], ((1,), (1,))).astype(BF)
        out_sum[...] += dot(ctx_ref[place, :], chunk, ((0,), (0,)))
        for i in range(3):

            @pl.when(s == i + 1)
            def _():
                for load in (loads[:2], loads[2:4], loads[4:])[i]:
                    load.wait()

                def put(at, value):
                    part[i, :, at] = value[:ff_rows].astype(BF)

                dot_columns(put, lhs[i], rhs.at[min(i, 1)], ((0,), (0,)))
                core_copy(i).start()

            @pl.when(s == i + 3)
            def _():
                core_copy(i).wait()
                total = part[i, :, of_core(core)].astype(F32) + core_land[i].astype(F32)
                mine_ref[i] = total.astype(BF)
                if i == 0:
                    for k in range(n_x - 1):
                        slot_copy(k).start()

    ring_gather(n, x_ref, land, send_sem, recv_sem, sides, work)
    out_ref[...] = out_sum[...].astype(BF)
    for k in range(n_x - 1):
        slot_copy(k).wait()


def back_gather(n, n_x, ff_dev, x, w, context, inner, d_gu, grad, act):
    rows, width = x.shape
    ff_pad = inner.shape[1]
    ff_rows = -(-ff_dev // 16) * 16
    buf, sems = ring_scratch(n, rows, width)
    return pl.pallas_call(
        functools.partial(back_kernel, n, n_x),
        in_specs=[VMEM_SPEC] * 3 + [ANY_SPEC] * 4,
        out_specs=[VMEM_SPEC] * 3 + [ANY_SPEC],
        out_shape=[
            jax.ShapeDtypeStruct((n * rows, w.shape[0]), BF),
            jax.ShapeDtypeStruct(w.shape, BF),
            jax.ShapeDtypeStruct((3, ff_rows, width // 2), BF),
            jax.ShapeDtypeStruct((n_x, ff_rows, width // 2), BF),
        ],
        scratch_shapes=buf
        + [
            pltpu.VMEM((3, n * rows, ff_pad), BF),
            pltpu.VMEM((2, n * rows, width), BF),
            pltpu.VMEM((3, ff_rows, width), BF),
            pltpu.VMEM((3, ff_rows, width // 2), BF),
            pltpu.VMEM(w.shape, F32),
        ]
        + sems
        + [
            pltpu.SemaphoreType.DMA((5,)),
            pltpu.SemaphoreType.DMA((2, 3)),
            pltpu.SemaphoreType.DMA((2, n_x - 1)),
        ],
        compiler_params=pltpu.CompilerParams(
            collective_id=3, has_side_effects=True, vmem_limit_bytes=60 << 20
        ),
        cost_estimate=cost(80),
    )(x, w, context, inner, d_gu, grad, act)


def ffn_kernel(
    n, n_x, heads, inner_ref, w_ref, hidden_ref, thr_ref, qkv_ref, d_ctx_ref, lse_ref,
    out_part_ref, act_hbm, mine_hbm,
    out_ref, d_qkv_ref, slots_hbm, qkv_mine_ref, out_mine_ref,
    land, term_buf, q_ref, k_ref, v_ref, do_ref, dk_sum, dv_sum,
    act_buf, part, qkv_land, out_land,
    send_sem, recv_sem, act_sem, core_sem, slot_sem,
):
    rows = hidden_ref.shape[0]
    pos, sides = neighbours(n)
    partner = other_core()
    core = lax.rem(lax.axis_index("dp"), 2)
    chip, chips = other_chips(n_x)
    block = act_buf.shape[2]
    blocks = act_hbm.shape[1] // block
    tall, wide = qkv_land.shape[0], out_land.shape[1]
    tall_of = lambda c: pl.ds(pl.multiple_of(c * tall, tall), tall)
    wide_of = lambda c: pl.ds(pl.multiple_of(c * wide, wide), wide)

    def act_load(j):
        return pltpu.make_async_copy(
            act_hbm.at[:, pl.ds(j * block, block)], act_buf.at[j % 2], act_sem.at[j]
        )

    def core_copy(i):
        src, dst = (
            (part.at[tall_of(1 - core)], qkv_land),
            (out_part_ref.at[:, wide_of(1 - core)], out_land),
        )[i]
        return pltpu.make_async_remote_copy(
            src_ref=src, dst_ref=dst, send_sem=core_sem.at[0, i], recv_sem=core_sem.at[1, i],
            device_id=partner, device_id_type=PUSH,
        )

    def slot_copy(k):
        return pltpu.make_async_remote_copy(
            src_ref=mine_hbm.at[pl.ds(1, 2)], dst_ref=slots_hbm.at[chip], send_sem=slot_sem.at[0, k],
            recv_sem=slot_sem.at[1, k], device_id=chips[k], device_id_type=PUSH,
        )

    for j in range(2):
        act_load(j).start()
    greet(sides + [partner] + chips)
    core_copy(1).start()
    for k in range(n_x - 1):
        slot_copy(k).start()
    places = []
    place_of = [ring_order(n).index(t) for t in range(n)]
    for t in range(n):
        places.append(lax.rem(pos + (n - place_of[t]), n) * rows)
        places.append(lax.rem(place_of[t] - pos + n, n) * rows + rows // 2)

    def term(c):
        place = pl.ds(pl.multiple_of(c * rows, rows), rows)

        def put(at, value):
            term_buf[:, at] = value

        dot_columns(put, inner_ref[place, :], w_ref, ((1,), (0,)))

    def work(s):
        for h in range(heads):

            @pl.when(s == h + 1)
            def _():
                columns = lambda i: slice((i * heads + h) * HD, (i * heads + h + 1) * HD)
                for i, dst in enumerate((q_ref, k_ref, v_ref)):
                    to_order(places, qkv_ref, columns(i), dst)
                to_order(places, d_ctx_ref, columns(0), do_ref)
                attn_backward_head(
                    places, thr_ref, lse_ref.at[h], q_ref, k_ref, v_ref, do_ref, dk_sum, dv_sum,
                    d_qkv_ref, columns,
                )

        @pl.when(s == 1)
        def _():
            core_copy(1).wait()
            total = out_part_ref[:, wide_of(core)].astype(F32) + out_land[...].astype(F32)
            out_mine_ref[...] = total.astype(BF)

        for turn in range(blocks // 2):

            @pl.when(s == heads + 1 + turn)
            def _():
                for j in (2 * turn, 2 * turn + 1):
                    act_load(j).wait()
                    grad = dot(d_qkv_ref[...], act_buf[j % 2], ((0,), (0,)))
                    part[j * block : (j + 1) * block, :] = grad.T.astype(BF)
                for j in (2 * turn + 2, 2 * turn + 3):
                    if j < blocks:
                        act_load(j).start()
                if turn == blocks // 2 - 1:
                    core_copy(0).start()

        @pl.when(s == heads + 2 + blocks // 2)
        def _():
            core_copy(0).wait()
            total = part[tall_of(core), :].astype(F32) + qkv_land[...].astype(F32)
            qkv_mine_ref[...] = total.astype(BF)

    def finish(at, total):
        out_ref[at, :] = (hidden_ref[at, :] + total).astype(BF)

    ring_scatter(n, land, send_sem, recv_sem, sides, term_buf, term, work, finish)
    for k in range(n_x - 1):
        slot_copy(k).wait()


def ffn_scatter(n, n_x, inner, w, hidden, thr, qkv, d_context, lse, out_part, act, mine):
    rows, width = hidden.shape
    cols, block = d_context.shape[1], 512
    heads = d_context.shape[1] // HD
    buf, sems = ring_scratch(n, rows, width, PIECES)
    return pl.pallas_call(
        functools.partial(ffn_kernel, n, n_x, heads),
        in_specs=[VMEM_SPEC] * 8 + [ANY_SPEC] * 2,
        out_specs=[VMEM_SPEC] * 2 + [ANY_SPEC] + [VMEM_SPEC] * 2,
        out_shape=[
            jax.ShapeDtypeStruct((rows, width), BF),
            jax.ShapeDtypeStruct(qkv.shape, BF),
            jax.ShapeDtypeStruct((n_x, 2) + mine.shape[1:], BF),
            jax.ShapeDtypeStruct((width // 2, 3 * cols), BF),
            jax.ShapeDtypeStruct((cols, width // 2), BF),
        ],
        scratch_shapes=buf
        + [pltpu.VMEM((rows, width), F32)]
        + [pltpu.VMEM((SLOT, HD), BF)] * 4
        + [pltpu.VMEM((SLOT, HD), F32)] * 2
        + [
            pltpu.VMEM((2, n * rows, block), BF),
            pltpu.VMEM((width, 3 * cols), BF),
            pltpu.VMEM((width // 2, 3 * cols), BF),
            pltpu.VMEM((cols, width // 2), BF),
        ]
        + sems
        + [
            pltpu.SemaphoreType.DMA((width // block,)),
            pltpu.SemaphoreType.DMA((2, 2)),
            pltpu.SemaphoreType.DMA((2, n_x - 1)),
        ],
        compiler_params=pltpu.CompilerParams(
            collective_id=4, has_side_effects=True, vmem_limit_bytes=62 << 20
        ),
        cost_estimate=cost(95),
    )(inner, w, hidden, thr, qkv, d_context, lse, out_part, act, mine)


class DpSum:
    def __init__(self, n_dp, axis):
        self.n_dp, self.axis = n_dp, axis
        self.core = lax.rem(lax.axis_index("dp"), 2)

    def swap(self, y, bit):
        return lax.ppermute(y, "dp", [(i, i ^ bit) for i in range(self.n_dp)])

    def cores(self, x):
        half = x.shape[self.axis] // 2
        part = lambda c: lax.dynamic_slice_in_dim(x, c * half, half, self.axis)
        return (part(self.core).astype(F32) + self.swap(part(1 - self.core), 1).astype(F32)).astype(BF)

    def chips(self, mine):
        bit = 2
        while bit < self.n_dp:
            mine = (mine.astype(F32) + self.swap(mine, bit).astype(F32)).astype(BF)
            bit *= 2
        return mine

    def join(self, mine):
        other = self.swap(mine, 1)
        first = jnp.where(self.core == 0, mine, other)
        second = jnp.where(self.core == 0, other, mine)
        return jnp.concatenate([first, second], axis=self.axis)


def norm_stats(rows):
    mean_row = jnp.mean(rows, axis=-1, keepdims=True)
    centered = rows - mean_row
    variance = jnp.mean(centered * centered, axis=-1, keepdims=True)
    scale = lax.rsqrt(variance + ln_eps)
    return centered * scale, scale


def layer_norm(rows, gain, shift):
    return norm_stats(rows)[0] * gain + shift


def layer_norm_back(rows, gain, e):
    n, scale = norm_stats(rows)
    eg = e * gain
    dv = scale * (
        eg - jnp.mean(eg, axis=-1, keepdims=True) - n * jnp.mean(eg * n, axis=-1, keepdims=True)
    )
    return dv, jnp.stack([jnp.sum(e * n, axis=0), jnp.sum(e, axis=0)])


def seen_mask(thr_ref, q0, shape):
    thr = thr_ref[: shape[0], :]
    thr = jnp.concatenate([thr] * (shape[1] // thr.shape[1]), axis=1)
    q_pos = (q0 + lax.broadcasted_iota(jnp.int32, shape, 1)).astype(F32)
    return q_pos >= thr


def q_blocks():
    return [(q0, max(PREFIX_MAX, q0 + Q_BLOCK)) for q0 in range(0, SLOT, Q_BLOCK)]


def to_order(places, src_ref, columns, dst_ref):
    half = SLOT // len(places)
    for j, start in enumerate(places):
        place = pl.ds(pl.multiple_of(start, half), half)
        dst_ref[j * half : (j + 1) * half, :] = src_ref[place, columns]


def from_order(places, q0, value, dst_ref, columns):
    half = SLOT // len(places)
    for i in range(value.shape[0] // half):
        place = pl.ds(pl.multiple_of(places[q0 // half + i], half), half)
        dst_ref[place, columns] = value[i * half : (i + 1) * half, :]


def attn_forward_kernel(places, thr_ref, q_in, k_in, v_in, o_ref, lse_ref, q_ref, k_ref, v_ref):
    c = HD**-0.5 * LOG2E
    places = [places[j] for j in range(places.shape[0])]
    for src, dst in ((q_in, q_ref), (k_in, k_ref), (v_in, v_ref)):
        to_order(places, src, slice(None), dst)
    for q0, klim in q_blocks():
        raw = dot(k_ref[:klim, :], q_ref[q0 : q0 + Q_BLOCK, :], ((1,), (1,)))
        raw = jnp.where(seen_mask(thr_ref, q0, raw.shape), raw, masked_score)
        top = jnp.max(raw, axis=0, keepdims=True)
        p = jnp.exp2((raw - top) * c)
        total = jnp.sum(p, axis=0, keepdims=True)
        out = dot(v_ref[:klim, :], p.astype(BF), ((0,), (0,))) / total
        from_order(places, q0, out.T.astype(BF), o_ref, slice(None))
        lse_ref[0, :, q0 : q0 + Q_BLOCK] = top * c + jnp.log2(total)


def attn_backward_head(
    places, thr_ref, lse_ref, q_ref, k_ref, v_ref, do_ref, dk_sum, dv_sum, d_ref, columns
):
    scale = HD**-0.5
    dk_sum[...] = jnp.zeros_like(dk_sum)
    dv_sum[...] = jnp.zeros_like(dv_sum)
    for q0, klim in q_blocks():
        rows = slice(q0, q0 + Q_BLOCK)
        k, q, do = k_ref[:klim, :], q_ref[rows, :], do_ref[rows, :]
        raw = dot(k, q, ((1,), (1,)))
        p = jnp.exp2(raw * (scale * LOG2E) - lse_ref[:, rows])
        p = jnp.where(seen_mask(thr_ref, q0, raw.shape), p, 0.0)
        dv_sum[:klim, :] += dot(p.astype(BF), do, ((1,), (0,)))
        dp = dot(v_ref[:klim, :], do, ((1,), (1,)))
        delta = jnp.sum(p * dp, axis=0, keepdims=True)
        ds = (p * (dp - delta) * scale).astype(BF)
        dk_sum[:klim, :] += dot(ds, q, ((1,), (0,)))
        dq = dot(k, ds, ((0,), (0,))).T.astype(BF)
        from_order(places, q0, dq, d_ref, columns(0))
    from_order(places, 0, dk_sum[...].astype(BF), d_ref, columns(1))
    from_order(places, 0, dv_sum[...].astype(BF), d_ref, columns(2))


SMEM_SPEC = pl.BlockSpec(memory_space=pltpu.SMEM)
ATTN_PARAMS = pltpu.CompilerParams(vmem_limit_bytes=56 << 20)


def head_spec(k, heads):
    return pl.BlockSpec((SLOT, HD), lambda h: (0, k * heads + h))


def attn_forward(places, thr, qkv):
    heads = qkv.shape[1] // (3 * HD)
    lse = pl.BlockSpec((1, 1, SLOT), lambda h: (h, 0, 0))
    return pl.pallas_call(
        attn_forward_kernel,
        grid=(heads,),
        in_specs=[SMEM_SPEC, pl.BlockSpec((SLOT, 128), lambda h: (0, 0))]
        + [head_spec(k, heads) for k in range(3)],
        out_specs=[head_spec(0, heads), lse],
        out_shape=[
            jax.ShapeDtypeStruct((SLOT, heads * HD), BF),
            jax.ShapeDtypeStruct((heads, 1, SLOT), F32),
        ],
        scratch_shapes=[pltpu.VMEM((SLOT, HD), BF)] * 3,
        compiler_params=ATTN_PARAMS,
        cost_estimate=cost(6.5 * heads),
    )(places, thr, qkv, qkv, qkv)


def step_rate(update_sq, weight_sq, n_real):
    update_rms = jnp.sqrt(update_sq / n_real)
    weight_rms = jnp.sqrt(weight_sq / n_real)
    return rate_base * jnp.maximum(eps_two, weight_rms) / jnp.maximum(1.0, update_rms / clip_bound)


def apply_step(weight, grad, row_new, col_new, row_mean, rate):
    row = lax.rsqrt(row_new) * (rate * jnp.sqrt(row_mean))
    return weight.astype(F32) - grad * (row[:, None] * lax.rsqrt(col_new)[None, :])


def pair_kernel(factors, *refs):
    g_ref, u_ref = refs[:2]
    o_ref = refs[-1]
    g, u = g_ref[...].astype(F32), u_ref[...].astype(F32)
    if factors:
        wg_ref, wu_ref, row_ref, cg_ref, cu_ref = refs[2:7]
        row = row_ref[...]
        g = wg_ref[...].astype(F32) - g * (row * cg_ref[...])
        u = wu_ref[...].astype(F32) - u * (row * cu_ref[...])
    o_ref[:, 0, :] = g
    o_ref[:, 1, :] = u


def pair_rows(gate, up, step=None):
    ff, width = gate.shape
    block = 96
    grid = (-(-ff // block),)
    wide = pl.BlockSpec((block, width), lambda i: (i, 0))
    args, specs = [gate, up], [wide, wide]
    if step is not None:
        w_gu, row, col_gate, col_up = step
        shift = w_gu.shape[0] // 2 // block
        column = pl.BlockSpec((block, 1), lambda i: (i, 0))
        args += [w_gu, w_gu, row[None, :], col_gate[:, None], col_up[:, None]]
        specs += [
            wide,
            pl.BlockSpec((block, width), lambda i: (i + shift, 0)),
            pl.BlockSpec((1, width), lambda i: (0, 0)),
            column,
            column,
        ]
    return pl.pallas_call(
        functools.partial(pair_kernel, step is not None),
        grid=grid,
        in_specs=specs,
        out_specs=pl.BlockSpec((block, 2, width), lambda i: (i, 0, 0)),
        out_shape=jax.ShapeDtypeStruct((ff, 2, width), F32),
        compiler_params=pltpu.CompilerParams(vmem_limit_bytes=40 << 20),
        cost_estimate=pl.CostEstimate(flops=8 * ff * width, transcendentals=0, bytes_accessed=16 * ff * width),
    )(*args)


def wait_for(arrays):
    leaves = jax.tree.leaves(arrays)
    return sum(jnp.minimum(jnp.abs(a[(0,) * a.ndim].astype(F32)), 0.0) for a in leaves)


def tie(x, after):
    return lax.optimization_barrier((x, after))[0]


def exchange_kernel(n_dp, n, x_ref, o_ref, dp_buf, rows, part_buf, total, whole, sems):
    me_d, me = lax.axis_index("dp"), lax.axis_index("tensor")
    width = x_ref.shape[1] // n
    columns = lambda t: pl.ds(pl.multiple_of(t * width, width), width)
    dp_peers = [(k - 1, lax.rem(me_d + k, n_dp)) for k in range(1, n_dp)]
    peers = [(k - 1, lax.rem(me + k, n)) for k in range(1, n)]
    barrier = pltpu.get_barrier_semaphore()
    for _, d in dp_peers:
        pl.semaphore_signal(barrier, inc=1, device_id={"dp": d}, device_id_type=pl.DeviceIdType.MESH)
    for _, t in peers:
        pl.semaphore_signal(barrier, inc=1, device_id={"tensor": t}, device_id_type=pl.DeviceIdType.MESH)
    pl.semaphore_wait(barrier, n_dp + n - 2)

    def push(stage, src, dst, k, device):
        copy = pltpu.make_async_remote_copy(
            src_ref=src, dst_ref=dst, send_sem=sems.at[0, stage, k], recv_sem=sems.at[1, stage, k],
            device_id=device, device_id_type=pl.DeviceIdType.MESH,
        )
        copy.start()
        return copy

    first = [push(0, x_ref.at[pl.ds(0, 8)], dp_buf.at[me_d], k, {"dp": d}) for k, d in dp_peers]
    rows[...] = x_ref[...]
    dp_buf[me_d] = x_ref[0:8, :]
    for copy in first:
        copy.wait()
    rows[0:8, :] = sum(dp_buf[d] for d in range(n_dp))
    second = [push(1, rows.at[:, columns(t)], part_buf.at[me], k, {"tensor": t}) for k, t in peers]
    part_buf[me] = rows[:, columns(me)]
    for copy in second:
        copy.wait()
    total[...] = sum(part_buf[t] for t in range(n))
    third = [push(2, total, whole.at[me], k, {"tensor": t}) for k, t in peers]
    whole[me] = total[...]
    for copy in third:
        copy.wait()
    for t in range(n):
        o_ref[:, t * width : (t + 1) * width] = whole[t]


def exchange(x, n_dp, n):
    height, width = x.shape
    slots = pltpu.VMEM((n, height, width // n), F32)
    return pl.pallas_call(
        functools.partial(exchange_kernel, n_dp, n),
        out_shape=jax.ShapeDtypeStruct(x.shape, F32),
        in_specs=[pl.BlockSpec(memory_space=pltpu.VMEM)],
        out_specs=pl.BlockSpec(memory_space=pltpu.VMEM),
        scratch_shapes=[
            pltpu.VMEM((n_dp, 8, width), F32),
            pltpu.VMEM(x.shape, F32),
            slots,
            pltpu.VMEM((height, width // n), F32),
            slots,
            pltpu.SemaphoreType.DMA((2, 3, max(n, n_dp) - 1)),
        ],
        compiler_params=pltpu.CompilerParams(collective_id=0, has_side_effects=True),
        cost_estimate=cost(16),
    )(x)


def on_device(
    layer_in,
    cotangent,
    lengths,
    prefix,
    pad_mask,
    clusters,
    qkv_w,
    out_w,
    gate_up_w,
    down_w,
    ln_params,
    qkv_row,
    qkv_col,
    out_row,
    out_col,
    gu_row,
    gu_col,
    down_row,
    down_col,
    ln_second,
):
    n_data = lax.axis_size("dp")
    n_tensor = lax.axis_size("tensor")
    tensor_rank = lax.axis_index("tensor")
    data_rank = lax.axis_index("dp")
    rows_dev, width = layer_in.shape
    cols_dev = qkv_w.shape[2]
    heads_dev = cols_dev // HD
    ff_dev = gate_up_w.shape[2]
    ff_pad = -(-ff_dev // 128) * 128
    n_clusters = max(2, n_data // 2)
    decay_rate = 1.0 - STEP ** (-0.8)
    seq_length = lengths[0]
    seq_prefix = prefix[0]
    ring = Ring(n_tensor)

    onehot = (clusters[:, None] == jnp.arange(n_clusters, dtype=jnp.int32)[None, :]).astype(F32)
    counts = jnp.sum(onehot, axis=0)
    own_row = jnp.sum(
        jnp.where((jnp.arange(n_data, dtype=jnp.int32) == data_rank)[:, None], onehot, 0.0), axis=0
    )
    seq_weight = jnp.sum(own_row / jnp.maximum(counts, 1.0))
    own_pos = tensor_rank * rows_dev + jnp.arange(rows_dev, dtype=jnp.int32)
    live_rows = ((own_pos < seq_length) & (pad_mask == 1)).astype(F32)
    grad_out = cotangent.astype(F32) * (live_rows * seq_weight)[:, None]
    grad_low = grad_out.astype(BF)

    key_live = (own_pos == 0) | (own_pos < seq_length) & (pad_mask == 1)
    seen_from = jnp.where(key_live, jnp.where(own_pos < seq_prefix, 0, own_pos), 2 * SLOT)
    seen = jnp.broadcast_to(seen_from.astype(F32)[None], (8, rows_dev))

    col_index = tensor_rank * ff_dev + jnp.arange(ff_pad, dtype=jnp.int32)
    ff_real = ((col_index < FF) & (jnp.arange(ff_pad) < ff_dev)).astype(F32)
    ff_mask = ff_real[:ff_dev]

    layer_own = layer_in.astype(F32)
    places = ring.places(rows_dev)
    act_one_all, qkv, seen_all = first_gather(
        n_tensor, layer_in, seen, ln_params, jnp.transpose(qkv_w, (1, 0, 2))
    )
    thr = jnp.broadcast_to(seen_all[:, 0].reshape(SLOT, 1), (SLOT, 128))

    pair = ring.halves(tie(grad_low, qkv))
    grad_pairs = [pair, ring.step(*pair)]
    context, lse = attn_forward(places, thr, qkv)
    pair = tie(grad_pairs[1], context)
    for s in range(2, n_tensor):
        pair = ring.step(*pair)
        grad_pairs.append(pair)
    grad_chunks = [jnp.concatenate(p, axis=0) for p in grad_pairs]
    pad = ((0, ff_pad - ff_dev), (0, 0))
    gate_up_late, down_late = tie(
        (jnp.transpose(gate_up_w, (2, 1, 0)), down_w), grad_chunks[min(3, n_tensor - 1)]
    )
    w_gu = jnp.concatenate([jnp.pad(gate_up_late[:, i], pad) for i in range(2)], axis=0)
    w_down = jnp.pad(down_late, pad)
    part_of = lambda x, s: x[s * rows_dev : (s + 1) * rows_dev]
    acc = None
    for s in ring.scatter_order():
        received = None if acc is None else ring.send(acc)
        acc = ring.add(received, dot(part_of(context, s), out_w, ((1,), (0,))))
    attn_own = jnp.concatenate(acc, axis=0)
    hidden_own = layer_own + attn_own
    norm_two = layer_norm(hidden_own, ln_params[2], ln_params[3]).astype(BF)

    act_two, inner, d_gu = [], [], []
    pair = ring.halves(norm_two)
    for s in range(n_tensor):
        pair = ring.step(*pair) if s else pair
        act = jnp.concatenate(pair, axis=0)
        act_two.append(act)
        gate_up = dot(act, w_gu, ((1,), (1,)))
        gate, up = gate_up[:, :ff_pad], gate_up[:, ff_pad:]
        gelu_gate, gelu_back = jax.vjp(jax.nn.gelu, gate)
        inner.append((gelu_gate * up * ff_real).astype(BF))
        d_inner = dot(grad_chunks[s], w_down, ((1,), (1,))) * ff_real
        d_gate = gelu_back(d_inner * up)[0]
        d_gu.append(jnp.concatenate([d_gate, d_inner * gelu_gate], axis=1).astype(BF))
    acc = None
    for s in ring.scatter_order():
        received = None if acc is None else ring.send(acc)
        acc = ring.add(received, dot(d_gu[s], w_gu, ((1,), (0,))))
    d_norm_two = jnp.concatenate(acc, axis=0)

    d_hidden_ln, ln_two_part = layer_norm_back(hidden_own, ln_params[2], d_norm_two)
    d_hidden = grad_out + d_hidden_ln
    whole = lambda chunks: jnp.concatenate(chunks, axis=0)
    inner_all = whole(inner)
    n_x = n_data // 2
    d_context, out_part, ff_mine, down_slots = back_gather(
        n_tensor, n_x, ff_dev, d_hidden.astype(BF), out_w, context,
        inner_all, whole(d_gu), whole(grad_chunks), whole(act_two),
    )
    layer_out, d_qkv, gu_slots, qkv_mine, out_mine = ffn_scatter(
        n_tensor, n_x, inner_all, w_down, hidden_own, thr, qkv, d_context, lse,
        out_part, act_one_all, ff_mine,
    )

    dp_wide, dp_tall = DpSum(n_data, 1), DpSum(n_data, 0)
    w_qkv = tie(qkv_w, d_context).reshape(width, 3 * cols_dev)
    qkv_mid, out_mid = dp_tall.chips(qkv_mine), dp_wide.chips(out_mine)
    chips_sum = lambda own, slots: sum(
        jnp.where(data_rank // 2 == x, own, slots[x]).astype(F32) for x in range(n_x)
    ).astype(BF)
    down_low = dp_wide.join(chips_sum(ff_mine[0], down_slots))[:ff_dev]
    gate_low = dp_wide.join(chips_sum(ff_mine[1], gu_slots[:, 0]))[:ff_dev]
    up_low = dp_wide.join(chips_sum(ff_mine[2], gu_slots[:, 1]))[:ff_dev]
    out_low, qkv_low = dp_wide.join(out_mid), dp_tall.join(qkv_mid)

    qkv_sum, out_sum, down_sum = qkv_low.astype(F32), out_low.astype(F32), down_low.astype(F32)
    gu_sum = (gate_low.astype(F32), up_low.astype(F32))
    gu_weights = (w_gu[:ff_dev], w_gu[ff_pad : ff_pad + ff_dev])
    gu_grad = pair_rows(gate_low, up_low)
    out_t, down_t, gu_t, qkv_t = tie((out_w, down_w, gu_weights, w_qkv), d_qkv)
    ff_col = ff_mask[:, None]
    blend = lambda old, total: decay_rate * old + (1.0 - decay_rate) * total
    square = lambda grad: grad * grad + eps_one
    square_sum = lambda w: jnp.sum(jnp.square(w.astype(F32)))

    qkv_sq, gu_sq = square(qkv_sum), [square(g) * ff_col for g in gu_sum]
    out_sq, down_sq = square(out_sum), square(down_sum) * ff_col
    qkv_col_new = blend(qkv_col.reshape(-1), jnp.sum(qkv_sq, axis=0) / width)
    gu_col_new = [blend(gu_col[i], jnp.sum(gu_sq[i], axis=1) / width) for i in range(2)]
    out_row_new = blend(out_row, jnp.sum(out_sq, axis=1) / width)
    down_row_new = blend(down_row, jnp.sum(down_sq, axis=1) / width)
    clean = lambda grad: grad * grad
    scalars = jnp.stack(
        [
            square_sum(qkv_t),
            sum(jnp.sum(jnp.square(w.astype(F32)) * ff_col) for w in gu_t),
            square_sum(out_t),
            jnp.sum(jnp.square(down_t.astype(F32)) * ff_col),
            jnp.sum(out_row_new),
            jnp.sum(down_row_new * ff_mask),
        ]
    )
    sums = dict(
        qkv=(jnp.sum(qkv_sq, axis=1), jnp.sum(clean(qkv_sum) / qkv_col_new[None, :], axis=1)),
        gu=(
            sum(jnp.sum(sq, axis=0) for sq in gu_sq),
            sum(
                jnp.sum(clean(g) * (ff_mask / col)[:, None], axis=0)
                for g, col in zip(gu_sum, gu_col_new)
            ),
        ),
        out=(jnp.sum(out_sq, axis=0), jnp.sum(clean(out_sum) / out_row_new[:, None], axis=0)),
        down=(
            jnp.sum(down_sq, axis=0),
            jnp.sum(clean(down_sum) * (ff_mask / down_row_new)[:, None], axis=0),
        ),
    )

    pace = {
        2: down_low,
        3: gate_low,
        4: (up_low, out_mid),
        5: (qkv_mid, sums["down"], sums["out"]),
        6: (qkv_low, sums["gu"], scalars),
        7: gu_grad,
    }
    acc = None
    for i, s in enumerate(ring.scatter_order()):
        received = None if acc is None else ring.send(acc)
        term = dot(part_of(d_qkv, s), w_qkv, ((1,), (1,)))
        acc = ring.add(received, term)
        if i in pace:
            acc = tuple(a + wait_for(pace[i]) for a in acc)
    d_norm_one = jnp.concatenate(acc, axis=0)
    d_input_ln, ln_one_part = layer_norm_back(layer_own, ln_params[0], d_norm_one)
    input_grad = (d_hidden + d_input_ln).astype(BF)

    packed = jnp.concatenate(
        [
            ln_one_part,
            ln_two_part,
            jnp.pad(scalars / n_data, (0, width - scalars.shape[0]))[None],
            jnp.zeros((3, width), F32),
            jnp.stack([*sums["qkv"], *sums["gu"], *sums["out"], *sums["down"]]),
        ],
        axis=0,
    )
    packed = exchange(packed, n_data, n_tensor)
    ln_tot = packed[:4]
    qkv_wtot, gu_wtot, out_wtot, down_wtot, out_rtot, down_rtot = (packed[4, i] for i in range(6))
    qkv_tot, qkv_usq, gu_tot, gu_usq, out_tot, out_usq, down_tot, down_usq = (
        packed[8 + i] for i in range(8)
    )

    qkv_cols_all = 3 * cols_dev * n_tensor
    out_rows_all = cols_dev * n_tensor
    qkv_row_new = blend(qkv_row, qkv_tot / qkv_cols_all)
    qkv_mean = jnp.sum(qkv_row_new) / width
    gu_row_new = blend(gu_row, gu_tot / (2 * FF))
    gu_mean = jnp.sum(gu_row_new) / width
    out_col_new = blend(out_col, out_tot / out_rows_all)
    out_mean = out_rtot / out_rows_all
    down_col_new = blend(down_col, down_tot / FF)
    down_mean = down_rtot / FF
    qkv_rate = step_rate(jnp.sum(qkv_usq / qkv_row_new) * qkv_mean, qkv_wtot, width * qkv_cols_all)
    gu_rate = step_rate(jnp.sum(gu_usq / gu_row_new) * gu_mean, gu_wtot, width * 2 * FF)
    out_rate = step_rate(jnp.sum(out_usq / out_col_new) * out_mean, out_wtot, out_rows_all * width)
    down_rate = step_rate(jnp.sum(down_usq / down_col_new) * down_mean, down_wtot, FF * width)

    qkv_new = apply_step(w_qkv, qkv_sum, qkv_row_new, qkv_col_new, qkv_mean, qkv_rate)
    out_new = apply_step(out_w, out_sum, out_row_new, out_col_new, out_mean, out_rate)
    down_new = apply_step(down_w, down_sum, down_row_new, down_col_new, down_mean, down_rate)
    gu_scale = lax.rsqrt(gu_row_new) * (gu_rate * jnp.sqrt(gu_mean))
    gu_new = pair_rows(gate_low, up_low, (w_gu, gu_scale, *map(lax.rsqrt, gu_col_new)))
    ln_second_new = blend(ln_second, ln_tot * ln_tot + eps_one)
    ln_update = ln_tot * lax.rsqrt(ln_second_new)
    ln_urms = jnp.sqrt(jnp.mean(ln_update * ln_update, axis=1, keepdims=True))
    ln_wrms = jnp.sqrt(jnp.mean(ln_params * ln_params, axis=1, keepdims=True))
    ln_new = ln_params - rate_base * jnp.maximum(eps_two, ln_wrms) * ln_update / jnp.maximum(
        1.0, ln_urms / clip_bound
    )
    return (
        layer_out,
        input_grad,
        qkv_sum.reshape(qkv_w.shape),
        qkv_new.reshape(qkv_w.shape),
        qkv_row_new,
        qkv_col_new.reshape(3, -1),
        out_sum,
        out_new,
        out_row_new,
        out_col_new,
        jnp.transpose(gu_grad, (2, 1, 0)),
        jnp.transpose(gu_new, (2, 1, 0)),
        gu_row_new,
        jnp.stack(gu_col_new),
        down_sum,
        down_new,
        down_row_new,
        down_col_new,
        ln_tot,
        ln_second_new,
        ln_new,
    )


def solution(mesh):
    in_specs = (
        P(("dp", "tensor"), None),
        P(("dp", "tensor"), None),
        P("dp"),
        P("dp"),
        P(("dp", "tensor")),
        P(),
        P(None, None, "tensor"),
        P("tensor", None),
        P(None, None, "tensor"),
        P("tensor", None),
        P(),
        P(),
        P(None, "tensor"),
        P("tensor"),
        P(),
        P(),
        P(None, "tensor"),
        P("tensor"),
        P(),
        P(),
    )
    out_specs = (
        P(("dp", "tensor"), None),
        P(("dp", "tensor"), None),
        P(None, None, "tensor"),
        P(None, None, "tensor"),
        P(),
        P(None, "tensor"),
        P("tensor", None),
        P("tensor", None),
        P("tensor"),
        P(),
        P(None, None, "tensor"),
        P(None, None, "tensor"),
        P(),
        P(None, "tensor"),
        P("tensor", None),
        P("tensor", None),
        P("tensor"),
        P(),
        P(),
        P(),
        P(),
    )
    return jax.shard_map(
        on_device, mesh=mesh, in_specs=in_specs, out_specs=out_specs, check_vma=False
    )
```

```python
import functools

import jax
import jax.numpy as jnp
from jax import lax
from jax.experimental import pallas as pl
from jax.experimental.pallas import tpu as pltpu
from jax.sharding import PartitionSpec as P

HD = 128
FF = 5461
SLOT = 2048
STEP = 10
DECAY = 1.0 - STEP ** (-0.8)
PREFIX_MAX = SLOT // 2
Q_BLOCK = 512

ln_eps = 1e-05
eps_one = 1e-30
eps_two = 0.001
clip_bound = 1.0
rate_base = 1.0
masked_score = -1e30
LOG2E = 1.4426950408889634
BF = jnp.bfloat16
F32 = jnp.float32


def dot(a, b, dims):
    return lax.dot_general(a, b, (dims, ((), ())), preferred_element_type=F32)


def ring_order(n):
    b_size = 2 if n <= 8 else 4
    a_size = n // b_size
    order = []
    for a in range(a_size):
        cols = list(range(1, b_size))
        order += [a * b_size + c for c in (cols[::-1] if a % 2 else cols)]
    for a in range(a_size - 1, -1, -1):
        order.append(a * b_size)
    return order


class Ring:
    def __init__(self, n):
        self.n = n
        order = ring_order(n)
        self.fw = [(order[i], order[(i + 1) % n]) for i in range(n)]
        self.bw = [(order[i], order[(i - 1) % n]) for i in range(n)]
        place = [0] * n
        for p, t in enumerate(order):
            place[t] = p
        self.place = jnp.array(place, jnp.int32)
        self.pos = self.place[lax.axis_index("tensor")]

    def step(self, a, b):
        return lax.ppermute(a, "tensor", self.fw), lax.ppermute(b, "tensor", self.bw)

    def halves(self, x):
        half = x.shape[0] // 2
        return x[:half], x[half:]

    def scatter_order(self):
        return list(range(1, self.n)) + [0]

    def add(self, received, term, after=()):
        term = lax.optimization_barrier((term, after))[0]
        parts = self.halves(term)
        if received is not None:
            parts = tuple(r.astype(F32) + t for r, t in zip(received, parts))
        return parts

    def low(self, parts):
        return tuple(p.astype(BF) for p in parts)

    def send(self, parts):
        return self.step(*self.low(parts))

    def places(self, rows):
        t = jnp.arange(self.n, dtype=jnp.int32)
        step = self.place[t] - self.pos
        first = lax.rem(2 * self.n - step, self.n) * rows
        second = lax.rem(step + self.n, self.n) * rows + rows // 2
        return jnp.stack([first, second], axis=1).reshape(-1)


def cost(micros):
    return pl.CostEstimate(flops=int(micros * 1e9), transcendentals=0, bytes_accessed=4 << 20)


PUSH = pl.DeviceIdType.MESH
PIECES = 2


def pick(index, table):
    out = jnp.int32(table[0])
    for k in range(1, len(table)):
        out = jnp.where(index == k, jnp.int32(table[k]), out)
    return out


def neighbours(n):
    order = ring_order(n)
    pos = pick(lax.axis_index("tensor"), [order.index(t) for t in range(n)])
    ahead = pick(lax.rem(pos + 1, n), order)
    behind = pick(lax.rem(pos + n - 1, n), order)
    return pos, [{"tensor": ahead}, {"tensor": behind}]


def other_core():
    me = lax.axis_index("dp")
    return {"dp": me + 1 - 2 * lax.rem(me, 2)}


def other_chips(n_x):
    core, chip = lax.rem(lax.axis_index("dp"), 2), lax.axis_index("dp") // 2
    return chip, [{"dp": 2 * lax.rem(chip + k, n_x) + core} for k in range(1, n_x)]


def greet(devices):
    barrier = pltpu.get_barrier_semaphore()
    for device in devices:
        pl.semaphore_signal(barrier, inc=1, device_id=device, device_id_type=PUSH)
    pl.semaphore_wait(barrier, len(devices))


def ring_copy(land, send_sem, recv_sem, sides, d, s, piece=None):
    src, dst, sem = land.at[d, s], land.at[d, s + 1], d
    if piece is not None:
        size = land.shape[2] // PIECES
        rows = pl.ds(piece * size, size)
        src, dst, sem = land.at[d, s, rows], land.at[d, s + 1, rows], d * PIECES + piece
    return pltpu.make_async_remote_copy(
        src_ref=src,
        dst_ref=dst,
        send_sem=send_sem.at[sem, s],
        recv_sem=recv_sem.at[sem, s],
        device_id=sides[d],
        device_id_type=PUSH,
    )


def ring_sent(n, copy, pieces=(None,)):
    def sent(s, carry):
        for d in range(2):
            for piece in pieces:
                copy(d, s, piece).wait_send()
        return carry

    lax.fori_loop(0, n - 1, sent, 0)


def ring_gather(n, x_ref, land, send_sem, recv_sem, sides, work):
    copy = functools.partial(ring_copy, land, send_sem, recv_sem, sides)
    half = x_ref.shape[0] // 2
    land[0, 0] = x_ref[:half, :]
    land[1, 0] = x_ref[half:, :]

    def step(s, carry):
        for d in range(2):

            @pl.when(s > 0)
            def _():
                copy(d, s - 1).wait_recv()

            @pl.when(s < n - 1)
            def _():
                copy(d, s).start()

        work(s)
        return carry

    lax.fori_loop(0, n, step, 0)
    ring_sent(n, copy)


def ring_scatter(n, land, send_sem, recv_sem, sides, term_buf, term, work, finish):
    copy = functools.partial(ring_copy, land, send_sem, recv_sem, sides)
    half = term_buf.shape[0] // 2
    size = half // PIECES
    for d in range(2):
        land[d, 0] = jnp.zeros(land.shape[2:], land.dtype)

    def step(s, carry):
        term(lax.rem(s + 1, n))
        for piece in range(PIECES):
            for d in range(2):
                part = slice(piece * size, (piece + 1) * size)
                rows = slice(d * half + piece * size, d * half + (piece + 1) * size)

                @pl.when(s > 0)
                def _():
                    copy(d, s - 1, piece).wait_recv()

                total = land[d, s, part].astype(F32) + term_buf[rows, :]

                @pl.when(s < n - 1)
                def _():
                    land[d, s, part] = total.astype(BF)
                    copy(d, s, piece).start()

                @pl.when(s == n - 1)
                def _():
                    finish(rows, total)

        work(s)
        return carry

    lax.fori_loop(0, n, step, 0)
    ring_sent(n, copy, range(PIECES))


def dot_columns(out, a, b, dims, block=512):
    width = b.shape[1]

    def columns(j, carry):
        at = pl.ds(pl.multiple_of(j * block, block), block)
        out(at, dot(a, b[:, at], dims))
        return carry

    lax.fori_loop(0, width // block, columns, 0)


def first_kernel(
    n, x_ref, seen_ref, ln_ref, w_ref, act_ref, qkv_ref, seen_all,
    land, act_buf, seen_buf, send_sem, recv_sem, act_sem, seen_sem,
):
    rows, cols = x_ref.shape[0], w_ref.shape[2]
    me = lax.axis_index("tensor")
    peers = [lax.rem(me + k, n) for k in range(1, n)]
    sides = neighbours(n)[1]
    greet([{"tensor": t} for t in peers])

    def seen_copy(k):
        return pltpu.make_async_remote_copy(
            src_ref=seen_ref, dst_ref=seen_buf.at[me], send_sem=seen_sem.at[0, k],
            recv_sem=seen_sem.at[1, k], device_id={"tensor": peers[k]}, device_id_type=PUSH,
        )

    def act_copy(s):
        place = pl.ds(pl.multiple_of(s * rows, rows), rows)
        return pltpu.make_async_copy(act_buf.at[s], act_ref.at[place], act_sem.at[s])

    def work(s):
        @pl.when(s == 0)
        def _():
            for k in range(n - 1):
                seen_copy(k).start()

        chunk = jnp.concatenate([land[0, s], land[1, s]], axis=0).astype(F32)
        act = layer_norm(chunk, ln_ref[0:1, :], ln_ref[1:2, :]).astype(BF)
        act_buf[s] = act
        act_copy(s).start()
        place = pl.ds(pl.multiple_of(s * rows, rows), rows)
        for k in range(3):
            qkv_ref[place, k * cols : (k + 1) * cols] = dot(act, w_ref[k], ((1,), (0,))).astype(BF)

    ring_gather(n, x_ref, land, send_sem, recv_sem, sides, work)
    seen_buf[me] = seen_ref[...]
    for k in range(n - 1):
        seen_copy(k).wait()
    seen_all[...] = seen_buf[...]

    def written(s, carry):
        act_copy(s).wait()
        return carry

    lax.fori_loop(0, n, written, 0)


def ring_scratch(n, rows, width, pieces=1):
    return [pltpu.VMEM((2, n, rows // 2, width), BF)], [
        pltpu.SemaphoreType.DMA((2 * pieces, n - 1)),
        pltpu.SemaphoreType.DMA((2 * pieces, n - 1)),
    ]


VMEM_SPEC = pl.BlockSpec(memory_space=pltpu.VMEM)
ANY_SPEC = pl.BlockSpec(memory_space=pl.ANY)


def first_gather(n, x, seen, ln_params, w):
    rows, width = x.shape
    cols = w.shape[2]
    buf, sems = ring_scratch(n, rows, width)
    return pl.pallas_call(
        functools.partial(first_kernel, n),
        in_specs=[VMEM_SPEC] * 4,
        out_specs=[ANY_SPEC, VMEM_SPEC, VMEM_SPEC],
        out_shape=[
            jax.ShapeDtypeStruct((n * rows, width), BF),
            jax.ShapeDtypeStruct((n * rows, 3 * cols), BF),
            jax.ShapeDtypeStruct((n,) + seen.shape, F32),
        ],
        scratch_shapes=buf
        + [pltpu.VMEM((n, rows, width), BF), pltpu.VMEM((n,) + seen.shape, F32)]
        + sems
        + [pltpu.SemaphoreType.DMA((n,)), pltpu.SemaphoreType.DMA((2, n - 1))],
        compiler_params=pltpu.CompilerParams(
            collective_id=1, has_side_effects=True, vmem_limit_bytes=56 << 20
        ),
        cost_estimate=pl.CostEstimate(
            flops=6 * n * rows * width * cols, transcendentals=0, bytes_accessed=40 << 20
        ),
    )(x, seen, ln_params, w)


def back_kernel(
    n, n_x, x_ref, w_ref, ctx_ref, inner_hbm, d_gu_hbm, grad_hbm, act_hbm, _,
    d_ctx_ref, out_ref, mine_ref, slots_hbm,
    land, lhs, rhs, part, core_land, out_sum, send_sem, recv_sem, load_sem, core_sem, slot_sem,
):
    rows, ff_pad = x_ref.shape[0], lhs.shape[2]
    ff_rows, half = core_land.shape[1:]
    sides, partner = neighbours(n)[1], other_core()
    core = lax.rem(lax.axis_index("dp"), 2)
    of_core = lambda c: pl.ds(pl.multiple_of(c * half, half), half)
    loads = [
        pltpu.make_async_copy(src, dst, load_sem.at[i])
        for i, (src, dst) in enumerate(
            (
                (inner_hbm, lhs.at[0]),
                (grad_hbm, rhs.at[0]),
                (d_gu_hbm.at[:, pl.ds(0, ff_pad)], lhs.at[1]),
                (act_hbm, rhs.at[1]),
                (d_gu_hbm.at[:, pl.ds(ff_pad, ff_pad)], lhs.at[2]),
            )
        )
    ]
    for load in loads:
        load.start()
    out_sum[...] = jnp.zeros_like(out_sum)
    chip, chips = other_chips(n_x)
    greet(sides + [partner] + chips)

    def slot_copy(k):
        return pltpu.make_async_remote_copy(
            src_ref=mine_ref.at[0], dst_ref=slots_hbm.at[chip], send_sem=slot_sem.at[0, k],
            recv_sem=slot_sem.at[1, k], device_id=chips[k], device_id_type=PUSH,
        )

    def core_copy(i):
        return pltpu.make_async_remote_copy(
            src_ref=part.at[i, :, of_core(1 - core)],
            dst_ref=core_land.at[i],
            send_sem=core_sem.at[0, i],
            recv_sem=core_sem.at[1, i],
            device_id=partner,
            device_id_type=PUSH,
        )

    def work(s):
        chunk = jnp.concatenate([land[0, s], land[1, s]], axis=0)
        place = pl.ds(pl.multiple_of(s * rows, rows), rows)
        d_ctx_ref[place, :] = dot(chunk, w_ref[...], ((1,), (1,))).astype(BF)
        out_sum[...] += dot(ctx_ref[place, :], chunk, ((0,), (0,)))
        for i in range(3):

            @pl.when(s == i + 1)
            def _():
                for load in (loads[:2], loads[2:4], loads[4:])[i]:
                    load.wait()

                def put(at, value):
                    part[i, :, at] = value[:ff_rows].astype(BF)

                dot_columns(put, lhs[i], rhs.at[min(i, 1)], ((0,), (0,)))
                core_copy(i).start()

            @pl.when(s == i + 3)
            def _():
                core_copy(i).wait()
                total = part[i, :, of_core(core)].astype(F32) + core_land[i].astype(F32)
                mine_ref[i] = total.astype(BF)
                if i == 0:
                    for k in range(n_x - 1):
                        slot_copy(k).start()

    ring_gather(n, x_ref, land, send_sem, recv_sem, sides, work)
    out_ref[...] = out_sum[...].astype(BF)
    for k in range(n_x - 1):
        slot_copy(k).wait()


def back_gather(n, n_x, ff_dev, x, w, context, inner, d_gu, grad, act, early):
    rows, width = x.shape
    ff_pad = inner.shape[1]
    ff_rows = -(-ff_dev // 16) * 16
    buf, sems = ring_scratch(n, rows, width)
    return pl.pallas_call(
        functools.partial(back_kernel, n, n_x),
        in_specs=[VMEM_SPEC] * 3 + [ANY_SPEC] * 5,
        out_specs=[VMEM_SPEC] * 3 + [ANY_SPEC],
        out_shape=[
            jax.ShapeDtypeStruct((n * rows, w.shape[0]), BF),
            jax.ShapeDtypeStruct(w.shape, BF),
            jax.ShapeDtypeStruct((3, ff_rows, width // 2), BF),
            jax.ShapeDtypeStruct((n_x, ff_rows, width // 2), BF),
        ],
        scratch_shapes=buf
        + [
            pltpu.VMEM((3, n * rows, ff_pad), BF),
            pltpu.VMEM((2, n * rows, width), BF),
            pltpu.VMEM((3, ff_rows, width), BF),
            pltpu.VMEM((3, ff_rows, width // 2), BF),
            pltpu.VMEM(w.shape, F32),
        ]
        + sems
        + [
            pltpu.SemaphoreType.DMA((5,)),
            pltpu.SemaphoreType.DMA((2, 3)),
            pltpu.SemaphoreType.DMA((2, n_x - 1)),
        ],
        compiler_params=pltpu.CompilerParams(
            collective_id=3, has_side_effects=True, vmem_limit_bytes=60 << 20
        ),
        cost_estimate=cost(80),
    )(x, w, context, inner, d_gu, grad, act, early)


def ffn_kernel(
    n, n_x, heads, inner_ref, w_ref, hidden_ref, thr_ref, qkv_ref, d_ctx_ref, lse_ref,
    out_part_ref, act_hbm, mine_hbm,
    out_ref, d_qkv_ref, slots_hbm, oq_mine_ref,
    land, term_buf, q_ref, k_ref, v_ref, do_ref, dk_sum, dv_sum,
    act_buf, part, qkv_land, out_land,
    send_sem, recv_sem, act_sem, core_sem, slot_sem,
):
    rows = hidden_ref.shape[0]
    pos, sides = neighbours(n)
    partner = other_core()
    core = lax.rem(lax.axis_index("dp"), 2)
    chip, chips = other_chips(n_x)
    block = act_buf.shape[2]
    blocks = act_hbm.shape[1] // block
    qkv_cols, wide = qkv_land.shape
    wide_of = lambda c: pl.ds(pl.multiple_of(c * wide, wide), wide)

    def act_load(j):
        return pltpu.make_async_copy(
            act_hbm.at[:, pl.ds(j * block, block)], act_buf.at[j % 2], act_sem.at[j]
        )

    def core_copy(i):
        src, dst = (
            (part.at[:, wide_of(1 - core)], qkv_land),
            (out_part_ref.at[:, wide_of(1 - core)], out_land),
        )[i]
        return pltpu.make_async_remote_copy(
            src_ref=src, dst_ref=dst, send_sem=core_sem.at[0, i], recv_sem=core_sem.at[1, i],
            device_id=partner, device_id_type=PUSH,
        )

    def slot_copy(k):
        return pltpu.make_async_remote_copy(
            src_ref=mine_hbm.at[pl.ds(1, 2)], dst_ref=slots_hbm.at[chip], send_sem=slot_sem.at[0, k],
            recv_sem=slot_sem.at[1, k], device_id=chips[k], device_id_type=PUSH,
        )

    for j in range(2):
        act_load(j).start()
    greet(sides + [partner] + chips)
    core_copy(1).start()
    for k in range(n_x - 1):
        slot_copy(k).start()
    places = []
    place_of = [ring_order(n).index(t) for t in range(n)]
    for t in range(n):
        places.append(lax.rem(pos + (n - place_of[t]), n) * rows)
        places.append(lax.rem(place_of[t] - pos + n, n) * rows + rows // 2)

    def term(c):
        place = pl.ds(pl.multiple_of(c * rows, rows), rows)

        def put(at, value):
            term_buf[:, at] = value

        dot_columns(put, inner_ref[place, :], w_ref, ((1,), (0,)))

    def work(s):
        for h in range(heads):

            @pl.when(s == h + 1)
            def _():
                columns = lambda i: slice((i * heads + h) * HD, (i * heads + h + 1) * HD)
                for i, dst in enumerate((q_ref, k_ref, v_ref)):
                    to_order(places, qkv_ref, columns(i), dst)
                to_order(places, d_ctx_ref, columns(0), do_ref)
                attn_backward_head(
                    places, thr_ref, lse_ref.at[h], q_ref, k_ref, v_ref, do_ref, dk_sum, dv_sum,
                    d_qkv_ref, columns,
                )

        @pl.when(s == 1)
        def _():
            core_copy(1).wait()
            total = out_part_ref[:, wide_of(core)].astype(F32) + out_land[...].astype(F32)
            oq_mine_ref[qkv_cols:, :] = total.astype(BF)

        for turn in range(blocks // 2):

            @pl.when(s == heads + 1 + turn)
            def _():
                for j in (2 * turn, 2 * turn + 1):
                    act_load(j).wait()
                    grad = dot(d_qkv_ref[...], act_buf[j % 2], ((0,), (0,)))
                    part[:, j * block : (j + 1) * block] = grad.astype(BF)
                for j in (2 * turn + 2, 2 * turn + 3):
                    if j < blocks:
                        act_load(j).start()
                if turn == blocks // 2 - 1:
                    core_copy(0).start()

        @pl.when(s == heads + 2 + blocks // 2)
        def _():
            core_copy(0).wait()
            total = part[:, wide_of(core)].astype(F32) + qkv_land[...].astype(F32)
            oq_mine_ref[:qkv_cols, :] = total.astype(BF)

    def finish(at, total):
        out_ref[at, :] = (hidden_ref[at, :] + total).astype(BF)

    ring_scatter(n, land, send_sem, recv_sem, sides, term_buf, term, work, finish)
    for k in range(n_x - 1):
        slot_copy(k).wait()


def ffn_scatter(n, n_x, inner, w, hidden, thr, qkv, d_context, lse, out_part, act, mine):
    rows, width = hidden.shape
    cols, block = d_context.shape[1], 512
    heads = d_context.shape[1] // HD
    buf, sems = ring_scratch(n, rows, width, PIECES)
    return pl.pallas_call(
        functools.partial(ffn_kernel, n, n_x, heads),
        in_specs=[VMEM_SPEC] * 8 + [ANY_SPEC] * 2,
        out_specs=[VMEM_SPEC] * 2 + [ANY_SPEC, VMEM_SPEC],
        out_shape=[
            jax.ShapeDtypeStruct((rows, width), BF),
            jax.ShapeDtypeStruct(qkv.shape, BF),
            jax.ShapeDtypeStruct((n_x, 2) + mine.shape[1:], BF),
            jax.ShapeDtypeStruct((4 * cols, width // 2), BF),
        ],
        scratch_shapes=buf
        + [pltpu.VMEM((rows, width), F32)]
        + [pltpu.VMEM((SLOT, HD), BF)] * 4
        + [pltpu.VMEM((SLOT, HD), F32)] * 2
        + [
            pltpu.VMEM((2, n * rows, block), BF),
            pltpu.VMEM((3 * cols, width), BF),
            pltpu.VMEM((3 * cols, width // 2), BF),
            pltpu.VMEM((cols, width // 2), BF),
        ]
        + sems
        + [
            pltpu.SemaphoreType.DMA((width // block,)),
            pltpu.SemaphoreType.DMA((2, 2)),
            pltpu.SemaphoreType.DMA((2, n_x - 1)),
        ],
        compiler_params=pltpu.CompilerParams(
            collective_id=4, has_side_effects=True, vmem_limit_bytes=62 << 20
        ),
        cost_estimate=cost(95),
    )(inner, w, hidden, thr, qkv, d_context, lse, out_part, act, mine)


def row_sums(grad_ref, old_ref, real_ref, new_ref, c_ref, t_ref):
    width = grad_ref.shape[1]
    block = 16

    def rows(i, carry):
        at = pl.ds(pl.multiple_of(i * block, block), block)
        grad = grad_ref[at, :].astype(F32)
        square = grad * grad
        real = real_ref[at, :]
        total = (jnp.sum(square, axis=1, keepdims=True) + width * eps_one) * real
        new = DECAY * old_ref[at, :] + (1.0 - DECAY) * (total / width)
        new_ref[at, :] = new
        c = (square + eps_one) * real
        t = square * (real / new)
        c_ref[...] += c[:8] + c[8:]
        t_ref[...] += t[:8] + t[8:]
        return carry

    lax.fori_loop(0, grad_ref.shape[0] // block, rows, 0)


def last_kernel(
    n, n_x, d_qkv_ref, w_ref, oq_mine_ref, oq_old, oq_real, ff_old, ff_real, mine_hbm, down_hbm, gu_hbm,
    out_ref, goq_ref, gff_ref, oq_new, ff_new, sums_ref,
    land, term_buf, oq_land, ff_own, ff_slots, c_sum, t_sum,
    send_sem, recv_sem, oq_sem, load_sem, join_sem,
):
    rows = term_buf.shape[0]
    cols, width = w_ref.shape[2], term_buf.shape[1]
    sides, partner = neighbours(n)[1], other_core()
    core = lax.rem(lax.axis_index("dp"), 2)
    chip, chips = other_chips(n_x)
    half = width // 2
    own = pl.ds(pl.multiple_of(core * half, half), half)

    def loads(i):
        slots = down_hbm if i == 0 else gu_hbm.at[:, i - 1]
        return [
            pltpu.make_async_copy(mine_hbm.at[i], ff_own.at[i], load_sem.at[0, i]),
            pltpu.make_async_copy(slots, ff_slots.at[i], load_sem.at[1, i]),
        ]

    def oq_copy(k):
        return pltpu.make_async_remote_copy(
            src_ref=oq_mine_ref, dst_ref=oq_land.at[chip], send_sem=oq_sem.at[0, k],
            recv_sem=oq_sem.at[1, k], device_id=chips[k], device_id_type=PUSH,
        )

    def join(i):
        ref = goq_ref.at[:, own] if i == 3 else gff_ref.at[i, :, own]
        return pltpu.make_async_remote_copy(
            src_ref=ref, dst_ref=ref, send_sem=join_sem.at[0, i], recv_sem=join_sem.at[1, i],
            device_id=partner, device_id_type=PUSH,
        )

    def chip_sum(own_half, slots):
        total = jnp.zeros(own_half.shape, F32)
        for x in range(n_x):
            total = total + jnp.where(chip == x, own_half, slots[x]).astype(F32)
        return total.astype(BF)

    for i in range(3):
        for load in loads(i):
            load.start()
    greet(sides + [partner] + chips)
    for k in range(n_x - 1):
        oq_copy(k).start()

    def term(c):
        place = pl.ds(pl.multiple_of(c * rows, rows), rows)
        block = 512

        def columns(j, carry):
            at = pl.ds(pl.multiple_of(j * block, block), block)
            term_buf[:, at] = sum(
                dot(d_qkv_ref[place, k * cols : (k + 1) * cols], w_ref[k, at, :], ((1,), (1,)))
                for k in range(3)
            )
            return carry

        lax.fori_loop(0, width // block, columns, 0)

    def sums(group, refs):
        c_sum[...] = jnp.zeros_like(c_sum)
        t_sum[...] = jnp.zeros_like(t_sum)
        for ref in refs:
            row_sums(*ref, c_sum, t_sum)
        sums_ref[2 * group : 2 * group + 1, :] = jnp.sum(c_sum[...], axis=0, keepdims=True)
        sums_ref[2 * group + 1 : 2 * group + 2, :] = jnp.sum(t_sum[...], axis=0, keepdims=True)

    ff_refs = lambda i: (gff_ref.at[i], ff_old.at[i], ff_real, ff_new.at[i])
    oq_refs = lambda at: tuple(ref.at[at] for ref in (goq_ref, oq_old, oq_real, oq_new))

    def work(s):
        for i in range(3):

            @pl.when(s == i)
            def _():
                for load in loads(i):
                    load.wait()
                gff_ref[i, :, own] = chip_sum(ff_own[i], ff_slots.at[i])
                join(i).start()

        @pl.when(s == 4)
        def _():
            for k in range(n_x - 1):
                oq_copy(k).wait()
            goq_ref[:, own] = chip_sum(oq_mine_ref[...], oq_land)
            join(3).start()

        @pl.when(s == 5)
        def _():
            join(0).wait()
            sums(3, [ff_refs(0)])
            join(1).wait()
            join(2).wait()
            sums(1, [ff_refs(1), ff_refs(2)])

    def finish(at, total):
        out_ref[at, :] = total

    ring_scatter(n, land, send_sem, recv_sem, sides, term_buf, term, work, finish)
    join(3).wait()
    sums(0, [oq_refs(pl.ds(0, 3 * cols))])
    sums(2, [oq_refs(pl.ds(3 * cols, cols))])


def last_scatter(n, n_x, d_qkv, w, oq_mine, oq_old, oq_real, ff_old, ff_real, ff_mine, down_slots, gu_slots):
    width, cols = w.shape[1:]
    rows = d_qkv.shape[0] // n
    half = width // 2
    ff_rows = ff_mine.shape[1]
    buf, sems = ring_scratch(n, rows, width, PIECES)
    return pl.pallas_call(
        functools.partial(last_kernel, n, n_x),
        in_specs=[VMEM_SPEC] * 7 + [ANY_SPEC] * 3,
        out_specs=[VMEM_SPEC] * 6,
        out_shape=[
            jax.ShapeDtypeStruct((rows, width), F32),
            jax.ShapeDtypeStruct((4 * cols, width), BF),
            jax.ShapeDtypeStruct((3, ff_rows, width), BF),
            jax.ShapeDtypeStruct(oq_old.shape, F32),
            jax.ShapeDtypeStruct(ff_old.shape, F32),
            jax.ShapeDtypeStruct((8, width), F32),
        ],
        scratch_shapes=buf
        + [
            pltpu.VMEM((rows, width), F32),
            pltpu.VMEM((n_x,) + oq_mine.shape, BF),
            pltpu.VMEM((3, ff_rows, half), BF),
            pltpu.VMEM((3, n_x, ff_rows, half), BF),
            pltpu.VMEM((8, width), F32),
            pltpu.VMEM((8, width), F32),
        ]
        + sems
        + [
            pltpu.SemaphoreType.DMA((2, n_x - 1)),
            pltpu.SemaphoreType.DMA((2, 3)),
            pltpu.SemaphoreType.DMA((2, 4)),
        ],
        compiler_params=pltpu.CompilerParams(
            collective_id=2, has_side_effects=True, vmem_limit_bytes=62 << 20
        ),
        cost_estimate=cost(90),
    )(d_qkv, w, oq_mine, oq_old, oq_real, ff_old, ff_real, ff_mine, down_slots, gu_slots)


def norm_stats(rows):
    mean_row = jnp.mean(rows, axis=-1, keepdims=True)
    centered = rows - mean_row
    variance = jnp.mean(centered * centered, axis=-1, keepdims=True)
    scale = lax.rsqrt(variance + ln_eps)
    return centered * scale, scale


def layer_norm(rows, gain, shift):
    return norm_stats(rows)[0] * gain + shift


def layer_norm_back(rows, gain, e):
    n, scale = norm_stats(rows)
    eg = e * gain
    dv = scale * (
        eg - jnp.mean(eg, axis=-1, keepdims=True) - n * jnp.mean(eg * n, axis=-1, keepdims=True)
    )
    return dv, jnp.stack([jnp.sum(e * n, axis=0), jnp.sum(e, axis=0)])


def seen_mask(thr_ref, q0, shape):
    thr = thr_ref[: shape[0], :]
    thr = jnp.concatenate([thr] * (shape[1] // thr.shape[1]), axis=1)
    q_pos = (q0 + lax.broadcasted_iota(jnp.int32, shape, 1)).astype(F32)
    return q_pos >= thr


def q_blocks():
    return [(q0, max(PREFIX_MAX, q0 + Q_BLOCK)) for q0 in range(0, SLOT, Q_BLOCK)]


def to_order(places, src_ref, columns, dst_ref):
    half = SLOT // len(places)
    for j, start in enumerate(places):
        place = pl.ds(pl.multiple_of(start, half), half)
        dst_ref[j * half : (j + 1) * half, :] = src_ref[place, columns]


def from_order(places, q0, value, dst_ref, columns):
    half = SLOT // len(places)
    for i in range(value.shape[0] // half):
        place = pl.ds(pl.multiple_of(places[q0 // half + i], half), half)
        dst_ref[place, columns] = value[i * half : (i + 1) * half, :]


def attn_forward_kernel(places, thr_ref, q_in, k_in, v_in, o_ref, lse_ref, q_ref, k_ref, v_ref):
    c = HD**-0.5 * LOG2E
    places = [places[j] for j in range(places.shape[0])]
    for src, dst in ((q_in, q_ref), (k_in, k_ref), (v_in, v_ref)):
        to_order(places, src, slice(None), dst)
    for q0, klim in q_blocks():
        raw = dot(k_ref[:klim, :], q_ref[q0 : q0 + Q_BLOCK, :], ((1,), (1,)))
        raw = jnp.where(seen_mask(thr_ref, q0, raw.shape), raw, masked_score)
        top = jnp.max(raw, axis=0, keepdims=True)
        p = jnp.exp2((raw - top) * c)
        total = jnp.sum(p, axis=0, keepdims=True)
        out = dot(v_ref[:klim, :], p.astype(BF), ((0,), (0,))) / total
        from_order(places, q0, out.T.astype(BF), o_ref, slice(None))
        lse_ref[0, :, q0 : q0 + Q_BLOCK] = top * c + jnp.log2(total)


def attn_backward_head(
    places, thr_ref, lse_ref, q_ref, k_ref, v_ref, do_ref, dk_sum, dv_sum, d_ref, columns
):
    scale = HD**-0.5
    dk_sum[...] = jnp.zeros_like(dk_sum)
    dv_sum[...] = jnp.zeros_like(dv_sum)
    for q0, klim in q_blocks():
        rows = slice(q0, q0 + Q_BLOCK)
        k, q, do = k_ref[:klim, :], q_ref[rows, :], do_ref[rows, :]
        raw = dot(k, q, ((1,), (1,)))
        p = jnp.exp2(raw * (scale * LOG2E) - lse_ref[:, rows])
        p = jnp.where(seen_mask(thr_ref, q0, raw.shape), p, 0.0)
        dv_sum[:klim, :] += dot(p.astype(BF), do, ((1,), (0,)))
        dp = dot(v_ref[:klim, :], do, ((1,), (1,)))
        delta = jnp.sum(p * dp, axis=0, keepdims=True)
        ds = (p * (dp - delta) * scale).astype(BF)
        dk_sum[:klim, :] += dot(ds, q, ((1,), (0,)))
        dq = dot(k, ds, ((0,), (0,))).T.astype(BF)
        from_order(places, q0, dq, d_ref, columns(0))
    from_order(places, 0, dk_sum[...].astype(BF), d_ref, columns(1))
    from_order(places, 0, dv_sum[...].astype(BF), d_ref, columns(2))


SMEM_SPEC = pl.BlockSpec(memory_space=pltpu.SMEM)
ATTN_PARAMS = pltpu.CompilerParams(vmem_limit_bytes=56 << 20)


def head_spec(k, heads):
    return pl.BlockSpec((SLOT, HD), lambda h: (0, k * heads + h))


def attn_forward(places, thr, qkv):
    heads = qkv.shape[1] // (3 * HD)
    lse = pl.BlockSpec((1, 1, SLOT), lambda h: (h, 0, 0))
    return pl.pallas_call(
        attn_forward_kernel,
        grid=(heads,),
        in_specs=[SMEM_SPEC, pl.BlockSpec((SLOT, 128), lambda h: (0, 0))]
        + [head_spec(k, heads) for k in range(3)],
        out_specs=[head_spec(0, heads), lse],
        out_shape=[
            jax.ShapeDtypeStruct((SLOT, heads * HD), BF),
            jax.ShapeDtypeStruct((heads, 1, SLOT), F32),
        ],
        scratch_shapes=[pltpu.VMEM((SLOT, HD), BF)] * 3,
        compiler_params=ATTN_PARAMS,
        cost_estimate=cost(6.5 * heads),
    )(places, thr, qkv, qkv, qkv)


def step_rate(update_sq, weight_sq, n_real):
    update_rms = jnp.sqrt(update_sq / n_real)
    weight_rms = jnp.sqrt(weight_sq / n_real)
    return rate_base * jnp.maximum(eps_two, weight_rms) / jnp.maximum(1.0, update_rms / clip_bound)


def apply_step(weight, grad, row_new, col_new, row_mean, rate):
    row = lax.rsqrt(row_new) * (rate * jnp.sqrt(row_mean))
    return weight.astype(F32) - grad * (row[:, None] * lax.rsqrt(col_new)[None, :])


def pair_kernel(factors, *refs):
    g_ref, u_ref = refs[:2]
    o_ref = refs[-1]
    g, u = g_ref[0].astype(F32), u_ref[0].astype(F32)
    if factors:
        wg_ref, wu_ref, row_ref, cg_ref, cu_ref = refs[2:7]
        row = row_ref[...]
        g = wg_ref[...].astype(F32) - g * (row * cg_ref[0])
        u = wu_ref[...].astype(F32) - u * (row * cu_ref[0])
    o_ref[:, 0, :] = g
    o_ref[:, 1, :] = u


def pair_rows(grads, ff, step=None):
    width = grads.shape[2]
    block = 96
    grid = (-(-ff // block),)
    third = lambda k, last: pl.BlockSpec((1, block, last), lambda i: (k, i, 0))
    args, specs = [grads, grads], [third(1, width), third(2, width)]
    if step is not None:
        w_gu, row, scales = step
        shift = w_gu.shape[0] // 2 // block
        args += [w_gu, w_gu, row[None, :], scales, scales]
        specs += [
            pl.BlockSpec((block, width), lambda i: (i, 0)),
            pl.BlockSpec((block, width), lambda i: (i + shift, 0)),
            pl.BlockSpec((1, width), lambda i: (0, 0)),
            third(1, 1),
            third(2, 1),
        ]
    return pl.pallas_call(
        functools.partial(pair_kernel, step is not None),
        grid=grid,
        in_specs=specs,
        out_specs=pl.BlockSpec((block, 2, width), lambda i: (i, 0, 0)),
        out_shape=jax.ShapeDtypeStruct((ff, 2, width), F32),
        compiler_params=pltpu.CompilerParams(vmem_limit_bytes=40 << 20),
        cost_estimate=cost(8),
    )(*args)


def qkv_kernel(g_ref, w_ref, row_ref, col_ref, grad_ref, new_ref):
    grad = g_ref[...].astype(F32)
    grad_ref[0] = grad.T
    new_ref[0] = w_ref[0].astype(F32) - (grad * (row_ref[...] * col_ref[...])).T


def qkv_results(grads, w, row, scales):
    kinds, width, cols = w.shape
    block = 512
    result = pl.BlockSpec((1, block, cols), lambda k, i: (k, i, 0))
    shape = jax.ShapeDtypeStruct(w.shape, F32)
    return pl.pallas_call(
        qkv_kernel,
        grid=(kinds, width // block),
        in_specs=[
            pl.BlockSpec((cols, block), lambda k, i: (k, i)),
            result,
            pl.BlockSpec((1, block), lambda k, i: (0, i)),
            pl.BlockSpec((cols, 1), lambda k, i: (k, 0)),
        ],
        out_specs=[result, result],
        out_shape=[shape, shape],
        compiler_params=pltpu.CompilerParams(vmem_limit_bytes=40 << 20),
        cost_estimate=cost(8),
    )(grads, w, row[None, :], scales)


def tie(x, after):
    return lax.optimization_barrier((x, after))[0]


def exchange_kernel(n_dp, n, x_ref, o_ref, dp_buf, rows, part_buf, total, whole, sems):
    me_d, me = lax.axis_index("dp"), lax.axis_index("tensor")
    width = x_ref.shape[1] // n
    columns = lambda t: pl.ds(pl.multiple_of(t * width, width), width)
    dp_peers = [(k - 1, lax.rem(me_d + k, n_dp)) for k in range(1, n_dp)]
    peers = [(k - 1, lax.rem(me + k, n)) for k in range(1, n)]
    barrier = pltpu.get_barrier_semaphore()
    for _, d in dp_peers:
        pl.semaphore_signal(barrier, inc=1, device_id={"dp": d}, device_id_type=pl.DeviceIdType.MESH)
    for _, t in peers:
        pl.semaphore_signal(barrier, inc=1, device_id={"tensor": t}, device_id_type=pl.DeviceIdType.MESH)
    pl.semaphore_wait(barrier, n_dp + n - 2)

    def push(stage, src, dst, k, device):
        copy = pltpu.make_async_remote_copy(
            src_ref=src, dst_ref=dst, send_sem=sems.at[0, stage, k], recv_sem=sems.at[1, stage, k],
            device_id=device, device_id_type=pl.DeviceIdType.MESH,
        )
        copy.start()
        return copy

    first = [push(0, x_ref.at[pl.ds(0, 8)], dp_buf.at[me_d], k, {"dp": d}) for k, d in dp_peers]
    rows[...] = x_ref[...]
    dp_buf[me_d] = x_ref[0:8, :]
    for copy in first:
        copy.wait()
    rows[0:8, :] = sum(dp_buf[d] for d in range(n_dp))
    second = [push(1, rows.at[:, columns(t)], part_buf.at[me], k, {"tensor": t}) for k, t in peers]
    part_buf[me] = rows[:, columns(me)]
    for copy in second:
        copy.wait()
    total[...] = sum(part_buf[t] for t in range(n))
    third = [push(2, total, whole.at[me], k, {"tensor": t}) for k, t in peers]
    whole[me] = total[...]
    for copy in third:
        copy.wait()
    for t in range(n):
        o_ref[:, t * width : (t + 1) * width] = whole[t]


def exchange(x, n_dp, n):
    height, width = x.shape
    slots = pltpu.VMEM((n, height, width // n), F32)
    return pl.pallas_call(
        functools.partial(exchange_kernel, n_dp, n),
        out_shape=jax.ShapeDtypeStruct(x.shape, F32),
        in_specs=[pl.BlockSpec(memory_space=pltpu.VMEM)],
        out_specs=pl.BlockSpec(memory_space=pltpu.VMEM),
        scratch_shapes=[
            pltpu.VMEM((n_dp, 8, width), F32),
            pltpu.VMEM(x.shape, F32),
            slots,
            pltpu.VMEM((height, width // n), F32),
            slots,
            pltpu.SemaphoreType.DMA((2, 3, max(n, n_dp) - 1)),
        ],
        compiler_params=pltpu.CompilerParams(collective_id=0, has_side_effects=True),
        cost_estimate=cost(16),
    )(x)


def on_device(
    layer_in,
    cotangent,
    lengths,
    prefix,
    pad_mask,
    clusters,
    qkv_w,
    out_w,
    gate_up_w,
    down_w,
    ln_params,
    qkv_row,
    qkv_col,
    out_row,
    out_col,
    gu_row,
    gu_col,
    down_row,
    down_col,
    ln_second,
):
    n_data = lax.axis_size("dp")
    n_tensor = lax.axis_size("tensor")
    tensor_rank = lax.axis_index("tensor")
    data_rank = lax.axis_index("dp")
    rows_dev, width = layer_in.shape
    cols_dev = qkv_w.shape[2]
    heads_dev = cols_dev // HD
    ff_dev = gate_up_w.shape[2]
    ff_pad = -(-ff_dev // 128) * 128
    n_clusters = max(2, n_data // 2)
    seq_length = lengths[0]
    seq_prefix = prefix[0]
    ring = Ring(n_tensor)

    onehot = (clusters[:, None] == jnp.arange(n_clusters, dtype=jnp.int32)[None, :]).astype(F32)
    counts = jnp.sum(onehot, axis=0)
    own_row = jnp.sum(
        jnp.where((jnp.arange(n_data, dtype=jnp.int32) == data_rank)[:, None], onehot, 0.0), axis=0
    )
    seq_weight = jnp.sum(own_row / jnp.maximum(counts, 1.0))
    own_pos = tensor_rank * rows_dev + jnp.arange(rows_dev, dtype=jnp.int32)
    live_rows = ((own_pos < seq_length) & (pad_mask == 1)).astype(F32)
    grad_out = cotangent.astype(F32) * (live_rows * seq_weight)[:, None]
    grad_low = grad_out.astype(BF)

    key_live = (own_pos == 0) | (own_pos < seq_length) & (pad_mask == 1)
    seen_from = jnp.where(key_live, jnp.where(own_pos < seq_prefix, 0, own_pos), 2 * SLOT)
    seen = jnp.broadcast_to(seen_from.astype(F32)[None], (8, rows_dev))

    col_index = tensor_rank * ff_dev + jnp.arange(ff_pad, dtype=jnp.int32)
    ff_real = ((col_index < FF) & (jnp.arange(ff_pad) < ff_dev)).astype(F32)
    ff_mask = ff_real[:ff_dev]

    layer_own = layer_in.astype(F32)
    places = ring.places(rows_dev)
    act_one_all, qkv, seen_all = first_gather(
        n_tensor, layer_in, seen, ln_params, jnp.transpose(qkv_w, (1, 0, 2))
    )
    thr = jnp.broadcast_to(seen_all[:, 0].reshape(SLOT, 1), (SLOT, 128))

    pair = ring.halves(tie(grad_low, qkv))
    grad_pairs = [pair, ring.step(*pair)]
    context, lse = attn_forward(places, thr, qkv)
    pair = tie(grad_pairs[1], context)
    for s in range(2, n_tensor):
        pair = ring.step(*pair)
        grad_pairs.append(pair)
    grad_chunks = [jnp.concatenate(p, axis=0) for p in grad_pairs]
    pad = ((0, ff_pad - ff_dev), (0, 0))
    gate_up_late, down_late = tie(
        (jnp.transpose(gate_up_w, (2, 1, 0)), down_w), grad_chunks[min(3, n_tensor - 1)]
    )
    w_gu = jnp.concatenate([jnp.pad(gate_up_late[:, i], pad) for i in range(2)], axis=0)
    w_down = jnp.pad(down_late, pad)
    part_of = lambda x, s: x[s * rows_dev : (s + 1) * rows_dev]
    acc = None
    for s in ring.scatter_order():
        received = None if acc is None else ring.send(acc)
        acc = ring.add(received, dot(part_of(context, s), out_w, ((1,), (0,))))
    attn_own = jnp.concatenate(acc, axis=0)
    hidden_own = layer_own + attn_own
    norm_two = layer_norm(hidden_own, ln_params[2], ln_params[3]).astype(BF)

    act_two, inner, d_gu = [], [], []
    pair = ring.halves(norm_two)
    for s in range(n_tensor):
        pair = ring.step(*pair) if s else pair
        act = jnp.concatenate(pair, axis=0)
        act_two.append(act)
        gate_up = dot(act, w_gu, ((1,), (1,)))
        gate, up = gate_up[:, :ff_pad], gate_up[:, ff_pad:]
        gelu_gate, gelu_back = jax.vjp(jax.nn.gelu, gate)
        inner.append((gelu_gate * up * ff_real).astype(BF))
        d_inner = dot(grad_chunks[s], w_down, ((1,), (1,))) * ff_real
        d_gate = gelu_back(d_inner * up)[0]
        d_gu.append(jnp.concatenate([d_gate, d_inner * gelu_gate], axis=1).astype(BF))
    acc = None
    for s in ring.scatter_order():
        received = None if acc is None else ring.send(acc)
        acc = ring.add(received, dot(d_gu[s], w_gu, ((1,), (0,))))
    d_norm_two = jnp.concatenate(acc, axis=0)

    d_hidden_ln, ln_two_part = layer_norm_back(hidden_own, ln_params[2], d_norm_two)
    d_hidden = grad_out + d_hidden_ln
    whole = lambda chunks: jnp.concatenate(chunks, axis=0)
    inner_all = whole(inner)
    n_x = n_data // 2
    ff_col = jnp.pad(ff_mask, (0, ff_pad - ff_dev))[:, None]
    square_sum = lambda w: jnp.sum(jnp.square(w.astype(F32)))
    weight_squares = jnp.stack(
        [
            square_sum(qkv_w),
            square_sum(w_gu * jnp.concatenate([ff_col, ff_col]).astype(BF)),
            square_sum(out_w),
            square_sum(w_down * ff_col.astype(BF)),
        ]
    )
    d_context, out_part, ff_mine, down_slots = back_gather(
        n_tensor, n_x, ff_dev, d_hidden.astype(BF), out_w, context,
        inner_all, whole(d_gu), whole(grad_chunks), whole(act_two), weight_squares,
    )

    layer_out, d_qkv, gu_slots, oq_mine = ffn_scatter(
        n_tensor, n_x, inner_all, w_down, hidden_own, thr, qkv, d_context, lse,
        out_part, act_one_all, ff_mine,
    )

    blend = lambda old, total: DECAY * old + (1.0 - DECAY) * total
    ff_rows = ff_mine.shape[1]
    more = ((0, 0), (0, ff_rows - ff_dev))
    oq_old = jnp.concatenate([qkv_col.reshape(-1), out_row])[:, None]
    ff_old = jnp.pad(jnp.concatenate([down_row[None], gu_col]), more, constant_values=1.0)[:, :, None]
    ff_real = jnp.pad(ff_mask, (0, ff_rows - ff_dev))[:, None]
    qkv_t = jnp.transpose(qkv_w, (1, 0, 2))
    d_norm_one, goq, gff, oq_new, ff_new, sums = last_scatter(
        n_tensor, n_x, d_qkv, qkv_t, oq_mine, oq_old, jnp.ones_like(oq_old), ff_old, ff_real,
        ff_mine, down_slots, gu_slots,
    )
    d_input_ln, ln_one_part = layer_norm_back(layer_own, ln_params[0], d_norm_one)
    input_grad = (d_hidden + d_input_ln).astype(BF)
    qkv_col_new, out_row_new = oq_new[: 3 * cols_dev, 0], oq_new[3 * cols_dev :, 0]
    down_row_new, gu_col_new = ff_new[0, :ff_dev, 0], ff_new[1:, :ff_dev, 0]
    scalars = jnp.concatenate(
        [weight_squares, jnp.stack([jnp.sum(out_row_new), jnp.sum(down_row_new * ff_mask)])]
    )
    packed = jnp.concatenate(
        [
            ln_one_part,
            ln_two_part,
            jnp.pad(scalars / n_data, (0, width - scalars.shape[0]))[None],
            jnp.zeros((3, width), F32),
            sums,
        ],
        axis=0,
    )
    packed = exchange(packed, n_data, n_tensor)
    ln_tot = packed[:4]
    qkv_wtot, gu_wtot, out_wtot, down_wtot, out_rtot, down_rtot = (packed[4, i] for i in range(6))
    qkv_tot, qkv_usq, gu_tot, gu_usq, out_tot, out_usq, down_tot, down_usq = (
        packed[8 + i] for i in range(8)
    )

    qkv_cols_all = 3 * cols_dev * n_tensor
    out_rows_all = cols_dev * n_tensor
    qkv_row_new = blend(qkv_row, qkv_tot / qkv_cols_all)
    qkv_mean = jnp.sum(qkv_row_new) / width
    gu_row_new = blend(gu_row, gu_tot / (2 * FF))
    gu_mean = jnp.sum(gu_row_new) / width
    out_col_new = blend(out_col, out_tot / out_rows_all)
    out_mean = out_rtot / out_rows_all
    down_col_new = blend(down_col, down_tot / FF)
    down_mean = down_rtot / FF
    qkv_rate = step_rate(jnp.sum(qkv_usq / qkv_row_new) * qkv_mean, qkv_wtot, width * qkv_cols_all)
    gu_rate = step_rate(jnp.sum(gu_usq / gu_row_new) * gu_mean, gu_wtot, width * 2 * FF)
    out_rate = step_rate(jnp.sum(out_usq / out_col_new) * out_mean, out_wtot, out_rows_all * width)
    down_rate = step_rate(jnp.sum(down_usq / down_col_new) * down_mean, down_wtot, FF * width)

    scale_of = lambda new, mean, rate: lax.rsqrt(new) * (rate * jnp.sqrt(mean))
    qkv_grad, qkv_new = qkv_results(
        goq, qkv_t, scale_of(qkv_row_new, qkv_mean, qkv_rate), lax.rsqrt(oq_new)
    )
    out_sum, down_sum = goq[3 * cols_dev :].astype(F32), gff[0, :ff_dev].astype(F32)
    out_new = apply_step(out_w, out_sum, out_row_new, out_col_new, out_mean, out_rate)
    down_new = apply_step(down_w, down_sum, down_row_new, down_col_new, down_mean, down_rate)
    gu_grad = pair_rows(gff, ff_dev)
    gu_new = pair_rows(
        gff, ff_dev, (w_gu, scale_of(gu_row_new, gu_mean, gu_rate), lax.rsqrt(ff_new))
    )
    qkv_back = lambda x: jnp.transpose(x, (1, 0, 2))
    ln_second_new = blend(ln_second, ln_tot * ln_tot + eps_one)
    ln_update = ln_tot * lax.rsqrt(ln_second_new)
    ln_urms = jnp.sqrt(jnp.mean(ln_update * ln_update, axis=1, keepdims=True))
    ln_wrms = jnp.sqrt(jnp.mean(ln_params * ln_params, axis=1, keepdims=True))
    ln_new = ln_params - rate_base * jnp.maximum(eps_two, ln_wrms) * ln_update / jnp.maximum(
        1.0, ln_urms / clip_bound
    )
    return (
        layer_out,
        input_grad,
        qkv_back(qkv_grad),
        qkv_back(qkv_new),
        qkv_row_new,
        qkv_col_new.reshape(3, -1),
        out_sum,
        out_new,
        out_row_new,
        out_col_new,
        jnp.transpose(gu_grad, (2, 1, 0)),
        jnp.transpose(gu_new, (2, 1, 0)),
        gu_row_new,
        gu_col_new,
        down_sum,
        down_new,
        down_row_new,
        down_col_new,
        ln_tot,
        ln_second_new,
        ln_new,
    )


def solution(mesh):
    in_specs = (
        P(("dp", "tensor"), None),
        P(("dp", "tensor"), None),
        P("dp"),
        P("dp"),
        P(("dp", "tensor")),
        P(),
        P(None, None, "tensor"),
        P("tensor", None),
        P(None, None, "tensor"),
        P("tensor", None),
        P(),
        P(),
        P(None, "tensor"),
        P("tensor"),
        P(),
        P(),
        P(None, "tensor"),
        P("tensor"),
        P(),
        P(),
    )
    out_specs = (
        P(("dp", "tensor"), None),
        P(("dp", "tensor"), None),
        P(None, None, "tensor"),
        P(None, None, "tensor"),
        P(),
        P(None, "tensor"),
        P("tensor", None),
        P("tensor", None),
        P("tensor"),
        P(),
        P(None, None, "tensor"),
        P(None, None, "tensor"),
        P(),
        P(None, "tensor"),
        P("tensor", None),
        P("tensor", None),
        P("tensor"),
        P(),
        P(),
        P(),
        P(),
    )
    return jax.shard_map(
        on_device, mesh=mesh, in_specs=in_specs, out_specs=out_specs, check_vma=False
    )
```

```python
import functools

import jax
import jax.numpy as jnp
from jax import lax
from jax.experimental import pallas as pl
from jax.experimental.pallas import tpu as pltpu
from jax.sharding import PartitionSpec as P

HD = 128
FF = 5461
SLOT = 2048
STEP = 10
DECAY = 1.0 - STEP ** (-0.8)
PREFIX_MAX = SLOT // 2
Q_BLOCK = 512

ln_eps = 1e-05
eps_one = 1e-30
eps_two = 0.001
clip_bound = 1.0
rate_base = 1.0
masked_score = -1e30
LOG2E = 1.4426950408889634
BF = jnp.bfloat16
F32 = jnp.float32


def dot(a, b, dims):
    return lax.dot_general(a, b, (dims, ((), ())), preferred_element_type=F32)


def ring_order(n):
    b_size = 2 if n <= 8 else 4
    a_size = n // b_size
    order = []
    for a in range(a_size):
        cols = list(range(1, b_size))
        order += [a * b_size + c for c in (cols[::-1] if a % 2 else cols)]
    for a in range(a_size - 1, -1, -1):
        order.append(a * b_size)
    return order


class Ring:
    def __init__(self, n):
        self.n = n
        order = ring_order(n)
        self.fw = [(order[i], order[(i + 1) % n]) for i in range(n)]
        self.bw = [(order[i], order[(i - 1) % n]) for i in range(n)]
        place = [0] * n
        for p, t in enumerate(order):
            place[t] = p
        self.place = jnp.array(place, jnp.int32)
        self.pos = self.place[lax.axis_index("tensor")]

    def step(self, a, b):
        return lax.ppermute(a, "tensor", self.fw), lax.ppermute(b, "tensor", self.bw)

    def halves(self, x):
        half = x.shape[0] // 2
        return x[:half], x[half:]

    def scatter_order(self):
        return list(range(1, self.n)) + [0]

    def add(self, received, term, after=()):
        term = lax.optimization_barrier((term, after))[0]
        parts = self.halves(term)
        if received is not None:
            parts = tuple(r.astype(F32) + t for r, t in zip(received, parts))
        return parts

    def low(self, parts):
        return tuple(p.astype(BF) for p in parts)

    def send(self, parts):
        return self.step(*self.low(parts))


def cost(micros):
    return pl.CostEstimate(flops=int(micros * 1e9), transcendentals=0, bytes_accessed=4 << 20)


PUSH = pl.DeviceIdType.MESH
PIECES = 2
ROW_BLOCK = 64


def pick(index, table):
    out = jnp.int32(table[0])
    for k in range(1, len(table)):
        out = jnp.where(index == k, jnp.int32(table[k]), out)
    return out


def neighbours(n):
    order = ring_order(n)
    pos = pick(lax.axis_index("tensor"), [order.index(t) for t in range(n)])
    ahead = pick(lax.rem(pos + 1, n), order)
    behind = pick(lax.rem(pos + n - 1, n), order)
    return pos, [{"tensor": ahead}, {"tensor": behind}]


def chunk_places(n, pos, rows):
    places = []
    for t in range(n):
        place = ring_order(n).index(t)
        places.append(lax.rem(pos + (n - place), n) * rows)
        places.append(lax.rem(place - pos + n, n) * rows + rows // 2)
    return places


def other_core():
    me = lax.axis_index("dp")
    return {"dp": me + 1 - 2 * lax.rem(me, 2)}


def other_chips(n_x):
    core, chip = lax.rem(lax.axis_index("dp"), 2), lax.axis_index("dp") // 2
    return chip, [{"dp": 2 * lax.rem(chip + k, n_x) + core} for k in range(1, n_x)]


def greet(devices):
    barrier = pltpu.get_barrier_semaphore()
    for device in devices:
        pl.semaphore_signal(barrier, inc=1, device_id=device, device_id_type=PUSH)
    pl.semaphore_wait(barrier, len(devices))


def ring_copy(land, send_sem, recv_sem, sides, d, s, piece=None):
    src, dst, sem = land.at[d, s], land.at[d, s + 1], d
    if piece is not None:
        size = land.shape[2] // PIECES
        rows = pl.ds(piece * size, size)
        src, dst, sem = land.at[d, s, rows], land.at[d, s + 1, rows], d * PIECES + piece
    return pltpu.make_async_remote_copy(
        src_ref=src,
        dst_ref=dst,
        send_sem=send_sem.at[sem, s],
        recv_sem=recv_sem.at[sem, s],
        device_id=sides[d],
        device_id_type=PUSH,
    )


def ring_sent(n, copy, pieces=(None,)):
    def sent(s, carry):
        for d in range(2):
            for piece in pieces:
                copy(d, s, piece).wait_send()
        return carry

    lax.fori_loop(0, n - 1, sent, 0)


def ring_gather(n, x_ref, land, send_sem, recv_sem, sides, work):
    copy = functools.partial(ring_copy, land, send_sem, recv_sem, sides)
    half = x_ref.shape[0] // 2
    land[0, 0] = x_ref[:half, :]
    land[1, 0] = x_ref[half:, :]

    def step(s, carry):
        for d in range(2):

            @pl.when(s > 0)
            def _():
                copy(d, s - 1).wait_recv()

            @pl.when(s < n - 1)
            def _():
                copy(d, s).start()

        work(s)
        return carry

    lax.fori_loop(0, n, step, 0)
    ring_sent(n, copy)


def ring_scatter(n, land, send_sem, recv_sem, sides, term_buf, term, work, finish):
    copy = functools.partial(ring_copy, land, send_sem, recv_sem, sides)
    half = term_buf.shape[0] // 2
    size = half // PIECES
    for d in range(2):
        land[d, 0] = jnp.zeros(land.shape[2:], land.dtype)

    def step(s, carry):
        term(lax.rem(s + 1, n))
        for piece in range(PIECES):
            for d in range(2):
                part = slice(piece * size, (piece + 1) * size)
                rows = slice(d * half + piece * size, d * half + (piece + 1) * size)

                @pl.when(s > 0)
                def _():
                    copy(d, s - 1, piece).wait_recv()

                total = land[d, s, part].astype(F32) + term_buf[rows, :]

                @pl.when(s < n - 1)
                def _():
                    land[d, s, part] = total.astype(BF)
                    copy(d, s, piece).start()

                @pl.when(s == n - 1)
                def _():
                    finish(rows, total)

        work(s)
        return carry

    lax.fori_loop(0, n, step, 0)
    ring_sent(n, copy, range(PIECES))


def dot_columns(out, a, b, dims, block=512):
    width = b.shape[1]

    def columns(j, carry):
        at = pl.ds(pl.multiple_of(j * block, block), block)
        out(at, dot(a, b[:, at], dims))
        return carry

    lax.fori_loop(0, width // block, columns, 0)


def first_kernel(
    n, x_ref, seen_ref, ln_ref, w_ref, act_ref, qkv_ref, seen_all,
    land, act_buf, seen_buf, send_sem, recv_sem, act_sem, seen_sem,
):
    rows, cols = x_ref.shape[0], w_ref.shape[2]
    me = lax.axis_index("tensor")
    peers = [lax.rem(me + k, n) for k in range(1, n)]
    sides = neighbours(n)[1]
    greet([{"tensor": t} for t in peers])

    def seen_copy(k):
        return pltpu.make_async_remote_copy(
            src_ref=seen_ref, dst_ref=seen_buf.at[me], send_sem=seen_sem.at[0, k],
            recv_sem=seen_sem.at[1, k], device_id={"tensor": peers[k]}, device_id_type=PUSH,
        )

    def act_copy(s):
        place = pl.ds(pl.multiple_of(s * rows, rows), rows)
        return pltpu.make_async_copy(act_buf.at[s], act_ref.at[place], act_sem.at[s])

    def work(s):
        @pl.when(s == 0)
        def _():
            for k in range(n - 1):
                seen_copy(k).start()

        chunk = jnp.concatenate([land[0, s], land[1, s]], axis=0).astype(F32)
        act = layer_norm(chunk, ln_ref[0:1, :], ln_ref[1:2, :]).astype(BF)
        act_buf[s] = act
        act_copy(s).start()
        place = pl.ds(pl.multiple_of(s * rows, rows), rows)
        for k in range(3):
            qkv_ref[place, k * cols : (k + 1) * cols] = dot(act, w_ref[k], ((1,), (0,))).astype(BF)

    ring_gather(n, x_ref, land, send_sem, recv_sem, sides, work)
    seen_buf[me] = seen_ref[...]
    for k in range(n - 1):
        seen_copy(k).wait()
    seen_all[...] = seen_buf[...]

    def written(s, carry):
        act_copy(s).wait()
        return carry

    lax.fori_loop(0, n, written, 0)


def ring_scratch(n, rows, width, pieces=1):
    return [pltpu.VMEM((2, n, rows // 2, width), BF)], [
        pltpu.SemaphoreType.DMA((2 * pieces, n - 1)),
        pltpu.SemaphoreType.DMA((2 * pieces, n - 1)),
    ]


VMEM_SPEC = pl.BlockSpec(memory_space=pltpu.VMEM)
ANY_SPEC = pl.BlockSpec(memory_space=pl.ANY)


def first_gather(n, x, seen, ln_params, w):
    rows, width = x.shape
    cols = w.shape[2]
    buf, sems = ring_scratch(n, rows, width)
    return pl.pallas_call(
        functools.partial(first_kernel, n),
        in_specs=[VMEM_SPEC] * 4,
        out_specs=[ANY_SPEC, VMEM_SPEC, VMEM_SPEC],
        out_shape=[
            jax.ShapeDtypeStruct((n * rows, width), BF),
            jax.ShapeDtypeStruct((n * rows, 3 * cols), BF),
            jax.ShapeDtypeStruct((n,) + seen.shape, F32),
        ],
        scratch_shapes=buf
        + [pltpu.VMEM((n, rows, width), BF), pltpu.VMEM((n,) + seen.shape, F32)]
        + sems
        + [pltpu.SemaphoreType.DMA((n,)), pltpu.SemaphoreType.DMA((2, n - 1))],
        compiler_params=pltpu.CompilerParams(
            collective_id=1, has_side_effects=True, vmem_limit_bytes=56 << 20
        ),
        cost_estimate=pl.CostEstimate(
            flops=6 * n * rows * width * cols, transcendentals=0, bytes_accessed=40 << 20
        ),
    )(x, seen, ln_params, w)


def grad_kernel(
    n, heads, x_ref, qkv_ref, thr_ref, real_ref, qkv_w_ref, gu_w_ref, out_w_ref, down_w_ref,
    all_ref, ctx_ref, lse_ref, square_ref,
    land, q_ref, k_ref, v_ref, send_sem, recv_sem, all_sem,
):
    rows = x_ref.shape[0]
    half = rows // 2
    pos, sides = neighbours(n)
    places = chunk_places(n, pos, rows)
    greet(sides)

    def all_copy(d, s):
        place = pl.ds(pl.multiple_of(s * rows + d * half, half), half)
        return pltpu.make_async_copy(land.at[d, s], all_ref.at[place], all_sem.at[d, s])

    def squares(i, ref, real):
        block, cols = ROW_BLOCK, ref.shape[1]

        def add(j, carry):
            at = pl.multiple_of(j * block, block)
            value = ref[pl.ds(at, block), :].astype(F32)
            value = value * value
            if real is not None:
                value = value * real[pl.ds(lax.rem(at, real.shape[0]), block), :]
            square_ref[i, :, :cols] += sum(value[k : k + 8] for k in range(0, block, 8))
            return carry

        lax.fori_loop(0, ref.shape[0] // block, add, 0)

    def work(s):
        for d in range(2):
            all_copy(d, s).start()
        for h in range(heads):

            @pl.when(s == h)
            def _():
                columns = lambda i: slice((i * heads + h) * HD, (i * heads + h + 1) * HD)
                for i, dst in enumerate((q_ref, k_ref, v_ref)):
                    to_order(places, qkv_ref, columns(i), dst)
                attn_forward_head(
                    places, thr_ref, lse_ref.at[h], q_ref, k_ref, v_ref, ctx_ref, columns(0)
                )

        @pl.when(s == heads)
        def _():
            square_ref[...] = jnp.zeros_like(square_ref)
            for k in range(3):
                squares(0, qkv_w_ref.at[k], None)

        @pl.when(s == heads + 1)
        def _():
            squares(1, gu_w_ref, real_ref)

        @pl.when(s == heads + 2)
        def _():
            squares(2, out_w_ref, None)
            squares(3, down_w_ref, real_ref)

    ring_gather(n, x_ref, land, send_sem, recv_sem, sides, work)

    def written(s, carry):
        for d in range(2):
            all_copy(d, s).wait()
        return carry

    lax.fori_loop(0, n, written, 0)


def grad_gather(n, x, qkv, thr, real, qkv_w, gu_w, out_w, down_w):
    rows, width = x.shape
    cols = out_w.shape[0]
    heads = cols // HD
    buf, sems = ring_scratch(n, rows, width)
    return pl.pallas_call(
        functools.partial(grad_kernel, n, heads),
        in_specs=[VMEM_SPEC] * 8,
        out_specs=[ANY_SPEC] + [VMEM_SPEC] * 3,
        out_shape=[
            jax.ShapeDtypeStruct((n * rows, width), BF),
            jax.ShapeDtypeStruct((n * rows, cols), BF),
            jax.ShapeDtypeStruct((heads, 1, SLOT), F32),
            jax.ShapeDtypeStruct((4, 8, width), F32),
        ],
        scratch_shapes=buf
        + [pltpu.VMEM((SLOT, HD), BF)] * 3
        + sems
        + [pltpu.SemaphoreType.DMA((2, n))],
        compiler_params=pltpu.CompilerParams(
            collective_id=5, has_side_effects=True, vmem_limit_bytes=60 << 20
        ),
        cost_estimate=cost(80),
    )(x, qkv, thr, real, qkv_w, gu_w, out_w, down_w)


def mix_kernel(
    n, ctx_ref, w_ref, x_ref, ln_ref, hidden_ref, norm_ref, land, term_buf, send_sem, recv_sem
):
    rows = x_ref.shape[0]
    sides = neighbours(n)[1]
    greet(sides)

    def term(c):
        place = pl.ds(pl.multiple_of(c * rows, rows), rows)

        def put(at, value):
            term_buf[:, at] = value

        dot_columns(put, ctx_ref[place, :], w_ref, ((1,), (0,)))

    def finish(at, total):
        hidden = x_ref[at, :].astype(F32) + total
        hidden_ref[at, :] = hidden
        norm_ref[at, :] = layer_norm(hidden, ln_ref[2:3, :], ln_ref[3:4, :]).astype(BF)

    ring_scatter(n, land, send_sem, recv_sem, sides, term_buf, term, lambda s: None, finish)


def mix_scatter(n, context, w, x, ln_params):
    rows, width = x.shape
    buf, sems = ring_scratch(n, rows, width, PIECES)
    return pl.pallas_call(
        functools.partial(mix_kernel, n),
        in_specs=[VMEM_SPEC] * 4,
        out_specs=[VMEM_SPEC] * 2,
        out_shape=[
            jax.ShapeDtypeStruct((rows, width), F32),
            jax.ShapeDtypeStruct((rows, width), BF),
        ],
        scratch_shapes=buf + [pltpu.VMEM((rows, width), F32)] + sems,
        compiler_params=pltpu.CompilerParams(
            collective_id=6, has_side_effects=True, vmem_limit_bytes=40 << 20
        ),
        cost_estimate=cost(80),
    )(context, w, x, ln_params)


def back_kernel(
    n, n_x, x_ref, w_ref, ctx_ref, inner_hbm, d_gu_hbm, grad_hbm, act_hbm,
    d_ctx_ref, out_ref, mine_ref, slots_hbm,
    land, lhs, rhs, part, core_land, out_sum, send_sem, recv_sem, load_sem, core_sem, slot_sem,
):
    rows, ff_pad = x_ref.shape[0], lhs.shape[2]
    ff_rows, half = core_land.shape[1:]
    sides, partner = neighbours(n)[1], other_core()
    core = lax.rem(lax.axis_index("dp"), 2)
    of_core = lambda c: pl.ds(pl.multiple_of(c * half, half), half)
    loads = [
        pltpu.make_async_copy(src, dst, load_sem.at[i])
        for i, (src, dst) in enumerate(
            (
                (inner_hbm, lhs.at[0]),
                (grad_hbm, rhs.at[0]),
                (d_gu_hbm.at[:, pl.ds(0, ff_pad)], lhs.at[1]),
                (act_hbm, rhs.at[1]),
                (d_gu_hbm.at[:, pl.ds(ff_pad, ff_pad)], lhs.at[2]),
            )
        )
    ]
    for load in loads:
        load.start()
    out_sum[...] = jnp.zeros_like(out_sum)
    chip, chips = other_chips(n_x)
    greet(sides + [partner] + chips)

    def slot_copy(k):
        return pltpu.make_async_remote_copy(
            src_ref=mine_ref.at[0], dst_ref=slots_hbm.at[chip], send_sem=slot_sem.at[0, k],
            recv_sem=slot_sem.at[1, k], device_id=chips[k], device_id_type=PUSH,
        )

    def core_copy(i):
        return pltpu.make_async_remote_copy(
            src_ref=part.at[i, :, of_core(1 - core)],
            dst_ref=core_land.at[i],
            send_sem=core_sem.at[0, i],
            recv_sem=core_sem.at[1, i],
            device_id=partner,
            device_id_type=PUSH,
        )

    def work(s):
        chunk = jnp.concatenate([land[0, s], land[1, s]], axis=0)
        place = pl.ds(pl.multiple_of(s * rows, rows), rows)
        d_ctx_ref[place, :] = dot(chunk, w_ref[...], ((1,), (1,))).astype(BF)
        out_sum[...] += dot(ctx_ref[place, :], chunk, ((0,), (0,)))
        for i in range(3):

            @pl.when(s == i + 1)
            def _():
                for load in (loads[:2], loads[2:4], loads[4:])[i]:
                    load.wait()

                def put(at, value):
                    part[i, :, at] = value[:ff_rows].astype(BF)

                dot_columns(put, lhs[i], rhs.at[min(i, 1)], ((0,), (0,)))
                core_copy(i).start()

            @pl.when(s == i + 3)
            def _():
                core_copy(i).wait()
                total = part[i, :, of_core(core)].astype(F32) + core_land[i].astype(F32)
                mine_ref[i] = total.astype(BF)
                if i == 0:
                    for k in range(n_x - 1):
                        slot_copy(k).start()

    ring_gather(n, x_ref, land, send_sem, recv_sem, sides, work)
    out_ref[...] = out_sum[...].astype(BF)
    for k in range(n_x - 1):
        slot_copy(k).wait()


def back_gather(n, n_x, ff_dev, x, w, context, inner, d_gu, grad, act):
    rows, width = x.shape
    ff_pad = inner.shape[1]
    ff_rows = -(-ff_dev // ROW_BLOCK) * ROW_BLOCK
    buf, sems = ring_scratch(n, rows, width)
    return pl.pallas_call(
        functools.partial(back_kernel, n, n_x),
        in_specs=[VMEM_SPEC] * 3 + [ANY_SPEC] * 4,
        out_specs=[VMEM_SPEC] * 3 + [ANY_SPEC],
        out_shape=[
            jax.ShapeDtypeStruct((n * rows, w.shape[0]), BF),
            jax.ShapeDtypeStruct(w.shape, BF),
            jax.ShapeDtypeStruct((3, ff_rows, width // 2), BF),
            jax.ShapeDtypeStruct((n_x, ff_rows, width // 2), BF),
        ],
        scratch_shapes=buf
        + [
            pltpu.VMEM((3, n * rows, ff_pad), BF),
            pltpu.VMEM((2, n * rows, width), BF),
            pltpu.VMEM((3, ff_rows, width), BF),
            pltpu.VMEM((3, ff_rows, width // 2), BF),
            pltpu.VMEM(w.shape, F32),
        ]
        + sems
        + [
            pltpu.SemaphoreType.DMA((5,)),
            pltpu.SemaphoreType.DMA((2, 3)),
            pltpu.SemaphoreType.DMA((2, n_x - 1)),
        ],
        compiler_params=pltpu.CompilerParams(
            collective_id=3, has_side_effects=True, vmem_limit_bytes=60 << 20
        ),
        cost_estimate=cost(80),
    )(x, w, context, inner, d_gu, grad, act)


def ffn_kernel(
    n, n_x, heads, inner_ref, w_ref, hidden_ref, thr_ref, qkv_ref, d_ctx_ref, lse_ref,
    out_part_ref, act_hbm, mine_hbm,
    out_ref, d_qkv_ref, slots_hbm, oq_mine_ref,
    land, term_buf, q_ref, k_ref, v_ref, do_ref, dk_sum, dv_sum,
    act_buf, part, qkv_land, out_land,
    send_sem, recv_sem, act_sem, core_sem, slot_sem,
):
    rows = hidden_ref.shape[0]
    pos, sides = neighbours(n)
    partner = other_core()
    core = lax.rem(lax.axis_index("dp"), 2)
    chip, chips = other_chips(n_x)
    block = act_buf.shape[2]
    blocks = act_hbm.shape[1] // block
    qkv_cols, wide = qkv_land.shape
    wide_of = lambda c: pl.ds(pl.multiple_of(c * wide, wide), wide)

    def act_load(j):
        return pltpu.make_async_copy(
            act_hbm.at[:, pl.ds(j * block, block)], act_buf.at[j % 2], act_sem.at[j]
        )

    def core_copy(i):
        src, dst = (
            (part.at[:, wide_of(1 - core)], qkv_land),
            (out_part_ref.at[:, wide_of(1 - core)], out_land),
        )[i]
        return pltpu.make_async_remote_copy(
            src_ref=src, dst_ref=dst, send_sem=core_sem.at[0, i], recv_sem=core_sem.at[1, i],
            device_id=partner, device_id_type=PUSH,
        )

    def slot_copy(k):
        return pltpu.make_async_remote_copy(
            src_ref=mine_hbm.at[pl.ds(1, 2)], dst_ref=slots_hbm.at[chip], send_sem=slot_sem.at[0, k],
            recv_sem=slot_sem.at[1, k], device_id=chips[k], device_id_type=PUSH,
        )

    for j in range(2):
        act_load(j).start()
    greet(sides + [partner] + chips)
    core_copy(1).start()
    for k in range(n_x - 1):
        slot_copy(k).start()
    places = chunk_places(n, pos, rows)

    def term(c):
        place = pl.ds(pl.multiple_of(c * rows, rows), rows)

        def put(at, value):
            term_buf[:, at] = value

        dot_columns(put, inner_ref[place, :], w_ref, ((1,), (0,)))

    def work(s):
        for h in range(heads):

            @pl.when(s == h + 1)
            def _():
                columns = lambda i: slice((i * heads + h) * HD, (i * heads + h + 1) * HD)
                for i, dst in enumerate((q_ref, k_ref, v_ref)):
                    to_order(places, qkv_ref, columns(i), dst)
                to_order(places, d_ctx_ref, columns(0), do_ref)
                attn_backward_head(
                    places, thr_ref, lse_ref.at[h], q_ref, k_ref, v_ref, do_ref, dk_sum, dv_sum,
                    d_qkv_ref, columns,
                )

        @pl.when(s == 1)
        def _():
            core_copy(1).wait()
            total = out_part_ref[:, wide_of(core)].astype(F32) + out_land[...].astype(F32)
            oq_mine_ref[qkv_cols:, :] = total.astype(BF)

        for turn in range(blocks // 2):

            @pl.when(s == heads + 1 + turn)
            def _():
                for j in (2 * turn, 2 * turn + 1):
                    act_load(j).wait()
                    grad = dot(d_qkv_ref[...], act_buf[j % 2], ((0,), (0,)))
                    part[:, j * block : (j + 1) * block] = grad.astype(BF)
                for j in (2 * turn + 2, 2 * turn + 3):
                    if j < blocks:
                        act_load(j).start()
                if turn == blocks // 2 - 1:
                    core_copy(0).start()

        @pl.when(s == heads + 2 + blocks // 2)
        def _():
            core_copy(0).wait()
            total = part[:, wide_of(core)].astype(F32) + qkv_land[...].astype(F32)
            oq_mine_ref[:qkv_cols, :] = total.astype(BF)

    def finish(at, total):
        out_ref[at, :] = (hidden_ref[at, :] + total).astype(BF)

    ring_scatter(n, land, send_sem, recv_sem, sides, term_buf, term, work, finish)
    for k in range(n_x - 1):
        slot_copy(k).wait()


def ffn_scatter(n, n_x, inner, w, hidden, thr, qkv, d_context, lse, out_part, act, mine):
    rows, width = hidden.shape
    cols, block = d_context.shape[1], 512
    heads = d_context.shape[1] // HD
    buf, sems = ring_scratch(n, rows, width, PIECES)
    return pl.pallas_call(
        functools.partial(ffn_kernel, n, n_x, heads),
        in_specs=[VMEM_SPEC] * 8 + [ANY_SPEC] * 2,
        out_specs=[VMEM_SPEC] * 2 + [ANY_SPEC, VMEM_SPEC],
        out_shape=[
            jax.ShapeDtypeStruct((rows, width), BF),
            jax.ShapeDtypeStruct(qkv.shape, BF),
            jax.ShapeDtypeStruct((n_x, 2) + mine.shape[1:], BF),
            jax.ShapeDtypeStruct((4 * cols, width // 2), BF),
        ],
        scratch_shapes=buf
        + [pltpu.VMEM((rows, width), F32)]
        + [pltpu.VMEM((SLOT, HD), BF)] * 4
        + [pltpu.VMEM((SLOT, HD), F32)] * 2
        + [
            pltpu.VMEM((2, n * rows, block), BF),
            pltpu.VMEM((3 * cols, width), BF),
            pltpu.VMEM((3 * cols, width // 2), BF),
            pltpu.VMEM((cols, width // 2), BF),
        ]
        + sems
        + [
            pltpu.SemaphoreType.DMA((width // block,)),
            pltpu.SemaphoreType.DMA((2, 2)),
            pltpu.SemaphoreType.DMA((2, n_x - 1)),
        ],
        compiler_params=pltpu.CompilerParams(
            collective_id=4, has_side_effects=True, vmem_limit_bytes=62 << 20
        ),
        cost_estimate=cost(95),
    )(inner, w, hidden, thr, qkv, d_context, lse, out_part, act, mine)


def row_sums(grad_ref, old_ref, real_ref, new_ref, c_ref, t_ref):
    width = grad_ref.shape[1]
    block = ROW_BLOCK

    def rows(i, carry):
        at = pl.ds(pl.multiple_of(i * block, block), block)
        grad = grad_ref[at, :].astype(F32)
        square = grad * grad
        real = real_ref[at, :]
        total = (jnp.sum(square, axis=1, keepdims=True) + width * eps_one) * real
        new = DECAY * old_ref[at, :] + (1.0 - DECAY) * (total / width)
        new_ref[at, :] = new
        c = (square + eps_one) * real
        t = square * (real / new)
        c_ref[...] += sum(c[k : k + 8] for k in range(0, block, 8))
        t_ref[...] += sum(t[k : k + 8] for k in range(0, block, 8))
        return carry

    lax.fori_loop(0, grad_ref.shape[0] // block, rows, 0)


def last_kernel(
    n, n_x, d_qkv_ref, w_ref, oq_mine_ref, oq_old, oq_real, ff_old, ff_real, mine_hbm, down_hbm, gu_hbm,
    out_ref, goq_ref, gff_ref, oq_new, ff_new, sums_ref,
    land, term_buf, oq_land, ff_own, ff_slots, c_sum, t_sum,
    send_sem, recv_sem, oq_sem, load_sem, join_sem,
):
    rows = term_buf.shape[0]
    cols, width = w_ref.shape[2], term_buf.shape[1]
    sides, partner = neighbours(n)[1], other_core()
    core = lax.rem(lax.axis_index("dp"), 2)
    chip, chips = other_chips(n_x)
    half = width // 2
    own = pl.ds(pl.multiple_of(core * half, half), half)

    def loads(i):
        slots = down_hbm if i == 0 else gu_hbm.at[:, i - 1]
        return [
            pltpu.make_async_copy(mine_hbm.at[i], ff_own.at[i], load_sem.at[0, i]),
            pltpu.make_async_copy(slots, ff_slots.at[i], load_sem.at[1, i]),
        ]

    def oq_copy(k):
        return pltpu.make_async_remote_copy(
            src_ref=oq_mine_ref, dst_ref=oq_land.at[chip], send_sem=oq_sem.at[0, k],
            recv_sem=oq_sem.at[1, k], device_id=chips[k], device_id_type=PUSH,
        )

    def join(i):
        ref = goq_ref.at[:, own] if i == 3 else gff_ref.at[i, :, own]
        return pltpu.make_async_remote_copy(
            src_ref=ref, dst_ref=ref, send_sem=join_sem.at[0, i], recv_sem=join_sem.at[1, i],
            device_id=partner, device_id_type=PUSH,
        )

    def chip_sum(own_half, slots):
        total = jnp.zeros(own_half.shape, F32)
        for x in range(n_x):
            total = total + jnp.where(chip == x, own_half, slots[x]).astype(F32)
        return total.astype(BF)

    for i in range(3):
        for load in loads(i):
            load.start()
    greet(sides + [partner] + chips)
    for k in range(n_x - 1):
        oq_copy(k).start()

    def term(c):
        place = pl.ds(pl.multiple_of(c * rows, rows), rows)
        block = 512

        def columns(j, carry):
            at = pl.ds(pl.multiple_of(j * block, block), block)
            term_buf[:, at] = sum(
                dot(d_qkv_ref[place, k * cols : (k + 1) * cols], w_ref[k, at, :], ((1,), (1,)))
                for k in range(3)
            )
            return carry

        lax.fori_loop(0, width // block, columns, 0)

    def sums(group, ref, first=True):
        if first:
            c_sum[...] = jnp.zeros_like(c_sum)
            t_sum[...] = jnp.zeros_like(t_sum)
        row_sums(*ref, c_sum, t_sum)
        sums_ref[2 * group : 2 * group + 1, :] = jnp.sum(c_sum[...], axis=0, keepdims=True)
        sums_ref[2 * group + 1 : 2 * group + 2, :] = jnp.sum(t_sum[...], axis=0, keepdims=True)

    ff_refs = lambda i: (gff_ref.at[i], ff_old.at[i], ff_real, ff_new.at[i])
    oq_refs = lambda at: tuple(ref.at[at] for ref in (goq_ref, oq_old, oq_real, oq_new))

    def work(s):
        for i in range(3):

            @pl.when(s == i)
            def _():
                for load in loads(i):
                    load.wait()
                gff_ref[i, :, own] = chip_sum(ff_own[i], ff_slots.at[i])
                join(i).start()

        @pl.when(s == 4)
        def _():
            for k in range(n_x - 1):
                oq_copy(k).wait()
            goq_ref[:, own] = chip_sum(oq_mine_ref[...], oq_land)
            join(3).start()

        @pl.when(s == 3)
        def _():
            join(0).wait()
            sums(3, ff_refs(0))

        @pl.when(s == 5)
        def _():
            join(1).wait()
            sums(1, ff_refs(1))

        @pl.when(s == 6)
        def _():
            join(2).wait()
            sums(1, ff_refs(2), first=False)

    def finish(at, total):
        out_ref[at, :] = total

    ring_scatter(n, land, send_sem, recv_sem, sides, term_buf, term, work, finish)
    join(3).wait()
    sums(0, oq_refs(pl.ds(0, 3 * cols)))
    sums(2, oq_refs(pl.ds(3 * cols, cols)))


def last_scatter(n, n_x, d_qkv, w, oq_mine, oq_old, oq_real, ff_old, ff_real, ff_mine, down_slots, gu_slots):
    width, cols = w.shape[1:]
    rows = d_qkv.shape[0] // n
    half = width // 2
    ff_rows = ff_mine.shape[1]
    buf, sems = ring_scratch(n, rows, width, PIECES)
    return pl.pallas_call(
        functools.partial(last_kernel, n, n_x),
        in_specs=[VMEM_SPEC] * 7 + [ANY_SPEC] * 3,
        out_specs=[VMEM_SPEC] * 6,
        out_shape=[
            jax.ShapeDtypeStruct((rows, width), F32),
            jax.ShapeDtypeStruct((4 * cols, width), BF),
            jax.ShapeDtypeStruct((3, ff_rows, width), BF),
            jax.ShapeDtypeStruct(oq_old.shape, F32),
            jax.ShapeDtypeStruct(ff_old.shape, F32),
            jax.ShapeDtypeStruct((8, width), F32),
        ],
        scratch_shapes=buf
        + [
            pltpu.VMEM((rows, width), F32),
            pltpu.VMEM((n_x,) + oq_mine.shape, BF),
            pltpu.VMEM((3, ff_rows, half), BF),
            pltpu.VMEM((3, n_x, ff_rows, half), BF),
            pltpu.VMEM((8, width), F32),
            pltpu.VMEM((8, width), F32),
        ]
        + sems
        + [
            pltpu.SemaphoreType.DMA((2, n_x - 1)),
            pltpu.SemaphoreType.DMA((2, 3)),
            pltpu.SemaphoreType.DMA((2, 4)),
        ],
        compiler_params=pltpu.CompilerParams(
            collective_id=2, has_side_effects=True, vmem_limit_bytes=62 << 20
        ),
        cost_estimate=cost(90),
    )(d_qkv, w, oq_mine, oq_old, oq_real, ff_old, ff_real, ff_mine, down_slots, gu_slots)


def norm_stats(rows):
    mean_row = jnp.mean(rows, axis=-1, keepdims=True)
    centered = rows - mean_row
    variance = jnp.mean(centered * centered, axis=-1, keepdims=True)
    scale = lax.rsqrt(variance + ln_eps)
    return centered * scale, scale


def layer_norm(rows, gain, shift):
    return norm_stats(rows)[0] * gain + shift


def layer_norm_back(rows, gain, e):
    n, scale = norm_stats(rows)
    eg = e * gain
    dv = scale * (
        eg - jnp.mean(eg, axis=-1, keepdims=True) - n * jnp.mean(eg * n, axis=-1, keepdims=True)
    )
    return dv, jnp.stack([jnp.sum(e * n, axis=0), jnp.sum(e, axis=0)])


def seen_mask(thr_ref, q0, shape):
    thr = thr_ref[: shape[0], :]
    thr = jnp.concatenate([thr] * (shape[1] // thr.shape[1]), axis=1)
    q_pos = (q0 + lax.broadcasted_iota(jnp.int32, shape, 1)).astype(F32)
    return q_pos >= thr


def q_blocks():
    return [(q0, max(PREFIX_MAX, q0 + Q_BLOCK)) for q0 in range(0, SLOT, Q_BLOCK)]


def to_order(places, src_ref, columns, dst_ref):
    half = SLOT // len(places)
    for j, start in enumerate(places):
        place = pl.ds(pl.multiple_of(start, half), half)
        dst_ref[j * half : (j + 1) * half, :] = src_ref[place, columns]


def from_order(places, q0, value, dst_ref, columns):
    half = SLOT // len(places)
    for i in range(value.shape[0] // half):
        place = pl.ds(pl.multiple_of(places[q0 // half + i], half), half)
        dst_ref[place, columns] = value[i * half : (i + 1) * half, :]


def attn_forward_head(places, thr_ref, lse_ref, q_ref, k_ref, v_ref, o_ref, columns):
    c = HD**-0.5 * LOG2E
    for q0, klim in q_blocks():
        raw = dot(k_ref[:klim, :], q_ref[q0 : q0 + Q_BLOCK, :], ((1,), (1,)))
        raw = jnp.where(seen_mask(thr_ref, q0, raw.shape), raw, masked_score)
        top = jnp.max(raw, axis=0, keepdims=True)
        p = jnp.exp2((raw - top) * c)
        total = jnp.sum(p, axis=0, keepdims=True)
        out = dot(v_ref[:klim, :], p.astype(BF), ((0,), (0,))) / total
        from_order(places, q0, out.T.astype(BF), o_ref, columns)
        lse_ref[:, q0 : q0 + Q_BLOCK] = top * c + jnp.log2(total)


def attn_backward_head(
    places, thr_ref, lse_ref, q_ref, k_ref, v_ref, do_ref, dk_sum, dv_sum, d_ref, columns
):
    scale = HD**-0.5
    dk_sum[...] = jnp.zeros_like(dk_sum)
    dv_sum[...] = jnp.zeros_like(dv_sum)
    for q0, klim in q_blocks():
        rows = slice(q0, q0 + Q_BLOCK)
        k, q, do = k_ref[:klim, :], q_ref[rows, :], do_ref[rows, :]
        raw = dot(k, q, ((1,), (1,)))
        p = jnp.exp2(raw * (scale * LOG2E) - lse_ref[:, rows])
        p = jnp.where(seen_mask(thr_ref, q0, raw.shape), p, 0.0)
        dv_sum[:klim, :] += dot(p.astype(BF), do, ((1,), (0,)))
        dp = dot(v_ref[:klim, :], do, ((1,), (1,)))
        delta = jnp.sum(p * dp, axis=0, keepdims=True)
        ds = (p * (dp - delta) * scale).astype(BF)
        dk_sum[:klim, :] += dot(ds, q, ((1,), (0,)))
        dq = dot(k, ds, ((0,), (0,))).T.astype(BF)
        from_order(places, q0, dq, d_ref, columns(0))
    from_order(places, 0, dk_sum[...].astype(BF), d_ref, columns(1))
    from_order(places, 0, dv_sum[...].astype(BF), d_ref, columns(2))


def step_rate(update_sq, weight_sq, n_real):
    update_rms = jnp.sqrt(update_sq / n_real)
    weight_rms = jnp.sqrt(weight_sq / n_real)
    return rate_base * jnp.maximum(eps_two, weight_rms) / jnp.maximum(1.0, update_rms / clip_bound)


def apply_step(weight, grad, row_new, col_new, row_mean, rate):
    row = lax.rsqrt(row_new) * (rate * jnp.sqrt(row_mean))
    return weight.astype(F32) - grad * (row[:, None] * lax.rsqrt(col_new)[None, :])


def pair_kernel(factors, *refs):
    g_ref, u_ref = refs[:2]
    o_ref = refs[-1]
    g, u = g_ref[0].astype(F32), u_ref[0].astype(F32)
    if factors:
        wg_ref, wu_ref, row_ref, cg_ref, cu_ref = refs[2:7]
        row = row_ref[...]
        g = wg_ref[...].astype(F32) - g * (row * cg_ref[0])
        u = wu_ref[...].astype(F32) - u * (row * cu_ref[0])
    o_ref[:, 0, :] = g
    o_ref[:, 1, :] = u


def pair_rows(grads, ff, step=None):
    width = grads.shape[2]
    block = 96
    grid = (-(-ff // block),)
    third = lambda k, last: pl.BlockSpec((1, block, last), lambda i: (k, i, 0))
    args, specs = [grads, grads], [third(1, width), third(2, width)]
    if step is not None:
        w_gu, row, scales = step
        shift = w_gu.shape[0] // 2 // block
        args += [w_gu, w_gu, row[None, :], scales, scales]
        specs += [
            pl.BlockSpec((block, width), lambda i: (i, 0)),
            pl.BlockSpec((block, width), lambda i: (i + shift, 0)),
            pl.BlockSpec((1, width), lambda i: (0, 0)),
            third(1, 1),
            third(2, 1),
        ]
    return pl.pallas_call(
        functools.partial(pair_kernel, step is not None),
        grid=grid,
        in_specs=specs,
        out_specs=pl.BlockSpec((block, 2, width), lambda i: (i, 0, 0)),
        out_shape=jax.ShapeDtypeStruct((ff, 2, width), F32),
        compiler_params=pltpu.CompilerParams(vmem_limit_bytes=40 << 20),
        cost_estimate=cost(8),
    )(*args)


def qkv_kernel(g_ref, w_ref, row_ref, col_ref, grad_ref, new_ref):
    grad = g_ref[...].astype(F32)
    grad_ref[0] = grad.T
    new_ref[0] = w_ref[0].astype(F32) - (grad * (row_ref[...] * col_ref[...])).T


def qkv_results(grads, w, row, scales):
    kinds, width, cols = w.shape
    block = 512
    result = pl.BlockSpec((1, block, cols), lambda k, i: (k, i, 0))
    shape = jax.ShapeDtypeStruct(w.shape, F32)
    return pl.pallas_call(
        qkv_kernel,
        grid=(kinds, width // block),
        in_specs=[
            pl.BlockSpec((cols, block), lambda k, i: (k, i)),
            result,
            pl.BlockSpec((1, block), lambda k, i: (0, i)),
            pl.BlockSpec((cols, 1), lambda k, i: (k, 0)),
        ],
        out_specs=[result, result],
        out_shape=[shape, shape],
        compiler_params=pltpu.CompilerParams(vmem_limit_bytes=40 << 20),
        cost_estimate=cost(8),
    )(grads, w, row[None, :], scales)


def tie(x, after):
    return lax.optimization_barrier((x, after))[0]


def exchange_kernel(n_dp, n, x_ref, o_ref, dp_buf, rows, part_buf, total, whole, sems):
    me_d, me = lax.axis_index("dp"), lax.axis_index("tensor")
    width = x_ref.shape[1] // n
    columns = lambda t: pl.ds(pl.multiple_of(t * width, width), width)
    dp_peers = [(k - 1, lax.rem(me_d + k, n_dp)) for k in range(1, n_dp)]
    peers = [(k - 1, lax.rem(me + k, n)) for k in range(1, n)]
    barrier = pltpu.get_barrier_semaphore()
    for _, d in dp_peers:
        pl.semaphore_signal(barrier, inc=1, device_id={"dp": d}, device_id_type=pl.DeviceIdType.MESH)
    for _, t in peers:
        pl.semaphore_signal(barrier, inc=1, device_id={"tensor": t}, device_id_type=pl.DeviceIdType.MESH)
    pl.semaphore_wait(barrier, n_dp + n - 2)

    def push(stage, src, dst, k, device):
        copy = pltpu.make_async_remote_copy(
            src_ref=src, dst_ref=dst, send_sem=sems.at[0, stage, k], recv_sem=sems.at[1, stage, k],
            device_id=device, device_id_type=pl.DeviceIdType.MESH,
        )
        copy.start()
        return copy

    first = [push(0, x_ref.at[pl.ds(0, 8)], dp_buf.at[me_d], k, {"dp": d}) for k, d in dp_peers]
    rows[...] = x_ref[...]
    dp_buf[me_d] = x_ref[0:8, :]
    for copy in first:
        copy.wait()
    rows[0:8, :] = sum(dp_buf[d] for d in range(n_dp))
    second = [push(1, rows.at[:, columns(t)], part_buf.at[me], k, {"tensor": t}) for k, t in peers]
    part_buf[me] = rows[:, columns(me)]
    for copy in second:
        copy.wait()
    total[...] = sum(part_buf[t] for t in range(n))
    third = [push(2, total, whole.at[me], k, {"tensor": t}) for k, t in peers]
    whole[me] = total[...]
    for copy in third:
        copy.wait()
    for t in range(n):
        o_ref[:, t * width : (t + 1) * width] = whole[t]


def exchange(x, n_dp, n):
    height, width = x.shape
    slots = pltpu.VMEM((n, height, width // n), F32)
    return pl.pallas_call(
        functools.partial(exchange_kernel, n_dp, n),
        out_shape=jax.ShapeDtypeStruct(x.shape, F32),
        in_specs=[pl.BlockSpec(memory_space=pltpu.VMEM)],
        out_specs=pl.BlockSpec(memory_space=pltpu.VMEM),
        scratch_shapes=[
            pltpu.VMEM((n_dp, 8, width), F32),
            pltpu.VMEM(x.shape, F32),
            slots,
            pltpu.VMEM((height, width // n), F32),
            slots,
            pltpu.SemaphoreType.DMA((2, 3, max(n, n_dp) - 1)),
        ],
        compiler_params=pltpu.CompilerParams(collective_id=0, has_side_effects=True),
        cost_estimate=cost(16),
    )(x)


def on_device(
    layer_in,
    cotangent,
    lengths,
    prefix,
    pad_mask,
    clusters,
    qkv_w,
    out_w,
    gate_up_w,
    down_w,
    ln_params,
    qkv_row,
    qkv_col,
    out_row,
    out_col,
    gu_row,
    gu_col,
    down_row,
    down_col,
    ln_second,
):
    n_data = lax.axis_size("dp")
    n_tensor = lax.axis_size("tensor")
    tensor_rank = lax.axis_index("tensor")
    data_rank = lax.axis_index("dp")
    rows_dev, width = layer_in.shape
    cols_dev = qkv_w.shape[2]
    heads_dev = cols_dev // HD
    ff_dev = gate_up_w.shape[2]
    ff_pad = -(-ff_dev // 128) * 128
    n_clusters = max(2, n_data // 2)
    seq_length = lengths[0]
    seq_prefix = prefix[0]
    ring = Ring(n_tensor)

    onehot = (clusters[:, None] == jnp.arange(n_clusters, dtype=jnp.int32)[None, :]).astype(F32)
    counts = jnp.sum(onehot, axis=0)
    own_row = jnp.sum(
        jnp.where((jnp.arange(n_data, dtype=jnp.int32) == data_rank)[:, None], onehot, 0.0), axis=0
    )
    seq_weight = jnp.sum(own_row / jnp.maximum(counts, 1.0))
    own_pos = tensor_rank * rows_dev + jnp.arange(rows_dev, dtype=jnp.int32)
    live_rows = ((own_pos < seq_length) & (pad_mask == 1)).astype(F32)
    grad_out = cotangent.astype(F32) * (live_rows * seq_weight)[:, None]
    grad_low = grad_out.astype(BF)

    key_live = (own_pos == 0) | (own_pos < seq_length) & (pad_mask == 1)
    seen_from = jnp.where(key_live, jnp.where(own_pos < seq_prefix, 0, own_pos), 2 * SLOT)
    seen = jnp.broadcast_to(seen_from.astype(F32)[None], (8, rows_dev))

    col_index = tensor_rank * ff_dev + jnp.arange(ff_pad, dtype=jnp.int32)
    ff_real = ((col_index < FF) & (jnp.arange(ff_pad) < ff_dev)).astype(F32)
    ff_mask = ff_real[:ff_dev]

    layer_own = layer_in.astype(F32)
    act_one_all, qkv, seen_all = first_gather(
        n_tensor, layer_in, seen, ln_params, jnp.transpose(qkv_w, (1, 0, 2))
    )
    thr = jnp.broadcast_to(seen_all[:, 0].reshape(SLOT, 1), (SLOT, 128))

    pad = ((0, ff_pad - ff_dev), (0, 0))
    gate_up_t = jnp.transpose(gate_up_w, (1, 2, 0))
    w_gu = jnp.pad(gate_up_t, ((0, 0),) + pad).reshape(2 * ff_pad, width)
    w_down = jnp.pad(down_w, pad)
    qkv_t = jnp.transpose(qkv_w, (1, 0, 2))

    grad_all, context, lse, squares = grad_gather(
        n_tensor, grad_low, qkv, thr, ff_real[:, None], qkv_t, w_gu, out_w, w_down
    )
    weight_squares = jnp.sum(squares, axis=(1, 2))
    hidden_own, norm_two = mix_scatter(n_tensor, context, out_w, layer_in, ln_params)
    part_of = lambda x, s: x[s * rows_dev : (s + 1) * rows_dev]

    act_two, inner, d_gu = [], [], []
    pair = ring.halves(norm_two)
    for s in range(n_tensor):
        pair = ring.step(*pair) if s else pair
        act = jnp.concatenate(pair, axis=0)
        act_two.append(act)
        gate_up = dot(act, w_gu, ((1,), (1,)))
        gate, up = gate_up[:, :ff_pad], gate_up[:, ff_pad:]
        gelu_gate, gelu_back = jax.vjp(jax.nn.gelu, gate)
        inner.append((gelu_gate * up * ff_real).astype(BF))
        d_inner = dot(part_of(grad_all, s), w_down, ((1,), (1,))) * ff_real
        d_gate = gelu_back(d_inner * up)[0]
        d_gu.append(jnp.concatenate([d_gate, d_inner * gelu_gate], axis=1).astype(BF))
    acc = None
    for s in ring.scatter_order():
        received = None if acc is None else ring.send(acc)
        acc = ring.add(received, dot(d_gu[s], w_gu, ((1,), (0,))))
    d_norm_two = jnp.concatenate(acc, axis=0)

    d_hidden_ln, ln_two_part = layer_norm_back(hidden_own, ln_params[2], d_norm_two)
    d_hidden = grad_out + d_hidden_ln
    whole = lambda chunks: jnp.concatenate(chunks, axis=0)
    inner_all = whole(inner)
    n_x = n_data // 2
    d_context, out_part, ff_mine, down_slots = back_gather(
        n_tensor, n_x, ff_dev, d_hidden.astype(BF), out_w, context,
        inner_all, whole(d_gu), grad_all, whole(act_two),
    )

    layer_out, d_qkv, gu_slots, oq_mine = ffn_scatter(
        n_tensor, n_x, inner_all, w_down, hidden_own, thr, qkv, d_context, lse,
        out_part, act_one_all, ff_mine,
    )

    blend = lambda old, total: DECAY * old + (1.0 - DECAY) * total
    ff_rows = ff_mine.shape[1]
    more = ((0, 0), (0, ff_rows - ff_dev))
    oq_old = jnp.concatenate([qkv_col.reshape(-1), out_row])[:, None]
    ff_old = jnp.pad(jnp.concatenate([down_row[None], gu_col]), more, constant_values=1.0)[:, :, None]
    ff_real = jnp.pad(ff_mask, (0, ff_rows - ff_dev))[:, None]
    d_norm_one, goq, gff, oq_new, ff_new, sums = last_scatter(
        n_tensor, n_x, d_qkv, qkv_t, oq_mine, oq_old, jnp.ones_like(oq_old), ff_old, ff_real,
        ff_mine, down_slots, gu_slots,
    )
    d_input_ln, ln_one_part = layer_norm_back(layer_own, ln_params[0], d_norm_one)
    input_grad = (d_hidden + d_input_ln).astype(BF)
    qkv_col_new, out_row_new = oq_new[: 3 * cols_dev, 0], oq_new[3 * cols_dev :, 0]
    down_row_new, gu_col_new = ff_new[0, :ff_dev, 0], ff_new[1:, :ff_dev, 0]
    scalars = jnp.concatenate(
        [weight_squares, jnp.stack([jnp.sum(out_row_new), jnp.sum(down_row_new * ff_mask)])]
    )
    packed = jnp.concatenate(
        [
            ln_one_part,
            ln_two_part,
            jnp.pad(scalars / n_data, (0, width - scalars.shape[0]))[None],
            jnp.zeros((3, width), F32),
            sums,
        ],
        axis=0,
    )
    packed = exchange(packed, n_data, n_tensor)
    ln_tot = packed[:4]
    qkv_wtot, gu_wtot, out_wtot, down_wtot, out_rtot, down_rtot = (packed[4, i] for i in range(6))
    qkv_tot, qkv_usq, gu_tot, gu_usq, out_tot, out_usq, down_tot, down_usq = (
        packed[8 + i] for i in range(8)
    )

    qkv_cols_all = 3 * cols_dev * n_tensor
    out_rows_all = cols_dev * n_tensor
    qkv_row_new = blend(qkv_row, qkv_tot / qkv_cols_all)
    qkv_mean = jnp.sum(qkv_row_new) / width
    gu_row_new = blend(gu_row, gu_tot / (2 * FF))
    gu_mean = jnp.sum(gu_row_new) / width
    out_col_new = blend(out_col, out_tot / out_rows_all)
    out_mean = out_rtot / out_rows_all
    down_col_new = blend(down_col, down_tot / FF)
    down_mean = down_rtot / FF
    qkv_rate = step_rate(jnp.sum(qkv_usq / qkv_row_new) * qkv_mean, qkv_wtot, width * qkv_cols_all)
    gu_rate = step_rate(jnp.sum(gu_usq / gu_row_new) * gu_mean, gu_wtot, width * 2 * FF)
    out_rate = step_rate(jnp.sum(out_usq / out_col_new) * out_mean, out_wtot, out_rows_all * width)
    down_rate = step_rate(jnp.sum(down_usq / down_col_new) * down_mean, down_wtot, FF * width)

    scale_of = lambda new, mean, rate: lax.rsqrt(new) * (rate * jnp.sqrt(mean))
    qkv_grad, qkv_new = qkv_results(
        goq, qkv_t, scale_of(qkv_row_new, qkv_mean, qkv_rate), lax.rsqrt(oq_new)
    )
    out_sum, down_sum = goq[3 * cols_dev :].astype(F32), gff[0, :ff_dev].astype(F32)
    out_new = apply_step(out_w, out_sum, out_row_new, out_col_new, out_mean, out_rate)
    down_new = apply_step(down_w, down_sum, down_row_new, down_col_new, down_mean, down_rate)
    gu_grad = pair_rows(gff, ff_dev)
    gu_new = pair_rows(
        gff, ff_dev, (w_gu, scale_of(gu_row_new, gu_mean, gu_rate), lax.rsqrt(ff_new))
    )
    qkv_back = lambda x: jnp.transpose(x, (1, 0, 2))
    ln_second_new = blend(ln_second, ln_tot * ln_tot + eps_one)
    ln_update = ln_tot * lax.rsqrt(ln_second_new)
    ln_urms = jnp.sqrt(jnp.mean(ln_update * ln_update, axis=1, keepdims=True))
    ln_wrms = jnp.sqrt(jnp.mean(ln_params * ln_params, axis=1, keepdims=True))
    ln_new = ln_params - rate_base * jnp.maximum(eps_two, ln_wrms) * ln_update / jnp.maximum(
        1.0, ln_urms / clip_bound
    )
    return (
        layer_out,
        input_grad,
        qkv_back(qkv_grad),
        qkv_back(qkv_new),
        qkv_row_new,
        qkv_col_new.reshape(3, -1),
        out_sum,
        out_new,
        out_row_new,
        out_col_new,
        jnp.transpose(gu_grad, (2, 1, 0)),
        jnp.transpose(gu_new, (2, 1, 0)),
        gu_row_new,
        gu_col_new,
        down_sum,
        down_new,
        down_row_new,
        down_col_new,
        ln_tot,
        ln_second_new,
        ln_new,
    )


def solution(mesh):
    in_specs = (
        P(("dp", "tensor"), None),
        P(("dp", "tensor"), None),
        P("dp"),
        P("dp"),
        P(("dp", "tensor")),
        P(),
        P(None, None, "tensor"),
        P("tensor", None),
        P(None, None, "tensor"),
        P("tensor", None),
        P(),
        P(),
        P(None, "tensor"),
        P("tensor"),
        P(),
        P(),
        P(None, "tensor"),
        P("tensor"),
        P(),
        P(),
    )
    out_specs = (
        P(("dp", "tensor"), None),
        P(("dp", "tensor"), None),
        P(None, None, "tensor"),
        P(None, None, "tensor"),
        P(),
        P(None, "tensor"),
        P("tensor", None),
        P("tensor", None),
        P("tensor"),
        P(),
        P(None, None, "tensor"),
        P(None, None, "tensor"),
        P(),
        P(None, "tensor"),
        P("tensor", None),
        P("tensor", None),
        P("tensor"),
        P(),
        P(),
        P(),
        P(),
    )
    return jax.shard_map(
        on_device, mesh=mesh, in_specs=in_specs, out_specs=out_specs, check_vma=False
    )
```

```python
import functools

import jax
import jax.numpy as jnp
from jax import lax
from jax.experimental import pallas as pl
from jax.experimental.pallas import tpu as pltpu
from jax.sharding import PartitionSpec as P

HD = 128
FF = 5461
SLOT = 2048
STEP = 10
DECAY = 1.0 - STEP ** (-0.8)
PREFIX_MAX = SLOT // 2
Q_BLOCK = 512

ln_eps = 1e-05
eps_one = 1e-30
eps_two = 0.001
clip_bound = 1.0
rate_base = 1.0
masked_score = -1e30
LOG2E = 1.4426950408889634
BF = jnp.bfloat16
F32 = jnp.float32


def dot(a, b, dims):
    return lax.dot_general(a, b, (dims, ((), ())), preferred_element_type=F32)


def ring_order(n):
    b_size = 2 if n <= 8 else 4
    a_size = n // b_size
    order = []
    for a in range(a_size):
        cols = list(range(1, b_size))
        order += [a * b_size + c for c in (cols[::-1] if a % 2 else cols)]
    for a in range(a_size - 1, -1, -1):
        order.append(a * b_size)
    return order


def cost(micros):
    return pl.CostEstimate(flops=int(micros * 1e9), transcendentals=0, bytes_accessed=4 << 20)


PUSH = pl.DeviceIdType.MESH
PIECES = 2
ROW_BLOCK = 64


def pick(index, table):
    out = jnp.int32(table[0])
    for k in range(1, len(table)):
        out = jnp.where(index == k, jnp.int32(table[k]), out)
    return out


def neighbours(n):
    order = ring_order(n)
    pos = pick(lax.axis_index("tensor"), [order.index(t) for t in range(n)])
    ahead = pick(lax.rem(pos + 1, n), order)
    behind = pick(lax.rem(pos + n - 1, n), order)
    return pos, [{"tensor": ahead}, {"tensor": behind}]


def chunk_places(n, pos, rows):
    places = []
    for t in range(n):
        place = ring_order(n).index(t)
        places.append(lax.rem(pos + (n - place), n) * rows)
        places.append(lax.rem(place - pos + n, n) * rows + rows // 2)
    return places


def other_core():
    me = lax.axis_index("dp")
    return {"dp": me + 1 - 2 * lax.rem(me, 2)}


def other_chips(n_x):
    core, chip = lax.rem(lax.axis_index("dp"), 2), lax.axis_index("dp") // 2
    return chip, [{"dp": 2 * lax.rem(chip + k, n_x) + core} for k in range(1, n_x)]


def greet(devices):
    barrier = pltpu.get_barrier_semaphore()
    for device in devices:
        pl.semaphore_signal(barrier, inc=1, device_id=device, device_id_type=PUSH)
    pl.semaphore_wait(barrier, len(devices))


def ring_copy(land, send_sem, recv_sem, sides, d, s, piece=None):
    src, dst, sem = land.at[d, s], land.at[d, s + 1], d
    if piece is not None:
        size = land.shape[2] // PIECES
        rows = pl.ds(piece * size, size)
        src, dst, sem = land.at[d, s, rows], land.at[d, s + 1, rows], d * PIECES + piece
    return pltpu.make_async_remote_copy(
        src_ref=src,
        dst_ref=dst,
        send_sem=send_sem.at[sem, s],
        recv_sem=recv_sem.at[sem, s],
        device_id=sides[d],
        device_id_type=PUSH,
    )


def ring_sent(n, copy, pieces=(None,)):
    def sent(s, carry):
        for d in range(2):
            for piece in pieces:
                copy(d, s, piece).wait_send()
        return carry

    lax.fori_loop(0, n - 1, sent, 0)


def gather_start(x_ref, land):
    half = x_ref.shape[0] // 2
    land[0, 0] = x_ref[:half, :]
    land[1, 0] = x_ref[half:, :]


def gather_step(n, copy, s):
    for d in range(2):

        @pl.when(s > 0)
        def _():
            copy(d, s - 1).wait_recv()

        @pl.when(s < n - 1)
        def _():
            copy(d, s).start()


def ring_gather(n, x_ref, land, send_sem, recv_sem, sides, work):
    copy = functools.partial(ring_copy, land, send_sem, recv_sem, sides)
    gather_start(x_ref, land)

    def step(s, carry):
        gather_step(n, copy, s)
        work(s)
        return carry

    lax.fori_loop(0, n, step, 0)
    ring_sent(n, copy)


def scatter_start(land):
    for d in range(2):
        land[d, 0] = jnp.zeros(land.shape[2:], land.dtype)


def scatter_step(n, copy, land, term_buf, finish, s):
    half = term_buf.shape[0] // 2
    size = half // PIECES
    for piece in range(PIECES):
        for d in range(2):
            part = slice(piece * size, (piece + 1) * size)
            rows = slice(d * half + piece * size, d * half + (piece + 1) * size)

            @pl.when(s > 0)
            def _():
                copy(d, s - 1, piece).wait_recv()

            total = land[d, s, part].astype(F32) + term_buf[rows, :]

            @pl.when(s < n - 1)
            def _():
                land[d, s, part] = total.astype(BF)
                copy(d, s, piece).start()

            @pl.when(s == n - 1)
            def _():
                finish(rows, total)


def ring_scatter(n, land, send_sem, recv_sem, sides, term_buf, term, work, finish):
    copy = functools.partial(ring_copy, land, send_sem, recv_sem, sides)
    scatter_start(land)

    def step(s, carry):
        term(lax.rem(s + 1, n))
        scatter_step(n, copy, land, term_buf, finish, s)
        work(s)
        return carry

    lax.fori_loop(0, n, step, 0)
    ring_sent(n, copy, range(PIECES))


def dot_columns(out, a, b, dims, block=512):
    width = b.shape[1]

    def columns(j, carry):
        at = pl.ds(pl.multiple_of(j * block, block), block)
        out(at, dot(a, b[:, at], dims))
        return carry

    lax.fori_loop(0, width // block, columns, 0)


def first_kernel(
    n, x_ref, seen_ref, ln_ref, w_ref, act_ref, qkv_ref, seen_all,
    land, act_buf, seen_buf, send_sem, recv_sem, act_sem, seen_sem,
):
    rows, cols = x_ref.shape[0], w_ref.shape[2]
    me = lax.axis_index("tensor")
    peers = [lax.rem(me + k, n) for k in range(1, n)]
    sides = neighbours(n)[1]
    greet([{"tensor": t} for t in peers])

    def seen_copy(k):
        return pltpu.make_async_remote_copy(
            src_ref=seen_ref, dst_ref=seen_buf.at[me], send_sem=seen_sem.at[0, k],
            recv_sem=seen_sem.at[1, k], device_id={"tensor": peers[k]}, device_id_type=PUSH,
        )

    def act_copy(s):
        place = pl.ds(pl.multiple_of(s * rows, rows), rows)
        return pltpu.make_async_copy(act_buf.at[s], act_ref.at[place], act_sem.at[s])

    def work(s):
        @pl.when(s == 0)
        def _():
            for k in range(n - 1):
                seen_copy(k).start()

        chunk = jnp.concatenate([land[0, s], land[1, s]], axis=0).astype(F32)
        act = layer_norm(chunk, ln_ref[0:1, :], ln_ref[1:2, :]).astype(BF)
        act_buf[s] = act
        act_copy(s).start()
        place = pl.ds(pl.multiple_of(s * rows, rows), rows)
        for k in range(3):
            qkv_ref[place, k * cols : (k + 1) * cols] = dot(act, w_ref[k], ((1,), (0,))).astype(BF)

    ring_gather(n, x_ref, land, send_sem, recv_sem, sides, work)
    seen_buf[me] = seen_ref[...]
    for k in range(n - 1):
        seen_copy(k).wait()
    seen_all[...] = seen_buf[...]

    def written(s, carry):
        act_copy(s).wait()
        return carry

    lax.fori_loop(0, n, written, 0)


def ring_scratch(n, rows, width, pieces=1):
    return [pltpu.VMEM((2, n, rows // 2, width), BF)], [
        pltpu.SemaphoreType.DMA((2 * pieces, n - 1)),
        pltpu.SemaphoreType.DMA((2 * pieces, n - 1)),
    ]


VMEM_SPEC = pl.BlockSpec(memory_space=pltpu.VMEM)
ANY_SPEC = pl.BlockSpec(memory_space=pl.ANY)


def first_gather(n, x, seen, ln_params, w):
    rows, width = x.shape
    cols = w.shape[2]
    buf, sems = ring_scratch(n, rows, width)
    return pl.pallas_call(
        functools.partial(first_kernel, n),
        in_specs=[VMEM_SPEC] * 4,
        out_specs=[ANY_SPEC, VMEM_SPEC, VMEM_SPEC],
        out_shape=[
            jax.ShapeDtypeStruct((n * rows, width), BF),
            jax.ShapeDtypeStruct((n * rows, 3 * cols), BF),
            jax.ShapeDtypeStruct((n,) + seen.shape, F32),
        ],
        scratch_shapes=buf
        + [pltpu.VMEM((n, rows, width), BF), pltpu.VMEM((n,) + seen.shape, F32)]
        + sems
        + [pltpu.SemaphoreType.DMA((n,)), pltpu.SemaphoreType.DMA((2, n - 1))],
        compiler_params=pltpu.CompilerParams(
            collective_id=1, has_side_effects=True, vmem_limit_bytes=56 << 20
        ),
        cost_estimate=pl.CostEstimate(
            flops=6 * n * rows * width * cols, transcendentals=0, bytes_accessed=40 << 20
        ),
    )(x, seen, ln_params, w)


def grad_kernel(
    n, heads, x_ref, qkv_ref, thr_ref, real_ref, qkv_w_ref, gu_w_ref, out_w_ref, down_w_ref,
    all_ref, ctx_ref, lse_ref, square_ref,
    land, q_ref, k_ref, v_ref, send_sem, recv_sem, all_sem,
):
    rows = x_ref.shape[0]
    half = rows // 2
    pos, sides = neighbours(n)
    places = chunk_places(n, pos, rows)
    greet(sides)

    def all_copy(d, s):
        place = pl.ds(pl.multiple_of(s * rows + d * half, half), half)
        return pltpu.make_async_copy(land.at[d, s], all_ref.at[place], all_sem.at[d, s])

    def squares(i, ref, real):
        block, cols = ROW_BLOCK, ref.shape[1]

        def add(j, carry):
            at = pl.multiple_of(j * block, block)
            value = ref[pl.ds(at, block), :].astype(F32)
            value = value * value
            if real is not None:
                value = value * real[pl.ds(lax.rem(at, real.shape[0]), block), :]
            square_ref[i, :, :cols] += sum(value[k : k + 8] for k in range(0, block, 8))
            return carry

        lax.fori_loop(0, ref.shape[0] // block, add, 0)

    def work(s):
        for d in range(2):
            all_copy(d, s).start()
        for h in range(heads):

            @pl.when(s == h)
            def _():
                columns = lambda i: slice((i * heads + h) * HD, (i * heads + h + 1) * HD)
                for i, dst in enumerate((q_ref, k_ref, v_ref)):
                    to_order(places, qkv_ref, columns(i), dst)
                attn_forward_head(
                    places, thr_ref, lse_ref.at[h], q_ref, k_ref, v_ref, ctx_ref, columns(0)
                )

        @pl.when(s == heads)
        def _():
            square_ref[...] = jnp.zeros_like(square_ref)
            for k in range(3):
                squares(0, qkv_w_ref.at[k], None)

        @pl.when(s == heads + 1)
        def _():
            squares(1, gu_w_ref, real_ref)

        @pl.when(s == heads + 2)
        def _():
            squares(2, out_w_ref, None)
            squares(3, down_w_ref, real_ref)

    ring_gather(n, x_ref, land, send_sem, recv_sem, sides, work)

    def written(s, carry):
        for d in range(2):
            all_copy(d, s).wait()
        return carry

    lax.fori_loop(0, n, written, 0)


def grad_gather(n, x, qkv, thr, real, qkv_w, gu_w, out_w, down_w):
    rows, width = x.shape
    cols = out_w.shape[0]
    heads = cols // HD
    buf, sems = ring_scratch(n, rows, width)
    return pl.pallas_call(
        functools.partial(grad_kernel, n, heads),
        in_specs=[VMEM_SPEC] * 8,
        out_specs=[ANY_SPEC] + [VMEM_SPEC] * 3,
        out_shape=[
            jax.ShapeDtypeStruct((n * rows, width), BF),
            jax.ShapeDtypeStruct((n * rows, cols), BF),
            jax.ShapeDtypeStruct((heads, 1, SLOT), F32),
            jax.ShapeDtypeStruct((4, 8, width), F32),
        ],
        scratch_shapes=buf
        + [pltpu.VMEM((SLOT, HD), BF)] * 3
        + sems
        + [pltpu.SemaphoreType.DMA((2, n))],
        compiler_params=pltpu.CompilerParams(
            collective_id=5, has_side_effects=True, vmem_limit_bytes=60 << 20
        ),
        cost_estimate=cost(80),
    )(x, qkv, thr, real, qkv_w, gu_w, out_w, down_w)


def mix_kernel(
    n, ctx_ref, w_ref, x_ref, ln_ref, hidden_ref, norm_ref, land, term_buf, send_sem, recv_sem
):
    rows = x_ref.shape[0]
    sides = neighbours(n)[1]
    greet(sides)

    def term(c):
        place = pl.ds(pl.multiple_of(c * rows, rows), rows)

        def put(at, value):
            term_buf[:, at] = value

        dot_columns(put, ctx_ref[place, :], w_ref, ((1,), (0,)))

    def finish(at, total):
        hidden = x_ref[at, :].astype(F32) + total
        hidden_ref[at, :] = hidden
        norm_ref[at, :] = layer_norm(hidden, ln_ref[2:3, :], ln_ref[3:4, :]).astype(BF)

    ring_scatter(n, land, send_sem, recv_sem, sides, term_buf, term, lambda s: None, finish)


def mix_scatter(n, context, w, x, ln_params):
    rows, width = x.shape
    buf, sems = ring_scratch(n, rows, width, PIECES)
    return pl.pallas_call(
        functools.partial(mix_kernel, n),
        in_specs=[VMEM_SPEC] * 4,
        out_specs=[VMEM_SPEC] * 2,
        out_shape=[
            jax.ShapeDtypeStruct((rows, width), F32),
            jax.ShapeDtypeStruct((rows, width), BF),
        ],
        scratch_shapes=buf + [pltpu.VMEM((rows, width), F32)] + sems,
        compiler_params=pltpu.CompilerParams(
            collective_id=6, has_side_effects=True, vmem_limit_bytes=40 << 20
        ),
        cost_estimate=cost(80),
    )(context, w, x, ln_params)


def gelu_pair(gate):
    c, a = (2.0 / jnp.pi) ** 0.5, 0.044715
    square = gate * gate
    t = jnp.tanh(c * gate * (1.0 + a * square))
    value = 0.5 * gate * (1.0 + t)
    slope = 0.5 * (1.0 + t) + 0.5 * gate * (1.0 - t * t) * (c * (1.0 + 3.0 * a * square))
    return value, slope


def both_kernel(
    n, x_ref, gu_w_ref, down_w_ref, real_ref, grad_hbm,
    act_ref, inner_ref, d_gu_ref, out_ref,
    land, sums, term_buf, gate_up, d_inner, grad_buf,
    send_sem, recv_sem, sum_send, sum_recv, act_sem, grad_sem,
):
    rows = x_ref.shape[0]
    half = rows // 2
    ff_pad = down_w_ref.shape[0]
    sides = neighbours(n)[1]
    copy = functools.partial(ring_copy, land, send_sem, recv_sem, sides)
    sum_copy = functools.partial(ring_copy, sums, sum_send, sum_recv, sides)

    def grad_load(s):
        place = pl.ds(pl.multiple_of(s * rows, rows), rows)
        slot = lax.rem(s, 2)
        return pltpu.make_async_copy(grad_hbm.at[place], grad_buf.at[slot], grad_sem.at[slot])

    def act_copy(d, s):
        place = pl.ds(pl.multiple_of(s * rows + d * half, half), half)
        return pltpu.make_async_copy(land.at[d, s], act_ref.at[place], act_sem.at[d, s])

    grad_load(0).start()
    grad_load(1).start()
    greet(sides)
    gather_start(x_ref, land)
    scatter_start(sums)

    def by_rows(out, a, w_ref):
        block = 384

        def some(j, carry):
            at = pl.ds(pl.multiple_of(j * block, block), block)
            out[:, at] = dot(a, w_ref[at, :], ((1,), (1,)))
            return carry

        lax.fori_loop(0, w_ref.shape[0] // block, some, 0)

    def term(c):
        place = pl.ds(pl.multiple_of(c * rows, rows), rows)

        def put(at, value):
            term_buf[:, at] = value

        dot_columns(put, d_gu_ref[place, :], gu_w_ref, ((1,), (0,)))

    def finish(at, total):
        out_ref[at, :] = total

    def step(s, carry):
        gather_step(n, copy, s)
        for d in range(2):
            act_copy(d, s).start()
        by_rows(gate_up, jnp.concatenate([land[0, s], land[1, s]], axis=0), gu_w_ref)
        grad_load(s).wait()
        by_rows(d_inner, grad_buf[lax.rem(s, 2)], down_w_ref)

        @pl.when(s < n - 2)
        def _():
            grad_load(s + 2).start()

        place = pl.ds(pl.multiple_of(s * rows, rows), rows)
        for at in range(0, ff_pad, 128):
            here, there = slice(at, at + 128), slice(ff_pad + at, ff_pad + at + 128)
            real = real_ref[:, here]
            gate, up = gate_up[:, here], gate_up[:, there]
            value, slope = gelu_pair(gate)
            back = d_inner[:, here] * real
            inner_ref[place, here] = (value * up * real).astype(BF)
            d_gu_ref[place, here] = (back * up * slope).astype(BF)
            d_gu_ref[place, there] = (back * value).astype(BF)

        @pl.when(s > 0)
        def _():
            term(s)
            scatter_step(n, sum_copy, sums, term_buf, finish, s - 1)

        return carry

    lax.fori_loop(0, n, step, 0)
    term(0)
    scatter_step(n, sum_copy, sums, term_buf, finish, n - 1)
    ring_sent(n, copy)
    ring_sent(n, sum_copy, range(PIECES))

    def written(s, carry):
        for d in range(2):
            act_copy(d, s).wait()
        return carry

    lax.fori_loop(0, n, written, 0)


def both_ways(n, x, gu_w, down_w, real, grad):
    rows, width = x.shape
    ff_pad = down_w.shape[0]
    buf, sems = ring_scratch(n, rows, width)
    sum_buf, sum_sems = ring_scratch(n, rows, width, PIECES)
    return pl.pallas_call(
        functools.partial(both_kernel, n),
        in_specs=[VMEM_SPEC] * 4 + [ANY_SPEC],
        out_specs=[ANY_SPEC] + [VMEM_SPEC] * 3,
        out_shape=[
            jax.ShapeDtypeStruct((n * rows, width), BF),
            jax.ShapeDtypeStruct((n * rows, ff_pad), BF),
            jax.ShapeDtypeStruct((n * rows, 2 * ff_pad), BF),
            jax.ShapeDtypeStruct((rows, width), F32),
        ],
        scratch_shapes=buf
        + sum_buf
        + [
            pltpu.VMEM((rows, width), F32),
            pltpu.VMEM((rows, 2 * ff_pad), F32),
            pltpu.VMEM((rows, ff_pad), F32),
            pltpu.VMEM((2, rows, width), BF),
        ]
        + sems
        + sum_sems
        + [pltpu.SemaphoreType.DMA((2, n)), pltpu.SemaphoreType.DMA((2,))],
        compiler_params=pltpu.CompilerParams(
            collective_id=7, has_side_effects=True, vmem_limit_bytes=60 << 20
        ),
        cost_estimate=cost(160),
    )(x, gu_w, down_w, real, grad)


def back_kernel(
    n, n_x, x_ref, w_ref, ctx_ref, inner_hbm, d_gu_hbm, grad_hbm, act_hbm,
    d_ctx_ref, out_ref, mine_ref, slots_hbm,
    land, lhs, rhs, part, core_land, out_sum, send_sem, recv_sem, load_sem, core_sem, slot_sem,
):
    rows, ff_pad = x_ref.shape[0], lhs.shape[2]
    ff_rows, half = core_land.shape[1:]
    sides, partner = neighbours(n)[1], other_core()
    core = lax.rem(lax.axis_index("dp"), 2)
    of_core = lambda c: pl.ds(pl.multiple_of(c * half, half), half)
    loads = [
        pltpu.make_async_copy(src, dst, load_sem.at[i])
        for i, (src, dst) in enumerate(
            (
                (inner_hbm, lhs.at[0]),
                (grad_hbm, rhs.at[0]),
                (d_gu_hbm.at[:, pl.ds(0, ff_pad)], lhs.at[1]),
                (act_hbm, rhs.at[1]),
                (d_gu_hbm.at[:, pl.ds(ff_pad, ff_pad)], lhs.at[2]),
            )
        )
    ]
    for load in loads:
        load.start()
    out_sum[...] = jnp.zeros_like(out_sum)
    chip, chips = other_chips(n_x)
    greet(sides + [partner] + chips)

    def slot_copy(k):
        return pltpu.make_async_remote_copy(
            src_ref=mine_ref.at[0], dst_ref=slots_hbm.at[chip], send_sem=slot_sem.at[0, k],
            recv_sem=slot_sem.at[1, k], device_id=chips[k], device_id_type=PUSH,
        )

    def core_copy(i):
        return pltpu.make_async_remote_copy(
            src_ref=part.at[i, :, of_core(1 - core)],
            dst_ref=core_land.at[i],
            send_sem=core_sem.at[0, i],
            recv_sem=core_sem.at[1, i],
            device_id=partner,
            device_id_type=PUSH,
        )

    def work(s):
        chunk = jnp.concatenate([land[0, s], land[1, s]], axis=0)
        place = pl.ds(pl.multiple_of(s * rows, rows), rows)
        d_ctx_ref[place, :] = dot(chunk, w_ref[...], ((1,), (1,))).astype(BF)
        out_sum[...] += dot(ctx_ref[place, :], chunk, ((0,), (0,)))
        for i in range(3):

            @pl.when(s == i + 1)
            def _():
                for load in (loads[:2], loads[2:4], loads[4:])[i]:
                    load.wait()

                def put(at, value):
                    part[i, :, at] = value[:ff_rows].astype(BF)

                dot_columns(put, lhs[i], rhs.at[min(i, 1)], ((0,), (0,)))
                core_copy(i).start()

            @pl.when(s == i + 3)
            def _():
                core_copy(i).wait()
                total = part[i, :, of_core(core)].astype(F32) + core_land[i].astype(F32)
                mine_ref[i] = total.astype(BF)
                if i == 0:
                    for k in range(n_x - 1):
                        slot_copy(k).start()

    ring_gather(n, x_ref, land, send_sem, recv_sem, sides, work)
    out_ref[...] = out_sum[...].astype(BF)
    for k in range(n_x - 1):
        slot_copy(k).wait()


def back_gather(n, n_x, ff_dev, x, w, context, inner, d_gu, grad, act):
    rows, width = x.shape
    ff_pad = inner.shape[1]
    ff_rows = -(-ff_dev // ROW_BLOCK) * ROW_BLOCK
    buf, sems = ring_scratch(n, rows, width)
    return pl.pallas_call(
        functools.partial(back_kernel, n, n_x),
        in_specs=[VMEM_SPEC] * 3 + [ANY_SPEC] * 4,
        out_specs=[VMEM_SPEC] * 3 + [ANY_SPEC],
        out_shape=[
            jax.ShapeDtypeStruct((n * rows, w.shape[0]), BF),
            jax.ShapeDtypeStruct(w.shape, BF),
            jax.ShapeDtypeStruct((3, ff_rows, width // 2), BF),
            jax.ShapeDtypeStruct((n_x, ff_rows, width // 2), BF),
        ],
        scratch_shapes=buf
        + [
            pltpu.VMEM((3, n * rows, ff_pad), BF),
            pltpu.VMEM((2, n * rows, width), BF),
            pltpu.VMEM((3, ff_rows, width), BF),
            pltpu.VMEM((3, ff_rows, width // 2), BF),
            pltpu.VMEM(w.shape, F32),
        ]
        + sems
        + [
            pltpu.SemaphoreType.DMA((5,)),
            pltpu.SemaphoreType.DMA((2, 3)),
            pltpu.SemaphoreType.DMA((2, n_x - 1)),
        ],
        compiler_params=pltpu.CompilerParams(
            collective_id=3, has_side_effects=True, vmem_limit_bytes=60 << 20
        ),
        cost_estimate=cost(80),
    )(x, w, context, inner, d_gu, grad, act)


def ffn_kernel(
    n, n_x, heads, inner_ref, w_ref, hidden_ref, thr_ref, qkv_ref, d_ctx_ref, lse_ref,
    out_part_ref, act_hbm, mine_hbm,
    out_ref, d_qkv_ref, slots_hbm, oq_mine_ref,
    land, term_buf, q_ref, k_ref, v_ref, do_ref, dk_sum, dv_sum,
    act_buf, part, qkv_land, out_land,
    send_sem, recv_sem, act_sem, core_sem, slot_sem,
):
    rows = hidden_ref.shape[0]
    pos, sides = neighbours(n)
    partner = other_core()
    core = lax.rem(lax.axis_index("dp"), 2)
    chip, chips = other_chips(n_x)
    block = act_buf.shape[2]
    blocks = act_hbm.shape[1] // block
    qkv_cols, wide = qkv_land.shape
    wide_of = lambda c: pl.ds(pl.multiple_of(c * wide, wide), wide)

    def act_load(j):
        return pltpu.make_async_copy(
            act_hbm.at[:, pl.ds(j * block, block)], act_buf.at[j % 2], act_sem.at[j]
        )

    def core_copy(i):
        src, dst = (
            (part.at[:, wide_of(1 - core)], qkv_land),
            (out_part_ref.at[:, wide_of(1 - core)], out_land),
        )[i]
        return pltpu.make_async_remote_copy(
            src_ref=src, dst_ref=dst, send_sem=core_sem.at[0, i], recv_sem=core_sem.at[1, i],
            device_id=partner, device_id_type=PUSH,
        )

    def slot_copy(k):
        return pltpu.make_async_remote_copy(
            src_ref=mine_hbm.at[pl.ds(1, 2)], dst_ref=slots_hbm.at[chip], send_sem=slot_sem.at[0, k],
            recv_sem=slot_sem.at[1, k], device_id=chips[k], device_id_type=PUSH,
        )

    for j in range(2):
        act_load(j).start()
    greet(sides + [partner] + chips)
    core_copy(1).start()
    for k in range(n_x - 1):
        slot_copy(k).start()
    places = chunk_places(n, pos, rows)

    def term(c):
        place = pl.ds(pl.multiple_of(c * rows, rows), rows)

        def put(at, value):
            term_buf[:, at] = value

        dot_columns(put, inner_ref[place, :], w_ref, ((1,), (0,)))

    def work(s):
        for h in range(heads):

            @pl.when(s == h + 1)
            def _():
                columns = lambda i: slice((i * heads + h) * HD, (i * heads + h + 1) * HD)
                for i, dst in enumerate((q_ref, k_ref, v_ref)):
                    to_order(places, qkv_ref, columns(i), dst)
                to_order(places, d_ctx_ref, columns(0), do_ref)
                attn_backward_head(
                    places, thr_ref, lse_ref.at[h], q_ref, k_ref, v_ref, do_ref, dk_sum, dv_sum,
                    d_qkv_ref, columns,
                )

        @pl.when(s == 1)
        def _():
            core_copy(1).wait()
            total = out_part_ref[:, wide_of(core)].astype(F32) + out_land[...].astype(F32)
            oq_mine_ref[qkv_cols:, :] = total.astype(BF)

        for turn in range(blocks // 2):

            @pl.when(s == heads + 1 + turn)
            def _():
                for j in (2 * turn, 2 * turn + 1):
                    act_load(j).wait()
                    grad = dot(d_qkv_ref[...], act_buf[j % 2], ((0,), (0,)))
                    part[:, j * block : (j + 1) * block] = grad.astype(BF)
                for j in (2 * turn + 2, 2 * turn + 3):
                    if j < blocks:
                        act_load(j).start()
                if turn == blocks // 2 - 1:
                    core_copy(0).start()

        @pl.when(s == heads + 2 + blocks // 2)
        def _():
            core_copy(0).wait()
            total = part[:, wide_of(core)].astype(F32) + qkv_land[...].astype(F32)
            oq_mine_ref[:qkv_cols, :] = total.astype(BF)

    def finish(at, total):
        out_ref[at, :] = (hidden_ref[at, :] + total).astype(BF)

    ring_scatter(n, land, send_sem, recv_sem, sides, term_buf, term, work, finish)
    for k in range(n_x - 1):
        slot_copy(k).wait()


def ffn_scatter(n, n_x, inner, w, hidden, thr, qkv, d_context, lse, out_part, act, mine):
    rows, width = hidden.shape
    cols, block = d_context.shape[1], 512
    heads = d_context.shape[1] // HD
    buf, sems = ring_scratch(n, rows, width, PIECES)
    return pl.pallas_call(
        functools.partial(ffn_kernel, n, n_x, heads),
        in_specs=[VMEM_SPEC] * 8 + [ANY_SPEC] * 2,
        out_specs=[VMEM_SPEC] * 2 + [ANY_SPEC, VMEM_SPEC],
        out_shape=[
            jax.ShapeDtypeStruct((rows, width), BF),
            jax.ShapeDtypeStruct(qkv.shape, BF),
            jax.ShapeDtypeStruct((n_x, 2) + mine.shape[1:], BF),
            jax.ShapeDtypeStruct((4 * cols, width // 2), BF),
        ],
        scratch_shapes=buf
        + [pltpu.VMEM((rows, width), F32)]
        + [pltpu.VMEM((SLOT, HD), BF)] * 4
        + [pltpu.VMEM((SLOT, HD), F32)] * 2
        + [
            pltpu.VMEM((2, n * rows, block), BF),
            pltpu.VMEM((3 * cols, width), BF),
            pltpu.VMEM((3 * cols, width // 2), BF),
            pltpu.VMEM((cols, width // 2), BF),
        ]
        + sems
        + [
            pltpu.SemaphoreType.DMA((width // block,)),
            pltpu.SemaphoreType.DMA((2, 2)),
            pltpu.SemaphoreType.DMA((2, n_x - 1)),
        ],
        compiler_params=pltpu.CompilerParams(
            collective_id=4, has_side_effects=True, vmem_limit_bytes=62 << 20
        ),
        cost_estimate=cost(95),
    )(inner, w, hidden, thr, qkv, d_context, lse, out_part, act, mine)


def row_sums(grad_ref, old_ref, real_ref, new_ref, c_ref, t_ref):
    width = grad_ref.shape[1]
    block = ROW_BLOCK

    def rows(i, carry):
        at = pl.ds(pl.multiple_of(i * block, block), block)
        grad = grad_ref[at, :].astype(F32)
        square = grad * grad
        real = real_ref[at, :]
        total = (jnp.sum(square, axis=1, keepdims=True) + width * eps_one) * real
        new = DECAY * old_ref[at, :] + (1.0 - DECAY) * (total / width)
        new_ref[at, :] = new
        c = (square + eps_one) * real
        t = square * (real / new)
        c_ref[...] += sum(c[k : k + 8] for k in range(0, block, 8))
        t_ref[...] += sum(t[k : k + 8] for k in range(0, block, 8))
        return carry

    lax.fori_loop(0, grad_ref.shape[0] // block, rows, 0)


def last_kernel(
    n, n_x, d_qkv_ref, w_ref, oq_mine_ref, oq_old, oq_real, ff_old, ff_real, mine_hbm, down_hbm, gu_hbm,
    out_ref, goq_ref, gff_ref, oq_new, ff_new, sums_ref,
    land, term_buf, oq_land, ff_own, ff_slots, c_sum, t_sum,
    send_sem, recv_sem, oq_sem, load_sem, join_sem,
):
    rows = term_buf.shape[0]
    cols, width = w_ref.shape[2], term_buf.shape[1]
    sides, partner = neighbours(n)[1], other_core()
    core = lax.rem(lax.axis_index("dp"), 2)
    chip, chips = other_chips(n_x)
    half = width // 2
    own = pl.ds(pl.multiple_of(core * half, half), half)

    def loads(i):
        slots = down_hbm if i == 0 else gu_hbm.at[:, i - 1]
        return [
            pltpu.make_async_copy(mine_hbm.at[i], ff_own.at[i], load_sem.at[0, i]),
            pltpu.make_async_copy(slots, ff_slots.at[i], load_sem.at[1, i]),
        ]

    def oq_copy(k):
        return pltpu.make_async_remote_copy(
            src_ref=oq_mine_ref, dst_ref=oq_land.at[chip], send_sem=oq_sem.at[0, k],
            recv_sem=oq_sem.at[1, k], device_id=chips[k], device_id_type=PUSH,
        )

    def join(i):
        ref = goq_ref.at[:, own] if i == 3 else gff_ref.at[i, :, own]
        return pltpu.make_async_remote_copy(
            src_ref=ref, dst_ref=ref, send_sem=join_sem.at[0, i], recv_sem=join_sem.at[1, i],
            device_id=partner, device_id_type=PUSH,
        )

    def chip_sum(own_half, slots):
        total = jnp.zeros(own_half.shape, F32)
        for x in range(n_x):
            total = total + jnp.where(chip == x, own_half, slots[x]).astype(F32)
        return total.astype(BF)

    for i in range(3):
        for load in loads(i):
            load.start()
    greet(sides + [partner] + chips)
    for k in range(n_x - 1):
        oq_copy(k).start()

    def term(c):
        place = pl.ds(pl.multiple_of(c * rows, rows), rows)
        block = 512

        def columns(j, carry):
            at = pl.ds(pl.multiple_of(j * block, block), block)
            term_buf[:, at] = sum(
                dot(d_qkv_ref[place, k * cols : (k + 1) * cols], w_ref[k, at, :], ((1,), (1,)))
                for k in range(3)
            )
            return carry

        lax.fori_loop(0, width // block, columns, 0)

    def sums(group, ref, first=True):
        if first:
            c_sum[...] = jnp.zeros_like(c_sum)
            t_sum[...] = jnp.zeros_like(t_sum)
        row_sums(*ref, c_sum, t_sum)
        sums_ref[2 * group : 2 * group + 1, :] = jnp.sum(c_sum[...], axis=0, keepdims=True)
        sums_ref[2 * group + 1 : 2 * group + 2, :] = jnp.sum(t_sum[...], axis=0, keepdims=True)

    ff_refs = lambda i: (gff_ref.at[i], ff_old.at[i], ff_real, ff_new.at[i])
    oq_refs = lambda at: tuple(ref.at[at] for ref in (goq_ref, oq_old, oq_real, oq_new))

    def work(s):
        for i in range(3):

            @pl.when(s == i)
            def _():
                for load in loads(i):
                    load.wait()
                gff_ref[i, :, own] = chip_sum(ff_own[i], ff_slots.at[i])
                join(i).start()

        @pl.when(s == 4)
        def _():
            for k in range(n_x - 1):
                oq_copy(k).wait()
            goq_ref[:, own] = chip_sum(oq_mine_ref[...], oq_land)
            join(3).start()

        @pl.when(s == 3)
        def _():
            join(0).wait()
            sums(3, ff_refs(0))

        @pl.when(s == 5)
        def _():
            join(1).wait()
            sums(1, ff_refs(1))

        @pl.when(s == 6)
        def _():
            join(2).wait()
            sums(1, ff_refs(2), first=False)

    def finish(at, total):
        out_ref[at, :] = total

    ring_scatter(n, land, send_sem, recv_sem, sides, term_buf, term, work, finish)
    join(3).wait()
    sums(0, oq_refs(pl.ds(0, 3 * cols)))
    sums(2, oq_refs(pl.ds(3 * cols, cols)))


def last_scatter(n, n_x, d_qkv, w, oq_mine, oq_old, oq_real, ff_old, ff_real, ff_mine, down_slots, gu_slots):
    width, cols = w.shape[1:]
    rows = d_qkv.shape[0] // n
    half = width // 2
    ff_rows = ff_mine.shape[1]
    buf, sems = ring_scratch(n, rows, width, PIECES)
    return pl.pallas_call(
        functools.partial(last_kernel, n, n_x),
        in_specs=[VMEM_SPEC] * 7 + [ANY_SPEC] * 3,
        out_specs=[VMEM_SPEC] * 6,
        out_shape=[
            jax.ShapeDtypeStruct((rows, width), F32),
            jax.ShapeDtypeStruct((4 * cols, width), BF),
            jax.ShapeDtypeStruct((3, ff_rows, width), BF),
            jax.ShapeDtypeStruct(oq_old.shape, F32),
            jax.ShapeDtypeStruct(ff_old.shape, F32),
            jax.ShapeDtypeStruct((8, width), F32),
        ],
        scratch_shapes=buf
        + [
            pltpu.VMEM((rows, width), F32),
            pltpu.VMEM((n_x,) + oq_mine.shape, BF),
            pltpu.VMEM((3, ff_rows, half), BF),
            pltpu.VMEM((3, n_x, ff_rows, half), BF),
            pltpu.VMEM((8, width), F32),
            pltpu.VMEM((8, width), F32),
        ]
        + sems
        + [
            pltpu.SemaphoreType.DMA((2, n_x - 1)),
            pltpu.SemaphoreType.DMA((2, 3)),
            pltpu.SemaphoreType.DMA((2, 4)),
        ],
        compiler_params=pltpu.CompilerParams(
            collective_id=2, has_side_effects=True, vmem_limit_bytes=62 << 20
        ),
        cost_estimate=cost(90),
    )(d_qkv, w, oq_mine, oq_old, oq_real, ff_old, ff_real, ff_mine, down_slots, gu_slots)


def norm_stats(rows):
    mean_row = jnp.mean(rows, axis=-1, keepdims=True)
    centered = rows - mean_row
    variance = jnp.mean(centered * centered, axis=-1, keepdims=True)
    scale = lax.rsqrt(variance + ln_eps)
    return centered * scale, scale


def layer_norm(rows, gain, shift):
    return norm_stats(rows)[0] * gain + shift


def layer_norm_back(rows, gain, e):
    n, scale = norm_stats(rows)
    eg = e * gain
    dv = scale * (
        eg - jnp.mean(eg, axis=-1, keepdims=True) - n * jnp.mean(eg * n, axis=-1, keepdims=True)
    )
    return dv, jnp.stack([jnp.sum(e * n, axis=0), jnp.sum(e, axis=0)])


def seen_mask(thr_ref, q0, shape):
    thr = thr_ref[: shape[0], :]
    thr = jnp.concatenate([thr] * (shape[1] // thr.shape[1]), axis=1)
    q_pos = (q0 + lax.broadcasted_iota(jnp.int32, shape, 1)).astype(F32)
    return q_pos >= thr


def q_blocks():
    return [(q0, max(PREFIX_MAX, q0 + Q_BLOCK)) for q0 in range(0, SLOT, Q_BLOCK)]


def to_order(places, src_ref, columns, dst_ref):
    half = SLOT // len(places)
    for j, start in enumerate(places):
        place = pl.ds(pl.multiple_of(start, half), half)
        dst_ref[j * half : (j + 1) * half, :] = src_ref[place, columns]


def from_order(places, q0, value, dst_ref, columns):
    half = SLOT // len(places)
    for i in range(value.shape[0] // half):
        place = pl.ds(pl.multiple_of(places[q0 // half + i], half), half)
        dst_ref[place, columns] = value[i * half : (i + 1) * half, :]


def attn_forward_head(places, thr_ref, lse_ref, q_ref, k_ref, v_ref, o_ref, columns):
    c = HD**-0.5 * LOG2E
    for q0, klim in q_blocks():
        raw = dot(k_ref[:klim, :], q_ref[q0 : q0 + Q_BLOCK, :], ((1,), (1,)))
        raw = jnp.where(seen_mask(thr_ref, q0, raw.shape), raw, masked_score)
        top = jnp.max(raw, axis=0, keepdims=True)
        p = jnp.exp2((raw - top) * c)
        total = jnp.sum(p, axis=0, keepdims=True)
        out = dot(v_ref[:klim, :], p.astype(BF), ((0,), (0,))) / total
        from_order(places, q0, out.T.astype(BF), o_ref, columns)
        lse_ref[:, q0 : q0 + Q_BLOCK] = top * c + jnp.log2(total)


def attn_backward_head(
    places, thr_ref, lse_ref, q_ref, k_ref, v_ref, do_ref, dk_sum, dv_sum, d_ref, columns
):
    scale = HD**-0.5
    dk_sum[...] = jnp.zeros_like(dk_sum)
    dv_sum[...] = jnp.zeros_like(dv_sum)
    for q0, klim in q_blocks():
        rows = slice(q0, q0 + Q_BLOCK)
        k, q, do = k_ref[:klim, :], q_ref[rows, :], do_ref[rows, :]
        raw = dot(k, q, ((1,), (1,)))
        p = jnp.exp2(raw * (scale * LOG2E) - lse_ref[:, rows])
        p = jnp.where(seen_mask(thr_ref, q0, raw.shape), p, 0.0)
        dv_sum[:klim, :] += dot(p.astype(BF), do, ((1,), (0,)))
        dp = dot(v_ref[:klim, :], do, ((1,), (1,)))
        delta = jnp.sum(p * dp, axis=0, keepdims=True)
        ds = (p * (dp - delta) * scale).astype(BF)
        dk_sum[:klim, :] += dot(ds, q, ((1,), (0,)))
        dq = dot(k, ds, ((0,), (0,))).T.astype(BF)
        from_order(places, q0, dq, d_ref, columns(0))
    from_order(places, 0, dk_sum[...].astype(BF), d_ref, columns(1))
    from_order(places, 0, dv_sum[...].astype(BF), d_ref, columns(2))


def step_rate(update_sq, weight_sq, n_real):
    update_rms = jnp.sqrt(update_sq / n_real)
    weight_rms = jnp.sqrt(weight_sq / n_real)
    return rate_base * jnp.maximum(eps_two, weight_rms) / jnp.maximum(1.0, update_rms / clip_bound)


def apply_step(weight, grad, row_new, col_new, row_mean, rate):
    row = lax.rsqrt(row_new) * (rate * jnp.sqrt(row_mean))
    return weight.astype(F32) - grad * (row[:, None] * lax.rsqrt(col_new)[None, :])


def pair_kernel(factors, *refs):
    g_ref, u_ref = refs[:2]
    o_ref = refs[-1]
    g, u = g_ref[0].astype(F32), u_ref[0].astype(F32)
    if factors:
        wg_ref, wu_ref, row_ref, cg_ref, cu_ref = refs[2:7]
        row = row_ref[...]
        g = wg_ref[...].astype(F32) - g * (row * cg_ref[0])
        u = wu_ref[...].astype(F32) - u * (row * cu_ref[0])
    o_ref[:, 0, :] = g
    o_ref[:, 1, :] = u


def pair_rows(grads, ff, step=None):
    width = grads.shape[2]
    block = 96
    grid = (-(-ff // block),)
    third = lambda k, last: pl.BlockSpec((1, block, last), lambda i: (k, i, 0))
    args, specs = [grads, grads], [third(1, width), third(2, width)]
    if step is not None:
        w_gu, row, scales = step
        shift = w_gu.shape[0] // 2 // block
        args += [w_gu, w_gu, row[None, :], scales, scales]
        specs += [
            pl.BlockSpec((block, width), lambda i: (i, 0)),
            pl.BlockSpec((block, width), lambda i: (i + shift, 0)),
            pl.BlockSpec((1, width), lambda i: (0, 0)),
            third(1, 1),
            third(2, 1),
        ]
    return pl.pallas_call(
        functools.partial(pair_kernel, step is not None),
        grid=grid,
        in_specs=specs,
        out_specs=pl.BlockSpec((block, 2, width), lambda i: (i, 0, 0)),
        out_shape=jax.ShapeDtypeStruct((ff, 2, width), F32),
        compiler_params=pltpu.CompilerParams(vmem_limit_bytes=40 << 20),
        cost_estimate=cost(8),
    )(*args)


def qkv_kernel(g_ref, w_ref, row_ref, col_ref, grad_ref, new_ref):
    grad = g_ref[...].astype(F32)
    grad_ref[0] = grad.T
    new_ref[0] = w_ref[0].astype(F32) - (grad * (row_ref[...] * col_ref[...])).T


def qkv_results(grads, w, row, scales):
    kinds, width, cols = w.shape
    block = 512
    result = pl.BlockSpec((1, block, cols), lambda k, i: (k, i, 0))
    shape = jax.ShapeDtypeStruct(w.shape, F32)
    return pl.pallas_call(
        qkv_kernel,
        grid=(kinds, width // block),
        in_specs=[
            pl.BlockSpec((cols, block), lambda k, i: (k, i)),
            result,
            pl.BlockSpec((1, block), lambda k, i: (0, i)),
            pl.BlockSpec((cols, 1), lambda k, i: (k, 0)),
        ],
        out_specs=[result, result],
        out_shape=[shape, shape],
        compiler_params=pltpu.CompilerParams(vmem_limit_bytes=40 << 20),
        cost_estimate=cost(8),
    )(grads, w, row[None, :], scales)


def exchange_kernel(n_dp, n, x_ref, o_ref, dp_buf, rows, part_buf, total, whole, sems):
    me_d, me = lax.axis_index("dp"), lax.axis_index("tensor")
    width = x_ref.shape[1] // n
    columns = lambda t: pl.ds(pl.multiple_of(t * width, width), width)
    dp_peers = [(k - 1, lax.rem(me_d + k, n_dp)) for k in range(1, n_dp)]
    peers = [(k - 1, lax.rem(me + k, n)) for k in range(1, n)]
    barrier = pltpu.get_barrier_semaphore()
    for _, d in dp_peers:
        pl.semaphore_signal(barrier, inc=1, device_id={"dp": d}, device_id_type=pl.DeviceIdType.MESH)
    for _, t in peers:
        pl.semaphore_signal(barrier, inc=1, device_id={"tensor": t}, device_id_type=pl.DeviceIdType.MESH)
    pl.semaphore_wait(barrier, n_dp + n - 2)

    def push(stage, src, dst, k, device):
        copy = pltpu.make_async_remote_copy(
            src_ref=src, dst_ref=dst, send_sem=sems.at[0, stage, k], recv_sem=sems.at[1, stage, k],
            device_id=device, device_id_type=pl.DeviceIdType.MESH,
        )
        copy.start()
        return copy

    first = [push(0, x_ref.at[pl.ds(0, 8)], dp_buf.at[me_d], k, {"dp": d}) for k, d in dp_peers]
    rows[...] = x_ref[...]
    dp_buf[me_d] = x_ref[0:8, :]
    for copy in first:
        copy.wait()
    rows[0:8, :] = sum(dp_buf[d] for d in range(n_dp))
    second = [push(1, rows.at[:, columns(t)], part_buf.at[me], k, {"tensor": t}) for k, t in peers]
    part_buf[me] = rows[:, columns(me)]
    for copy in second:
        copy.wait()
    total[...] = sum(part_buf[t] for t in range(n))
    third = [push(2, total, whole.at[me], k, {"tensor": t}) for k, t in peers]
    whole[me] = total[...]
    for copy in third:
        copy.wait()
    for t in range(n):
        o_ref[:, t * width : (t + 1) * width] = whole[t]


def exchange(x, n_dp, n):
    height, width = x.shape
    slots = pltpu.VMEM((n, height, width // n), F32)
    return pl.pallas_call(
        functools.partial(exchange_kernel, n_dp, n),
        out_shape=jax.ShapeDtypeStruct(x.shape, F32),
        in_specs=[pl.BlockSpec(memory_space=pltpu.VMEM)],
        out_specs=pl.BlockSpec(memory_space=pltpu.VMEM),
        scratch_shapes=[
            pltpu.VMEM((n_dp, 8, width), F32),
            pltpu.VMEM(x.shape, F32),
            slots,
            pltpu.VMEM((height, width // n), F32),
            slots,
            pltpu.SemaphoreType.DMA((2, 3, max(n, n_dp) - 1)),
        ],
        compiler_params=pltpu.CompilerParams(collective_id=0, has_side_effects=True),
        cost_estimate=cost(16),
    )(x)


def on_device(
    layer_in,
    cotangent,
    lengths,
    prefix,
    pad_mask,
    clusters,
    qkv_w,
    out_w,
    gate_up_w,
    down_w,
    ln_params,
    qkv_row,
    qkv_col,
    out_row,
    out_col,
    gu_row,
    gu_col,
    down_row,
    down_col,
    ln_second,
):
    n_data = lax.axis_size("dp")
    n_tensor = lax.axis_size("tensor")
    tensor_rank = lax.axis_index("tensor")
    data_rank = lax.axis_index("dp")
    rows_dev, width = layer_in.shape
    cols_dev = qkv_w.shape[2]
    heads_dev = cols_dev // HD
    ff_dev = gate_up_w.shape[2]
    ff_pad = -(-ff_dev // 128) * 128
    n_clusters = max(2, n_data // 2)
    seq_length = lengths[0]
    seq_prefix = prefix[0]

    onehot = (clusters[:, None] == jnp.arange(n_clusters, dtype=jnp.int32)[None, :]).astype(F32)
    counts = jnp.sum(onehot, axis=0)
    own_row = jnp.sum(
        jnp.where((jnp.arange(n_data, dtype=jnp.int32) == data_rank)[:, None], onehot, 0.0), axis=0
    )
    seq_weight = jnp.sum(own_row / jnp.maximum(counts, 1.0))
    own_pos = tensor_rank * rows_dev + jnp.arange(rows_dev, dtype=jnp.int32)
    live_rows = ((own_pos < seq_length) & (pad_mask == 1)).astype(F32)
    grad_out = cotangent.astype(F32) * (live_rows * seq_weight)[:, None]
    grad_low = grad_out.astype(BF)

    key_live = (own_pos == 0) | (own_pos < seq_length) & (pad_mask == 1)
    seen_from = jnp.where(key_live, jnp.where(own_pos < seq_prefix, 0, own_pos), 2 * SLOT)
    seen = jnp.broadcast_to(seen_from.astype(F32)[None], (8, rows_dev))

    col_index = tensor_rank * ff_dev + jnp.arange(ff_pad, dtype=jnp.int32)
    ff_real = ((col_index < FF) & (jnp.arange(ff_pad) < ff_dev)).astype(F32)
    ff_mask = ff_real[:ff_dev]

    layer_own = layer_in.astype(F32)
    act_one_all, qkv, seen_all = first_gather(
        n_tensor, layer_in, seen, ln_params, jnp.transpose(qkv_w, (1, 0, 2))
    )
    thr = jnp.broadcast_to(seen_all[:, 0].reshape(SLOT, 1), (SLOT, 128))

    pad = ((0, ff_pad - ff_dev), (0, 0))
    gate_up_t = jnp.transpose(gate_up_w, (1, 2, 0))
    w_gu = jnp.pad(gate_up_t, ((0, 0),) + pad).reshape(2 * ff_pad, width)
    w_down = jnp.pad(down_w, pad)
    qkv_t = jnp.transpose(qkv_w, (1, 0, 2))

    grad_all, context, lse, squares = grad_gather(
        n_tensor, grad_low, qkv, thr, ff_real[:, None], qkv_t, w_gu, out_w, w_down
    )
    weight_squares = jnp.sum(squares, axis=(1, 2))
    hidden_own, norm_two = mix_scatter(n_tensor, context, out_w, layer_in, ln_params)

    act_two_all, inner_all, d_gu_all, d_norm_two = both_ways(
        n_tensor, norm_two, w_gu, w_down, ff_real[None, :], grad_all
    )
    d_hidden_ln, ln_two_part = layer_norm_back(hidden_own, ln_params[2], d_norm_two)
    d_hidden = grad_out + d_hidden_ln
    n_x = n_data // 2
    d_context, out_part, ff_mine, down_slots = back_gather(
        n_tensor, n_x, ff_dev, d_hidden.astype(BF), out_w, context,
        inner_all, d_gu_all, grad_all, act_two_all,
    )

    layer_out, d_qkv, gu_slots, oq_mine = ffn_scatter(
        n_tensor, n_x, inner_all, w_down, hidden_own, thr, qkv, d_context, lse,
        out_part, act_one_all, ff_mine,
    )

    blend = lambda old, total: DECAY * old + (1.0 - DECAY) * total
    ff_rows = ff_mine.shape[1]
    more = ((0, 0), (0, ff_rows - ff_dev))
    oq_old = jnp.concatenate([qkv_col.reshape(-1), out_row])[:, None]
    ff_old = jnp.pad(jnp.concatenate([down_row[None], gu_col]), more, constant_values=1.0)[:, :, None]
    ff_real = jnp.pad(ff_mask, (0, ff_rows - ff_dev))[:, None]
    d_norm_one, goq, gff, oq_new, ff_new, sums = last_scatter(
        n_tensor, n_x, d_qkv, qkv_t, oq_mine, oq_old, jnp.ones_like(oq_old), ff_old, ff_real,
        ff_mine, down_slots, gu_slots,
    )
    d_input_ln, ln_one_part = layer_norm_back(layer_own, ln_params[0], d_norm_one)
    input_grad = (d_hidden + d_input_ln).astype(BF)
    qkv_col_new, out_row_new = oq_new[: 3 * cols_dev, 0], oq_new[3 * cols_dev :, 0]
    down_row_new, gu_col_new = ff_new[0, :ff_dev, 0], ff_new[1:, :ff_dev, 0]
    scalars = jnp.concatenate(
        [weight_squares, jnp.stack([jnp.sum(out_row_new), jnp.sum(down_row_new * ff_mask)])]
    )
    packed = jnp.concatenate(
        [
            ln_one_part,
            ln_two_part,
            jnp.pad(scalars / n_data, (0, width - scalars.shape[0]))[None],
            jnp.zeros((3, width), F32),
            sums,
        ],
        axis=0,
    )
    packed = exchange(packed, n_data, n_tensor)
    ln_tot = packed[:4]
    qkv_wtot, gu_wtot, out_wtot, down_wtot, out_rtot, down_rtot = (packed[4, i] for i in range(6))
    qkv_tot, qkv_usq, gu_tot, gu_usq, out_tot, out_usq, down_tot, down_usq = (
        packed[8 + i] for i in range(8)
    )

    qkv_cols_all = 3 * cols_dev * n_tensor
    out_rows_all = cols_dev * n_tensor
    qkv_row_new = blend(qkv_row, qkv_tot / qkv_cols_all)
    qkv_mean = jnp.sum(qkv_row_new) / width
    gu_row_new = blend(gu_row, gu_tot / (2 * FF))
    gu_mean = jnp.sum(gu_row_new) / width
    out_col_new = blend(out_col, out_tot / out_rows_all)
    out_mean = out_rtot / out_rows_all
    down_col_new = blend(down_col, down_tot / FF)
    down_mean = down_rtot / FF
    qkv_rate = step_rate(jnp.sum(qkv_usq / qkv_row_new) * qkv_mean, qkv_wtot, width * qkv_cols_all)
    gu_rate = step_rate(jnp.sum(gu_usq / gu_row_new) * gu_mean, gu_wtot, width * 2 * FF)
    out_rate = step_rate(jnp.sum(out_usq / out_col_new) * out_mean, out_wtot, out_rows_all * width)
    down_rate = step_rate(jnp.sum(down_usq / down_col_new) * down_mean, down_wtot, FF * width)

    scale_of = lambda new, mean, rate: lax.rsqrt(new) * (rate * jnp.sqrt(mean))
    qkv_grad, qkv_new = qkv_results(
        goq, qkv_t, scale_of(qkv_row_new, qkv_mean, qkv_rate), lax.rsqrt(oq_new)
    )
    out_sum, down_sum = goq[3 * cols_dev :].astype(F32), gff[0, :ff_dev].astype(F32)
    out_new = apply_step(out_w, out_sum, out_row_new, out_col_new, out_mean, out_rate)
    down_new = apply_step(down_w, down_sum, down_row_new, down_col_new, down_mean, down_rate)
    gu_grad = pair_rows(gff, ff_dev)
    gu_new = pair_rows(
        gff, ff_dev, (w_gu, scale_of(gu_row_new, gu_mean, gu_rate), lax.rsqrt(ff_new))
    )
    qkv_back = lambda x: jnp.transpose(x, (1, 0, 2))
    ln_second_new = blend(ln_second, ln_tot * ln_tot + eps_one)
    ln_update = ln_tot * lax.rsqrt(ln_second_new)
    ln_urms = jnp.sqrt(jnp.mean(ln_update * ln_update, axis=1, keepdims=True))
    ln_wrms = jnp.sqrt(jnp.mean(ln_params * ln_params, axis=1, keepdims=True))
    ln_new = ln_params - rate_base * jnp.maximum(eps_two, ln_wrms) * ln_update / jnp.maximum(
        1.0, ln_urms / clip_bound
    )
    return (
        layer_out,
        input_grad,
        qkv_back(qkv_grad),
        qkv_back(qkv_new),
        qkv_row_new,
        qkv_col_new.reshape(3, -1),
        out_sum,
        out_new,
        out_row_new,
        out_col_new,
        jnp.transpose(gu_grad, (2, 1, 0)),
        jnp.transpose(gu_new, (2, 1, 0)),
        gu_row_new,
        gu_col_new,
        down_sum,
        down_new,
        down_row_new,
        down_col_new,
        ln_tot,
        ln_second_new,
        ln_new,
    )


def solution(mesh):
    in_specs = (
        P(("dp", "tensor"), None),
        P(("dp", "tensor"), None),
        P("dp"),
        P("dp"),
        P(("dp", "tensor")),
        P(),
        P(None, None, "tensor"),
        P("tensor", None),
        P(None, None, "tensor"),
        P("tensor", None),
        P(),
        P(),
        P(None, "tensor"),
        P("tensor"),
        P(),
        P(),
        P(None, "tensor"),
        P("tensor"),
        P(),
        P(),
    )
    out_specs = (
        P(("dp", "tensor"), None),
        P(("dp", "tensor"), None),
        P(None, None, "tensor"),
        P(None, None, "tensor"),
        P(),
        P(None, "tensor"),
        P("tensor", None),
        P("tensor", None),
        P("tensor"),
        P(),
        P(None, None, "tensor"),
        P(None, None, "tensor"),
        P(),
        P(None, "tensor"),
        P("tensor", None),
        P("tensor", None),
        P("tensor"),
        P(),
        P(),
        P(),
        P(),
    )
    return jax.shard_map(
        on_device, mesh=mesh, in_specs=in_specs, out_specs=out_specs, check_vma=False
    )
```

```python
import functools

import jax
import jax.numpy as jnp
from jax import lax
from jax.experimental import pallas as pl
from jax.experimental.pallas import tpu as pltpu
from jax.sharding import PartitionSpec as P

HD = 128
FF = 5461
SLOT = 2048
STEP = 10
DECAY = 1.0 - STEP ** (-0.8)
PREFIX_MAX = SLOT // 2
Q_BLOCK = 512

ln_eps = 1e-05
eps_one = 1e-30
eps_two = 0.001
clip_bound = 1.0
rate_base = 1.0
masked_score = -1e30
LOG2E = 1.4426950408889634
BF = jnp.bfloat16
F32 = jnp.float32


def dot(a, b, dims):
    return lax.dot_general(a, b, (dims, ((), ())), preferred_element_type=F32)


def ring_order(n):
    b_size = 2 if n <= 8 else 4
    a_size = n // b_size
    order = []
    for a in range(a_size):
        cols = list(range(1, b_size))
        order += [a * b_size + c for c in (cols[::-1] if a % 2 else cols)]
    for a in range(a_size - 1, -1, -1):
        order.append(a * b_size)
    return order


def cost(micros):
    return pl.CostEstimate(flops=int(micros * 1e9), transcendentals=0, bytes_accessed=4 << 20)


PUSH = pl.DeviceIdType.MESH
PIECES = 2
ROW_BLOCK = 64


def pick(index, table):
    out = jnp.int32(table[0])
    for k in range(1, len(table)):
        out = jnp.where(index == k, jnp.int32(table[k]), out)
    return out


def neighbours(n):
    order = ring_order(n)
    pos = pick(lax.axis_index("tensor"), [order.index(t) for t in range(n)])
    ahead = pick(lax.rem(pos + 1, n), order)
    behind = pick(lax.rem(pos + n - 1, n), order)
    return pos, [{"tensor": ahead}, {"tensor": behind}]


def chunk_places(n, pos, rows):
    places = []
    for t in range(n):
        place = ring_order(n).index(t)
        places.append(lax.rem(pos + (n - place), n) * rows)
        places.append(lax.rem(place - pos + n, n) * rows + rows // 2)
    return places


def other_core():
    me = lax.axis_index("dp")
    return {"dp": me + 1 - 2 * lax.rem(me, 2)}


def other_chips(n_x):
    core, chip = lax.rem(lax.axis_index("dp"), 2), lax.axis_index("dp") // 2
    return chip, [{"dp": 2 * lax.rem(chip + k, n_x) + core} for k in range(1, n_x)]


def greet(devices):
    barrier = pltpu.get_barrier_semaphore()
    for device in devices:
        pl.semaphore_signal(barrier, inc=1, device_id=device, device_id_type=PUSH)
    pl.semaphore_wait(barrier, len(devices))


def ring_copy(land, send_sem, recv_sem, sides, d, s, piece=None):
    src, dst, sem = land.at[d, s], land.at[d, s + 1], d
    if piece is not None:
        size = land.shape[2] // PIECES
        rows = pl.ds(piece * size, size)
        src, dst, sem = land.at[d, s, rows], land.at[d, s + 1, rows], d * PIECES + piece
    return pltpu.make_async_remote_copy(
        src_ref=src,
        dst_ref=dst,
        send_sem=send_sem.at[sem, s],
        recv_sem=recv_sem.at[sem, s],
        device_id=sides[d],
        device_id_type=PUSH,
    )


def ring_sent(n, copy, pieces=(None,)):
    def sent(s, carry):
        for d in range(2):
            for piece in pieces:
                copy(d, s, piece).wait_send()
        return carry

    lax.fori_loop(0, n - 1, sent, 0)


def gather_start(x_ref, land):
    half = x_ref.shape[0] // 2
    land[0, 0] = x_ref[:half, :]
    land[1, 0] = x_ref[half:, :]


def gather_step(n, copy, s):
    for d in range(2):

        @pl.when(s > 0)
        def _():
            copy(d, s - 1).wait_recv()

        @pl.when(s < n - 1)
        def _():
            copy(d, s).start()


def ring_gather(n, x_ref, land, send_sem, recv_sem, sides, work):
    copy = functools.partial(ring_copy, land, send_sem, recv_sem, sides)
    gather_start(x_ref, land)

    def step(s, carry):
        gather_step(n, copy, s)
        work(s)
        return carry

    lax.fori_loop(0, n, step, 0)
    ring_sent(n, copy)


def scatter_start(land):
    for d in range(2):
        land[d, 0] = jnp.zeros(land.shape[2:], land.dtype)


def scatter_step(n, copy, land, term_buf, finish, s):
    half = term_buf.shape[0] // 2
    size = half // PIECES
    for piece in range(PIECES):
        for d in range(2):
            part = slice(piece * size, (piece + 1) * size)
            rows = slice(d * half + piece * size, d * half + (piece + 1) * size)

            @pl.when(s > 0)
            def _():
                copy(d, s - 1, piece).wait_recv()

            total = land[d, s, part].astype(F32) + term_buf[rows, :]

            @pl.when(s < n - 1)
            def _():
                land[d, s, part] = total.astype(BF)
                copy(d, s, piece).start()

            @pl.when(s == n - 1)
            def _():
                finish(rows, total)


def ring_scatter(n, land, send_sem, recv_sem, sides, term_buf, term, work, finish):
    copy = functools.partial(ring_copy, land, send_sem, recv_sem, sides)
    scatter_start(land)

    def step(s, carry):
        term(lax.rem(s + 1, n))
        scatter_step(n, copy, land, term_buf, finish, s)
        work(s)
        return carry

    lax.fori_loop(0, n, step, 0)
    ring_sent(n, copy, range(PIECES))


def dot_columns(out, a, b, dims, block=512):
    width = b.shape[1]

    def columns(j, carry):
        at = pl.ds(pl.multiple_of(j * block, block), block)
        out(at, dot(a, b[:, at], dims))
        return carry

    lax.fori_loop(0, width // block, columns, 0)


def first_kernel(
    n, x_ref, seen_ref, ln_ref, w_ref, act_ref, qkv_ref, seen_all,
    land, act_buf, seen_buf, send_sem, recv_sem, act_sem, seen_sem,
):
    rows, cols = x_ref.shape[0], w_ref.shape[2]
    me = lax.axis_index("tensor")
    peers = [lax.rem(me + k, n) for k in range(1, n)]
    sides = neighbours(n)[1]
    greet([{"tensor": t} for t in peers])

    def seen_copy(k):
        return pltpu.make_async_remote_copy(
            src_ref=seen_ref, dst_ref=seen_buf.at[me], send_sem=seen_sem.at[0, k],
            recv_sem=seen_sem.at[1, k], device_id={"tensor": peers[k]}, device_id_type=PUSH,
        )

    def act_copy(s):
        place = pl.ds(pl.multiple_of(s * rows, rows), rows)
        return pltpu.make_async_copy(act_buf.at[s], act_ref.at[place], act_sem.at[s])

    def work(s):
        @pl.when(s == 0)
        def _():
            for k in range(n - 1):
                seen_copy(k).start()

        chunk = jnp.concatenate([land[0, s], land[1, s]], axis=0).astype(F32)
        act = layer_norm(chunk, ln_ref[0:1, :], ln_ref[1:2, :]).astype(BF)
        act_buf[s] = act
        act_copy(s).start()
        place = pl.ds(pl.multiple_of(s * rows, rows), rows)
        for k in range(3):
            qkv_ref[place, k * cols : (k + 1) * cols] = dot(act, w_ref[k], ((1,), (0,))).astype(BF)

    ring_gather(n, x_ref, land, send_sem, recv_sem, sides, work)
    seen_buf[me] = seen_ref[...]
    for k in range(n - 1):
        seen_copy(k).wait()
    seen_all[...] = seen_buf[...]

    def written(s, carry):
        act_copy(s).wait()
        return carry

    lax.fori_loop(0, n, written, 0)


def ring_scratch(n, rows, width, pieces=1):
    return [pltpu.VMEM((2, n, rows // 2, width), BF)], [
        pltpu.SemaphoreType.DMA((2 * pieces, n - 1)),
        pltpu.SemaphoreType.DMA((2 * pieces, n - 1)),
    ]


VMEM_SPEC = pl.BlockSpec(memory_space=pltpu.VMEM)
ANY_SPEC = pl.BlockSpec(memory_space=pl.ANY)


def first_gather(n, x, seen, ln_params, w):
    rows, width = x.shape
    cols = w.shape[2]
    buf, sems = ring_scratch(n, rows, width)
    return pl.pallas_call(
        functools.partial(first_kernel, n),
        in_specs=[VMEM_SPEC] * 4,
        out_specs=[ANY_SPEC, VMEM_SPEC, VMEM_SPEC],
        out_shape=[
            jax.ShapeDtypeStruct((n * rows, width), BF),
            jax.ShapeDtypeStruct((n * rows, 3 * cols), BF),
            jax.ShapeDtypeStruct((n,) + seen.shape, F32),
        ],
        scratch_shapes=buf
        + [pltpu.VMEM((n, rows, width), BF), pltpu.VMEM((n,) + seen.shape, F32)]
        + sems
        + [pltpu.SemaphoreType.DMA((n,)), pltpu.SemaphoreType.DMA((2, n - 1))],
        compiler_params=pltpu.CompilerParams(
            collective_id=1, has_side_effects=True, vmem_limit_bytes=56 << 20
        ),
        cost_estimate=pl.CostEstimate(
            flops=6 * n * rows * width * cols, transcendentals=0, bytes_accessed=40 << 20
        ),
    )(x, seen, ln_params, w)


def grad_kernel(
    n, heads, x_ref, qkv_ref, thr_ref, real_ref, qkv_w_ref, gu_w_ref, out_w_ref, down_w_ref,
    all_ref, ctx_ref, lse_ref, square_ref,
    land, q_ref, k_ref, v_ref, send_sem, recv_sem, all_sem,
):
    rows = x_ref.shape[0]
    half = rows // 2
    pos, sides = neighbours(n)
    places = chunk_places(n, pos, rows)
    greet(sides)

    def all_copy(d, s):
        place = pl.ds(pl.multiple_of(s * rows + d * half, half), half)
        return pltpu.make_async_copy(land.at[d, s], all_ref.at[place], all_sem.at[d, s])

    def squares(i, ref, real):
        block, cols = ROW_BLOCK, ref.shape[1]

        def add(j, carry):
            at = pl.multiple_of(j * block, block)
            value = ref[pl.ds(at, block), :].astype(F32)
            value = value * value
            if real is not None:
                value = value * real[pl.ds(lax.rem(at, real.shape[0]), block), :]
            square_ref[i, :, :cols] += sum(value[k : k + 8] for k in range(0, block, 8))
            return carry

        lax.fori_loop(0, ref.shape[0] // block, add, 0)

    def work(s):
        for d in range(2):
            all_copy(d, s).start()
        for h in range(heads):

            @pl.when(s == h)
            def _():
                columns = lambda i: slice((i * heads + h) * HD, (i * heads + h + 1) * HD)
                for i, dst in enumerate((q_ref, k_ref, v_ref)):
                    to_order(places, qkv_ref, columns(i), dst)
                attn_forward_head(
                    places, thr_ref, lse_ref.at[h], q_ref, k_ref, v_ref, ctx_ref, columns(0)
                )

        @pl.when(s == heads)
        def _():
            square_ref[...] = jnp.zeros_like(square_ref)
            for k in range(3):
                squares(0, qkv_w_ref.at[k], None)

        @pl.when(s == heads + 1)
        def _():
            squares(1, gu_w_ref, real_ref)

        @pl.when(s == heads + 2)
        def _():
            squares(2, out_w_ref, None)
            squares(3, down_w_ref, real_ref)

    ring_gather(n, x_ref, land, send_sem, recv_sem, sides, work)

    def written(s, carry):
        for d in range(2):
            all_copy(d, s).wait()
        return carry

    lax.fori_loop(0, n, written, 0)


def grad_gather(n, x, qkv, thr, real, qkv_w, gu_w, out_w, down_w):
    rows, width = x.shape
    cols = out_w.shape[0]
    heads = cols // HD
    buf, sems = ring_scratch(n, rows, width)
    return pl.pallas_call(
        functools.partial(grad_kernel, n, heads),
        in_specs=[VMEM_SPEC] * 8,
        out_specs=[ANY_SPEC] + [VMEM_SPEC] * 3,
        out_shape=[
            jax.ShapeDtypeStruct((n * rows, width), BF),
            jax.ShapeDtypeStruct((n * rows, cols), BF),
            jax.ShapeDtypeStruct((heads, 1, SLOT), F32),
            jax.ShapeDtypeStruct((4, 8, width), F32),
        ],
        scratch_shapes=buf
        + [pltpu.VMEM((SLOT, HD), BF)] * 3
        + sems
        + [pltpu.SemaphoreType.DMA((2, n))],
        compiler_params=pltpu.CompilerParams(
            collective_id=5, has_side_effects=True, vmem_limit_bytes=60 << 20
        ),
        cost_estimate=cost(80),
    )(x, qkv, thr, real, qkv_w, gu_w, out_w, down_w)


def mix_kernel(
    n, ctx_ref, w_ref, x_ref, ln_ref, hidden_ref, norm_ref, land, term_buf, send_sem, recv_sem
):
    rows = x_ref.shape[0]
    sides = neighbours(n)[1]
    greet(sides)

    def term(c):
        place = pl.ds(pl.multiple_of(c * rows, rows), rows)

        def put(at, value):
            term_buf[:, at] = value

        dot_columns(put, ctx_ref[place, :], w_ref, ((1,), (0,)))

    def finish(at, total):
        hidden = x_ref[at, :].astype(F32) + total
        hidden_ref[at, :] = hidden
        norm_ref[at, :] = layer_norm(hidden, ln_ref[2:3, :], ln_ref[3:4, :]).astype(BF)

    ring_scatter(n, land, send_sem, recv_sem, sides, term_buf, term, lambda s: None, finish)


def mix_scatter(n, context, w, x, ln_params):
    rows, width = x.shape
    buf, sems = ring_scratch(n, rows, width, PIECES)
    return pl.pallas_call(
        functools.partial(mix_kernel, n),
        in_specs=[VMEM_SPEC] * 4,
        out_specs=[VMEM_SPEC] * 2,
        out_shape=[
            jax.ShapeDtypeStruct((rows, width), F32),
            jax.ShapeDtypeStruct((rows, width), BF),
        ],
        scratch_shapes=buf + [pltpu.VMEM((rows, width), F32)] + sems,
        compiler_params=pltpu.CompilerParams(
            collective_id=6, has_side_effects=True, vmem_limit_bytes=40 << 20
        ),
        cost_estimate=cost(80),
    )(context, w, x, ln_params)


def gelu_pair(gate):
    c, a = (2.0 / jnp.pi) ** 0.5, 0.044715
    square = gate * gate
    t = jnp.tanh(c * gate * (1.0 + a * square))
    value = 0.5 * gate * (1.0 + t)
    slope = 0.5 * (1.0 + t) + 0.5 * gate * (1.0 - t * t) * (c * (1.0 + 3.0 * a * square))
    return value, slope


def both_kernel(
    n, x_ref, gu_w_ref, down_w_ref, real_ref, grad_hbm,
    act_ref, inner_ref, d_gu_ref, out_ref,
    land, sums, term_buf, gate_up, d_inner, grad_buf,
    send_sem, recv_sem, sum_send, sum_recv, act_sem, grad_sem,
):
    rows = x_ref.shape[0]
    half = rows // 2
    ff_pad = down_w_ref.shape[0]
    sides = neighbours(n)[1]
    copy = functools.partial(ring_copy, land, send_sem, recv_sem, sides)
    sum_copy = functools.partial(ring_copy, sums, sum_send, sum_recv, sides)

    def grad_load(s):
        place = pl.ds(pl.multiple_of(s * rows, rows), rows)
        slot = lax.rem(s, 2)
        return pltpu.make_async_copy(grad_hbm.at[place], grad_buf.at[slot], grad_sem.at[slot])

    def act_copy(d, s):
        place = pl.ds(pl.multiple_of(s * rows + d * half, half), half)
        return pltpu.make_async_copy(land.at[d, s], act_ref.at[place], act_sem.at[d, s])

    grad_load(0).start()
    grad_load(1).start()
    greet(sides)
    gather_start(x_ref, land)
    scatter_start(sums)

    def by_rows(out, a, w_ref):
        block = 384

        def some(j, carry):
            at = pl.ds(pl.multiple_of(j * block, block), block)
            out[:, at] = dot(a, w_ref[at, :], ((1,), (1,)))
            return carry

        lax.fori_loop(0, w_ref.shape[0] // block, some, 0)

    def term(c):
        place = pl.ds(pl.multiple_of(c * rows, rows), rows)

        def put(at, value):
            term_buf[:, at] = value

        dot_columns(put, d_gu_ref[place, :], gu_w_ref, ((1,), (0,)))

    def finish(at, total):
        out_ref[at, :] = total

    def step(s, carry):
        gather_step(n, copy, s)
        for d in range(2):
            act_copy(d, s).start()
        by_rows(gate_up, jnp.concatenate([land[0, s], land[1, s]], axis=0), gu_w_ref)
        grad_load(s).wait()
        by_rows(d_inner, grad_buf[lax.rem(s, 2)], down_w_ref)

        @pl.when(s < n - 2)
        def _():
            grad_load(s + 2).start()

        place = pl.ds(pl.multiple_of(s * rows, rows), rows)
        for at in range(0, ff_pad, 128):
            here, there = slice(at, at + 128), slice(ff_pad + at, ff_pad + at + 128)
            real = real_ref[:, here]
            gate, up = gate_up[:, here], gate_up[:, there]
            value, slope = gelu_pair(gate)
            back = d_inner[:, here] * real
            inner_ref[place, here] = (value * up * real).astype(BF)
            d_gu_ref[place, here] = (back * up * slope).astype(BF)
            d_gu_ref[place, there] = (back * value).astype(BF)

        @pl.when(s > 0)
        def _():
            term(s)
            scatter_step(n, sum_copy, sums, term_buf, finish, s - 1)

        return carry

    lax.fori_loop(0, n, step, 0)
    term(0)
    scatter_step(n, sum_copy, sums, term_buf, finish, n - 1)
    ring_sent(n, copy)
    ring_sent(n, sum_copy, range(PIECES))

    def written(s, carry):
        for d in range(2):
            act_copy(d, s).wait()
        return carry

    lax.fori_loop(0, n, written, 0)


def both_ways(n, x, gu_w, down_w, real, grad):
    rows, width = x.shape
    ff_pad = down_w.shape[0]
    buf, sems = ring_scratch(n, rows, width)
    sum_buf, sum_sems = ring_scratch(n, rows, width, PIECES)
    return pl.pallas_call(
        functools.partial(both_kernel, n),
        in_specs=[VMEM_SPEC] * 4 + [ANY_SPEC],
        out_specs=[ANY_SPEC] + [VMEM_SPEC] * 3,
        out_shape=[
            jax.ShapeDtypeStruct((n * rows, width), BF),
            jax.ShapeDtypeStruct((n * rows, ff_pad), BF),
            jax.ShapeDtypeStruct((n * rows, 2 * ff_pad), BF),
            jax.ShapeDtypeStruct((rows, width), F32),
        ],
        scratch_shapes=buf
        + sum_buf
        + [
            pltpu.VMEM((rows, width), F32),
            pltpu.VMEM((rows, 2 * ff_pad), F32),
            pltpu.VMEM((rows, ff_pad), F32),
            pltpu.VMEM((2, rows, width), BF),
        ]
        + sems
        + sum_sems
        + [pltpu.SemaphoreType.DMA((2, n)), pltpu.SemaphoreType.DMA((2,))],
        compiler_params=pltpu.CompilerParams(
            collective_id=7, has_side_effects=True, vmem_limit_bytes=60 << 20
        ),
        cost_estimate=cost(160),
    )(x, gu_w, down_w, real, grad)


def back_kernel(
    n, n_x, x_ref, w_ref, ctx_ref, inner_hbm, d_gu_hbm, grad_hbm, act_hbm,
    d_ctx_ref, out_ref, mine_ref, slots_hbm,
    land, lhs, rhs, part, core_land, out_sum, send_sem, recv_sem, load_sem, core_sem, slot_sem,
):
    rows, ff_pad = x_ref.shape[0], lhs.shape[2]
    ff_rows, half = core_land.shape[1:]
    sides, partner = neighbours(n)[1], other_core()
    core = lax.rem(lax.axis_index("dp"), 2)
    loads = [
        pltpu.make_async_copy(src, dst, load_sem.at[i])
        for i, (src, dst) in enumerate(
            (
                (inner_hbm, lhs.at[0]),
                (grad_hbm, rhs.at[0]),
                (d_gu_hbm.at[:, pl.ds(0, ff_pad)], lhs.at[1]),
                (act_hbm, rhs.at[1]),
                (d_gu_hbm.at[:, pl.ds(ff_pad, ff_pad)], lhs.at[2]),
            )
        )
    ]
    for load in loads:
        load.start()
    out_sum[...] = jnp.zeros_like(out_sum)
    chip, chips = other_chips(n_x)
    greet(sides + [partner] + chips)

    def slot_copy(k):
        return pltpu.make_async_remote_copy(
            src_ref=mine_ref.at[0], dst_ref=slots_hbm.at[chip], send_sem=slot_sem.at[0, k],
            recv_sem=slot_sem.at[1, k], device_id=chips[k], device_id_type=PUSH,
        )

    def core_copy(i):
        return pltpu.make_async_remote_copy(
            src_ref=part.at[i, 1 - core],
            dst_ref=core_land.at[i],
            send_sem=core_sem.at[0, i],
            recv_sem=core_sem.at[1, i],
            device_id=partner,
            device_id_type=PUSH,
        )

    def work(s):
        chunk = jnp.concatenate([land[0, s], land[1, s]], axis=0)
        place = pl.ds(pl.multiple_of(s * rows, rows), rows)
        d_ctx_ref[place, :] = dot(chunk, w_ref[...], ((1,), (1,))).astype(BF)
        out_sum[...] += dot(ctx_ref[place, :], chunk, ((0,), (0,)))
        for i in range(3):
            for turn in range(2):

                @pl.when(s == 2 * i + turn)
                def _():
                    if turn == 0:
                        for load in (loads[:2], loads[2:4], loads[4:])[i]:
                            load.wait()
                    side = slice(turn * half, (turn + 1) * half)

                    def put(at, value):
                        part[i, turn, :, at] = value[:ff_rows].astype(BF)

                    dot_columns(put, lhs[i], rhs.at[min(i, 1), :, side], ((0,), (0,)))
                    if turn == 1:
                        core_copy(i).start()

            @pl.when(s == 2 * i + 3)
            def _():
                core_copy(i).wait()
                total = part[i, core].astype(F32) + core_land[i].astype(F32)
                mine_ref[i] = total.astype(BF)
                if i == 0:
                    for k in range(n_x - 1):
                        slot_copy(k).start()

    ring_gather(n, x_ref, land, send_sem, recv_sem, sides, work)
    out_ref[...] = out_sum[...].astype(BF)
    for k in range(n_x - 1):
        slot_copy(k).wait()


def back_gather(n, n_x, ff_dev, x, w, context, inner, d_gu, grad, act):
    rows, width = x.shape
    ff_pad = inner.shape[1]
    ff_rows = -(-ff_dev // ROW_BLOCK) * ROW_BLOCK
    buf, sems = ring_scratch(n, rows, width)
    return pl.pallas_call(
        functools.partial(back_kernel, n, n_x),
        in_specs=[VMEM_SPEC] * 3 + [ANY_SPEC] * 4,
        out_specs=[VMEM_SPEC] * 3 + [ANY_SPEC],
        out_shape=[
            jax.ShapeDtypeStruct((n * rows, w.shape[0]), BF),
            jax.ShapeDtypeStruct(w.shape, BF),
            jax.ShapeDtypeStruct((3, ff_rows, width // 2), BF),
            jax.ShapeDtypeStruct((n_x, ff_rows, width // 2), BF),
        ],
        scratch_shapes=buf
        + [
            pltpu.VMEM((3, n * rows, ff_pad), BF),
            pltpu.VMEM((2, n * rows, width), BF),
            pltpu.VMEM((3, 2, ff_rows, width // 2), BF),
            pltpu.VMEM((3, ff_rows, width // 2), BF),
            pltpu.VMEM(w.shape, F32),
        ]
        + sems
        + [
            pltpu.SemaphoreType.DMA((5,)),
            pltpu.SemaphoreType.DMA((2, 3)),
            pltpu.SemaphoreType.DMA((2, n_x - 1)),
        ],
        compiler_params=pltpu.CompilerParams(
            collective_id=3, has_side_effects=True, vmem_limit_bytes=60 << 20
        ),
        cost_estimate=cost(80),
    )(x, w, context, inner, d_gu, grad, act)


def ffn_kernel(
    n, n_x, heads, inner_ref, w_ref, hidden_ref, thr_ref, qkv_ref, d_ctx_ref, lse_ref,
    out_part_ref, act_hbm, mine_hbm,
    out_ref, d_qkv_ref, slots_hbm, out_slots_hbm, oq_mine_ref,
    land, term_buf, q_ref, k_ref, v_ref, do_ref, dk_sum, dv_sum,
    act_buf, part, qkv_land, out_land,
    send_sem, recv_sem, act_sem, core_sem, slot_sem,
):
    rows = hidden_ref.shape[0]
    pos, sides = neighbours(n)
    partner = other_core()
    core = lax.rem(lax.axis_index("dp"), 2)
    chip, chips = other_chips(n_x)
    block = act_buf.shape[2]
    blocks = act_hbm.shape[1] // block
    qkv_cols, wide = qkv_land.shape
    wide_of = lambda c: pl.ds(pl.multiple_of(c * wide, wide), wide)

    def act_load(j):
        return pltpu.make_async_copy(
            act_hbm.at[:, pl.ds(j * block, block)], act_buf.at[j % 2], act_sem.at[j]
        )

    def core_copy(i):
        src, dst = (
            (part.at[:, wide_of(1 - core)], qkv_land),
            (out_part_ref.at[:, wide_of(1 - core)], out_land),
        )[i]
        return pltpu.make_async_remote_copy(
            src_ref=src, dst_ref=dst, send_sem=core_sem.at[0, i], recv_sem=core_sem.at[1, i],
            device_id=partner, device_id_type=PUSH,
        )

    def slot_copy(i, k):
        src, dst = (
            (mine_hbm.at[pl.ds(1, 2)], slots_hbm),
            (oq_mine_ref.at[pl.ds(qkv_cols, oq_mine_ref.shape[0] - qkv_cols)], out_slots_hbm),
        )[i]
        return pltpu.make_async_remote_copy(
            src_ref=src, dst_ref=dst.at[chip], send_sem=slot_sem.at[0, i, k],
            recv_sem=slot_sem.at[1, i, k], device_id=chips[k], device_id_type=PUSH,
        )

    for j in range(2):
        act_load(j).start()
    greet(sides + [partner] + chips)
    core_copy(1).start()
    for k in range(n_x - 1):
        slot_copy(0, k).start()
    places = chunk_places(n, pos, rows)

    def term(c):
        place = pl.ds(pl.multiple_of(c * rows, rows), rows)

        def put(at, value):
            term_buf[:, at] = value

        dot_columns(put, inner_ref[place, :], w_ref, ((1,), (0,)))

    def work(s):
        for h in range(heads):

            columns = lambda i: slice((i * heads + h) * HD, (i * heads + h + 1) * HD)
            for turn in range(2):

                @pl.when(s == 2 * h + turn)
                def _():
                    if turn == 0:
                        for i, dst in enumerate((q_ref, k_ref, v_ref)):
                            to_order(places, qkv_ref, columns(i), dst)
                        to_order(places, d_ctx_ref, columns(0), do_ref)
                    attn_backward_head(
                        turn, places, thr_ref, lse_ref.at[h], q_ref, k_ref, v_ref, do_ref,
                        dk_sum, dv_sum, d_qkv_ref, columns,
                    )

        @pl.when(s == 1)
        def _():
            core_copy(1).wait()
            total = out_part_ref[:, wide_of(core)].astype(F32) + out_land[...].astype(F32)
            oq_mine_ref[qkv_cols:, :] = total.astype(BF)
            for k in range(n_x - 1):
                slot_copy(1, k).start()

        for turn in range(blocks // 2):

            @pl.when(s == 2 * heads + turn)
            def _():
                for j in (2 * turn, 2 * turn + 1):
                    act_load(j).wait()
                    grad = dot(d_qkv_ref[...], act_buf[j % 2], ((0,), (0,)))
                    part[:, j * block : (j + 1) * block] = grad.astype(BF)
                for j in (2 * turn + 2, 2 * turn + 3):
                    if j < blocks:
                        act_load(j).start()
                if turn == blocks // 2 - 1:
                    core_copy(0).start()

    def finish(at, total):
        out_ref[at, :] = (hidden_ref[at, :] + total).astype(BF)

    ring_scatter(n, land, send_sem, recv_sem, sides, term_buf, term, work, finish)
    core_copy(0).wait()
    total = part[:, wide_of(core)].astype(F32) + qkv_land[...].astype(F32)
    oq_mine_ref[:qkv_cols, :] = total.astype(BF)
    for k in range(n_x - 1):
        slot_copy(0, k).wait()
        slot_copy(1, k).wait()


def ffn_scatter(n, n_x, inner, w, hidden, thr, qkv, d_context, lse, out_part, act, mine):
    rows, width = hidden.shape
    cols, block = d_context.shape[1], 512
    heads = d_context.shape[1] // HD
    buf, sems = ring_scratch(n, rows, width, PIECES)
    return pl.pallas_call(
        functools.partial(ffn_kernel, n, n_x, heads),
        in_specs=[VMEM_SPEC] * 8 + [ANY_SPEC] * 2,
        out_specs=[VMEM_SPEC] * 2 + [ANY_SPEC] * 2 + [VMEM_SPEC],
        out_shape=[
            jax.ShapeDtypeStruct((rows, width), BF),
            jax.ShapeDtypeStruct(qkv.shape, BF),
            jax.ShapeDtypeStruct((n_x, 2) + mine.shape[1:], BF),
            jax.ShapeDtypeStruct((n_x, cols, width // 2), BF),
            jax.ShapeDtypeStruct((4 * cols, width // 2), BF),
        ],
        scratch_shapes=buf
        + [pltpu.VMEM((rows, width), F32)]
        + [pltpu.VMEM((SLOT, HD), BF)] * 4
        + [pltpu.VMEM((SLOT, HD), F32)] * 2
        + [
            pltpu.VMEM((2, n * rows, block), BF),
            pltpu.VMEM((3 * cols, width), BF),
            pltpu.VMEM((3 * cols, width // 2), BF),
            pltpu.VMEM((cols, width // 2), BF),
        ]
        + sems
        + [
            pltpu.SemaphoreType.DMA((width // block,)),
            pltpu.SemaphoreType.DMA((2, 2)),
            pltpu.SemaphoreType.DMA((2, 2, n_x - 1)),
        ],
        compiler_params=pltpu.CompilerParams(
            collective_id=4, has_side_effects=True, vmem_limit_bytes=62 << 20
        ),
        cost_estimate=cost(95),
    )(inner, w, hidden, thr, qkv, d_context, lse, out_part, act, mine)


def row_sums(grad_ref, old_ref, real_ref, new_ref, c_ref, t_ref):
    width = grad_ref.shape[1]
    block = ROW_BLOCK

    def rows(i, carry):
        at = pl.ds(pl.multiple_of(i * block, block), block)
        grad = grad_ref[at, :].astype(F32)
        square = grad * grad
        real = real_ref[at, :]
        total = (jnp.sum(square, axis=1, keepdims=True) + width * eps_one) * real
        new = DECAY * old_ref[at, :] + (1.0 - DECAY) * (total / width)
        new_ref[at, :] = new
        c = (square + eps_one) * real
        t = square * (real / new)
        c_ref[...] += sum(c[k : k + 8] for k in range(0, block, 8))
        t_ref[...] += sum(t[k : k + 8] for k in range(0, block, 8))
        return carry

    lax.fori_loop(0, grad_ref.shape[0] // block, rows, 0)


def last_kernel(
    n, n_x, d_qkv_ref, w_ref, oq_mine_ref, oq_old, oq_real, ff_old, ff_real,
    mine_hbm, down_hbm, gu_hbm, out_hbm,
    out_ref, goq_hbm, gff_hbm, oq_new, ff_new, sums_ref,
    land, term_buf, goq_ref, gff_ref, qkv_land, out_slots, ff_own, ff_slots, c_sum, t_sum,
    send_sem, recv_sem, oq_sem, load_sem, join_sem, write_sem,
):
    rows = term_buf.shape[0]
    cols, width = w_ref.shape[2], term_buf.shape[1]
    sides, partner = neighbours(n)[1], other_core()
    core = lax.rem(lax.axis_index("dp"), 2)
    chip, chips = other_chips(n_x)
    half = width // 2
    own = pl.ds(pl.multiple_of(core * half, half), half)

    qkv_rows, out_rows = pl.ds(0, 3 * cols), pl.ds(3 * cols, cols)
    writes = [
        pltpu.make_async_copy(goq_ref, goq_hbm, write_sem.at[0]),
        pltpu.make_async_copy(gff_ref, gff_hbm, write_sem.at[1]),
    ]

    def loads(i):
        if i == 3:
            return [pltpu.make_async_copy(out_hbm, out_slots, load_sem.at[0, 3])]
        slots = down_hbm if i == 0 else gu_hbm.at[:, i - 1]
        return [
            pltpu.make_async_copy(mine_hbm.at[i], ff_own.at[i], load_sem.at[0, i]),
            pltpu.make_async_copy(slots, ff_slots.at[i], load_sem.at[1, i]),
        ]

    def oq_copy(k):
        return pltpu.make_async_remote_copy(
            src_ref=oq_mine_ref.at[qkv_rows], dst_ref=qkv_land.at[chip], send_sem=oq_sem.at[0, k],
            recv_sem=oq_sem.at[1, k], device_id=chips[k], device_id_type=PUSH,
        )

    def join(i):
        ref = gff_ref.at[i, :, own] if i < 3 else goq_ref.at[(qkv_rows, out_rows)[i - 3], own]
        return pltpu.make_async_remote_copy(
            src_ref=ref, dst_ref=ref, send_sem=join_sem.at[0, i], recv_sem=join_sem.at[1, i],
            device_id=partner, device_id_type=PUSH,
        )

    def chip_sum(own_half, slots):
        total = jnp.zeros(own_half.shape, F32)
        for x in range(n_x):
            total = total + jnp.where(chip == x, own_half, slots[x]).astype(F32)
        return total.astype(BF)

    for i in range(4):
        for load in loads(i):
            load.start()
    greet(sides + [partner] + chips)
    for k in range(n_x - 1):
        oq_copy(k).start()

    def term(c):
        place = pl.ds(pl.multiple_of(c * rows, rows), rows)
        block = 512

        def columns(j, carry):
            at = pl.ds(pl.multiple_of(j * block, block), block)
            term_buf[:, at] = sum(
                dot(d_qkv_ref[place, k * cols : (k + 1) * cols], w_ref[k, at, :], ((1,), (1,)))
                for k in range(3)
            )
            return carry

        lax.fori_loop(0, width // block, columns, 0)

    def sums(group, ref, first=True):
        if first:
            c_sum[...] = jnp.zeros_like(c_sum)
            t_sum[...] = jnp.zeros_like(t_sum)
        row_sums(*ref, c_sum, t_sum)
        sums_ref[2 * group : 2 * group + 1, :] = jnp.sum(c_sum[...], axis=0, keepdims=True)
        sums_ref[2 * group + 1 : 2 * group + 2, :] = jnp.sum(t_sum[...], axis=0, keepdims=True)

    ff_refs = lambda i: (gff_ref.at[i], ff_old.at[i], ff_real, ff_new.at[i])
    oq_refs = lambda at: tuple(ref.at[at] for ref in (goq_ref, oq_old, oq_real, oq_new))

    def work(s):
        for i in range(3):

            @pl.when(s == i)
            def _():
                for load in loads(i):
                    load.wait()
                gff_ref[i, :, own] = chip_sum(ff_own[i], ff_slots.at[i])
                join(i).start()

        @pl.when(s == 0)
        def _():
            for load in loads(3):
                load.wait()
            goq_ref[out_rows, own] = chip_sum(oq_mine_ref[out_rows, :], out_slots)
            join(4).start()

        @pl.when(s == 3)
        def _():
            join(0).wait()
            sums(3, ff_refs(0))

        @pl.when(s == 4)
        def _():
            for k in range(n_x - 1):
                oq_copy(k).wait()
            goq_ref[qkv_rows, own] = chip_sum(oq_mine_ref[qkv_rows, :], qkv_land)
            join(3).start()

        @pl.when(s == 5)
        def _():
            join(1).wait()
            sums(1, ff_refs(1))

        @pl.when(s == 6)
        def _():
            join(2).wait()
            sums(1, ff_refs(2), first=False)
            writes[1].start()
            join(4).wait()
            sums(2, oq_refs(out_rows))
            join(3).wait()
            sums(0, oq_refs(qkv_rows))
            writes[0].start()

    def finish(at, total):
        out_ref[at, :] = total

    ring_scatter(n, land, send_sem, recv_sem, sides, term_buf, term, work, finish)
    for write in writes:
        write.wait()


def last_scatter(
    n, n_x, d_qkv, w, oq_mine, oq_old, oq_real, ff_old, ff_real, ff_mine, down_slots, gu_slots, out_slots
):
    width, cols = w.shape[1:]
    rows = d_qkv.shape[0] // n
    half = width // 2
    ff_rows = ff_mine.shape[1]
    buf, sems = ring_scratch(n, rows, width, PIECES)
    return pl.pallas_call(
        functools.partial(last_kernel, n, n_x),
        in_specs=[VMEM_SPEC] * 7 + [ANY_SPEC] * 4,
        out_specs=[VMEM_SPEC] + [ANY_SPEC] * 2 + [VMEM_SPEC] * 3,
        out_shape=[
            jax.ShapeDtypeStruct((rows, width), F32),
            jax.ShapeDtypeStruct((4 * cols, width), BF),
            jax.ShapeDtypeStruct((3, ff_rows, width), BF),
            jax.ShapeDtypeStruct(oq_old.shape, F32),
            jax.ShapeDtypeStruct(ff_old.shape, F32),
            jax.ShapeDtypeStruct((8, width), F32),
        ],
        scratch_shapes=buf
        + [
            pltpu.VMEM((rows, width), F32),
            pltpu.VMEM((4 * cols, width), BF),
            pltpu.VMEM((3, ff_rows, width), BF),
            pltpu.VMEM((n_x, 3 * cols, half), BF),
            pltpu.VMEM((n_x, cols, half), BF),
            pltpu.VMEM((3, ff_rows, half), BF),
            pltpu.VMEM((3, n_x, ff_rows, half), BF),
            pltpu.VMEM((8, width), F32),
            pltpu.VMEM((8, width), F32),
        ]
        + sems
        + [
            pltpu.SemaphoreType.DMA((2, n_x - 1)),
            pltpu.SemaphoreType.DMA((2, 4)),
            pltpu.SemaphoreType.DMA((2, 5)),
            pltpu.SemaphoreType.DMA((2,)),
        ],
        compiler_params=pltpu.CompilerParams(
            collective_id=2, has_side_effects=True, vmem_limit_bytes=62 << 20
        ),
        cost_estimate=cost(90),
    )(
        d_qkv, w, oq_mine, oq_old, oq_real, ff_old, ff_real, ff_mine, down_slots, gu_slots, out_slots
    )


def norm_stats(rows):
    mean_row = jnp.mean(rows, axis=-1, keepdims=True)
    centered = rows - mean_row
    variance = jnp.mean(centered * centered, axis=-1, keepdims=True)
    scale = lax.rsqrt(variance + ln_eps)
    return centered * scale, scale


def layer_norm(rows, gain, shift):
    return norm_stats(rows)[0] * gain + shift


def layer_norm_back(rows, gain, e):
    n, scale = norm_stats(rows)
    eg = e * gain
    dv = scale * (
        eg - jnp.mean(eg, axis=-1, keepdims=True) - n * jnp.mean(eg * n, axis=-1, keepdims=True)
    )
    return dv, jnp.stack([jnp.sum(e * n, axis=0), jnp.sum(e, axis=0)])


def seen_mask(thr_ref, q0, shape):
    thr = thr_ref[: shape[0], :]
    thr = jnp.concatenate([thr] * (shape[1] // thr.shape[1]), axis=1)
    q_pos = (q0 + lax.broadcasted_iota(jnp.int32, shape, 1)).astype(F32)
    return q_pos >= thr


def q_blocks():
    return [(q0, max(PREFIX_MAX, q0 + Q_BLOCK)) for q0 in range(0, SLOT, Q_BLOCK)]


def to_order(places, src_ref, columns, dst_ref):
    half = SLOT // len(places)
    for j, start in enumerate(places):
        place = pl.ds(pl.multiple_of(start, half), half)
        dst_ref[j * half : (j + 1) * half, :] = src_ref[place, columns]


def from_order(places, q0, value, dst_ref, columns):
    half = SLOT // len(places)
    for i in range(value.shape[0] // half):
        place = pl.ds(pl.multiple_of(places[q0 // half + i], half), half)
        dst_ref[place, columns] = value[i * half : (i + 1) * half, :]


def attn_forward_head(places, thr_ref, lse_ref, q_ref, k_ref, v_ref, o_ref, columns):
    c = HD**-0.5 * LOG2E
    for q0, klim in q_blocks():
        raw = dot(k_ref[:klim, :], q_ref[q0 : q0 + Q_BLOCK, :], ((1,), (1,)))
        raw = jnp.where(seen_mask(thr_ref, q0, raw.shape), raw, masked_score)
        top = jnp.max(raw, axis=0, keepdims=True)
        p = jnp.exp2((raw - top) * c)
        total = jnp.sum(p, axis=0, keepdims=True)
        out = dot(v_ref[:klim, :], p.astype(BF), ((0,), (0,))) / total
        from_order(places, q0, out.T.astype(BF), o_ref, columns)
        lse_ref[:, q0 : q0 + Q_BLOCK] = top * c + jnp.log2(total)


def attn_backward_head(
    turn, places, thr_ref, lse_ref, q_ref, k_ref, v_ref, do_ref, dk_sum, dv_sum, d_ref, columns
):
    scale = HD**-0.5
    blocks = q_blocks()
    if turn == 0:
        dk_sum[...] = jnp.zeros_like(dk_sum)
        dv_sum[...] = jnp.zeros_like(dv_sum)
    for q0, klim in (blocks[-1:] + blocks[:1], blocks[1:-1])[turn]:
        rows = slice(q0, q0 + Q_BLOCK)
        k, q, do = k_ref[:klim, :], q_ref[rows, :], do_ref[rows, :]
        raw = dot(k, q, ((1,), (1,)))
        p = jnp.exp2(raw * (scale * LOG2E) - lse_ref[:, rows])
        p = jnp.where(seen_mask(thr_ref, q0, raw.shape), p, 0.0)
        dv_sum[:klim, :] += dot(p.astype(BF), do, ((1,), (0,)))
        dp = dot(v_ref[:klim, :], do, ((1,), (1,)))
        delta = jnp.sum(p * dp, axis=0, keepdims=True)
        ds = (p * (dp - delta) * scale).astype(BF)
        dk_sum[:klim, :] += dot(ds, q, ((1,), (0,)))
        dq = dot(k, ds, ((0,), (0,))).T.astype(BF)
        from_order(places, q0, dq, d_ref, columns(0))
    if turn == 1:
        from_order(places, 0, dk_sum[...].astype(BF), d_ref, columns(1))
        from_order(places, 0, dv_sum[...].astype(BF), d_ref, columns(2))


def step_rate(update_sq, weight_sq, n_real):
    update_rms = jnp.sqrt(update_sq / n_real)
    weight_rms = jnp.sqrt(weight_sq / n_real)
    return rate_base * jnp.maximum(eps_two, weight_rms) / jnp.maximum(1.0, update_rms / clip_bound)


def results_kernel(
    counts, factor_ref, goq_qkv, goq_out, gff_down, gff_gate, gff_up,
    w_qkv, w_out, w_down, w_gate, w_up, r_qkv, r_out, r_down, r_gate, r_up,
    qkv_grad, qkv_new, out_grad, out_new, gu_grad, gu_new, down_grad, down_new,
):
    t = pl.program_id(0)
    n_gu, n_qkv, n_down, n_out = counts

    def after(grad, weight, row, factor):
        return weight.astype(F32) - grad * (lax.rsqrt(row) * factor)

    @pl.when(t < n_gu)
    def _():
        factor = factor_ref[1:2, :]
        for i, (g, w, r) in enumerate(((gff_gate, w_gate, r_gate), (gff_up, w_up, r_up))):
            grad = g[0].astype(F32)
            gu_grad[:, i, :] = grad
            gu_new[:, i, :] = after(grad, w[...], r[0], factor)

    start = n_gu
    @pl.when((t >= start) & (t < start + n_qkv))
    def _():
        block = goq_qkv.shape[1]
        at = lax.rem(t - n_gu, factor_ref.shape[1] // block) * block
        factor = factor_ref[0:1, pl.ds(pl.multiple_of(at, block), block)]
        grad = goq_qkv[...].astype(F32)
        qkv_grad[0] = grad.T
        qkv_new[0] = w_qkv[0].astype(F32) - (grad * (lax.rsqrt(r_qkv[...]) * factor)).T

    start = n_gu + n_qkv

    @pl.when((t >= start) & (t < start + n_down))
    def _():
        grad = gff_down[0].astype(F32)
        down_grad[...] = grad
        down_new[...] = after(grad, w_down[...], r_down[0], factor_ref[3:4, :])

    @pl.when(t >= n_gu + n_qkv + n_down)
    def _():
        grad = goq_out[...].astype(F32)
        out_grad[...] = grad
        out_new[...] = after(grad, w_out[...], r_out[...], factor_ref[2:3, :])


def results(ff, factors, goq, gff, w_qkv, w_out, w_down, w_gu, oq_new, ff_new):
    kinds, width, cols = w_qkv.shape
    rows, wide, high = 96, 1024, 128
    counts = (-(-ff // rows), kinds * width // wide, -(-ff // rows), cols // high)
    starts = [sum(counts[:i]) for i in range(4)]
    per_kind = width // wide
    place = lambda part: lambda t: jnp.clip(t - starts[part], 0, counts[part] - 1)
    gu, qkv, down, out = (place(part) for part in range(4))
    shift = w_gu.shape[0] // 2 // rows
    third = lambda k, part, last: pl.BlockSpec((1, rows, last), lambda t: (k, part(t), 0))
    by_kind = lambda t: (qkv(t) // per_kind, lax.rem(qkv(t), per_kind), 0)
    out_at = 3 * cols // high
    qkv_spec = pl.BlockSpec((1, wide, cols), by_kind)
    out_spec = pl.BlockSpec((high, width), lambda t: (out(t), 0))
    gu_spec = pl.BlockSpec((rows, 2, width), lambda t: (gu(t), 0, 0))
    down_spec = pl.BlockSpec((rows, width), lambda t: (down(t), 0))
    shape = lambda *dims: jax.ShapeDtypeStruct(dims, F32)
    return pl.pallas_call(
        functools.partial(results_kernel, counts),
        grid=(sum(counts),),
        in_specs=[
            pl.BlockSpec(factors.shape, lambda t: (0, 0)),
            pl.BlockSpec((cols, wide), lambda t: by_kind(t)[:2]),
            pl.BlockSpec((high, width), lambda t: (out_at + out(t), 0)),
            third(0, down, width),
            third(1, gu, width),
            third(2, gu, width),
            qkv_spec,
            out_spec,
            down_spec,
            pl.BlockSpec((rows, width), lambda t: (gu(t), 0)),
            pl.BlockSpec((rows, width), lambda t: (gu(t) + shift, 0)),
            pl.BlockSpec((cols, 1), lambda t: (by_kind(t)[0], 0)),
            pl.BlockSpec((high, 1), lambda t: (out_at + out(t), 0)),
            third(0, down, 1),
            third(1, gu, 1),
            third(2, gu, 1),
        ],
        out_specs=[qkv_spec, qkv_spec, out_spec, out_spec, gu_spec, gu_spec, down_spec, down_spec],
        out_shape=[shape(kinds, width, cols)] * 2
        + [shape(cols, width)] * 2
        + [shape(ff, 2, width)] * 2
        + [shape(ff, width)] * 2,
        compiler_params=pltpu.CompilerParams(vmem_limit_bytes=56 << 20),
        cost_estimate=cost(28),
    )(
        factors, goq, goq, gff, gff, gff, w_qkv, w_out, w_down, w_gu, w_gu,
        oq_new, oq_new, ff_new, ff_new, ff_new,
    )


def exchange_kernel(n_dp, n, x_ref, o_ref, dp_buf, rows, part_buf, total, whole, sems):
    me_d, me = lax.axis_index("dp"), lax.axis_index("tensor")
    width = x_ref.shape[1] // n
    columns = lambda t: pl.ds(pl.multiple_of(t * width, width), width)
    dp_peers = [(k - 1, lax.rem(me_d + k, n_dp)) for k in range(1, n_dp)]
    peers = [(k - 1, lax.rem(me + k, n)) for k in range(1, n)]
    barrier = pltpu.get_barrier_semaphore()
    for _, d in dp_peers:
        pl.semaphore_signal(barrier, inc=1, device_id={"dp": d}, device_id_type=pl.DeviceIdType.MESH)
    for _, t in peers:
        pl.semaphore_signal(barrier, inc=1, device_id={"tensor": t}, device_id_type=pl.DeviceIdType.MESH)
    pl.semaphore_wait(barrier, n_dp + n - 2)

    def push(stage, src, dst, k, device):
        copy = pltpu.make_async_remote_copy(
            src_ref=src, dst_ref=dst, send_sem=sems.at[0, stage, k], recv_sem=sems.at[1, stage, k],
            device_id=device, device_id_type=pl.DeviceIdType.MESH,
        )
        copy.start()
        return copy

    first = [push(0, x_ref.at[pl.ds(0, 8)], dp_buf.at[me_d], k, {"dp": d}) for k, d in dp_peers]
    rows[...] = x_ref[...]
    dp_buf[me_d] = x_ref[0:8, :]
    for copy in first:
        copy.wait()
    rows[0:8, :] = sum(dp_buf[d] for d in range(n_dp))
    second = [push(1, rows.at[:, columns(t)], part_buf.at[me], k, {"tensor": t}) for k, t in peers]
    part_buf[me] = rows[:, columns(me)]
    for copy in second:
        copy.wait()
    total[...] = sum(part_buf[t] for t in range(n))
    third = [push(2, total, whole.at[me], k, {"tensor": t}) for k, t in peers]
    whole[me] = total[...]
    for copy in third:
        copy.wait()
    for t in range(n):
        o_ref[:, t * width : (t + 1) * width] = whole[t]


def exchange(x, n_dp, n):
    height, width = x.shape
    slots = pltpu.VMEM((n, height, width // n), F32)
    return pl.pallas_call(
        functools.partial(exchange_kernel, n_dp, n),
        out_shape=jax.ShapeDtypeStruct(x.shape, F32),
        in_specs=[pl.BlockSpec(memory_space=pltpu.VMEM)],
        out_specs=pl.BlockSpec(memory_space=pltpu.VMEM),
        scratch_shapes=[
            pltpu.VMEM((n_dp, 8, width), F32),
            pltpu.VMEM(x.shape, F32),
            slots,
            pltpu.VMEM((height, width // n), F32),
            slots,
            pltpu.SemaphoreType.DMA((2, 3, max(n, n_dp) - 1)),
        ],
        compiler_params=pltpu.CompilerParams(collective_id=0, has_side_effects=True),
        cost_estimate=cost(16),
    )(x)


def on_device(
    layer_in,
    cotangent,
    lengths,
    prefix,
    pad_mask,
    clusters,
    qkv_w,
    out_w,
    gate_up_w,
    down_w,
    ln_params,
    qkv_row,
    qkv_col,
    out_row,
    out_col,
    gu_row,
    gu_col,
    down_row,
    down_col,
    ln_second,
):
    n_data = lax.axis_size("dp")
    n_tensor = lax.axis_size("tensor")
    tensor_rank = lax.axis_index("tensor")
    data_rank = lax.axis_index("dp")
    rows_dev, width = layer_in.shape
    cols_dev = qkv_w.shape[2]
    heads_dev = cols_dev // HD
    ff_dev = gate_up_w.shape[2]
    ff_pad = -(-ff_dev // 128) * 128
    n_clusters = max(2, n_data // 2)
    seq_length = lengths[0]
    seq_prefix = prefix[0]

    onehot = (clusters[:, None] == jnp.arange(n_clusters, dtype=jnp.int32)[None, :]).astype(F32)
    counts = jnp.sum(onehot, axis=0)
    own_row = jnp.sum(
        jnp.where((jnp.arange(n_data, dtype=jnp.int32) == data_rank)[:, None], onehot, 0.0), axis=0
    )
    seq_weight = jnp.sum(own_row / jnp.maximum(counts, 1.0))
    own_pos = tensor_rank * rows_dev + jnp.arange(rows_dev, dtype=jnp.int32)
    live_rows = ((own_pos < seq_length) & (pad_mask == 1)).astype(F32)
    grad_out = cotangent.astype(F32) * (live_rows * seq_weight)[:, None]
    grad_low = grad_out.astype(BF)

    key_live = (own_pos == 0) | (own_pos < seq_length) & (pad_mask == 1)
    seen_from = jnp.where(key_live, jnp.where(own_pos < seq_prefix, 0, own_pos), 2 * SLOT)
    seen = jnp.broadcast_to(seen_from.astype(F32)[None], (8, rows_dev))

    col_index = tensor_rank * ff_dev + jnp.arange(ff_pad, dtype=jnp.int32)
    ff_real = ((col_index < FF) & (jnp.arange(ff_pad) < ff_dev)).astype(F32)
    ff_mask = ff_real[:ff_dev]

    layer_own = layer_in.astype(F32)
    act_one_all, qkv, seen_all = first_gather(
        n_tensor, layer_in, seen, ln_params, jnp.transpose(qkv_w, (1, 0, 2))
    )
    thr = jnp.broadcast_to(seen_all[:, 0].reshape(SLOT, 1), (SLOT, 128))

    pad = ((0, ff_pad - ff_dev), (0, 0))
    gate_up_t = jnp.transpose(gate_up_w, (1, 2, 0))
    w_gu = jnp.pad(gate_up_t, ((0, 0),) + pad).reshape(2 * ff_pad, width)
    w_down = jnp.pad(down_w, pad)
    qkv_t = jnp.transpose(qkv_w, (1, 0, 2))

    grad_all, context, lse, squares = grad_gather(
        n_tensor, grad_low, qkv, thr, ff_real[:, None], qkv_t, w_gu, out_w, w_down
    )
    weight_squares = jnp.sum(squares, axis=(1, 2))
    hidden_own, norm_two = mix_scatter(n_tensor, context, out_w, layer_in, ln_params)

    act_two_all, inner_all, d_gu_all, d_norm_two = both_ways(
        n_tensor, norm_two, w_gu, w_down, ff_real[None, :], grad_all
    )
    d_hidden_ln, ln_two_part = layer_norm_back(hidden_own, ln_params[2], d_norm_two)
    d_hidden = grad_out + d_hidden_ln
    n_x = n_data // 2
    d_context, out_part, ff_mine, down_slots = back_gather(
        n_tensor, n_x, ff_dev, d_hidden.astype(BF), out_w, context,
        inner_all, d_gu_all, grad_all, act_two_all,
    )

    layer_out, d_qkv, gu_slots, out_slots, oq_mine = ffn_scatter(
        n_tensor, n_x, inner_all, w_down, hidden_own, thr, qkv, d_context, lse,
        out_part, act_one_all, ff_mine,
    )

    blend = lambda old, total: DECAY * old + (1.0 - DECAY) * total
    ff_rows = ff_mine.shape[1]
    more = ((0, 0), (0, ff_rows - ff_dev))
    oq_old = jnp.concatenate([qkv_col.reshape(-1), out_row])[:, None]
    ff_old = jnp.pad(jnp.concatenate([down_row[None], gu_col]), more, constant_values=1.0)[:, :, None]
    ff_real = jnp.pad(ff_mask, (0, ff_rows - ff_dev))[:, None]
    d_norm_one, goq, gff, oq_new, ff_new, sums = last_scatter(
        n_tensor, n_x, d_qkv, qkv_t, oq_mine, oq_old, jnp.ones_like(oq_old), ff_old, ff_real,
        ff_mine, down_slots, gu_slots, out_slots,
    )
    d_input_ln, ln_one_part = layer_norm_back(layer_own, ln_params[0], d_norm_one)
    input_grad = (d_hidden + d_input_ln).astype(BF)
    qkv_col_new, out_row_new = oq_new[: 3 * cols_dev, 0], oq_new[3 * cols_dev :, 0]
    down_row_new, gu_col_new = ff_new[0, :ff_dev, 0], ff_new[1:, :ff_dev, 0]
    scalars = jnp.concatenate(
        [weight_squares, jnp.stack([jnp.sum(out_row_new), jnp.sum(down_row_new * ff_mask)])]
    )
    packed = jnp.concatenate(
        [
            ln_one_part,
            ln_two_part,
            jnp.pad(scalars / n_data, (0, width - scalars.shape[0]))[None],
            jnp.zeros((3, width), F32),
            sums,
        ],
        axis=0,
    )
    packed = exchange(packed, n_data, n_tensor)
    ln_tot = packed[:4]
    qkv_wtot, gu_wtot, out_wtot, down_wtot, out_rtot, down_rtot = (packed[4, i] for i in range(6))
    qkv_tot, qkv_usq, gu_tot, gu_usq, out_tot, out_usq, down_tot, down_usq = (
        packed[8 + i] for i in range(8)
    )

    qkv_cols_all = 3 * cols_dev * n_tensor
    out_rows_all = cols_dev * n_tensor
    qkv_row_new = blend(qkv_row, qkv_tot / qkv_cols_all)
    qkv_mean = jnp.sum(qkv_row_new) / width
    gu_row_new = blend(gu_row, gu_tot / (2 * FF))
    gu_mean = jnp.sum(gu_row_new) / width
    out_col_new = blend(out_col, out_tot / out_rows_all)
    out_mean = out_rtot / out_rows_all
    down_col_new = blend(down_col, down_tot / FF)
    down_mean = down_rtot / FF
    qkv_rate = step_rate(jnp.sum(qkv_usq / qkv_row_new) * qkv_mean, qkv_wtot, width * qkv_cols_all)
    gu_rate = step_rate(jnp.sum(gu_usq / gu_row_new) * gu_mean, gu_wtot, width * 2 * FF)
    out_rate = step_rate(jnp.sum(out_usq / out_col_new) * out_mean, out_wtot, out_rows_all * width)
    down_rate = step_rate(jnp.sum(down_usq / down_col_new) * down_mean, down_wtot, FF * width)

    scale_of = lambda new, mean, rate: lax.rsqrt(new) * (rate * jnp.sqrt(mean))
    factors = jnp.stack(
        [
            scale_of(qkv_row_new, qkv_mean, qkv_rate),
            scale_of(gu_row_new, gu_mean, gu_rate),
            scale_of(out_col_new, out_mean, out_rate),
            scale_of(down_col_new, down_mean, down_rate),
        ]
    )
    qkv_grad, qkv_new, out_sum, out_new, gu_grad, gu_new, down_sum, down_new = results(
        ff_dev, factors, goq, gff, qkv_t, out_w, w_down, w_gu, oq_new, ff_new
    )
    qkv_back = lambda x: jnp.transpose(x, (1, 0, 2))
    ln_second_new = blend(ln_second, ln_tot * ln_tot + eps_one)
    ln_update = ln_tot * lax.rsqrt(ln_second_new)
    ln_urms = jnp.sqrt(jnp.mean(ln_update * ln_update, axis=1, keepdims=True))
    ln_wrms = jnp.sqrt(jnp.mean(ln_params * ln_params, axis=1, keepdims=True))
    ln_new = ln_params - rate_base * jnp.maximum(eps_two, ln_wrms) * ln_update / jnp.maximum(
        1.0, ln_urms / clip_bound
    )
    return (
        layer_out,
        input_grad,
        qkv_back(qkv_grad),
        qkv_back(qkv_new),
        qkv_row_new,
        qkv_col_new.reshape(3, -1),
        out_sum,
        out_new,
        out_row_new,
        out_col_new,
        jnp.transpose(gu_grad, (2, 1, 0)),
        jnp.transpose(gu_new, (2, 1, 0)),
        gu_row_new,
        gu_col_new,
        down_sum,
        down_new,
        down_row_new,
        down_col_new,
        ln_tot,
        ln_second_new,
        ln_new,
    )


def solution(mesh):
    in_specs = (
        P(("dp", "tensor"), None),
        P(("dp", "tensor"), None),
        P("dp"),
        P("dp"),
        P(("dp", "tensor")),
        P(),
        P(None, None, "tensor"),
        P("tensor", None),
        P(None, None, "tensor"),
        P("tensor", None),
        P(),
        P(),
        P(None, "tensor"),
        P("tensor"),
        P(),
        P(),
        P(None, "tensor"),
        P("tensor"),
        P(),
        P(),
    )
    out_specs = (
        P(("dp", "tensor"), None),
        P(("dp", "tensor"), None),
        P(None, None, "tensor"),
        P(None, None, "tensor"),
        P(),
        P(None, "tensor"),
        P("tensor", None),
        P("tensor", None),
        P("tensor"),
        P(),
        P(None, None, "tensor"),
        P(None, None, "tensor"),
        P(),
        P(None, "tensor"),
        P("tensor", None),
        P("tensor", None),
        P("tensor"),
        P(),
        P(),
        P(),
        P(),
    )
    return jax.shard_map(
        on_device, mesh=mesh, in_specs=in_specs, out_specs=out_specs, check_vma=False
    )
```

```python
import functools

import jax
import jax.numpy as jnp
from jax import lax
from jax.experimental import pallas as pl
from jax.experimental.pallas import tpu as pltpu
from jax.sharding import PartitionSpec as P

HD = 128
FF = 5461
SLOT = 2048
STEP = 10
DECAY = 1.0 - STEP ** (-0.8)
PREFIX_MAX = SLOT // 2
Q_BLOCK = 512

ln_eps = 1e-05
eps_one = 1e-30
eps_two = 0.001
clip_bound = 1.0
rate_base = 1.0
masked_score = -1e30
LOG2E = 1.4426950408889634
BF = jnp.bfloat16
F32 = jnp.float32


def dot(a, b, dims):
    return lax.dot_general(a, b, (dims, ((), ())), preferred_element_type=F32)


def ring_order(n):
    b_size = 2 if n <= 8 else 4
    a_size = n // b_size
    order = []
    for a in range(a_size):
        cols = list(range(1, b_size))
        order += [a * b_size + c for c in (cols[::-1] if a % 2 else cols)]
    for a in range(a_size - 1, -1, -1):
        order.append(a * b_size)
    return order


def cost(micros):
    return pl.CostEstimate(flops=int(micros * 1e9), transcendentals=0, bytes_accessed=4 << 20)


PUSH = pl.DeviceIdType.MESH
PIECES = 2
ROW_BLOCK = 64


def pick(index, table):
    out = jnp.int32(table[0])
    for k in range(1, len(table)):
        out = jnp.where(index == k, jnp.int32(table[k]), out)
    return out


def neighbours(n):
    order = ring_order(n)
    pos = pick(lax.axis_index("tensor"), [order.index(t) for t in range(n)])
    ahead = pick(lax.rem(pos + 1, n), order)
    behind = pick(lax.rem(pos + n - 1, n), order)
    return pos, [{"tensor": ahead}, {"tensor": behind}]


def chunk_places(n, pos, rows):
    places = []
    for t in range(n):
        place = ring_order(n).index(t)
        places.append(lax.rem(pos + (n - place), n) * rows)
        places.append(lax.rem(place - pos + n, n) * rows + rows // 2)
    return places


def other_core():
    me = lax.axis_index("dp")
    return {"dp": me + 1 - 2 * lax.rem(me, 2)}


def other_chips(n_x):
    core, chip = lax.rem(lax.axis_index("dp"), 2), lax.axis_index("dp") // 2
    return chip, [{"dp": 2 * lax.rem(chip + k, n_x) + core} for k in range(1, n_x)]


def greet(devices):
    barrier = pltpu.get_barrier_semaphore()
    for device in devices:
        pl.semaphore_signal(barrier, inc=1, device_id=device, device_id_type=PUSH)
    pl.semaphore_wait(barrier, len(devices))


def ring_copy(land, send_sem, recv_sem, sides, d, s, piece=None):
    src, dst, sem = land.at[d, s], land.at[d, s + 1], d
    if piece is not None:
        size = land.shape[2] // PIECES
        rows = pl.ds(piece * size, size)
        src, dst, sem = land.at[d, s, rows], land.at[d, s + 1, rows], d * PIECES + piece
    return pltpu.make_async_remote_copy(
        src_ref=src,
        dst_ref=dst,
        send_sem=send_sem.at[sem, s],
        recv_sem=recv_sem.at[sem, s],
        device_id=sides[d],
        device_id_type=PUSH,
    )


def ring_sent(n, copy, pieces=(None,)):
    def sent(s, carry):
        for d in range(2):
            for piece in pieces:
                copy(d, s, piece).wait_send()
        return carry

    lax.fori_loop(0, n - 1, sent, 0)


def gather_start(x_ref, land):
    half = x_ref.shape[0] // 2
    land[0, 0] = x_ref[:half, :]
    land[1, 0] = x_ref[half:, :]


def gather_step(n, copy, s):
    for d in range(2):

        @pl.when(s > 0)
        def _():
            copy(d, s - 1).wait_recv()

        @pl.when(s < n - 1)
        def _():
            copy(d, s).start()


def ring_gather(n, x_ref, land, send_sem, recv_sem, sides, work):
    copy = functools.partial(ring_copy, land, send_sem, recv_sem, sides)
    gather_start(x_ref, land)

    def step(s, carry):
        gather_step(n, copy, s)
        work(s)
        return carry

    lax.fori_loop(0, n, step, 0)
    ring_sent(n, copy)


def scatter_start(land):
    for d in range(2):
        land[d, 0] = jnp.zeros(land.shape[2:], land.dtype)


def scatter_step(n, copy, land, term_buf, finish, s):
    half = term_buf.shape[0] // 2
    size = half // PIECES
    for piece in range(PIECES):
        for d in range(2):
            part = slice(piece * size, (piece + 1) * size)
            rows = slice(d * half + piece * size, d * half + (piece + 1) * size)

            @pl.when(s > 0)
            def _():
                copy(d, s - 1, piece).wait_recv()

            total = land[d, s, part].astype(F32) + term_buf[rows, :]

            @pl.when(s < n - 1)
            def _():
                land[d, s, part] = total.astype(BF)
                copy(d, s, piece).start()

            @pl.when(s == n - 1)
            def _():
                finish(rows, total)


def ring_scatter(n, land, send_sem, recv_sem, sides, term_buf, term, work, finish):
    copy = functools.partial(ring_copy, land, send_sem, recv_sem, sides)
    scatter_start(land)

    def step(s, carry):
        term(lax.rem(s + 1, n))
        scatter_step(n, copy, land, term_buf, finish, s)
        work(s)
        return carry

    lax.fori_loop(0, n, step, 0)
    ring_sent(n, copy, range(PIECES))


def dot_columns(out, a, b, dims, block=512):
    width = b.shape[1]

    def columns(j, carry):
        at = pl.ds(pl.multiple_of(j * block, block), block)
        out(at, dot(a, b[:, at], dims))
        return carry

    lax.fori_loop(0, width // block, columns, 0)


def first_kernel(
    n, x_ref, seen_ref, ln_ref, w_ref, act_ref, qkv_ref, seen_all,
    land, act_buf, seen_buf, send_sem, recv_sem, act_sem, seen_sem,
):
    rows, cols = x_ref.shape[0], w_ref.shape[2]
    me = lax.axis_index("tensor")
    peers = [lax.rem(me + k, n) for k in range(1, n)]
    sides = neighbours(n)[1]
    greet([{"tensor": t} for t in peers])

    def seen_copy(k):
        return pltpu.make_async_remote_copy(
            src_ref=seen_ref, dst_ref=seen_buf.at[me], send_sem=seen_sem.at[0, k],
            recv_sem=seen_sem.at[1, k], device_id={"tensor": peers[k]}, device_id_type=PUSH,
        )

    def act_copy(s):
        place = pl.ds(pl.multiple_of(s * rows, rows), rows)
        return pltpu.make_async_copy(act_buf.at[s], act_ref.at[place], act_sem.at[s])

    def work(s):
        @pl.when(s == 0)
        def _():
            for k in range(n - 1):
                seen_copy(k).start()

        chunk = jnp.concatenate([land[0, s], land[1, s]], axis=0).astype(F32)
        act = layer_norm(chunk, ln_ref[0:1, :], ln_ref[1:2, :]).astype(BF)
        act_buf[s] = act
        act_copy(s).start()
        place = pl.ds(pl.multiple_of(s * rows, rows), rows)
        for k in range(3):
            qkv_ref[place, k * cols : (k + 1) * cols] = dot(act, w_ref[k], ((1,), (0,))).astype(BF)

    ring_gather(n, x_ref, land, send_sem, recv_sem, sides, work)
    seen_buf[me] = seen_ref[...]
    for k in range(n - 1):
        seen_copy(k).wait()
    seen_all[...] = seen_buf[...]

    def written(s, carry):
        act_copy(s).wait()
        return carry

    lax.fori_loop(0, n, written, 0)


def ring_scratch(n, rows, width, pieces=1):
    return [pltpu.VMEM((2, n, rows // 2, width), BF)], [
        pltpu.SemaphoreType.DMA((2 * pieces, n - 1)),
        pltpu.SemaphoreType.DMA((2 * pieces, n - 1)),
    ]


VMEM_SPEC = pl.BlockSpec(memory_space=pltpu.VMEM)
ANY_SPEC = pl.BlockSpec(memory_space=pl.ANY)


def first_gather(n, x, seen, ln_params, w):
    rows, width = x.shape
    cols = w.shape[2]
    buf, sems = ring_scratch(n, rows, width)
    return pl.pallas_call(
        functools.partial(first_kernel, n),
        in_specs=[VMEM_SPEC] * 4,
        out_specs=[ANY_SPEC, VMEM_SPEC, VMEM_SPEC],
        out_shape=[
            jax.ShapeDtypeStruct((n * rows, width), BF),
            jax.ShapeDtypeStruct((n * rows, 3 * cols), BF),
            jax.ShapeDtypeStruct((n,) + seen.shape, F32),
        ],
        scratch_shapes=buf
        + [pltpu.VMEM((n, rows, width), BF), pltpu.VMEM((n,) + seen.shape, F32)]
        + sems
        + [pltpu.SemaphoreType.DMA((n,)), pltpu.SemaphoreType.DMA((2, n - 1))],
        compiler_params=pltpu.CompilerParams(
            collective_id=1, has_side_effects=True, vmem_limit_bytes=56 << 20
        ),
        cost_estimate=pl.CostEstimate(
            flops=6 * n * rows * width * cols, transcendentals=0, bytes_accessed=40 << 20
        ),
    )(x, seen, ln_params, w)


def grad_kernel(
    n, heads, x_ref, weight_ref, qkv_ref, thr_ref, real_ref, qkv_w_ref, gu_w_ref, out_w_ref, down_w_ref,
    all_ref, ctx_ref, lse_ref, square_ref,
    land, own_ref, q_ref, k_ref, v_ref, send_sem, recv_sem, all_sem,
):
    rows = x_ref.shape[0]
    half = rows // 2
    pos, sides = neighbours(n)
    places = chunk_places(n, pos, rows)
    own_ref[...] = (x_ref[...].astype(F32) * weight_ref[...]).astype(BF)
    greet(sides)

    def all_copy(d, s):
        place = pl.ds(pl.multiple_of(s * rows + d * half, half), half)
        return pltpu.make_async_copy(land.at[d, s], all_ref.at[place], all_sem.at[d, s])

    def squares(i, ref, real):
        block, cols = ROW_BLOCK, ref.shape[1]

        def add(j, carry):
            at = pl.multiple_of(j * block, block)
            value = ref[pl.ds(at, block), :].astype(F32)
            value = value * value
            if real is not None:
                value = value * real[pl.ds(lax.rem(at, real.shape[0]), block), :]
            square_ref[i, :, :cols] += sum(value[k : k + 8] for k in range(0, block, 8))
            return carry

        lax.fori_loop(0, ref.shape[0] // block, add, 0)

    def work(s):
        for d in range(2):
            all_copy(d, s).start()
        for h in range(heads):

            @pl.when(s == h)
            def _():
                columns = lambda i: slice((i * heads + h) * HD, (i * heads + h + 1) * HD)
                for i, dst in enumerate((q_ref, k_ref, v_ref)):
                    to_order(places, qkv_ref, columns(i), dst)
                attn_forward_head(
                    places, thr_ref, lse_ref.at[h], q_ref, k_ref, v_ref, ctx_ref, columns(0)
                )

        @pl.when(s == heads)
        def _():
            square_ref[...] = jnp.zeros_like(square_ref)
            for k in range(3):
                squares(0, qkv_w_ref.at[k], None)

        @pl.when(s == heads + 1)
        def _():
            squares(1, gu_w_ref, real_ref)

        @pl.when(s == heads + 2)
        def _():
            squares(2, out_w_ref, None)
            squares(3, down_w_ref, real_ref)

    ring_gather(n, own_ref, land, send_sem, recv_sem, sides, work)

    def written(s, carry):
        for d in range(2):
            all_copy(d, s).wait()
        return carry

    lax.fori_loop(0, n, written, 0)


def grad_gather(n, x, weight, qkv, thr, real, qkv_w, gu_w, out_w, down_w):
    rows, width = x.shape
    cols = out_w.shape[0]
    heads = cols // HD
    buf, sems = ring_scratch(n, rows, width)
    return pl.pallas_call(
        functools.partial(grad_kernel, n, heads),
        in_specs=[VMEM_SPEC] * 9,
        out_specs=[ANY_SPEC] + [VMEM_SPEC] * 3,
        out_shape=[
            jax.ShapeDtypeStruct((n * rows, width), BF),
            jax.ShapeDtypeStruct((n * rows, cols), BF),
            jax.ShapeDtypeStruct((heads, 1, SLOT), F32),
            jax.ShapeDtypeStruct((4, 8, width), F32),
        ],
        scratch_shapes=buf
        + [pltpu.VMEM((rows, width), BF)]
        + [pltpu.VMEM((SLOT, HD), BF)] * 3
        + sems
        + [pltpu.SemaphoreType.DMA((2, n))],
        compiler_params=pltpu.CompilerParams(
            collective_id=5, has_side_effects=True, vmem_limit_bytes=60 << 20
        ),
        cost_estimate=cost(80),
    )(x, weight, qkv, thr, real, qkv_w, gu_w, out_w, down_w)


def mix_kernel(
    n, ctx_ref, w_ref, x_ref, ln_ref, hidden_ref, norm_ref, land, term_buf, send_sem, recv_sem
):
    rows = x_ref.shape[0]
    sides = neighbours(n)[1]
    greet(sides)

    def term(c):
        place = pl.ds(pl.multiple_of(c * rows, rows), rows)

        def put(at, value):
            term_buf[:, at] = value

        dot_columns(put, ctx_ref[place, :], w_ref, ((1,), (0,)))

    def finish(at, total):
        hidden = x_ref[at, :].astype(F32) + total
        hidden_ref[at, :] = hidden
        norm_ref[at, :] = layer_norm(hidden, ln_ref[2:3, :], ln_ref[3:4, :]).astype(BF)

    ring_scatter(n, land, send_sem, recv_sem, sides, term_buf, term, lambda s: None, finish)


def mix_scatter(n, context, w, x, ln_params):
    rows, width = x.shape
    buf, sems = ring_scratch(n, rows, width, PIECES)
    return pl.pallas_call(
        functools.partial(mix_kernel, n),
        in_specs=[VMEM_SPEC] * 4,
        out_specs=[VMEM_SPEC] * 2,
        out_shape=[
            jax.ShapeDtypeStruct((rows, width), F32),
            jax.ShapeDtypeStruct((rows, width), BF),
        ],
        scratch_shapes=buf + [pltpu.VMEM((rows, width), F32)] + sems,
        compiler_params=pltpu.CompilerParams(
            collective_id=6, has_side_effects=True, vmem_limit_bytes=40 << 20
        ),
        cost_estimate=cost(80),
    )(context, w, x, ln_params)


def gelu_pair(gate):
    c, a = (2.0 / jnp.pi) ** 0.5, 0.044715
    square = gate * gate
    t = jnp.tanh(c * gate * (1.0 + a * square))
    value = 0.5 * gate * (1.0 + t)
    slope = 0.5 * (1.0 + t) + 0.5 * gate * (1.0 - t * t) * (c * (1.0 + 3.0 * a * square))
    return value, slope


def both_kernel(
    n, x_ref, gu_w_ref, down_w_ref, real_ref, hidden_ref, cot_ref, weight_ref, ln_ref, grad_hbm,
    act_ref, inner_ref, d_gu_ref, out_ref, low_ref, ln_sum,
    land, sums, term_buf, gate_up, d_inner, grad_buf,
    send_sem, recv_sem, sum_send, sum_recv, act_sem, grad_sem,
):
    rows = x_ref.shape[0]
    half = rows // 2
    ff_pad = down_w_ref.shape[0]
    sides = neighbours(n)[1]
    copy = functools.partial(ring_copy, land, send_sem, recv_sem, sides)
    sum_copy = functools.partial(ring_copy, sums, sum_send, sum_recv, sides)

    def grad_load(s):
        place = pl.ds(pl.multiple_of(s * rows, rows), rows)
        slot = lax.rem(s, 2)
        return pltpu.make_async_copy(grad_hbm.at[place], grad_buf.at[slot], grad_sem.at[slot])

    def act_copy(d, s):
        place = pl.ds(pl.multiple_of(s * rows + d * half, half), half)
        return pltpu.make_async_copy(land.at[d, s], act_ref.at[place], act_sem.at[d, s])

    grad_load(0).start()
    grad_load(1).start()
    greet(sides)
    gather_start(x_ref, land)
    ln_sum[...] = jnp.zeros_like(ln_sum)
    scatter_start(sums)

    def by_rows(out, a, w_ref):
        block = 384

        def some(j, carry):
            at = pl.ds(pl.multiple_of(j * block, block), block)
            out[:, at] = dot(a, w_ref[at, :], ((1,), (1,)))
            return carry

        lax.fori_loop(0, w_ref.shape[0] // block, some, 0)

    def term(c):
        place = pl.ds(pl.multiple_of(c * rows, rows), rows)

        def put(at, value):
            term_buf[:, at] = value

        dot_columns(put, d_gu_ref[place, :], gu_w_ref, ((1,), (0,)))

    def finish(at, total):
        d_rows, sums_two = layer_norm_back(hidden_ref[at, :], ln_ref[2:3, :], total)
        d_rows = cot_ref[at, :].astype(F32) * weight_ref[at, :] + d_rows
        out_ref[at, :] = d_rows
        low_ref[at, :] = d_rows.astype(BF)
        ln_sum[...] += sums_two

    def step(s, carry):
        gather_step(n, copy, s)
        for d in range(2):
            act_copy(d, s).start()
        by_rows(gate_up, jnp.concatenate([land[0, s], land[1, s]], axis=0), gu_w_ref)
        grad_load(s).wait()
        by_rows(d_inner, grad_buf[lax.rem(s, 2)], down_w_ref)

        @pl.when(s < n - 2)
        def _():
            grad_load(s + 2).start()

        place = pl.ds(pl.multiple_of(s * rows, rows), rows)
        for at in range(0, ff_pad, 128):
            here, there = slice(at, at + 128), slice(ff_pad + at, ff_pad + at + 128)
            real = real_ref[:, here]
            gate, up = gate_up[:, here], gate_up[:, there]
            value, slope = gelu_pair(gate)
            back = d_inner[:, here] * real
            inner_ref[place, here] = (value * up * real).astype(BF)
            d_gu_ref[place, here] = (back * up * slope).astype(BF)
            d_gu_ref[place, there] = (back * value).astype(BF)

        @pl.when(s > 0)
        def _():
            term(s)
            scatter_step(n, sum_copy, sums, term_buf, finish, s - 1)

        return carry

    lax.fori_loop(0, n, step, 0)
    term(0)
    scatter_step(n, sum_copy, sums, term_buf, finish, n - 1)
    ring_sent(n, copy)
    ring_sent(n, sum_copy, range(PIECES))

    def written(s, carry):
        for d in range(2):
            act_copy(d, s).wait()
        return carry

    lax.fori_loop(0, n, written, 0)


def both_ways(n, x, gu_w, down_w, real, hidden, cotangent, weight, ln_params, grad):
    rows, width = x.shape
    ff_pad = down_w.shape[0]
    buf, sems = ring_scratch(n, rows, width)
    sum_buf, sum_sems = ring_scratch(n, rows, width, PIECES)
    return pl.pallas_call(
        functools.partial(both_kernel, n),
        in_specs=[VMEM_SPEC] * 8 + [ANY_SPEC],
        out_specs=[ANY_SPEC] + [VMEM_SPEC] * 5,
        out_shape=[
            jax.ShapeDtypeStruct((n * rows, width), BF),
            jax.ShapeDtypeStruct((n * rows, ff_pad), BF),
            jax.ShapeDtypeStruct((n * rows, 2 * ff_pad), BF),
            jax.ShapeDtypeStruct((rows, width), F32),
            jax.ShapeDtypeStruct((rows, width), BF),
            jax.ShapeDtypeStruct((2, width), F32),
        ],
        scratch_shapes=buf
        + sum_buf
        + [
            pltpu.VMEM((rows, width), F32),
            pltpu.VMEM((rows, 2 * ff_pad), F32),
            pltpu.VMEM((rows, ff_pad), F32),
            pltpu.VMEM((2, rows, width), BF),
        ]
        + sems
        + sum_sems
        + [pltpu.SemaphoreType.DMA((2, n)), pltpu.SemaphoreType.DMA((2,))],
        compiler_params=pltpu.CompilerParams(
            collective_id=7, has_side_effects=True, vmem_limit_bytes=60 << 20
        ),
        cost_estimate=cost(160),
    )(x, gu_w, down_w, real, hidden, cotangent, weight, ln_params, grad)


def back_kernel(
    n, n_x, x_ref, w_ref, ctx_ref, inner_hbm, d_gu_hbm, grad_hbm, act_hbm,
    d_ctx_ref, out_ref, mine_ref, slots_hbm,
    land, lhs, rhs, part, core_land, out_sum, send_sem, recv_sem, load_sem, core_sem, slot_sem,
):
    rows, ff_pad = x_ref.shape[0], lhs.shape[2]
    ff_rows, half = core_land.shape[1:]
    sides, partner = neighbours(n)[1], other_core()
    core = lax.rem(lax.axis_index("dp"), 2)
    loads = [
        pltpu.make_async_copy(src, dst, load_sem.at[i])
        for i, (src, dst) in enumerate(
            (
                (inner_hbm, lhs.at[0]),
                (grad_hbm, rhs.at[0]),
                (d_gu_hbm.at[:, pl.ds(0, ff_pad)], lhs.at[1]),
                (act_hbm, rhs.at[1]),
                (d_gu_hbm.at[:, pl.ds(ff_pad, ff_pad)], lhs.at[2]),
            )
        )
    ]
    for load in loads:
        load.start()
    out_sum[...] = jnp.zeros_like(out_sum)
    chip, chips = other_chips(n_x)
    greet(sides + [partner] + chips)

    def slot_copy(k):
        return pltpu.make_async_remote_copy(
            src_ref=mine_ref.at[0], dst_ref=slots_hbm.at[chip], send_sem=slot_sem.at[0, k],
            recv_sem=slot_sem.at[1, k], device_id=chips[k], device_id_type=PUSH,
        )

    def core_copy(i):
        return pltpu.make_async_remote_copy(
            src_ref=part.at[i, 1 - core],
            dst_ref=core_land.at[i],
            send_sem=core_sem.at[0, i],
            recv_sem=core_sem.at[1, i],
            device_id=partner,
            device_id_type=PUSH,
        )

    def work(s):
        chunk = jnp.concatenate([land[0, s], land[1, s]], axis=0)
        place = pl.ds(pl.multiple_of(s * rows, rows), rows)
        d_ctx_ref[place, :] = dot(chunk, w_ref[...], ((1,), (1,))).astype(BF)
        out_sum[...] += dot(ctx_ref[place, :], chunk, ((0,), (0,)))
        for i in range(3):
            for turn in range(2):

                @pl.when(s == 2 * i + turn)
                def _():
                    if turn == 0:
                        for load in (loads[:2], loads[2:4], loads[4:])[i]:
                            load.wait()
                    side = slice(turn * half, (turn + 1) * half)

                    def put(at, value):
                        part[i, turn, :, at] = value[:ff_rows].astype(BF)

                    dot_columns(put, lhs[i], rhs.at[min(i, 1), :, side], ((0,), (0,)))
                    if turn == 1:
                        core_copy(i).start()

            @pl.when(s == 2 * i + 3)
            def _():
                core_copy(i).wait()
                total = part[i, core].astype(F32) + core_land[i].astype(F32)
                mine_ref[i] = total.astype(BF)
                if i == 0:
                    for k in range(n_x - 1):
                        slot_copy(k).start()

    ring_gather(n, x_ref, land, send_sem, recv_sem, sides, work)
    out_ref[...] = out_sum[...].astype(BF)
    for k in range(n_x - 1):
        slot_copy(k).wait()


def back_gather(n, n_x, ff_dev, x, w, context, inner, d_gu, grad, act):
    rows, width = x.shape
    ff_pad = inner.shape[1]
    ff_rows = -(-ff_dev // ROW_BLOCK) * ROW_BLOCK
    buf, sems = ring_scratch(n, rows, width)
    return pl.pallas_call(
        functools.partial(back_kernel, n, n_x),
        in_specs=[VMEM_SPEC] * 3 + [ANY_SPEC] * 4,
        out_specs=[VMEM_SPEC] * 3 + [ANY_SPEC],
        out_shape=[
            jax.ShapeDtypeStruct((n * rows, w.shape[0]), BF),
            jax.ShapeDtypeStruct(w.shape, BF),
            jax.ShapeDtypeStruct((3, ff_rows, width // 2), BF),
            jax.ShapeDtypeStruct((n_x, ff_rows, width // 2), BF),
        ],
        scratch_shapes=buf
        + [
            pltpu.VMEM((3, n * rows, ff_pad), BF),
            pltpu.VMEM((2, n * rows, width), BF),
            pltpu.VMEM((3, 2, ff_rows, width // 2), BF),
            pltpu.VMEM((3, ff_rows, width // 2), BF),
            pltpu.VMEM(w.shape, F32),
        ]
        + sems
        + [
            pltpu.SemaphoreType.DMA((5,)),
            pltpu.SemaphoreType.DMA((2, 3)),
            pltpu.SemaphoreType.DMA((2, n_x - 1)),
        ],
        compiler_params=pltpu.CompilerParams(
            collective_id=3, has_side_effects=True, vmem_limit_bytes=60 << 20
        ),
        cost_estimate=cost(80),
    )(x, w, context, inner, d_gu, grad, act)


def ffn_kernel(
    n, n_x, heads, inner_ref, w_ref, hidden_ref, thr_ref, qkv_ref, d_ctx_ref, lse_ref,
    out_part_ref, act_hbm, mine_hbm,
    out_ref, d_qkv_ref, slots_hbm, out_slots_hbm, oq_mine_ref,
    land, term_buf, q_ref, k_ref, v_ref, do_ref, dk_sum, dv_sum,
    act_buf, part, qkv_land, out_land,
    send_sem, recv_sem, act_sem, core_sem, slot_sem,
):
    rows = hidden_ref.shape[0]
    pos, sides = neighbours(n)
    partner = other_core()
    core = lax.rem(lax.axis_index("dp"), 2)
    chip, chips = other_chips(n_x)
    block = act_buf.shape[2]
    blocks = act_hbm.shape[1] // block
    qkv_cols, wide = qkv_land.shape
    wide_of = lambda c: pl.ds(pl.multiple_of(c * wide, wide), wide)

    def act_load(j):
        return pltpu.make_async_copy(
            act_hbm.at[:, pl.ds(j * block, block)], act_buf.at[j % 2], act_sem.at[j]
        )

    def core_copy(i):
        src, dst = (
            (part.at[:, wide_of(1 - core)], qkv_land),
            (out_part_ref.at[:, wide_of(1 - core)], out_land),
        )[i]
        return pltpu.make_async_remote_copy(
            src_ref=src, dst_ref=dst, send_sem=core_sem.at[0, i], recv_sem=core_sem.at[1, i],
            device_id=partner, device_id_type=PUSH,
        )

    def slot_copy(i, k):
        src, dst = (
            (mine_hbm.at[pl.ds(1, 2)], slots_hbm),
            (oq_mine_ref.at[pl.ds(qkv_cols, oq_mine_ref.shape[0] - qkv_cols)], out_slots_hbm),
        )[i]
        return pltpu.make_async_remote_copy(
            src_ref=src, dst_ref=dst.at[chip], send_sem=slot_sem.at[0, i, k],
            recv_sem=slot_sem.at[1, i, k], device_id=chips[k], device_id_type=PUSH,
        )

    for j in range(2):
        act_load(j).start()
    greet(sides + [partner] + chips)
    core_copy(1).start()
    for k in range(n_x - 1):
        slot_copy(0, k).start()
    places = chunk_places(n, pos, rows)

    def term(c):
        place = pl.ds(pl.multiple_of(c * rows, rows), rows)

        def put(at, value):
            term_buf[:, at] = value

        dot_columns(put, inner_ref[place, :], w_ref, ((1,), (0,)))

    def work(s):
        for h in range(heads):

            columns = lambda i: slice((i * heads + h) * HD, (i * heads + h + 1) * HD)
            for turn in range(2):

                @pl.when(s == 2 * h + turn)
                def _():
                    if turn == 0:
                        for i, dst in enumerate((q_ref, k_ref, v_ref)):
                            to_order(places, qkv_ref, columns(i), dst)
                        to_order(places, d_ctx_ref, columns(0), do_ref)
                    attn_backward_head(
                        turn, places, thr_ref, lse_ref.at[h], q_ref, k_ref, v_ref, do_ref,
                        dk_sum, dv_sum, d_qkv_ref, columns,
                    )

        @pl.when(s == 1)
        def _():
            core_copy(1).wait()
            total = out_part_ref[:, wide_of(core)].astype(F32) + out_land[...].astype(F32)
            oq_mine_ref[qkv_cols:, :] = total.astype(BF)
            for k in range(n_x - 1):
                slot_copy(1, k).start()

        for turn in range(blocks // 2):

            @pl.when(s == 2 * heads + turn)
            def _():
                for j in (2 * turn, 2 * turn + 1):
                    act_load(j).wait()
                    grad = dot(d_qkv_ref[...], act_buf[j % 2], ((0,), (0,)))
                    part[:, j * block : (j + 1) * block] = grad.astype(BF)
                for j in (2 * turn + 2, 2 * turn + 3):
                    if j < blocks:
                        act_load(j).start()
                if turn == blocks // 2 - 1:
                    core_copy(0).start()

    def finish(at, total):
        out_ref[at, :] = (hidden_ref[at, :] + total).astype(BF)

    ring_scatter(n, land, send_sem, recv_sem, sides, term_buf, term, work, finish)
    core_copy(0).wait()
    total = part[:, wide_of(core)].astype(F32) + qkv_land[...].astype(F32)
    oq_mine_ref[:qkv_cols, :] = total.astype(BF)
    for k in range(n_x - 1):
        slot_copy(0, k).wait()
        slot_copy(1, k).wait()


def ffn_scatter(n, n_x, inner, w, hidden, thr, qkv, d_context, lse, out_part, act, mine):
    rows, width = hidden.shape
    cols, block = d_context.shape[1], 512
    heads = d_context.shape[1] // HD
    buf, sems = ring_scratch(n, rows, width, PIECES)
    return pl.pallas_call(
        functools.partial(ffn_kernel, n, n_x, heads),
        in_specs=[VMEM_SPEC] * 8 + [ANY_SPEC] * 2,
        out_specs=[VMEM_SPEC] * 2 + [ANY_SPEC] * 2 + [VMEM_SPEC],
        out_shape=[
            jax.ShapeDtypeStruct((rows, width), BF),
            jax.ShapeDtypeStruct(qkv.shape, BF),
            jax.ShapeDtypeStruct((n_x, 2) + mine.shape[1:], BF),
            jax.ShapeDtypeStruct((n_x, cols, width // 2), BF),
            jax.ShapeDtypeStruct((4 * cols, width // 2), BF),
        ],
        scratch_shapes=buf
        + [pltpu.VMEM((rows, width), F32)]
        + [pltpu.VMEM((SLOT, HD), BF)] * 4
        + [pltpu.VMEM((SLOT, HD), F32)] * 2
        + [
            pltpu.VMEM((2, n * rows, block), BF),
            pltpu.VMEM((3 * cols, width), BF),
            pltpu.VMEM((3 * cols, width // 2), BF),
            pltpu.VMEM((cols, width // 2), BF),
        ]
        + sems
        + [
            pltpu.SemaphoreType.DMA((width // block,)),
            pltpu.SemaphoreType.DMA((2, 2)),
            pltpu.SemaphoreType.DMA((2, 2, n_x - 1)),
        ],
        compiler_params=pltpu.CompilerParams(
            collective_id=4, has_side_effects=True, vmem_limit_bytes=62 << 20
        ),
        cost_estimate=cost(95),
    )(inner, w, hidden, thr, qkv, d_context, lse, out_part, act, mine)


def row_sums(grad_ref, old_ref, real_ref, new_ref, c_ref, t_ref):
    width = grad_ref.shape[1]
    block = ROW_BLOCK

    def rows(i, carry):
        at = pl.ds(pl.multiple_of(i * block, block), block)
        grad = grad_ref[at, :].astype(F32)
        square = grad * grad
        real = real_ref[at, :]
        total = (jnp.sum(square, axis=1, keepdims=True) + width * eps_one) * real
        new = DECAY * old_ref[at, :] + (1.0 - DECAY) * (total / width)
        new_ref[at, :] = new
        c = (square + eps_one) * real
        t = square * (real / new)
        c_ref[...] += sum(c[k : k + 8] for k in range(0, block, 8))
        t_ref[...] += sum(t[k : k + 8] for k in range(0, block, 8))
        return carry

    lax.fori_loop(0, grad_ref.shape[0] // block, rows, 0)


def last_kernel(
    n, n_x, d_qkv_ref, w_ref, oq_mine_ref, oq_old, oq_real, ff_old, ff_real,
    x_ref, d_hidden_ref, ln_ref,
    mine_hbm, down_hbm, gu_hbm, out_hbm,
    out_ref, goq_hbm, gff_hbm, oq_new, ff_new, sums_ref, ln_sum, totals_ref,
    land, term_buf, goq_ref, gff_ref, qkv_land, out_slots, ff_own, ff_slots, c_sum, t_sum,
    send_sem, recv_sem, oq_sem, load_sem, join_sem, write_sem,
):
    rows = term_buf.shape[0]
    cols, width = w_ref.shape[2], term_buf.shape[1]
    sides, partner = neighbours(n)[1], other_core()
    core = lax.rem(lax.axis_index("dp"), 2)
    chip, chips = other_chips(n_x)
    half = width // 2
    own = pl.ds(pl.multiple_of(core * half, half), half)

    qkv_rows, out_rows = pl.ds(0, 3 * cols), pl.ds(3 * cols, cols)
    writes = [
        pltpu.make_async_copy(goq_ref, goq_hbm, write_sem.at[0]),
        pltpu.make_async_copy(gff_ref, gff_hbm, write_sem.at[1]),
    ]

    def loads(i):
        if i == 3:
            return [pltpu.make_async_copy(out_hbm, out_slots, load_sem.at[0, 3])]
        slots = down_hbm if i == 0 else gu_hbm.at[:, i - 1]
        return [
            pltpu.make_async_copy(mine_hbm.at[i], ff_own.at[i], load_sem.at[0, i]),
            pltpu.make_async_copy(slots, ff_slots.at[i], load_sem.at[1, i]),
        ]

    def oq_copy(k):
        return pltpu.make_async_remote_copy(
            src_ref=oq_mine_ref.at[qkv_rows], dst_ref=qkv_land.at[chip], send_sem=oq_sem.at[0, k],
            recv_sem=oq_sem.at[1, k], device_id=chips[k], device_id_type=PUSH,
        )

    def join(i):
        ref = gff_ref.at[i, :, own] if i < 3 else goq_ref.at[(qkv_rows, out_rows)[i - 3], own]
        return pltpu.make_async_remote_copy(
            src_ref=ref, dst_ref=ref, send_sem=join_sem.at[0, i], recv_sem=join_sem.at[1, i],
            device_id=partner, device_id_type=PUSH,
        )

    def chip_sum(own_half, slots):
        total = jnp.zeros(own_half.shape, F32)
        for x in range(n_x):
            total = total + jnp.where(chip == x, own_half, slots[x]).astype(F32)
        return total.astype(BF)

    for i in range(4):
        for load in loads(i):
            load.start()
    ln_sum[...] = jnp.zeros_like(ln_sum)
    greet(sides + [partner] + chips)
    for k in range(n_x - 1):
        oq_copy(k).start()

    def term(c):
        place = pl.ds(pl.multiple_of(c * rows, rows), rows)
        block = 512

        def columns(j, carry):
            at = pl.ds(pl.multiple_of(j * block, block), block)
            term_buf[:, at] = sum(
                dot(d_qkv_ref[place, k * cols : (k + 1) * cols], w_ref[k, at, :], ((1,), (1,)))
                for k in range(3)
            )
            return carry

        lax.fori_loop(0, width // block, columns, 0)

    def sums(group, ref, first=True):
        if first:
            c_sum[...] = jnp.zeros_like(c_sum)
            t_sum[...] = jnp.zeros_like(t_sum)
        row_sums(*ref, c_sum, t_sum)
        sums_ref[2 * group : 2 * group + 1, :] = jnp.sum(c_sum[...], axis=0, keepdims=True)
        sums_ref[2 * group + 1 : 2 * group + 2, :] = jnp.sum(t_sum[...], axis=0, keepdims=True)

    ff_refs = lambda i: (gff_ref.at[i], ff_old.at[i], ff_real, ff_new.at[i])
    oq_refs = lambda at: tuple(ref.at[at] for ref in (goq_ref, oq_old, oq_real, oq_new))

    def work(s):
        for i in range(3):

            @pl.when(s == i)
            def _():
                for load in loads(i):
                    load.wait()
                gff_ref[i, :, own] = chip_sum(ff_own[i], ff_slots.at[i])
                join(i).start()

        @pl.when(s == 0)
        def _():
            for load in loads(3):
                load.wait()
            goq_ref[out_rows, own] = chip_sum(oq_mine_ref[out_rows, :], out_slots)
            join(4).start()

        @pl.when(s == 3)
        def _():
            join(0).wait()
            sums(3, ff_refs(0))

        @pl.when(s == 4)
        def _():
            for k in range(n_x - 1):
                oq_copy(k).wait()
            goq_ref[qkv_rows, own] = chip_sum(oq_mine_ref[qkv_rows, :], qkv_land)
            join(3).start()

        @pl.when(s == 5)
        def _():
            join(1).wait()
            sums(1, ff_refs(1))

        @pl.when(s == 6)
        def _():
            join(2).wait()
            sums(1, ff_refs(2), first=False)
            writes[1].start()
            join(4).wait()
            sums(2, oq_refs(out_rows))
            join(3).wait()
            sums(0, oq_refs(qkv_rows))
            writes[0].start()
            down_new = ff_new[0] * ff_real[...]
            for i, new in enumerate((oq_new[out_rows, :], down_new)):
                total = jnp.sum(new, axis=0, keepdims=True)
                totals_ref[i : i + 1, :] = jnp.broadcast_to(total, (1, totals_ref.shape[1]))

    def finish(at, total):
        d_rows, sums_one = layer_norm_back(x_ref[at, :].astype(F32), ln_ref[0:1, :], total)
        out_ref[at, :] = (d_hidden_ref[at, :] + d_rows).astype(BF)
        ln_sum[...] += sums_one

    ring_scatter(n, land, send_sem, recv_sem, sides, term_buf, term, work, finish)
    for write in writes:
        write.wait()


def last_scatter(
    n, n_x, d_qkv, w, oq_mine, oq_old, oq_real, ff_old, ff_real, ff_mine, down_slots, gu_slots, out_slots,
    x, d_hidden, ln_params,
):
    width, cols = w.shape[1:]
    rows = d_qkv.shape[0] // n
    half = width // 2
    ff_rows = ff_mine.shape[1]
    buf, sems = ring_scratch(n, rows, width, PIECES)
    return pl.pallas_call(
        functools.partial(last_kernel, n, n_x),
        in_specs=[VMEM_SPEC] * 10 + [ANY_SPEC] * 4,
        out_specs=[VMEM_SPEC] + [ANY_SPEC] * 2 + [VMEM_SPEC] * 5,
        out_shape=[
            jax.ShapeDtypeStruct((rows, width), BF),
            jax.ShapeDtypeStruct((4 * cols, width), BF),
            jax.ShapeDtypeStruct((3, ff_rows, width), BF),
            jax.ShapeDtypeStruct(oq_old.shape, F32),
            jax.ShapeDtypeStruct(ff_old.shape, F32),
            jax.ShapeDtypeStruct((8, width), F32),
            jax.ShapeDtypeStruct((2, width), F32),
            jax.ShapeDtypeStruct((8, 128), F32),
        ],
        scratch_shapes=buf
        + [
            pltpu.VMEM((rows, width), F32),
            pltpu.VMEM((4 * cols, width), BF),
            pltpu.VMEM((3, ff_rows, width), BF),
            pltpu.VMEM((n_x, 3 * cols, half), BF),
            pltpu.VMEM((n_x, cols, half), BF),
            pltpu.VMEM((3, ff_rows, half), BF),
            pltpu.VMEM((3, n_x, ff_rows, half), BF),
            pltpu.VMEM((8, width), F32),
            pltpu.VMEM((8, width), F32),
        ]
        + sems
        + [
            pltpu.SemaphoreType.DMA((2, n_x - 1)),
            pltpu.SemaphoreType.DMA((2, 4)),
            pltpu.SemaphoreType.DMA((2, 5)),
            pltpu.SemaphoreType.DMA((2,)),
        ],
        compiler_params=pltpu.CompilerParams(
            collective_id=2, has_side_effects=True, vmem_limit_bytes=62 << 20
        ),
        cost_estimate=cost(90),
    )(
        d_qkv, w, oq_mine, oq_old, oq_real, ff_old, ff_real, x, d_hidden, ln_params,
        ff_mine, down_slots, gu_slots, out_slots,
    )


def norm_stats(rows):
    mean_row = jnp.mean(rows, axis=-1, keepdims=True)
    centered = rows - mean_row
    variance = jnp.mean(centered * centered, axis=-1, keepdims=True)
    scale = lax.rsqrt(variance + ln_eps)
    return centered * scale, scale


def layer_norm(rows, gain, shift):
    return norm_stats(rows)[0] * gain + shift


def layer_norm_back(rows, gain, e):
    n, scale = norm_stats(rows)
    eg = e * gain
    dv = scale * (
        eg - jnp.mean(eg, axis=-1, keepdims=True) - n * jnp.mean(eg * n, axis=-1, keepdims=True)
    )
    sums = [jnp.sum(x, axis=0, keepdims=True) for x in (e * n, e)]
    return dv, jnp.concatenate(sums, axis=0)


def seen_mask(thr_ref, q0, shape):
    thr = thr_ref[: shape[0], :]
    thr = jnp.concatenate([thr] * (shape[1] // thr.shape[1]), axis=1)
    q_pos = (q0 + lax.broadcasted_iota(jnp.int32, shape, 1)).astype(F32)
    return q_pos >= thr


def q_blocks():
    return [(q0, max(PREFIX_MAX, q0 + Q_BLOCK)) for q0 in range(0, SLOT, Q_BLOCK)]


def to_order(places, src_ref, columns, dst_ref):
    half = SLOT // len(places)
    for j, start in enumerate(places):
        place = pl.ds(pl.multiple_of(start, half), half)
        dst_ref[j * half : (j + 1) * half, :] = src_ref[place, columns]


def from_order(places, q0, value, dst_ref, columns):
    half = SLOT // len(places)
    for i in range(value.shape[0] // half):
        place = pl.ds(pl.multiple_of(places[q0 // half + i], half), half)
        dst_ref[place, columns] = value[i * half : (i + 1) * half, :]


def attn_forward_head(places, thr_ref, lse_ref, q_ref, k_ref, v_ref, o_ref, columns):
    c = HD**-0.5 * LOG2E
    for q0, klim in q_blocks():
        raw = dot(k_ref[:klim, :], q_ref[q0 : q0 + Q_BLOCK, :], ((1,), (1,)))
        raw = jnp.where(seen_mask(thr_ref, q0, raw.shape), raw, masked_score)
        top = jnp.max(raw, axis=0, keepdims=True)
        p = jnp.exp2((raw - top) * c)
        total = jnp.sum(p, axis=0, keepdims=True)
        out = dot(v_ref[:klim, :], p.astype(BF), ((0,), (0,))) / total
        from_order(places, q0, out.T.astype(BF), o_ref, columns)
        lse_ref[:, q0 : q0 + Q_BLOCK] = top * c + jnp.log2(total)


def attn_backward_head(
    turn, places, thr_ref, lse_ref, q_ref, k_ref, v_ref, do_ref, dk_sum, dv_sum, d_ref, columns
):
    scale = HD**-0.5
    blocks = q_blocks()
    if turn == 0:
        dk_sum[...] = jnp.zeros_like(dk_sum)
        dv_sum[...] = jnp.zeros_like(dv_sum)
    for q0, klim in (blocks[-1:] + blocks[:1], blocks[1:-1])[turn]:
        rows = slice(q0, q0 + Q_BLOCK)
        k, q, do = k_ref[:klim, :], q_ref[rows, :], do_ref[rows, :]
        raw = dot(k, q, ((1,), (1,)))
        p = jnp.exp2(raw * (scale * LOG2E) - lse_ref[:, rows])
        p = jnp.where(seen_mask(thr_ref, q0, raw.shape), p, 0.0)
        dv_sum[:klim, :] += dot(p.astype(BF), do, ((1,), (0,)))
        dp = dot(v_ref[:klim, :], do, ((1,), (1,)))
        delta = jnp.sum(p * dp, axis=0, keepdims=True)
        ds = (p * (dp - delta) * scale).astype(BF)
        dk_sum[:klim, :] += dot(ds, q, ((1,), (0,)))
        dq = dot(k, ds, ((0,), (0,))).T.astype(BF)
        from_order(places, q0, dq, d_ref, columns(0))
    if turn == 1:
        from_order(places, 0, dk_sum[...].astype(BF), d_ref, columns(1))
        from_order(places, 0, dv_sum[...].astype(BF), d_ref, columns(2))


def step_rate(update_sq, weight_sq, n_real):
    update_rms = jnp.sqrt(update_sq / n_real)
    weight_rms = jnp.sqrt(weight_sq / n_real)
    return rate_base * jnp.maximum(eps_two, weight_rms) / jnp.maximum(1.0, update_rms / clip_bound)


def results_kernel(
    counts, factor_ref, goq_qkv, goq_out, gff_down, gff_gate, gff_up,
    w_qkv, w_out, w_down, w_gate, w_up, r_qkv, r_out, r_down, r_gate, r_up,
    qkv_grad, qkv_new, out_grad, out_new, gu_grad, gu_new, down_grad, down_new,
):
    t = pl.program_id(0)
    n_gu, n_qkv, n_down, n_out = counts

    def after(grad, weight, row, factor):
        return weight.astype(F32) - grad * (lax.rsqrt(row) * factor)

    @pl.when(t < n_gu)
    def _():
        factor = factor_ref[1:2, :]
        for i, (g, w, r) in enumerate(((gff_gate, w_gate, r_gate), (gff_up, w_up, r_up))):
            grad = g[0].astype(F32)
            gu_grad[:, i, :] = grad
            gu_new[:, i, :] = after(grad, w[...], r[0], factor)

    start = n_gu
    @pl.when((t >= start) & (t < start + n_qkv))
    def _():
        block = goq_qkv.shape[1]
        at = lax.rem(t - n_gu, factor_ref.shape[1] // block) * block
        factor = factor_ref[0:1, pl.ds(pl.multiple_of(at, block), block)]
        grad = goq_qkv[...].astype(F32)
        qkv_grad[0] = grad.T
        qkv_new[0] = w_qkv[0].astype(F32) - (grad * (lax.rsqrt(r_qkv[...]) * factor)).T

    start = n_gu + n_qkv

    @pl.when((t >= start) & (t < start + n_down))
    def _():
        grad = gff_down[0].astype(F32)
        down_grad[...] = grad
        down_new[...] = after(grad, w_down[...], r_down[0], factor_ref[3:4, :])

    @pl.when(t >= n_gu + n_qkv + n_down)
    def _():
        grad = goq_out[...].astype(F32)
        out_grad[...] = grad
        out_new[...] = after(grad, w_out[...], r_out[...], factor_ref[2:3, :])


def results(ff, factors, goq, gff, w_qkv, w_out, w_down, w_gu, oq_new, ff_new):
    kinds, width, cols = w_qkv.shape
    rows, wide, high = 96, 1024, 128
    counts = (-(-ff // rows), kinds * width // wide, -(-ff // rows), cols // high)
    starts = [sum(counts[:i]) for i in range(4)]
    per_kind = width // wide
    place = lambda part: lambda t: jnp.clip(t - starts[part], 0, counts[part] - 1)
    gu, qkv, down, out = (place(part) for part in range(4))
    shift = w_gu.shape[0] // 2 // rows
    third = lambda k, part, last: pl.BlockSpec((1, rows, last), lambda t: (k, part(t), 0))
    by_kind = lambda t: (qkv(t) // per_kind, lax.rem(qkv(t), per_kind), 0)
    out_at = 3 * cols // high
    qkv_spec = pl.BlockSpec((1, wide, cols), by_kind)
    out_spec = pl.BlockSpec((high, width), lambda t: (out(t), 0))
    gu_spec = pl.BlockSpec((rows, 2, width), lambda t: (gu(t), 0, 0))
    down_spec = pl.BlockSpec((rows, width), lambda t: (down(t), 0))
    shape = lambda *dims: jax.ShapeDtypeStruct(dims, F32)
    return pl.pallas_call(
        functools.partial(results_kernel, counts),
        grid=(sum(counts),),
        in_specs=[
            pl.BlockSpec(factors.shape, lambda t: (0, 0)),
            pl.BlockSpec((cols, wide), lambda t: by_kind(t)[:2]),
            pl.BlockSpec((high, width), lambda t: (out_at + out(t), 0)),
            third(0, down, width),
            third(1, gu, width),
            third(2, gu, width),
            qkv_spec,
            out_spec,
            down_spec,
            pl.BlockSpec((rows, width), lambda t: (gu(t), 0)),
            pl.BlockSpec((rows, width), lambda t: (gu(t) + shift, 0)),
            pl.BlockSpec((cols, 1), lambda t: (by_kind(t)[0], 0)),
            pl.BlockSpec((high, 1), lambda t: (out_at + out(t), 0)),
            third(0, down, 1),
            third(1, gu, 1),
            third(2, gu, 1),
        ],
        out_specs=[qkv_spec, qkv_spec, out_spec, out_spec, gu_spec, gu_spec, down_spec, down_spec],
        out_shape=[shape(kinds, width, cols)] * 2
        + [shape(cols, width)] * 2
        + [shape(ff, 2, width)] * 2
        + [shape(ff, width)] * 2,
        compiler_params=pltpu.CompilerParams(vmem_limit_bytes=56 << 20),
        cost_estimate=cost(28),
    )(
        factors, goq, goq, gff, gff, gff, w_qkv, w_out, w_down, w_gu, w_gu,
        oq_new, oq_new, ff_new, ff_new, ff_new,
    )


def exchange_kernel(
    n_dp, n, cells, one_ref, two_ref, sums_ref, totals_ref, squares_ref, old_ref, ln_ref, second_ref,
    factor_ref, qkv_row, gu_row, out_col, down_col, ln_tot, ln_second, ln_new,
    x_ref, o_ref, dp_buf, rows, part_buf, total, whole, sems,
):
    me_d, me = lax.axis_index("dp"), lax.axis_index("tensor")
    width = x_ref.shape[1] // n
    columns = lambda t: pl.ds(pl.multiple_of(t * width, width), width)
    dp_peers = [(k - 1, lax.rem(me_d + k, n_dp)) for k in range(1, n_dp)]
    peers = [(k - 1, lax.rem(me + k, n)) for k in range(1, n)]
    barrier = pltpu.get_barrier_semaphore()
    for _, d in dp_peers:
        pl.semaphore_signal(barrier, inc=1, device_id={"dp": d}, device_id_type=pl.DeviceIdType.MESH)
    for _, t in peers:
        pl.semaphore_signal(barrier, inc=1, device_id={"tensor": t}, device_id_type=pl.DeviceIdType.MESH)
    pl.semaphore_wait(barrier, n_dp + n - 2)

    def push(stage, src, dst, k, device):
        copy = pltpu.make_async_remote_copy(
            src_ref=src, dst_ref=dst, send_sem=sems.at[0, stage, k], recv_sem=sems.at[1, stage, k],
            device_id=device, device_id_type=pl.DeviceIdType.MESH,
        )
        copy.start()
        return copy

    x_ref[0:2, :] = one_ref[...]
    x_ref[2:4, :] = two_ref[...]
    x_ref[4:8, :] = jnp.zeros((4, x_ref.shape[1]), F32)
    lane = lax.broadcasted_iota(jnp.int32, (1, 128), 1)
    add_up = lambda v: jnp.sum(jnp.sum(v, axis=0, keepdims=True), axis=1, keepdims=True)
    scalars = [add_up(squares_ref[i]) for i in range(4)] + [totals_ref[i : i + 1, 0:1] for i in range(2)]
    x_ref[4:5, 0:128] = sum(jnp.where(lane == i, v, 0.0) for i, v in enumerate(scalars)) / n_dp
    x_ref[8:16, :] = sums_ref[...]
    first = [push(0, x_ref.at[pl.ds(0, 8)], dp_buf.at[me_d], k, {"dp": d}) for k, d in dp_peers]
    rows[...] = x_ref[...]
    dp_buf[me_d] = x_ref[0:8, :]
    for copy in first:
        copy.wait()
    rows[0:8, :] = sum(dp_buf[d] for d in range(n_dp))
    second = [push(1, rows.at[:, columns(t)], part_buf.at[me], k, {"tensor": t}) for k, t in peers]
    part_buf[me] = rows[:, columns(me)]
    for copy in second:
        copy.wait()
    total[...] = sum(part_buf[t] for t in range(n))
    third = [push(2, total, whole.at[me], k, {"tensor": t}) for k, t in peers]
    whole[me] = total[...]
    for copy in third:
        copy.wait()
    for t in range(n):
        o_ref[:, t * width : (t + 1) * width] = whole[t]

    columns_all = x_ref.shape[1]
    blend = lambda old, new: DECAY * old + (1.0 - DECAY) * new
    mean_of = lambda v: jnp.sum(v, axis=1, keepdims=True) / columns_all
    at = lambda i: o_ref[i : i + 1, :]
    scalar = lambda i: o_ref[4:5, i : i + 1]
    news = (qkv_row, gu_row, out_col, down_col)
    for i, (new_ref, (count, real, by_row)) in enumerate(zip(news, cells)):
        new = blend(old_ref[i : i + 1, :], at(8 + 2 * i) / count)
        new_ref[...] = new
        mean = mean_of(new) if by_row else scalar(2 + i) / count
        update_sq = jnp.sum(at(9 + 2 * i) / new, axis=1, keepdims=True) * mean
        rate = step_rate(update_sq, scalar(i), real)
        factor_ref[i : i + 1, :] = lax.rsqrt(new) * (rate * jnp.sqrt(mean))
    grad, weight = o_ref[0:4, :], ln_ref[...]
    second = blend(second_ref[...], grad * grad + eps_one)
    update = grad * lax.rsqrt(second)
    update_rms = jnp.sqrt(mean_of(update * update))
    weight_rms = jnp.sqrt(mean_of(weight * weight))
    ln_tot[...] = grad
    ln_second[...] = second
    ln_new[...] = weight - rate_base * jnp.maximum(eps_two, weight_rms) * update / jnp.maximum(
        1.0, update_rms / clip_bound
    )


def exchange(n_dp, n, cells, ln_one, ln_two, sums, totals, squares, old, ln_params, ln_second):
    height, width = 16, sums.shape[1]
    slots = pltpu.VMEM((n, height, width // n), F32)
    shape = lambda *dims: jax.ShapeDtypeStruct(dims, F32)
    return pl.pallas_call(
        functools.partial(exchange_kernel, n_dp, n, cells),
        out_shape=[shape(4, width)] + [shape(1, width)] * 4 + [shape(4, width)] * 3,
        in_specs=[VMEM_SPEC] * 8,
        out_specs=[VMEM_SPEC] * 8,
        scratch_shapes=[
            pltpu.VMEM((height, width), F32),
            pltpu.VMEM((height, width), F32),
            pltpu.VMEM((n_dp, 8, width), F32),
            pltpu.VMEM((height, width), F32),
            slots,
            pltpu.VMEM((height, width // n), F32),
            slots,
            pltpu.SemaphoreType.DMA((2, 3, max(n, n_dp) - 1)),
        ],
        compiler_params=pltpu.CompilerParams(collective_id=0, has_side_effects=True),
        cost_estimate=cost(18),
    )(ln_one, ln_two, sums, totals, squares, old, ln_params, ln_second)


def on_device(
    layer_in,
    cotangent,
    lengths,
    prefix,
    pad_mask,
    clusters,
    qkv_w,
    out_w,
    gate_up_w,
    down_w,
    ln_params,
    qkv_row,
    qkv_col,
    out_row,
    out_col,
    gu_row,
    gu_col,
    down_row,
    down_col,
    ln_second,
):
    n_data = lax.axis_size("dp")
    n_tensor = lax.axis_size("tensor")
    tensor_rank = lax.axis_index("tensor")
    data_rank = lax.axis_index("dp")
    rows_dev, width = layer_in.shape
    cols_dev = qkv_w.shape[2]
    heads_dev = cols_dev // HD
    ff_dev = gate_up_w.shape[2]
    ff_pad = -(-ff_dev // 128) * 128
    n_clusters = max(2, n_data // 2)
    seq_length = lengths[0]
    seq_prefix = prefix[0]

    onehot = (clusters[:, None] == jnp.arange(n_clusters, dtype=jnp.int32)[None, :]).astype(F32)
    counts = jnp.sum(onehot, axis=0)
    own_row = jnp.sum(
        jnp.where((jnp.arange(n_data, dtype=jnp.int32) == data_rank)[:, None], onehot, 0.0), axis=0
    )
    seq_weight = jnp.sum(own_row / jnp.maximum(counts, 1.0))
    own_pos = tensor_rank * rows_dev + jnp.arange(rows_dev, dtype=jnp.int32)
    live_rows = ((own_pos < seq_length) & (pad_mask == 1)).astype(F32)
    row_weight = (live_rows * seq_weight)[:, None]

    key_live = (own_pos == 0) | (own_pos < seq_length) & (pad_mask == 1)
    seen_from = jnp.where(key_live, jnp.where(own_pos < seq_prefix, 0, own_pos), 2 * SLOT)
    seen = jnp.broadcast_to(seen_from.astype(F32)[None], (8, rows_dev))

    col_index = tensor_rank * ff_dev + jnp.arange(ff_pad, dtype=jnp.int32)
    ff_real = ((col_index < FF) & (jnp.arange(ff_pad) < ff_dev)).astype(F32)
    ff_mask = ff_real[:ff_dev]

    act_one_all, qkv, seen_all = first_gather(
        n_tensor, layer_in, seen, ln_params, jnp.transpose(qkv_w, (1, 0, 2))
    )
    thr = jnp.broadcast_to(seen_all[:, 0].reshape(SLOT, 1), (SLOT, 128))

    pad = ((0, ff_pad - ff_dev), (0, 0))
    gate_up_t = jnp.transpose(gate_up_w, (1, 2, 0))
    w_gu = jnp.pad(gate_up_t, ((0, 0),) + pad).reshape(2 * ff_pad, width)
    w_down = jnp.pad(down_w, pad)
    qkv_t = jnp.transpose(qkv_w, (1, 0, 2))

    grad_all, context, lse, squares = grad_gather(
        n_tensor, cotangent, row_weight, qkv, thr, ff_real[:, None], qkv_t, w_gu, out_w, w_down
    )
    hidden_own, norm_two = mix_scatter(n_tensor, context, out_w, layer_in, ln_params)

    act_two_all, inner_all, d_gu_all, d_hidden, d_hidden_low, ln_two_part = both_ways(
        n_tensor, norm_two, w_gu, w_down, ff_real[None, :], hidden_own, cotangent, row_weight,
        ln_params, grad_all,
    )

    n_x = n_data // 2
    d_context, out_part, ff_mine, down_slots = back_gather(
        n_tensor, n_x, ff_dev, d_hidden_low, out_w, context,
        inner_all, d_gu_all, grad_all, act_two_all,
    )

    layer_out, d_qkv, gu_slots, out_slots, oq_mine = ffn_scatter(
        n_tensor, n_x, inner_all, w_down, hidden_own, thr, qkv, d_context, lse,
        out_part, act_one_all, ff_mine,
    )

    ff_rows = ff_mine.shape[1]
    more = ((0, 0), (0, ff_rows - ff_dev))
    oq_old = jnp.concatenate([qkv_col.reshape(-1), out_row])[:, None]
    ff_old = jnp.pad(jnp.concatenate([down_row[None], gu_col]), more, constant_values=1.0)[:, :, None]
    ff_real = jnp.pad(ff_mask, (0, ff_rows - ff_dev))[:, None]
    input_grad, goq, gff, oq_new, ff_new, sums, ln_one_part, totals = last_scatter(
        n_tensor, n_x, d_qkv, qkv_t, oq_mine, oq_old, jnp.ones_like(oq_old), ff_old, ff_real,
        ff_mine, down_slots, gu_slots, out_slots, layer_in, d_hidden, ln_params,
    )
    qkv_col_new, out_row_new = oq_new[: 3 * cols_dev, 0], oq_new[3 * cols_dev :, 0]
    down_row_new, gu_col_new = ff_new[0, :ff_dev, 0], ff_new[1:, :ff_dev, 0]

    rows_all = cols_dev * n_tensor
    cells = (
        (3 * rows_all, width * 3 * rows_all, True),
        (2 * FF, width * 2 * FF, True),
        (rows_all, rows_all * width, False),
        (FF, FF * width, False),
    )
    factors, qkv_row_new, gu_row_new, out_col_new, down_col_new, ln_tot, ln_second_new, ln_new = exchange(
        n_data, n_tensor, cells, ln_one_part, ln_two_part, sums, totals, squares,
        jnp.stack([qkv_row, gu_row, out_col, down_col]), ln_params, ln_second,
    )
    qkv_grad, qkv_new, out_sum, out_new, gu_grad, gu_new, down_sum, down_new = results(
        ff_dev, factors, goq, gff, qkv_t, out_w, w_down, w_gu, oq_new, ff_new
    )
    qkv_back = lambda x: jnp.transpose(x, (1, 0, 2))
    return (
        layer_out,
        input_grad,
        qkv_back(qkv_grad),
        qkv_back(qkv_new),
        qkv_row_new[0],
        qkv_col_new.reshape(3, -1),
        out_sum,
        out_new,
        out_row_new,
        out_col_new[0],
        jnp.transpose(gu_grad, (2, 1, 0)),
        jnp.transpose(gu_new, (2, 1, 0)),
        gu_row_new[0],
        gu_col_new,
        down_sum,
        down_new,
        down_row_new,
        down_col_new[0],
        ln_tot,
        ln_second_new,
        ln_new,
    )


def solution(mesh):
    in_specs = (
        P(("dp", "tensor"), None),
        P(("dp", "tensor"), None),
        P("dp"),
        P("dp"),
        P(("dp", "tensor")),
        P(),
        P(None, None, "tensor"),
        P("tensor", None),
        P(None, None, "tensor"),
        P("tensor", None),
        P(),
        P(),
        P(None, "tensor"),
        P("tensor"),
        P(),
        P(),
        P(None, "tensor"),
        P("tensor"),
        P(),
        P(),
    )
    out_specs = (
        P(("dp", "tensor"), None),
        P(("dp", "tensor"), None),
        P(None, None, "tensor"),
        P(None, None, "tensor"),
        P(),
        P(None, "tensor"),
        P("tensor", None),
        P("tensor", None),
        P("tensor"),
        P(),
        P(None, None, "tensor"),
        P(None, None, "tensor"),
        P(),
        P(None, "tensor"),
        P("tensor", None),
        P("tensor", None),
        P("tensor"),
        P(),
        P(),
        P(),
        P(),
    )
    return jax.shard_map(
        on_device, mesh=mesh, in_specs=in_specs, out_specs=out_specs, check_vma=False
    )
```

```python
import functools

import jax
import jax.numpy as jnp
from jax import lax
from jax.experimental import pallas as pl
from jax.experimental.pallas import tpu as pltpu
from jax.sharding import PartitionSpec as P

HD = 128
FF = 5461
SLOT = 2048
STEP = 10
DECAY = 1.0 - STEP ** (-0.8)
PREFIX_MAX = SLOT // 2
Q_BLOCK = 512

ln_eps = 1e-05
eps_one = 1e-30
eps_two = 0.001
clip_bound = 1.0
rate_base = 1.0
masked_score = -1e30
LOG2E = 1.4426950408889634
BF = jnp.bfloat16
F32 = jnp.float32


def dot(a, b, dims):
    return lax.dot_general(a, b, (dims, ((), ())), preferred_element_type=F32)


def ring_order(n):
    b_size = 2 if n <= 8 else 4
    a_size = n // b_size
    order = []
    for a in range(a_size):
        cols = list(range(1, b_size))
        order += [a * b_size + c for c in (cols[::-1] if a % 2 else cols)]
    for a in range(a_size - 1, -1, -1):
        order.append(a * b_size)
    return order


def cost(micros):
    return pl.CostEstimate(flops=int(micros * 1e9), transcendentals=0, bytes_accessed=4 << 20)


PUSH = pl.DeviceIdType.MESH
PIECES = 2
ROW_BLOCK = 64


def pick(index, table):
    out = jnp.int32(table[0])
    for k in range(1, len(table)):
        out = jnp.where(index == k, jnp.int32(table[k]), out)
    return out


def neighbours(n):
    order = ring_order(n)
    pos = pick(lax.axis_index("tensor"), [order.index(t) for t in range(n)])
    ahead = pick(lax.rem(pos + 1, n), order)
    behind = pick(lax.rem(pos + n - 1, n), order)
    return pos, [{"tensor": ahead}, {"tensor": behind}]


def chunk_places(n, pos, rows):
    places = []
    for t in range(n):
        place = ring_order(n).index(t)
        places.append(lax.rem(pos + (n - place), n) * rows)
        places.append(lax.rem(place - pos + n, n) * rows + rows // 2)
    return places


def other_core():
    me = lax.axis_index("dp")
    return {"dp": me + 1 - 2 * lax.rem(me, 2)}


def other_chips(n_x):
    core, chip = lax.rem(lax.axis_index("dp"), 2), lax.axis_index("dp") // 2
    return chip, [{"dp": 2 * lax.rem(chip + k, n_x) + core} for k in range(1, n_x)]


def greet(devices):
    barrier = pltpu.get_barrier_semaphore()
    for device in devices:
        pl.semaphore_signal(barrier, inc=1, device_id=device, device_id_type=PUSH)
    pl.semaphore_wait(barrier, len(devices))


def ring_copy(land, send_sem, recv_sem, sides, d, s, piece=None):
    src, dst, sem = land.at[d, s], land.at[d, s + 1], d
    if piece is not None:
        size = land.shape[2] // PIECES
        rows = pl.ds(piece * size, size)
        src, dst, sem = land.at[d, s, rows], land.at[d, s + 1, rows], d * PIECES + piece
    return pltpu.make_async_remote_copy(
        src_ref=src,
        dst_ref=dst,
        send_sem=send_sem.at[sem, s],
        recv_sem=recv_sem.at[sem, s],
        device_id=sides[d],
        device_id_type=PUSH,
    )


def ring_sent(n, copy, pieces=(None,)):
    def sent(s, carry):
        for d in range(2):
            for piece in pieces:
                copy(d, s, piece).wait_send()
        return carry

    lax.fori_loop(0, n - 1, sent, 0)


def gather_start(x_ref, land):
    half = x_ref.shape[0] // 2
    land[0, 0] = x_ref[:half, :]
    land[1, 0] = x_ref[half:, :]


def gather_step(n, copy, s):
    for d in range(2):

        @pl.when(s > 0)
        def _():
            copy(d, s - 1).wait_recv()

        @pl.when(s < n - 1)
        def _():
            copy(d, s).start()


def ring_gather(n, x_ref, land, send_sem, recv_sem, sides, work):
    copy = functools.partial(ring_copy, land, send_sem, recv_sem, sides)
    gather_start(x_ref, land)

    def step(s, carry):
        gather_step(n, copy, s)
        work(s)
        return carry

    lax.fori_loop(0, n, step, 0)
    ring_sent(n, copy)


def scatter_start(land):
    for d in range(2):
        land[d, 0] = jnp.zeros(land.shape[2:], land.dtype)


def scatter_step(n, copy, land, term_buf, finish, s):
    half = term_buf.shape[0] // 2
    size = half // PIECES
    for piece in range(PIECES):
        for d in range(2):
            part = slice(piece * size, (piece + 1) * size)
            rows = slice(d * half + piece * size, d * half + (piece + 1) * size)

            @pl.when(s > 0)
            def _():
                copy(d, s - 1, piece).wait_recv()

            total = land[d, s, part].astype(F32) + term_buf[rows, :]

            @pl.when(s < n - 1)
            def _():
                land[d, s, part] = total.astype(BF)
                copy(d, s, piece).start()

            @pl.when(s == n - 1)
            def _():
                finish(rows, total)


def ring_scatter(n, land, send_sem, recv_sem, sides, term_buf, term, work, finish):
    copy = functools.partial(ring_copy, land, send_sem, recv_sem, sides)
    scatter_start(land)

    def step(s, carry):
        term(lax.rem(s + 1, n))
        scatter_step(n, copy, land, term_buf, finish, s)
        work(s)
        return carry

    lax.fori_loop(0, n, step, 0)
    ring_sent(n, copy, range(PIECES))


def dot_columns(out, a, b, dims, block=512):
    width = b.shape[1]

    def columns(j, carry):
        at = pl.ds(pl.multiple_of(j * block, block), block)
        out(at, dot(a, b[:, at], dims))
        return carry

    lax.fori_loop(0, width // block, columns, 0)


def first_kernel(
    n, x_ref, seen_ref, ln_ref, w_ref, pair_hbm, act_ref, qkv_ref, seen_all, gu_ref,
    land, act_buf, seen_buf, pair_buf, send_sem, recv_sem, act_sem, seen_sem, pair_sem,
):
    ff, block = pair_hbm.shape[0], pair_buf.shape[1]
    ff_pad = gu_ref.shape[0] // 2
    n_pairs = ff_pad // block

    def pair_load(b):
        rows = min(block, ff - b * block)
        return pltpu.make_async_copy(
            pair_hbm.at[pl.ds(b * block, rows)], pair_buf.at[b % 2, pl.ds(0, rows)], pair_sem.at[b % 2]
        )

    def pair_start(b):
        if b * block + block > ff:
            pair_buf[b % 2] = jnp.zeros(pair_buf.shape[1:], BF)
        pair_load(b).start()

    for b in range(min(2, n_pairs)):
        pair_start(b)
    rows, cols = x_ref.shape[0], w_ref.shape[2]
    me = lax.axis_index("tensor")
    peers = [lax.rem(me + k, n) for k in range(1, n)]
    sides = neighbours(n)[1]
    greet([{"tensor": t} for t in peers])

    def seen_copy(k):
        return pltpu.make_async_remote_copy(
            src_ref=seen_ref, dst_ref=seen_buf.at[me], send_sem=seen_sem.at[0, k],
            recv_sem=seen_sem.at[1, k], device_id={"tensor": peers[k]}, device_id_type=PUSH,
        )

    def act_copy(s):
        place = pl.ds(pl.multiple_of(s * rows, rows), rows)
        return pltpu.make_async_copy(act_buf.at[s], act_ref.at[place], act_sem.at[s])

    def work(s):
        @pl.when(s == 0)
        def _():
            for k in range(n - 1):
                seen_copy(k).start()

        chunk = jnp.concatenate([land[0, s], land[1, s]], axis=0).astype(F32)
        act = layer_norm(chunk, ln_ref[0:1, :], ln_ref[1:2, :]).astype(BF)
        act_buf[s] = act
        act_copy(s).start()
        place = pl.ds(pl.multiple_of(s * rows, rows), rows)
        for k in range(3):
            qkv_ref[place, k * cols : (k + 1) * cols] = dot(act, w_ref[k], ((1,), (0,))).astype(BF)
        for b in range(n_pairs):

            @pl.when(s == b)
            def _():
                pair_load(b).wait()
                for i in range(2):
                    at = i * ff_pad + b * block
                    gu_ref[at : at + block, :] = pair_buf[b % 2, :, i, :]
                if b + 2 < n_pairs:
                    pair_start(b + 2)

    ring_gather(n, x_ref, land, send_sem, recv_sem, sides, work)
    seen_buf[me] = seen_ref[...]
    for k in range(n - 1):
        seen_copy(k).wait()
    seen_all[...] = seen_buf[...]

    def written(s, carry):
        act_copy(s).wait()
        return carry

    lax.fori_loop(0, n, written, 0)


def ring_scratch(n, rows, width, pieces=1):
    return [pltpu.VMEM((2, n, rows // 2, width), BF)], [
        pltpu.SemaphoreType.DMA((2 * pieces, n - 1)),
        pltpu.SemaphoreType.DMA((2 * pieces, n - 1)),
    ]


VMEM_SPEC = pl.BlockSpec(memory_space=pltpu.VMEM)
ANY_SPEC = pl.BlockSpec(memory_space=pl.ANY)


def first_gather(n, x, seen, ln_params, w, pairs):
    rows, width = x.shape
    cols = w.shape[2]
    block = 96
    ff_pad = -(-pairs.shape[0] // block) * block
    buf, sems = ring_scratch(n, rows, width)
    return pl.pallas_call(
        functools.partial(first_kernel, n),
        in_specs=[VMEM_SPEC] * 4 + [ANY_SPEC],
        out_specs=[ANY_SPEC] + [VMEM_SPEC] * 3,
        out_shape=[
            jax.ShapeDtypeStruct((n * rows, width), BF),
            jax.ShapeDtypeStruct((n * rows, 3 * cols), BF),
            jax.ShapeDtypeStruct((n,) + seen.shape, F32),
            jax.ShapeDtypeStruct((2 * ff_pad, width), BF),
        ],
        scratch_shapes=buf
        + [pltpu.VMEM((n, rows, width), BF), pltpu.VMEM((n,) + seen.shape, F32)]
        + [pltpu.VMEM((2, block, 2, width), BF)]
        + sems
        + [pltpu.SemaphoreType.DMA((n,)), pltpu.SemaphoreType.DMA((2, n - 1))]
        + [pltpu.SemaphoreType.DMA((2,))],
        compiler_params=pltpu.CompilerParams(
            collective_id=1, has_side_effects=True, vmem_limit_bytes=56 << 20
        ),
        cost_estimate=pl.CostEstimate(
            flops=6 * n * rows * width * cols, transcendentals=0, bytes_accessed=40 << 20
        ),
    )(x, seen, ln_params, w, pairs)


def grad_kernel(
    n, heads, x_ref, weight_ref, qkv_ref, thr_ref, real_ref, out_w_ref, qkv_w_hbm, gu_w_hbm, down_w_hbm,
    all_ref, ctx_ref, lse_ref, square_ref,
    land, own_ref, q_ref, k_ref, v_ref, qkv_w_ref, gu_w_ref, down_w_ref, send_sem, recv_sem, all_sem,
    load_sem,
):
    rows = x_ref.shape[0]
    half = rows // 2
    pos, sides = neighbours(n)
    places = chunk_places(n, pos, rows)
    loads = [
        pltpu.make_async_copy(src, dst, load_sem.at[i])
        for i, (src, dst) in enumerate(
            ((qkv_w_hbm, qkv_w_ref), (gu_w_hbm, gu_w_ref), (down_w_hbm, down_w_ref))
        )
    ]
    for load in loads:
        load.start()
    own_ref[...] = (x_ref[...].astype(F32) * weight_ref[...]).astype(BF)
    greet(sides)

    def all_copy(d, s):
        place = pl.ds(pl.multiple_of(s * rows + d * half, half), half)
        return pltpu.make_async_copy(land.at[d, s], all_ref.at[place], all_sem.at[d, s])

    def squares(i, ref, real):
        block, cols = ROW_BLOCK, ref.shape[1]

        def add(j, carry):
            at = pl.multiple_of(j * block, block)
            value = ref[pl.ds(at, block), :].astype(F32)
            value = value * value
            if real is not None:
                value = value * real[pl.ds(lax.rem(at, real.shape[0]), block), :]
            square_ref[i, :, :cols] += sum(value[k : k + 8] for k in range(0, block, 8))
            return carry

        lax.fori_loop(0, ref.shape[0] // block, add, 0)

    def work(s):
        for d in range(2):
            all_copy(d, s).start()
        for h in range(heads):

            @pl.when(s == h)
            def _():
                columns = lambda i: slice((i * heads + h) * HD, (i * heads + h + 1) * HD)
                for i, dst in enumerate((q_ref, k_ref, v_ref)):
                    to_order(places, qkv_ref, columns(i), dst)
                attn_forward_head(
                    places, thr_ref, lse_ref.at[h], q_ref, k_ref, v_ref, ctx_ref, columns(0)
                )

        @pl.when(s == heads)
        def _():
            square_ref[...] = jnp.zeros_like(square_ref)
            loads[0].wait()
            for k in range(3):
                squares(0, qkv_w_ref.at[k], None)

        @pl.when(s == heads + 1)
        def _():
            loads[1].wait()
            squares(1, gu_w_ref, real_ref)

        @pl.when(s == heads + 2)
        def _():
            squares(2, out_w_ref, None)
            loads[2].wait()
            squares(3, down_w_ref, real_ref)

    ring_gather(n, own_ref, land, send_sem, recv_sem, sides, work)

    def written(s, carry):
        for d in range(2):
            all_copy(d, s).wait()
        return carry

    lax.fori_loop(0, n, written, 0)


def grad_gather(n, x, weight, qkv, thr, real, qkv_w, gu_w, out_w, down_w):
    rows, width = x.shape
    cols = out_w.shape[0]
    heads = cols // HD
    buf, sems = ring_scratch(n, rows, width)
    return pl.pallas_call(
        functools.partial(grad_kernel, n, heads),
        in_specs=[VMEM_SPEC] * 6 + [ANY_SPEC] * 3,
        out_specs=[ANY_SPEC] + [VMEM_SPEC] * 3,
        out_shape=[
            jax.ShapeDtypeStruct((n * rows, width), BF),
            jax.ShapeDtypeStruct((n * rows, cols), BF),
            jax.ShapeDtypeStruct((heads, 1, SLOT), F32),
            jax.ShapeDtypeStruct((4, 8, width), F32),
        ],
        scratch_shapes=buf
        + [pltpu.VMEM((rows, width), BF)]
        + [pltpu.VMEM((SLOT, HD), BF)] * 3
        + [pltpu.VMEM(w.shape, BF) for w in (qkv_w, gu_w, down_w)]
        + sems
        + [pltpu.SemaphoreType.DMA((2, n)), pltpu.SemaphoreType.DMA((3,))],
        compiler_params=pltpu.CompilerParams(
            collective_id=5, has_side_effects=True, vmem_limit_bytes=60 << 20
        ),
        cost_estimate=cost(80),
    )(x, weight, qkv, thr, real, out_w, qkv_w, gu_w, down_w)


def mix_kernel(
    n, ctx_ref, w_ref, x_ref, ln_ref, hidden_ref, norm_ref, land, term_buf, send_sem, recv_sem
):
    rows = x_ref.shape[0]
    sides = neighbours(n)[1]
    greet(sides)

    def term(c):
        place = pl.ds(pl.multiple_of(c * rows, rows), rows)

        def put(at, value):
            term_buf[:, at] = value

        dot_columns(put, ctx_ref[place, :], w_ref, ((1,), (0,)))

    def finish(at, total):
        hidden = x_ref[at, :].astype(F32) + total
        hidden_ref[at, :] = hidden
        norm_ref[at, :] = layer_norm(hidden, ln_ref[2:3, :], ln_ref[3:4, :]).astype(BF)

    ring_scatter(n, land, send_sem, recv_sem, sides, term_buf, term, lambda s: None, finish)


def mix_scatter(n, context, w, x, ln_params):
    rows, width = x.shape
    buf, sems = ring_scratch(n, rows, width, PIECES)
    return pl.pallas_call(
        functools.partial(mix_kernel, n),
        in_specs=[VMEM_SPEC] * 4,
        out_specs=[VMEM_SPEC] * 2,
        out_shape=[
            jax.ShapeDtypeStruct((rows, width), F32),
            jax.ShapeDtypeStruct((rows, width), BF),
        ],
        scratch_shapes=buf + [pltpu.VMEM((rows, width), F32)] + sems,
        compiler_params=pltpu.CompilerParams(
            collective_id=6, has_side_effects=True, vmem_limit_bytes=40 << 20
        ),
        cost_estimate=cost(80),
    )(context, w, x, ln_params)


def gelu_pair(gate):
    c, a = (2.0 / jnp.pi) ** 0.5, 0.044715
    square = gate * gate
    t = jnp.tanh(c * gate * (1.0 + a * square))
    value = 0.5 * gate * (1.0 + t)
    slope = 0.5 * (1.0 + t) + 0.5 * gate * (1.0 - t * t) * (c * (1.0 + 3.0 * a * square))
    return value, slope


def both_kernel(
    n, x_ref, gu_w_ref, down_w_ref, real_ref, hidden_ref, cot_ref, weight_ref, ln_ref, grad_hbm,
    act_ref, inner_ref, d_gu_ref, out_ref, low_ref, ln_sum,
    land, sums, term_buf, gate_up, d_inner, grad_buf,
    send_sem, recv_sem, sum_send, sum_recv, act_sem, grad_sem,
):
    rows = x_ref.shape[0]
    half = rows // 2
    ff_pad = down_w_ref.shape[0]
    sides = neighbours(n)[1]
    copy = functools.partial(ring_copy, land, send_sem, recv_sem, sides)
    sum_copy = functools.partial(ring_copy, sums, sum_send, sum_recv, sides)

    def grad_load(s):
        place = pl.ds(pl.multiple_of(s * rows, rows), rows)
        slot = lax.rem(s, 2)
        return pltpu.make_async_copy(grad_hbm.at[place], grad_buf.at[slot], grad_sem.at[slot])

    def act_copy(d, s):
        place = pl.ds(pl.multiple_of(s * rows + d * half, half), half)
        return pltpu.make_async_copy(land.at[d, s], act_ref.at[place], act_sem.at[d, s])

    grad_load(0).start()
    grad_load(1).start()
    greet(sides)
    gather_start(x_ref, land)
    ln_sum[...] = jnp.zeros_like(ln_sum)
    scatter_start(sums)

    def by_rows(out, a, w_ref):
        block = 384

        def some(j, carry):
            at = pl.ds(pl.multiple_of(j * block, block), block)
            out[:, at] = dot(a, w_ref[at, :], ((1,), (1,)))
            return carry

        lax.fori_loop(0, w_ref.shape[0] // block, some, 0)

    def term(c):
        place = pl.ds(pl.multiple_of(c * rows, rows), rows)

        def put(at, value):
            term_buf[:, at] = value

        dot_columns(put, d_gu_ref[place, :], gu_w_ref, ((1,), (0,)))

    def finish(at, total):
        d_rows, sums_two = layer_norm_back(hidden_ref[at, :], ln_ref[2:3, :], total)
        d_rows = cot_ref[at, :].astype(F32) * weight_ref[at, :] + d_rows
        out_ref[at, :] = d_rows
        low_ref[at, :] = d_rows.astype(BF)
        ln_sum[...] += sums_two

    def step(s, carry):
        gather_step(n, copy, s)
        for d in range(2):
            act_copy(d, s).start()
        by_rows(gate_up, jnp.concatenate([land[0, s], land[1, s]], axis=0), gu_w_ref)
        grad_load(s).wait()
        by_rows(d_inner, grad_buf[lax.rem(s, 2)], down_w_ref)

        @pl.when(s < n - 2)
        def _():
            grad_load(s + 2).start()

        place = pl.ds(pl.multiple_of(s * rows, rows), rows)
        for at in range(0, ff_pad, 128):
            here, there = slice(at, at + 128), slice(ff_pad + at, ff_pad + at + 128)
            real = real_ref[:, here]
            gate, up = gate_up[:, here], gate_up[:, there]
            value, slope = gelu_pair(gate)
            back = d_inner[:, here] * real
            inner_ref[place, here] = (value * up * real).astype(BF)
            d_gu_ref[place, here] = (back * up * slope).astype(BF)
            d_gu_ref[place, there] = (back * value).astype(BF)

        @pl.when(s > 0)
        def _():
            term(s)
            scatter_step(n, sum_copy, sums, term_buf, finish, s - 1)

        return carry

    lax.fori_loop(0, n, step, 0)
    term(0)
    scatter_step(n, sum_copy, sums, term_buf, finish, n - 1)
    ring_sent(n, copy)
    ring_sent(n, sum_copy, range(PIECES))

    def written(s, carry):
        for d in range(2):
            act_copy(d, s).wait()
        return carry

    lax.fori_loop(0, n, written, 0)


def both_ways(n, x, gu_w, down_w, real, hidden, cotangent, weight, ln_params, grad):
    rows, width = x.shape
    ff_pad = down_w.shape[0]
    buf, sems = ring_scratch(n, rows, width)
    sum_buf, sum_sems = ring_scratch(n, rows, width, PIECES)
    return pl.pallas_call(
        functools.partial(both_kernel, n),
        in_specs=[VMEM_SPEC] * 8 + [ANY_SPEC],
        out_specs=[ANY_SPEC] + [VMEM_SPEC] * 5,
        out_shape=[
            jax.ShapeDtypeStruct((n * rows, width), BF),
            jax.ShapeDtypeStruct((n * rows, ff_pad), BF),
            jax.ShapeDtypeStruct((n * rows, 2 * ff_pad), BF),
            jax.ShapeDtypeStruct((rows, width), F32),
            jax.ShapeDtypeStruct((rows, width), BF),
            jax.ShapeDtypeStruct((2, width), F32),
        ],
        scratch_shapes=buf
        + sum_buf
        + [
            pltpu.VMEM((rows, width), F32),
            pltpu.VMEM((rows, 2 * ff_pad), F32),
            pltpu.VMEM((rows, ff_pad), F32),
            pltpu.VMEM((2, rows, width), BF),
        ]
        + sems
        + sum_sems
        + [pltpu.SemaphoreType.DMA((2, n)), pltpu.SemaphoreType.DMA((2,))],
        compiler_params=pltpu.CompilerParams(
            collective_id=7, has_side_effects=True, vmem_limit_bytes=60 << 20
        ),
        cost_estimate=cost(160),
    )(x, gu_w, down_w, real, hidden, cotangent, weight, ln_params, grad)


def back_kernel(
    n, n_x, x_ref, w_ref, ctx_ref, inner_hbm, d_gu_hbm, grad_hbm, act_hbm,
    d_ctx_ref, out_ref, mine_ref, slots_hbm,
    land, lhs, rhs, part, core_land, out_sum, send_sem, recv_sem, load_sem, core_sem, slot_sem,
):
    rows, ff_pad = x_ref.shape[0], lhs.shape[2]
    ff_rows, half = core_land.shape[1:]
    sides, partner = neighbours(n)[1], other_core()
    core = lax.rem(lax.axis_index("dp"), 2)
    loads = [
        pltpu.make_async_copy(src, dst, load_sem.at[i])
        for i, (src, dst) in enumerate(
            (
                (inner_hbm, lhs.at[0]),
                (grad_hbm, rhs.at[0]),
                (d_gu_hbm.at[:, pl.ds(0, ff_pad)], lhs.at[1]),
                (act_hbm, rhs.at[1]),
                (d_gu_hbm.at[:, pl.ds(ff_pad, ff_pad)], lhs.at[2]),
            )
        )
    ]
    for load in loads:
        load.start()
    out_sum[...] = jnp.zeros_like(out_sum)
    chip, chips = other_chips(n_x)
    greet(sides + [partner] + chips)

    def slot_copy(k):
        return pltpu.make_async_remote_copy(
            src_ref=mine_ref.at[0], dst_ref=slots_hbm.at[chip], send_sem=slot_sem.at[0, k],
            recv_sem=slot_sem.at[1, k], device_id=chips[k], device_id_type=PUSH,
        )

    def core_copy(i):
        return pltpu.make_async_remote_copy(
            src_ref=part.at[i, 1 - core],
            dst_ref=core_land.at[i],
            send_sem=core_sem.at[0, i],
            recv_sem=core_sem.at[1, i],
            device_id=partner,
            device_id_type=PUSH,
        )

    def work(s):
        chunk = jnp.concatenate([land[0, s], land[1, s]], axis=0)
        place = pl.ds(pl.multiple_of(s * rows, rows), rows)
        d_ctx_ref[place, :] = dot(chunk, w_ref[...], ((1,), (1,))).astype(BF)
        out_sum[...] += dot(ctx_ref[place, :], chunk, ((0,), (0,)))
        for i in range(3):
            for turn in range(2):

                @pl.when(s == 2 * i + turn)
                def _():
                    if turn == 0:
                        for load in (loads[:2], loads[2:4], loads[4:])[i]:
                            load.wait()
                    side = slice(turn * half, (turn + 1) * half)

                    def put(at, value):
                        part[i, turn, :, at] = value[:ff_rows].astype(BF)

                    dot_columns(put, lhs[i], rhs.at[min(i, 1), :, side], ((0,), (0,)))
                    if turn == 1:
                        core_copy(i).start()

            @pl.when(s == 2 * i + 3)
            def _():
                core_copy(i).wait()
                total = part[i, core].astype(F32) + core_land[i].astype(F32)
                mine_ref[i] = total.astype(BF)
                if i == 0:
                    for k in range(n_x - 1):
                        slot_copy(k).start()

    ring_gather(n, x_ref, land, send_sem, recv_sem, sides, work)
    out_ref[...] = out_sum[...].astype(BF)
    for k in range(n_x - 1):
        slot_copy(k).wait()


def back_gather(n, n_x, ff_dev, x, w, context, inner, d_gu, grad, act):
    rows, width = x.shape
    ff_pad = inner.shape[1]
    ff_rows = -(-ff_dev // ROW_BLOCK) * ROW_BLOCK
    buf, sems = ring_scratch(n, rows, width)
    return pl.pallas_call(
        functools.partial(back_kernel, n, n_x),
        in_specs=[VMEM_SPEC] * 3 + [ANY_SPEC] * 4,
        out_specs=[VMEM_SPEC] * 3 + [ANY_SPEC],
        out_shape=[
            jax.ShapeDtypeStruct((n * rows, w.shape[0]), BF),
            jax.ShapeDtypeStruct(w.shape, BF),
            jax.ShapeDtypeStruct((3, ff_rows, width // 2), BF),
            jax.ShapeDtypeStruct((n_x, ff_rows, width // 2), BF),
        ],
        scratch_shapes=buf
        + [
            pltpu.VMEM((3, n * rows, ff_pad), BF),
            pltpu.VMEM((2, n * rows, width), BF),
            pltpu.VMEM((3, 2, ff_rows, width // 2), BF),
            pltpu.VMEM((3, ff_rows, width // 2), BF),
            pltpu.VMEM(w.shape, F32),
        ]
        + sems
        + [
            pltpu.SemaphoreType.DMA((5,)),
            pltpu.SemaphoreType.DMA((2, 3)),
            pltpu.SemaphoreType.DMA((2, n_x - 1)),
        ],
        compiler_params=pltpu.CompilerParams(
            collective_id=3, has_side_effects=True, vmem_limit_bytes=60 << 20
        ),
        cost_estimate=cost(80),
    )(x, w, context, inner, d_gu, grad, act)


def ffn_kernel(
    n, n_x, heads, inner_ref, w_ref, hidden_ref, thr_ref, qkv_ref, d_ctx_ref, lse_ref,
    out_part_ref, act_hbm, mine_hbm,
    out_ref, d_qkv_ref, slots_hbm, out_slots_hbm, oq_mine_ref,
    land, term_buf, q_ref, k_ref, v_ref, do_ref, dk_sum, dv_sum,
    act_buf, part, qkv_land, out_land,
    send_sem, recv_sem, act_sem, core_sem, slot_sem,
):
    rows = hidden_ref.shape[0]
    pos, sides = neighbours(n)
    partner = other_core()
    core = lax.rem(lax.axis_index("dp"), 2)
    chip, chips = other_chips(n_x)
    block = act_buf.shape[2]
    blocks = act_hbm.shape[1] // block
    qkv_cols, wide = qkv_land.shape
    wide_of = lambda c: pl.ds(pl.multiple_of(c * wide, wide), wide)

    def act_load(j):
        return pltpu.make_async_copy(
            act_hbm.at[:, pl.ds(j * block, block)], act_buf.at[j % 2], act_sem.at[j]
        )

    def core_copy(i):
        src, dst = (
            (part.at[:, wide_of(1 - core)], qkv_land),
            (out_part_ref.at[:, wide_of(1 - core)], out_land),
        )[i]
        return pltpu.make_async_remote_copy(
            src_ref=src, dst_ref=dst, send_sem=core_sem.at[0, i], recv_sem=core_sem.at[1, i],
            device_id=partner, device_id_type=PUSH,
        )

    def slot_copy(i, k):
        src, dst = (
            (mine_hbm.at[pl.ds(1, 2)], slots_hbm),
            (oq_mine_ref.at[pl.ds(qkv_cols, oq_mine_ref.shape[0] - qkv_cols)], out_slots_hbm),
        )[i]
        return pltpu.make_async_remote_copy(
            src_ref=src, dst_ref=dst.at[chip], send_sem=slot_sem.at[0, i, k],
            recv_sem=slot_sem.at[1, i, k], device_id=chips[k], device_id_type=PUSH,
        )

    for j in range(2):
        act_load(j).start()
    greet(sides + [partner] + chips)
    core_copy(1).start()
    for k in range(n_x - 1):
        slot_copy(0, k).start()
    places = chunk_places(n, pos, rows)

    def term(c):
        place = pl.ds(pl.multiple_of(c * rows, rows), rows)

        def put(at, value):
            term_buf[:, at] = value

        dot_columns(put, inner_ref[place, :], w_ref, ((1,), (0,)))

    def work(s):
        for h in range(heads):

            columns = lambda i: slice((i * heads + h) * HD, (i * heads + h + 1) * HD)
            for turn in range(2):

                @pl.when(s == 2 * h + turn)
                def _():
                    if turn == 0:
                        for i, dst in enumerate((q_ref, k_ref, v_ref)):
                            to_order(places, qkv_ref, columns(i), dst)
                        to_order(places, d_ctx_ref, columns(0), do_ref)
                    attn_backward_head(
                        turn, places, thr_ref, lse_ref.at[h], q_ref, k_ref, v_ref, do_ref,
                        dk_sum, dv_sum, d_qkv_ref, columns,
                    )

        @pl.when(s == 1)
        def _():
            core_copy(1).wait()
            total = out_part_ref[:, wide_of(core)].astype(F32) + out_land[...].astype(F32)
            oq_mine_ref[qkv_cols:, :] = total.astype(BF)
            for k in range(n_x - 1):
                slot_copy(1, k).start()

        for turn in range(blocks // 2):

            @pl.when(s == 2 * heads + turn)
            def _():
                for j in (2 * turn, 2 * turn + 1):
                    act_load(j).wait()
                    grad = dot(d_qkv_ref[...], act_buf[j % 2], ((0,), (0,)))
                    part[:, j * block : (j + 1) * block] = grad.astype(BF)
                for j in (2 * turn + 2, 2 * turn + 3):
                    if j < blocks:
                        act_load(j).start()
                if turn == blocks // 2 - 1:
                    core_copy(0).start()

    def finish(at, total):
        out_ref[at, :] = (hidden_ref[at, :] + total).astype(BF)

    ring_scatter(n, land, send_sem, recv_sem, sides, term_buf, term, work, finish)
    core_copy(0).wait()
    total = part[:, wide_of(core)].astype(F32) + qkv_land[...].astype(F32)
    oq_mine_ref[:qkv_cols, :] = total.astype(BF)
    for k in range(n_x - 1):
        slot_copy(0, k).wait()
        slot_copy(1, k).wait()


def ffn_scatter(n, n_x, inner, w, hidden, thr, qkv, d_context, lse, out_part, act, mine):
    rows, width = hidden.shape
    cols, block = d_context.shape[1], 512
    heads = d_context.shape[1] // HD
    buf, sems = ring_scratch(n, rows, width, PIECES)
    return pl.pallas_call(
        functools.partial(ffn_kernel, n, n_x, heads),
        in_specs=[VMEM_SPEC] * 8 + [ANY_SPEC] * 2,
        out_specs=[VMEM_SPEC] * 2 + [ANY_SPEC] * 2 + [VMEM_SPEC],
        out_shape=[
            jax.ShapeDtypeStruct((rows, width), BF),
            jax.ShapeDtypeStruct(qkv.shape, BF),
            jax.ShapeDtypeStruct((n_x, 2) + mine.shape[1:], BF),
            jax.ShapeDtypeStruct((n_x, cols, width // 2), BF),
            jax.ShapeDtypeStruct((4 * cols, width // 2), BF),
        ],
        scratch_shapes=buf
        + [pltpu.VMEM((rows, width), F32)]
        + [pltpu.VMEM((SLOT, HD), BF)] * 4
        + [pltpu.VMEM((SLOT, HD), F32)] * 2
        + [
            pltpu.VMEM((2, n * rows, block), BF),
            pltpu.VMEM((3 * cols, width), BF),
            pltpu.VMEM((3 * cols, width // 2), BF),
            pltpu.VMEM((cols, width // 2), BF),
        ]
        + sems
        + [
            pltpu.SemaphoreType.DMA((width // block,)),
            pltpu.SemaphoreType.DMA((2, 2)),
            pltpu.SemaphoreType.DMA((2, 2, n_x - 1)),
        ],
        compiler_params=pltpu.CompilerParams(
            collective_id=4, has_side_effects=True, vmem_limit_bytes=62 << 20
        ),
        cost_estimate=cost(95),
    )(inner, w, hidden, thr, qkv, d_context, lse, out_part, act, mine)


def row_sums(grad_ref, old_ref, real_ref, new_ref, c_ref, t_ref):
    width = grad_ref.shape[1]
    block = ROW_BLOCK

    def rows(i, carry):
        at = pl.ds(pl.multiple_of(i * block, block), block)
        grad = grad_ref[at, :].astype(F32)
        square = grad * grad
        real = 1.0 if real_ref is None else real_ref[at, :]
        total = (jnp.sum(square, axis=1, keepdims=True) + width * eps_one) * real
        new = DECAY * old_ref[at, :] + (1.0 - DECAY) * (total / width)
        new_ref[at, :] = new
        c = (square + eps_one) * real
        t = square * (real / new)
        c_ref[...] += sum(c[k : k + 8] for k in range(0, block, 8))
        t_ref[...] += sum(t[k : k + 8] for k in range(0, block, 8))
        return carry

    lax.fori_loop(0, grad_ref.shape[0] // block, rows, 0)


def last_kernel(
    n, n_x, d_qkv_ref, w_ref, oq_mine_ref, oq_old, ff_old, ff_real,
    x_ref, d_hidden_ref, ln_ref,
    mine_hbm, down_hbm, gu_hbm, out_hbm,
    out_ref, goq_hbm, gff_hbm, oq_new, ff_new, sums_ref, ln_sum, totals_ref,
    land, term_buf, goq_ref, gff_ref, qkv_land, out_slots, ff_own, ff_slots, c_sum, t_sum,
    send_sem, recv_sem, oq_sem, load_sem, join_sem, write_sem,
):
    rows = term_buf.shape[0]
    cols, width = w_ref.shape[2], term_buf.shape[1]
    sides, partner = neighbours(n)[1], other_core()
    core = lax.rem(lax.axis_index("dp"), 2)
    chip, chips = other_chips(n_x)
    half = width // 2
    own = pl.ds(pl.multiple_of(core * half, half), half)

    qkv_rows, out_rows = pl.ds(0, 3 * cols), pl.ds(3 * cols, cols)
    writes = [
        pltpu.make_async_copy(goq_ref, goq_hbm, write_sem.at[0]),
        pltpu.make_async_copy(gff_ref, gff_hbm, write_sem.at[1]),
    ]

    def loads(i):
        if i == 3:
            return [pltpu.make_async_copy(out_hbm, out_slots, load_sem.at[0, 3])]
        slots = down_hbm if i == 0 else gu_hbm.at[:, i - 1]
        return [
            pltpu.make_async_copy(mine_hbm.at[i], ff_own.at[i], load_sem.at[0, i]),
            pltpu.make_async_copy(slots, ff_slots.at[i], load_sem.at[1, i]),
        ]

    def oq_copy(k):
        return pltpu.make_async_remote_copy(
            src_ref=oq_mine_ref.at[qkv_rows], dst_ref=qkv_land.at[chip], send_sem=oq_sem.at[0, k],
            recv_sem=oq_sem.at[1, k], device_id=chips[k], device_id_type=PUSH,
        )

    def join(i):
        ref = gff_ref.at[i, :, own] if i < 3 else goq_ref.at[(qkv_rows, out_rows)[i - 3], own]
        return pltpu.make_async_remote_copy(
            src_ref=ref, dst_ref=ref, send_sem=join_sem.at[0, i], recv_sem=join_sem.at[1, i],
            device_id=partner, device_id_type=PUSH,
        )

    def chip_sum(own_half, slots):
        total = jnp.zeros(own_half.shape, F32)
        for x in range(n_x):
            total = total + jnp.where(chip == x, own_half, slots[x]).astype(F32)
        return total.astype(BF)

    for i in range(4):
        for load in loads(i):
            load.start()
    ln_sum[...] = jnp.zeros_like(ln_sum)
    greet(sides + [partner] + chips)
    for k in range(n_x - 1):
        oq_copy(k).start()

    def term(c):
        place = pl.ds(pl.multiple_of(c * rows, rows), rows)
        block = 512

        def columns(j, carry):
            at = pl.ds(pl.multiple_of(j * block, block), block)
            term_buf[:, at] = sum(
                dot(d_qkv_ref[place, k * cols : (k + 1) * cols], w_ref[k, at, :], ((1,), (1,)))
                for k in range(3)
            )
            return carry

        lax.fori_loop(0, width // block, columns, 0)

    def sums(group, ref, first=True):
        if first:
            c_sum[...] = jnp.zeros_like(c_sum)
            t_sum[...] = jnp.zeros_like(t_sum)
        row_sums(*ref, c_sum, t_sum)
        sums_ref[2 * group : 2 * group + 1, :] = jnp.sum(c_sum[...], axis=0, keepdims=True)
        sums_ref[2 * group + 1 : 2 * group + 2, :] = jnp.sum(t_sum[...], axis=0, keepdims=True)

    ff_refs = lambda i: (gff_ref.at[i], ff_old.at[i], ff_real, ff_new.at[i])
    oq_refs = lambda at: (goq_ref.at[at], oq_old.at[at], None, oq_new.at[at])

    def work(s):
        for i in range(3):

            @pl.when(s == i)
            def _():
                for load in loads(i):
                    load.wait()
                gff_ref[i, :, own] = chip_sum(ff_own[i], ff_slots.at[i])
                join(i).start()

        @pl.when(s == 0)
        def _():
            for load in loads(3):
                load.wait()
            goq_ref[out_rows, own] = chip_sum(oq_mine_ref[out_rows, :], out_slots)
            join(4).start()

        @pl.when(s == 3)
        def _():
            join(0).wait()
            sums(3, ff_refs(0))

        @pl.when(s == 4)
        def _():
            for k in range(n_x - 1):
                oq_copy(k).wait()
            goq_ref[qkv_rows, own] = chip_sum(oq_mine_ref[qkv_rows, :], qkv_land)
            join(3).start()

        @pl.when(s == 5)
        def _():
            join(1).wait()
            sums(1, ff_refs(1))

        @pl.when(s == 6)
        def _():
            join(2).wait()
            sums(1, ff_refs(2), first=False)
            writes[1].start()
            join(4).wait()
            sums(2, oq_refs(out_rows))
            join(3).wait()
            sums(0, oq_refs(qkv_rows))
            writes[0].start()
            down_new = ff_new[0] * ff_real[: ff_new.shape[1], :]
            for i, new in enumerate((oq_new[out_rows, :], down_new)):
                total = jnp.sum(new, axis=0, keepdims=True)
                totals_ref[i : i + 1, :] = jnp.broadcast_to(total, (1, totals_ref.shape[1]))

    def finish(at, total):
        d_rows, sums_one = layer_norm_back(x_ref[at, :].astype(F32), ln_ref[0:1, :], total)
        out_ref[at, :] = (d_hidden_ref[at, :] + d_rows).astype(BF)
        ln_sum[...] += sums_one

    ring_scatter(n, land, send_sem, recv_sem, sides, term_buf, term, work, finish)
    for write in writes:
        write.wait()


def last_scatter(
    n, n_x, d_qkv, w, oq_mine, oq_old, ff_old, ff_real, ff_mine, down_slots, gu_slots, out_slots,
    x, d_hidden, ln_params,
):
    width, cols = w.shape[1:]
    rows = d_qkv.shape[0] // n
    half = width // 2
    ff_rows = ff_mine.shape[1]
    buf, sems = ring_scratch(n, rows, width, PIECES)
    return pl.pallas_call(
        functools.partial(last_kernel, n, n_x),
        in_specs=[VMEM_SPEC] * 9 + [ANY_SPEC] * 4,
        out_specs=[VMEM_SPEC] + [ANY_SPEC] * 2 + [VMEM_SPEC] * 5,
        out_shape=[
            jax.ShapeDtypeStruct((rows, width), BF),
            jax.ShapeDtypeStruct((4 * cols, width), BF),
            jax.ShapeDtypeStruct((3, ff_rows, width), BF),
            jax.ShapeDtypeStruct(oq_old.shape, F32),
            jax.ShapeDtypeStruct(ff_old.shape, F32),
            jax.ShapeDtypeStruct((8, width), F32),
            jax.ShapeDtypeStruct((2, width), F32),
            jax.ShapeDtypeStruct((8, 128), F32),
        ],
        scratch_shapes=buf
        + [
            pltpu.VMEM((rows, width), F32),
            pltpu.VMEM((4 * cols, width), BF),
            pltpu.VMEM((3, ff_rows, width), BF),
            pltpu.VMEM((n_x, 3 * cols, half), BF),
            pltpu.VMEM((n_x, cols, half), BF),
            pltpu.VMEM((3, ff_rows, half), BF),
            pltpu.VMEM((3, n_x, ff_rows, half), BF),
            pltpu.VMEM((8, width), F32),
            pltpu.VMEM((8, width), F32),
        ]
        + sems
        + [
            pltpu.SemaphoreType.DMA((2, n_x - 1)),
            pltpu.SemaphoreType.DMA((2, 4)),
            pltpu.SemaphoreType.DMA((2, 5)),
            pltpu.SemaphoreType.DMA((2,)),
        ],
        compiler_params=pltpu.CompilerParams(
            collective_id=2, has_side_effects=True, vmem_limit_bytes=62 << 20
        ),
        cost_estimate=cost(90),
    )(
        d_qkv, w, oq_mine, oq_old, ff_old, ff_real, x, d_hidden, ln_params,
        ff_mine, down_slots, gu_slots, out_slots,
    )


def norm_stats(rows):
    mean_row = jnp.mean(rows, axis=-1, keepdims=True)
    centered = rows - mean_row
    variance = jnp.mean(centered * centered, axis=-1, keepdims=True)
    scale = lax.rsqrt(variance + ln_eps)
    return centered * scale, scale


def layer_norm(rows, gain, shift):
    return norm_stats(rows)[0] * gain + shift


def layer_norm_back(rows, gain, e):
    n, scale = norm_stats(rows)
    eg = e * gain
    dv = scale * (
        eg - jnp.mean(eg, axis=-1, keepdims=True) - n * jnp.mean(eg * n, axis=-1, keepdims=True)
    )
    sums = [jnp.sum(x, axis=0, keepdims=True) for x in (e * n, e)]
    return dv, jnp.concatenate(sums, axis=0)


def seen_mask(thr_ref, q0, shape):
    thr = thr_ref[: shape[0], :]
    thr = jnp.concatenate([thr] * (shape[1] // thr.shape[1]), axis=1)
    q_pos = (q0 + lax.broadcasted_iota(jnp.int32, shape, 1)).astype(F32)
    return q_pos >= thr


def q_blocks():
    return [(q0, max(PREFIX_MAX, q0 + Q_BLOCK)) for q0 in range(0, SLOT, Q_BLOCK)]


def to_order(places, src_ref, columns, dst_ref):
    half = SLOT // len(places)
    for j, start in enumerate(places):
        place = pl.ds(pl.multiple_of(start, half), half)
        dst_ref[j * half : (j + 1) * half, :] = src_ref[place, columns]


def from_order(places, q0, value, dst_ref, columns):
    half = SLOT // len(places)
    for i in range(value.shape[0] // half):
        place = pl.ds(pl.multiple_of(places[q0 // half + i], half), half)
        dst_ref[place, columns] = value[i * half : (i + 1) * half, :]


def attn_forward_head(places, thr_ref, lse_ref, q_ref, k_ref, v_ref, o_ref, columns):
    c = HD**-0.5 * LOG2E
    for q0, klim in q_blocks():
        raw = dot(k_ref[:klim, :], q_ref[q0 : q0 + Q_BLOCK, :], ((1,), (1,)))
        raw = jnp.where(seen_mask(thr_ref, q0, raw.shape), raw, masked_score)
        top = jnp.max(raw, axis=0, keepdims=True)
        p = jnp.exp2((raw - top) * c)
        total = jnp.sum(p, axis=0, keepdims=True)
        out = dot(v_ref[:klim, :], p.astype(BF), ((0,), (0,))) / total
        from_order(places, q0, out.T.astype(BF), o_ref, columns)
        lse_ref[:, q0 : q0 + Q_BLOCK] = top * c + jnp.log2(total)


def attn_backward_head(
    turn, places, thr_ref, lse_ref, q_ref, k_ref, v_ref, do_ref, dk_sum, dv_sum, d_ref, columns
):
    scale = HD**-0.5
    blocks = q_blocks()
    if turn == 0:
        dk_sum[...] = jnp.zeros_like(dk_sum)
        dv_sum[...] = jnp.zeros_like(dv_sum)
    for q0, klim in (blocks[-1:] + blocks[:1], blocks[1:-1])[turn]:
        rows = slice(q0, q0 + Q_BLOCK)
        k, q, do = k_ref[:klim, :], q_ref[rows, :], do_ref[rows, :]
        raw = dot(k, q, ((1,), (1,)))
        p = jnp.exp2(raw * (scale * LOG2E) - lse_ref[:, rows])
        p = jnp.where(seen_mask(thr_ref, q0, raw.shape), p, 0.0)
        dv_sum[:klim, :] += dot(p.astype(BF), do, ((1,), (0,)))
        dp = dot(v_ref[:klim, :], do, ((1,), (1,)))
        delta = jnp.sum(p * dp, axis=0, keepdims=True)
        ds = (p * (dp - delta) * scale).astype(BF)
        dk_sum[:klim, :] += dot(ds, q, ((1,), (0,)))
        dq = dot(k, ds, ((0,), (0,))).T.astype(BF)
        from_order(places, q0, dq, d_ref, columns(0))
    if turn == 1:
        from_order(places, 0, dk_sum[...].astype(BF), d_ref, columns(1))
        from_order(places, 0, dv_sum[...].astype(BF), d_ref, columns(2))


def step_rate(update_sq, weight_sq, n_real):
    update_rms = jnp.sqrt(update_sq / n_real)
    weight_rms = jnp.sqrt(weight_sq / n_real)
    return rate_base * jnp.maximum(eps_two, weight_rms) / jnp.maximum(1.0, update_rms / clip_bound)


def results_kernel(
    counts, factor_ref, goq_qkv, goq_out, gff_down, gff_gate, gff_up,
    w_qkv, w_out, w_down, w_gate, w_up, r_qkv, r_out, r_down, r_gate, r_up, *refs,
):
    n_small = (len(refs) - 8) // 2
    small, small_out = refs[:n_small], refs[n_small + 8 :]
    qkv_grad, qkv_new, out_grad, out_new, gu_grad, gu_new, down_grad, down_new = refs[n_small:][:8]
    t = pl.program_id(0)
    n_gu, n_qkv, n_down, n_out = counts

    def after(grad, weight, row, factor):
        return weight.astype(F32) - grad * (lax.rsqrt(row) * factor)

    @pl.when(t == 0)
    def _():
        for src, dst in zip(small, small_out):
            dst[...] = src[...]

    @pl.when(t < n_gu)
    def _():
        factor = factor_ref[1:2, :]
        for i, (g, w, r) in enumerate(((gff_gate, w_gate, r_gate), (gff_up, w_up, r_up))):
            grad = g[0].astype(F32)
            gu_grad[:, i, :] = grad
            gu_new[:, i, :] = after(grad, w[...], r[0], factor)

    start = n_gu
    @pl.when((t >= start) & (t < start + n_qkv))
    def _():
        block = goq_qkv.shape[1]
        at = lax.rem(t - n_gu, factor_ref.shape[1] // block) * block
        factor = factor_ref[0:1, pl.ds(pl.multiple_of(at, block), block)]
        grad = goq_qkv[...].astype(F32).T
        qkv_grad[0] = grad
        down = jnp.broadcast_to(factor, (128, block)).T[:, 0:1]
        along = jnp.broadcast_to(lax.rsqrt(r_qkv[...]), (grad.shape[1], 128)).T[0:1, :]
        qkv_new[0] = w_qkv[0].astype(F32) - grad * (down * along)

    start = n_gu + n_qkv

    @pl.when((t >= start) & (t < start + n_down))
    def _():
        grad = gff_down[0].astype(F32)
        down_grad[...] = grad
        down_new[...] = after(grad, w_down[...], r_down[0], factor_ref[3:4, :])

    @pl.when(t >= n_gu + n_qkv + n_down)
    def _():
        grad = goq_out[...].astype(F32)
        out_grad[...] = grad
        out_new[...] = after(grad, w_out[...], r_out[...], factor_ref[2:3, :])


def results(ff, factors, goq, gff, w_qkv, w_out, w_down, w_gu, oq_new, ff_new, small):
    kinds, width, cols = w_qkv.shape
    rows, wide, high = 96, 1024, 128
    counts = (-(-ff // rows), kinds * width // wide, -(-ff // rows), cols // high)
    starts = [sum(counts[:i]) for i in range(4)]
    per_kind = width // wide
    place = lambda part: lambda t: jnp.clip(t - starts[part], 0, counts[part] - 1)
    gu, qkv, down, out = (place(part) for part in range(4))
    shift = w_gu.shape[0] // 2 // rows
    third = lambda k, part, last: pl.BlockSpec((1, rows, last), lambda t: (k, part(t), 0))
    by_kind = lambda t: (qkv(t) // per_kind, lax.rem(qkv(t), per_kind), 0)
    out_at = 3 * cols // high
    qkv_spec = pl.BlockSpec((1, wide, cols), by_kind)
    out_spec = pl.BlockSpec((high, width), lambda t: (out(t), 0))
    gu_spec = pl.BlockSpec((rows, 2, width), lambda t: (gu(t), 0, 0))
    down_spec = pl.BlockSpec((rows, width), lambda t: (down(t), 0))
    shape = lambda *dims: jax.ShapeDtypeStruct(dims, F32)
    whole = [pl.BlockSpec(x.shape, lambda t: (0, 0)) for x in small]
    return pl.pallas_call(
        functools.partial(results_kernel, counts),
        grid=(sum(counts),),
        in_specs=[
            pl.BlockSpec(factors.shape, lambda t: (0, 0)),
            pl.BlockSpec((cols, wide), lambda t: by_kind(t)[:2]),
            pl.BlockSpec((high, width), lambda t: (out_at + out(t), 0)),
            third(0, down, width),
            third(1, gu, width),
            third(2, gu, width),
            qkv_spec,
            out_spec,
            down_spec,
            pl.BlockSpec((rows, width), lambda t: (gu(t), 0)),
            pl.BlockSpec((rows, width), lambda t: (gu(t) + shift, 0)),
            pl.BlockSpec((cols, 1), lambda t: (by_kind(t)[0], 0)),
            pl.BlockSpec((high, 1), lambda t: (out_at + out(t), 0)),
            third(0, down, 1),
            third(1, gu, 1),
            third(2, gu, 1),
        ]
        + whole,
        out_specs=[qkv_spec, qkv_spec, out_spec, out_spec, gu_spec, gu_spec, down_spec, down_spec]
        + whole,
        out_shape=[shape(kinds, width, cols)] * 2
        + [shape(cols, width)] * 2
        + [shape(ff, 2, width)] * 2
        + [shape(ff, width)] * 2
        + [shape(*x.shape) for x in small],
        compiler_params=pltpu.CompilerParams(vmem_limit_bytes=56 << 20),
        cost_estimate=cost(28),
    )(
        factors, goq, goq, gff, gff, gff, w_qkv, w_out, w_down, w_gu, w_gu,
        oq_new, oq_new, ff_new, ff_new, ff_new, *small,
    )


def exchange_kernel(
    n_dp, n, cells, one_ref, two_ref, sums_ref, totals_ref, squares_ref, old_ref, ln_ref, second_ref,
    factor_ref, qkv_row, gu_row, out_col, down_col, ln_tot, ln_second, ln_new,
    x_ref, o_ref, dp_buf, rows, part_buf, total, whole, sems,
):
    me_d, me = lax.axis_index("dp"), lax.axis_index("tensor")
    width = x_ref.shape[1] // n
    columns = lambda t: pl.ds(pl.multiple_of(t * width, width), width)
    dp_peers = [(k - 1, lax.rem(me_d + k, n_dp)) for k in range(1, n_dp)]
    peers = [(k - 1, lax.rem(me + k, n)) for k in range(1, n)]
    barrier = pltpu.get_barrier_semaphore()
    for _, d in dp_peers:
        pl.semaphore_signal(barrier, inc=1, device_id={"dp": d}, device_id_type=pl.DeviceIdType.MESH)
    for _, t in peers:
        pl.semaphore_signal(barrier, inc=1, device_id={"tensor": t}, device_id_type=pl.DeviceIdType.MESH)
    pl.semaphore_wait(barrier, n_dp + n - 2)

    def push(stage, src, dst, k, device):
        copy = pltpu.make_async_remote_copy(
            src_ref=src, dst_ref=dst, send_sem=sems.at[0, stage, k], recv_sem=sems.at[1, stage, k],
            device_id=device, device_id_type=pl.DeviceIdType.MESH,
        )
        copy.start()
        return copy

    x_ref[0:2, :] = one_ref[...]
    x_ref[2:4, :] = two_ref[...]
    x_ref[4:8, :] = jnp.zeros((4, x_ref.shape[1]), F32)
    lane = lax.broadcasted_iota(jnp.int32, (1, 128), 1)
    add_up = lambda v: jnp.sum(jnp.sum(v, axis=0, keepdims=True), axis=1, keepdims=True)
    scalars = [add_up(squares_ref[i]) for i in range(4)] + [totals_ref[i : i + 1, 0:1] for i in range(2)]
    x_ref[4:5, 0:128] = sum(jnp.where(lane == i, v, 0.0) for i, v in enumerate(scalars)) / n_dp
    x_ref[8:16, :] = sums_ref[...]
    first = [push(0, x_ref.at[pl.ds(0, 8)], dp_buf.at[me_d], k, {"dp": d}) for k, d in dp_peers]
    rows[...] = x_ref[...]
    dp_buf[me_d] = x_ref[0:8, :]
    for copy in first:
        copy.wait()
    rows[0:8, :] = sum(dp_buf[d] for d in range(n_dp))
    second = [push(1, rows.at[:, columns(t)], part_buf.at[me], k, {"tensor": t}) for k, t in peers]
    part_buf[me] = rows[:, columns(me)]
    for copy in second:
        copy.wait()
    total[...] = sum(part_buf[t] for t in range(n))
    third = [push(2, total, whole.at[me], k, {"tensor": t}) for k, t in peers]
    whole[me] = total[...]
    for copy in third:
        copy.wait()
    for t in range(n):
        o_ref[:, t * width : (t + 1) * width] = whole[t]

    columns_all = x_ref.shape[1]
    blend = lambda old, new: DECAY * old + (1.0 - DECAY) * new
    mean_of = lambda v: jnp.sum(v, axis=1, keepdims=True) / columns_all
    at = lambda i: o_ref[i : i + 1, :]
    scalar = lambda i: o_ref[4:5, i : i + 1]
    news = (qkv_row, gu_row, out_col, down_col)
    for i, (new_ref, (count, real, by_row)) in enumerate(zip(news, cells)):
        new = blend(old_ref[i : i + 1, :], at(8 + 2 * i) / count)
        new_ref[...] = new
        mean = mean_of(new) if by_row else scalar(2 + i) / count
        update_sq = jnp.sum(at(9 + 2 * i) / new, axis=1, keepdims=True) * mean
        rate = step_rate(update_sq, scalar(i), real)
        factor_ref[i : i + 1, :] = lax.rsqrt(new) * (rate * jnp.sqrt(mean))
    grad, weight = o_ref[0:4, :], ln_ref[...]
    second = blend(second_ref[...], grad * grad + eps_one)
    update = grad * lax.rsqrt(second)
    update_rms = jnp.sqrt(mean_of(update * update))
    weight_rms = jnp.sqrt(mean_of(weight * weight))
    ln_tot[...] = grad
    ln_second[...] = second
    ln_new[...] = weight - rate_base * jnp.maximum(eps_two, weight_rms) * update / jnp.maximum(
        1.0, update_rms / clip_bound
    )


def exchange(n_dp, n, cells, ln_one, ln_two, sums, totals, squares, old, ln_params, ln_second):
    height, width = 16, sums.shape[1]
    slots = pltpu.VMEM((n, height, width // n), F32)
    shape = lambda *dims: jax.ShapeDtypeStruct(dims, F32)
    return pl.pallas_call(
        functools.partial(exchange_kernel, n_dp, n, cells),
        out_shape=[shape(4, width)] + [shape(1, width)] * 4 + [shape(4, width)] * 3,
        in_specs=[VMEM_SPEC] * 8,
        out_specs=[VMEM_SPEC] * 8,
        scratch_shapes=[
            pltpu.VMEM((height, width), F32),
            pltpu.VMEM((height, width), F32),
            pltpu.VMEM((n_dp, 8, width), F32),
            pltpu.VMEM((height, width), F32),
            slots,
            pltpu.VMEM((height, width // n), F32),
            slots,
            pltpu.SemaphoreType.DMA((2, 3, max(n, n_dp) - 1)),
        ],
        compiler_params=pltpu.CompilerParams(collective_id=0, has_side_effects=True),
        cost_estimate=cost(18),
    )(ln_one, ln_two, sums, totals, squares, old, ln_params, ln_second)


def on_device(
    layer_in,
    cotangent,
    lengths,
    prefix,
    pad_mask,
    clusters,
    qkv_w,
    out_w,
    gate_up_w,
    down_w,
    ln_params,
    qkv_row,
    qkv_col,
    out_row,
    out_col,
    gu_row,
    gu_col,
    down_row,
    down_col,
    ln_second,
):
    n_data = lax.axis_size("dp")
    n_tensor = lax.axis_size("tensor")
    tensor_rank = lax.axis_index("tensor")
    data_rank = lax.axis_index("dp")
    rows_dev, width = layer_in.shape
    cols_dev = qkv_w.shape[2]
    heads_dev = cols_dev // HD
    ff_dev = gate_up_w.shape[2]
    ff_pad = -(-ff_dev // 384) * 384
    n_clusters = max(2, n_data // 2)
    seq_length = lengths[0]
    seq_prefix = prefix[0]

    onehot = (clusters[:, None] == jnp.arange(n_clusters, dtype=jnp.int32)[None, :]).astype(F32)
    counts = jnp.sum(onehot, axis=0)
    own_row = jnp.sum(
        jnp.where((jnp.arange(n_data, dtype=jnp.int32) == data_rank)[:, None], onehot, 0.0), axis=0
    )
    seq_weight = jnp.sum(own_row / jnp.maximum(counts, 1.0))
    own_pos = tensor_rank * rows_dev + jnp.arange(rows_dev, dtype=jnp.int32)
    live_rows = ((own_pos < seq_length) & (pad_mask == 1)).astype(F32)
    row_weight = (live_rows * seq_weight)[:, None]

    key_live = (own_pos == 0) | (own_pos < seq_length) & (pad_mask == 1)
    seen_from = jnp.where(key_live, jnp.where(own_pos < seq_prefix, 0, own_pos), 2 * SLOT)
    seen = jnp.broadcast_to(seen_from.astype(F32)[None], (8, rows_dev))

    col_index = tensor_rank * ff_dev + jnp.arange(ff_pad, dtype=jnp.int32)
    ff_real = ((col_index < FF) & (jnp.arange(ff_pad) < ff_dev)).astype(F32)
    ff_mask = ff_real[:ff_dev]

    act_one_all, qkv, seen_all, w_gu = first_gather(
        n_tensor, layer_in, seen, ln_params, jnp.transpose(qkv_w, (1, 0, 2)),
        jnp.transpose(gate_up_w, (2, 1, 0)),
    )
    thr = jnp.broadcast_to(seen_all[:, 0].reshape(SLOT, 1), (SLOT, 128))

    pad = ((0, ff_pad - ff_dev), (0, 0))
    w_down = jnp.pad(down_w, pad)
    real_column = ff_real[:, None]
    qkv_t = jnp.transpose(qkv_w, (1, 0, 2))

    grad_all, context, lse, squares = grad_gather(
        n_tensor, cotangent, row_weight, qkv, thr, real_column, qkv_t, w_gu, out_w, w_down
    )
    hidden_own, norm_two = mix_scatter(n_tensor, context, out_w, layer_in, ln_params)

    act_two_all, inner_all, d_gu_all, d_hidden, d_hidden_low, ln_two_part = both_ways(
        n_tensor, norm_two, w_gu, w_down, ff_real[None, :], hidden_own, cotangent, row_weight,
        ln_params, grad_all,
    )

    n_x = n_data // 2
    d_context, out_part, ff_mine, down_slots = back_gather(
        n_tensor, n_x, ff_dev, d_hidden_low, out_w, context,
        inner_all, d_gu_all, grad_all, act_two_all,
    )

    layer_out, d_qkv, gu_slots, out_slots, oq_mine = ffn_scatter(
        n_tensor, n_x, inner_all, w_down, hidden_own, thr, qkv, d_context, lse,
        out_part, act_one_all, ff_mine,
    )

    ff_rows = ff_mine.shape[1]
    more = ((0, 0), (0, ff_rows - ff_dev))
    oq_old = jnp.concatenate([qkv_col.reshape(-1), out_row])[:, None]
    ff_old = jnp.pad(jnp.concatenate([down_row[None], gu_col]), more, constant_values=1.0)[:, :, None]
    input_grad, goq, gff, oq_new, ff_new, sums, ln_one_part, totals = last_scatter(
        n_tensor, n_x, d_qkv, qkv_t, oq_mine, oq_old, ff_old, real_column,
        ff_mine, down_slots, gu_slots, out_slots, layer_in, d_hidden, ln_params,
    )
    qkv_col_new, out_row_new = oq_new[: 3 * cols_dev, 0], oq_new[3 * cols_dev :, 0]
    down_row_new, gu_col_new = ff_new[0, :ff_dev, 0], ff_new[1:, :ff_dev, 0]

    rows_all = cols_dev * n_tensor
    cells = (
        (3 * rows_all, width * 3 * rows_all, True),
        (2 * FF, width * 2 * FF, True),
        (rows_all, rows_all * width, False),
        (FF, FF * width, False),
    )
    factors, *small = exchange(
        n_data, n_tensor, cells, ln_one_part, ln_two_part, sums, totals, squares,
        jnp.stack([qkv_row, gu_row, out_col, down_col]), ln_params, ln_second,
    )
    qkv_grad, qkv_new, out_sum, out_new, gu_grad, gu_new, down_sum, down_new, *small = results(
        ff_dev, factors, goq, gff, qkv_t, out_w, w_down, w_gu, oq_new, ff_new, small
    )
    qkv_row_new, gu_row_new, out_col_new, down_col_new, ln_tot, ln_second_new, ln_new = small
    qkv_back = lambda x: jnp.transpose(x, (1, 0, 2))
    return (
        layer_out,
        input_grad,
        qkv_back(qkv_grad),
        qkv_back(qkv_new),
        qkv_row_new[0],
        qkv_col_new.reshape(3, -1),
        out_sum,
        out_new,
        out_row_new,
        out_col_new[0],
        jnp.transpose(gu_grad, (2, 1, 0)),
        jnp.transpose(gu_new, (2, 1, 0)),
        gu_row_new[0],
        gu_col_new,
        down_sum,
        down_new,
        down_row_new,
        down_col_new[0],
        ln_tot,
        ln_second_new,
        ln_new,
    )


def solution(mesh):
    in_specs = (
        P(("dp", "tensor"), None),
        P(("dp", "tensor"), None),
        P("dp"),
        P("dp"),
        P(("dp", "tensor")),
        P(),
        P(None, None, "tensor"),
        P("tensor", None),
        P(None, None, "tensor"),
        P("tensor", None),
        P(),
        P(),
        P(None, "tensor"),
        P("tensor"),
        P(),
        P(),
        P(None, "tensor"),
        P("tensor"),
        P(),
        P(),
    )
    out_specs = (
        P(("dp", "tensor"), None),
        P(("dp", "tensor"), None),
        P(None, None, "tensor"),
        P(None, None, "tensor"),
        P(),
        P(None, "tensor"),
        P("tensor", None),
        P("tensor", None),
        P("tensor"),
        P(),
        P(None, None, "tensor"),
        P(None, None, "tensor"),
        P(),
        P(None, "tensor"),
        P("tensor", None),
        P("tensor", None),
        P("tensor"),
        P(),
        P(),
        P(),
        P(),
    )
    return jax.shard_map(
        on_device, mesh=mesh, in_specs=in_specs, out_specs=out_specs, check_vma=False
    )
```

```python
import functools

import jax
import jax.numpy as jnp
from jax import lax
from jax.experimental import pallas as pl
from jax.experimental.pallas import tpu as pltpu
from jax.sharding import PartitionSpec as P

HD = 128
FF = 5461
SLOT = 2048
STEP = 10
DECAY = 1.0 - STEP ** (-0.8)
PREFIX_MAX = SLOT // 2
Q_BLOCK = 512

ln_eps = 1e-05
eps_one = 1e-30
eps_two = 0.001
clip_bound = 1.0
rate_base = 1.0
masked_score = -1e30
LOG2E = 1.4426950408889634
BF = jnp.bfloat16
F32 = jnp.float32


def dot(a, b, dims):
    return lax.dot_general(a, b, (dims, ((), ())), preferred_element_type=F32)


def ring_order(n):
    b_size = 2 if n <= 8 else 4
    a_size = n // b_size
    order = []
    for a in range(a_size):
        cols = list(range(1, b_size))
        order += [a * b_size + c for c in (cols[::-1] if a % 2 else cols)]
    for a in range(a_size - 1, -1, -1):
        order.append(a * b_size)
    return order


def cost(micros):
    return pl.CostEstimate(flops=int(micros * 1e9), transcendentals=0, bytes_accessed=4 << 20)


PUSH = pl.DeviceIdType.MESH
PIECES = 2
ROW_BLOCK = 64


def pick(index, table):
    out = jnp.int32(table[0])
    for k in range(1, len(table)):
        out = jnp.where(index == k, jnp.int32(table[k]), out)
    return out


def neighbours(n):
    order = ring_order(n)
    pos = pick(lax.axis_index("tensor"), [order.index(t) for t in range(n)])
    ahead = pick(lax.rem(pos + 1, n), order)
    behind = pick(lax.rem(pos + n - 1, n), order)
    return pos, [{"tensor": ahead}, {"tensor": behind}]


def chunk_places(n, pos, rows):
    places = []
    for t in range(n):
        place = ring_order(n).index(t)
        places.append(lax.rem(pos + (n - place), n) * rows)
        places.append(lax.rem(place - pos + n, n) * rows + rows // 2)
    return places


def other_core():
    me = lax.axis_index("dp")
    return {"dp": me + 1 - 2 * lax.rem(me, 2)}


def other_chips(n_x):
    core, chip = lax.rem(lax.axis_index("dp"), 2), lax.axis_index("dp") // 2
    return chip, [{"dp": 2 * lax.rem(chip + k, n_x) + core} for k in range(1, n_x)]


def greet(devices):
    barrier = pltpu.get_barrier_semaphore()
    for device in devices:
        pl.semaphore_signal(barrier, inc=1, device_id=device, device_id_type=PUSH)
    pl.semaphore_wait(barrier, len(devices))


def ring_copy(land, send_sem, recv_sem, sides, d, s, piece=None):
    src, dst, sem = land.at[d, s], land.at[d, s + 1], d
    if piece is not None:
        size = land.shape[2] // PIECES
        rows = pl.ds(piece * size, size)
        src, dst, sem = land.at[d, s, rows], land.at[d, s + 1, rows], d * PIECES + piece
    return pltpu.make_async_remote_copy(
        src_ref=src,
        dst_ref=dst,
        send_sem=send_sem.at[sem, s],
        recv_sem=recv_sem.at[sem, s],
        device_id=sides[d],
        device_id_type=PUSH,
    )


def ring_sent(n, copy, pieces=(None,)):
    def sent(s, carry):
        for d in range(2):
            for piece in pieces:
                copy(d, s, piece).wait_send()
        return carry

    lax.fori_loop(0, n - 1, sent, 0)


def gather_start(x_ref, land):
    half = x_ref.shape[0] // 2
    land[0, 0] = x_ref[:half, :]
    land[1, 0] = x_ref[half:, :]


def gather_step(n, copy, s):
    for piece in range(PIECES):
        for d in range(2):

            @pl.when(s > 0)
            def _():
                copy(d, s - 1, piece).wait_recv()

            @pl.when(s < n - 1)
            def _():
                copy(d, s, piece).start()


def ring_gather(n, x_ref, land, send_sem, recv_sem, sides, work):
    copy = functools.partial(ring_copy, land, send_sem, recv_sem, sides)
    gather_start(x_ref, land)

    def step(s, carry):
        gather_step(n, copy, s)
        work(s)
        return carry

    lax.fori_loop(0, n, step, 0)
    ring_sent(n, copy, range(PIECES))


def scatter_start(land):
    for d in range(2):
        land[d, 0] = jnp.zeros(land.shape[2:], land.dtype)


def scatter_step(n, copy, land, term_buf, finish, s):
    half = term_buf.shape[0] // 2
    size = half // PIECES
    for piece in range(PIECES):
        for d in range(2):
            part = slice(piece * size, (piece + 1) * size)
            rows = slice(d * half + piece * size, d * half + (piece + 1) * size)

            @pl.when(s > 0)
            def _():
                copy(d, s - 1, piece).wait_recv()

            total = land[d, s, part].astype(F32) + term_buf[rows, :]

            @pl.when(s < n - 1)
            def _():
                land[d, s, part] = total.astype(BF)
                copy(d, s, piece).start()

            @pl.when(s == n - 1)
            def _():
                finish(rows, total)


def ring_scatter(n, land, send_sem, recv_sem, sides, term_buf, term, work, finish):
    copy = functools.partial(ring_copy, land, send_sem, recv_sem, sides)
    scatter_start(land)

    def step(s, carry):
        term(lax.rem(s + 1, n))
        scatter_step(n, copy, land, term_buf, finish, s)
        work(s)
        return carry

    lax.fori_loop(0, n, step, 0)
    ring_sent(n, copy, range(PIECES))


def dot_columns(out, a, b, dims, block=512):
    width = b.shape[1]

    def columns(j, carry):
        at = pl.ds(pl.multiple_of(j * block, block), block)
        out(at, dot(a, b[:, at], dims))
        return carry

    lax.fori_loop(0, width // block, columns, 0)


def first_kernel(
    n, x_ref, seen_ref, ln_ref, w_ref, pair_hbm, act_ref, qkv_ref, seen_all, gu_ref,
    land, act_buf, seen_buf, pair_buf, send_sem, recv_sem, act_sem, seen_sem, pair_sem,
):
    ff, block = pair_hbm.shape[0], pair_buf.shape[1]
    ff_pad = gu_ref.shape[0] // 2
    n_pairs = ff_pad // block

    def pair_load(b):
        rows = min(block, ff - b * block)
        return pltpu.make_async_copy(
            pair_hbm.at[pl.ds(b * block, rows)], pair_buf.at[b % 2, pl.ds(0, rows)], pair_sem.at[b % 2]
        )

    def pair_start(b):
        if b * block + block > ff:
            pair_buf[b % 2] = jnp.zeros(pair_buf.shape[1:], BF)
        pair_load(b).start()

    for b in range(min(2, n_pairs)):
        pair_start(b)
    rows, cols = x_ref.shape[0], w_ref.shape[2]
    me = lax.axis_index("tensor")
    peers = [lax.rem(me + k, n) for k in range(1, n)]
    sides = neighbours(n)[1]
    greet([{"tensor": t} for t in peers])

    def seen_copy(k):
        return pltpu.make_async_remote_copy(
            src_ref=seen_ref, dst_ref=seen_buf.at[me], send_sem=seen_sem.at[0, k],
            recv_sem=seen_sem.at[1, k], device_id={"tensor": peers[k]}, device_id_type=PUSH,
        )

    def act_copy(s):
        place = pl.ds(pl.multiple_of(s * rows, rows), rows)
        return pltpu.make_async_copy(act_buf.at[s], act_ref.at[place], act_sem.at[s])

    def work(s):
        @pl.when(s == 0)
        def _():
            for k in range(n - 1):
                seen_copy(k).start()

        chunk = jnp.concatenate([land[0, s], land[1, s]], axis=0).astype(F32)
        act = layer_norm(chunk, ln_ref[0:1, :], ln_ref[1:2, :]).astype(BF)
        act_buf[s] = act
        act_copy(s).start()
        place = pl.ds(pl.multiple_of(s * rows, rows), rows)
        for k in range(3):
            qkv_ref[place, k * cols : (k + 1) * cols] = dot(act, w_ref[k], ((1,), (0,))).astype(BF)
        for b in range(n_pairs):

            @pl.when(s == b)
            def _():
                pair_load(b).wait()
                for i in range(2):
                    at = i * ff_pad + b * block
                    gu_ref[at : at + block, :] = pair_buf[b % 2, :, i, :]
                if b + 2 < n_pairs:
                    pair_start(b + 2)

    ring_gather(n, x_ref, land, send_sem, recv_sem, sides, work)
    seen_buf[me] = seen_ref[...]
    for k in range(n - 1):
        seen_copy(k).wait()
    seen_all[...] = seen_buf[...]

    def written(s, carry):
        act_copy(s).wait()
        return carry

    lax.fori_loop(0, n, written, 0)


def ring_scratch(n, rows, width, pieces):
    return [pltpu.VMEM((2, n, rows // 2, width), BF)], [
        pltpu.SemaphoreType.DMA((2 * pieces, n - 1)),
        pltpu.SemaphoreType.DMA((2 * pieces, n - 1)),
    ]


VMEM_SPEC = pl.BlockSpec(memory_space=pltpu.VMEM)
ANY_SPEC = pl.BlockSpec(memory_space=pl.ANY)


def first_gather(n, x, seen, ln_params, w, pairs):
    rows, width = x.shape
    cols = w.shape[2]
    block = 96
    ff_pad = -(-pairs.shape[0] // block) * block
    buf, sems = ring_scratch(n, rows, width, PIECES)
    return pl.pallas_call(
        functools.partial(first_kernel, n),
        in_specs=[VMEM_SPEC] * 4 + [ANY_SPEC],
        out_specs=[ANY_SPEC] + [VMEM_SPEC] * 3,
        out_shape=[
            jax.ShapeDtypeStruct((n * rows, width), BF),
            jax.ShapeDtypeStruct((n * rows, 3 * cols), BF),
            jax.ShapeDtypeStruct((n,) + seen.shape, F32),
            jax.ShapeDtypeStruct((2 * ff_pad, width), BF),
        ],
        scratch_shapes=buf
        + [pltpu.VMEM((n, rows, width), BF), pltpu.VMEM((n,) + seen.shape, F32)]
        + [pltpu.VMEM((2, block, 2, width), BF)]
        + sems
        + [pltpu.SemaphoreType.DMA((n,)), pltpu.SemaphoreType.DMA((2, n - 1))]
        + [pltpu.SemaphoreType.DMA((2,))],
        compiler_params=pltpu.CompilerParams(
            collective_id=1, has_side_effects=True, vmem_limit_bytes=56 << 20
        ),
        cost_estimate=pl.CostEstimate(
            flops=6 * n * rows * width * cols, transcendentals=0, bytes_accessed=40 << 20
        ),
    )(x, seen, ln_params, w, pairs)


def grad_kernel(
    n, heads, x_ref, weight_ref, qkv_ref, seen_ref, real_ref, out_w_ref, qkv_w_hbm, gu_w_hbm, down_w_hbm,
    all_ref, ctx_ref, lse_ref, square_ref, thr_ref,
    land, own_ref, q_ref, k_ref, v_ref, qkv_w_ref, gu_w_ref, down_w_ref, send_sem, recv_sem, all_sem,
    load_sem,
):
    rows = x_ref.shape[0]
    half = rows // 2
    pos, sides = neighbours(n)
    places = chunk_places(n, pos, rows)
    loads = [
        pltpu.make_async_copy(src, dst, load_sem.at[i])
        for i, (src, dst) in enumerate(
            ((qkv_w_hbm, qkv_w_ref), (gu_w_hbm, gu_w_ref), (down_w_hbm, down_w_ref))
        )
    ]
    for load in loads:
        load.start()
    own_ref[...] = (x_ref[...].astype(F32) * weight_ref[...]).astype(BF)
    for t in range(n):
        column = jnp.broadcast_to(seen_ref[t, 0:1, :], (128, rows)).T
        thr_ref[t * rows : (t + 1) * rows, :] = column
    greet(sides)

    def all_copy(d, s):
        place = pl.ds(pl.multiple_of(s * rows + d * half, half), half)
        return pltpu.make_async_copy(land.at[d, s], all_ref.at[place], all_sem.at[d, s])

    def squares(i, ref, real):
        block, cols = ROW_BLOCK, ref.shape[1]

        def add(j, carry):
            at = pl.multiple_of(j * block, block)
            value = ref[pl.ds(at, block), :].astype(F32)
            value = value * value
            if real is not None:
                value = value * real[pl.ds(lax.rem(at, real.shape[0]), block), :]
            square_ref[i, :, :cols] += sum(value[k : k + 8] for k in range(0, block, 8))
            return carry

        lax.fori_loop(0, ref.shape[0] // block, add, 0)

    def work(s):
        for d in range(2):
            all_copy(d, s).start()
        for h in range(heads):

            @pl.when(s == h)
            def _():
                columns = lambda i: slice((i * heads + h) * HD, (i * heads + h + 1) * HD)
                for i, dst in enumerate((q_ref, k_ref, v_ref)):
                    to_order(places, qkv_ref, columns(i), dst)
                attn_forward_head(
                    places, thr_ref, lse_ref.at[h], q_ref, k_ref, v_ref, ctx_ref, columns(0)
                )

        @pl.when(s == heads)
        def _():
            square_ref[...] = jnp.zeros_like(square_ref)
            loads[0].wait()
            for k in range(3):
                squares(0, qkv_w_ref.at[k], None)

        @pl.when(s == heads + 1)
        def _():
            loads[1].wait()
            squares(1, gu_w_ref, real_ref)

        @pl.when(s == heads + 2)
        def _():
            squares(2, out_w_ref, None)
            loads[2].wait()
            squares(3, down_w_ref, real_ref)

    ring_gather(n, own_ref, land, send_sem, recv_sem, sides, work)

    def written(s, carry):
        for d in range(2):
            all_copy(d, s).wait()
        return carry

    lax.fori_loop(0, n, written, 0)


def grad_gather(n, x, weight, qkv, thr, real, qkv_w, gu_w, out_w, down_w):
    rows, width = x.shape
    cols = out_w.shape[0]
    heads = cols // HD
    buf, sems = ring_scratch(n, rows, width, PIECES)
    return pl.pallas_call(
        functools.partial(grad_kernel, n, heads),
        in_specs=[VMEM_SPEC] * 6 + [ANY_SPEC] * 3,
        out_specs=[ANY_SPEC] + [VMEM_SPEC] * 4,
        out_shape=[
            jax.ShapeDtypeStruct((n * rows, width), BF),
            jax.ShapeDtypeStruct((n * rows, cols), BF),
            jax.ShapeDtypeStruct((heads, 1, SLOT), F32),
            jax.ShapeDtypeStruct((4, 8, width), F32),
            jax.ShapeDtypeStruct((SLOT, 128), F32),
        ],
        scratch_shapes=buf
        + [pltpu.VMEM((rows, width), BF)]
        + [pltpu.VMEM((SLOT, HD), BF)] * 3
        + [pltpu.VMEM(w.shape, BF) for w in (qkv_w, gu_w, down_w)]
        + sems
        + [pltpu.SemaphoreType.DMA((2, n)), pltpu.SemaphoreType.DMA((3,))],
        compiler_params=pltpu.CompilerParams(
            collective_id=5, has_side_effects=True, vmem_limit_bytes=60 << 20
        ),
        cost_estimate=cost(80),
    )(x, weight, qkv, thr, real, out_w, qkv_w, gu_w, down_w)


def mix_kernel(
    n, ctx_ref, w_ref, x_ref, ln_ref, hidden_ref, norm_ref, land, term_buf, send_sem, recv_sem
):
    rows = x_ref.shape[0]
    sides = neighbours(n)[1]
    greet(sides)

    def term(c):
        place = pl.ds(pl.multiple_of(c * rows, rows), rows)

        def put(at, value):
            term_buf[:, at] = value

        dot_columns(put, ctx_ref[place, :], w_ref, ((1,), (0,)))

    def finish(at, total):
        hidden = x_ref[at, :].astype(F32) + total
        hidden_ref[at, :] = hidden
        norm_ref[at, :] = layer_norm(hidden, ln_ref[2:3, :], ln_ref[3:4, :]).astype(BF)

    ring_scatter(n, land, send_sem, recv_sem, sides, term_buf, term, lambda s: None, finish)


def mix_scatter(n, context, w, x, ln_params):
    rows, width = x.shape
    buf, sems = ring_scratch(n, rows, width, PIECES)
    return pl.pallas_call(
        functools.partial(mix_kernel, n),
        in_specs=[VMEM_SPEC] * 4,
        out_specs=[VMEM_SPEC] * 2,
        out_shape=[
            jax.ShapeDtypeStruct((rows, width), F32),
            jax.ShapeDtypeStruct((rows, width), BF),
        ],
        scratch_shapes=buf + [pltpu.VMEM((rows, width), F32)] + sems,
        compiler_params=pltpu.CompilerParams(
            collective_id=6, has_side_effects=True, vmem_limit_bytes=40 << 20
        ),
        cost_estimate=cost(80),
    )(context, w, x, ln_params)


def gelu_pair(gate):
    c, a = (2.0 / jnp.pi) ** 0.5, 0.044715
    square = gate * gate
    t = jnp.tanh(c * gate * (1.0 + a * square))
    value = 0.5 * gate * (1.0 + t)
    slope = 0.5 * (1.0 + t) + 0.5 * gate * (1.0 - t * t) * (c * (1.0 + 3.0 * a * square))
    return value, slope


def both_kernel(
    n, x_ref, gu_w_ref, down_w_ref, real_ref, hidden_ref, cot_ref, weight_ref, ln_ref, grad_hbm,
    act_ref, inner_ref, d_gu_ref, out_ref, low_ref, ln_sum,
    land, sums, term_buf, gate_up, d_inner, grad_buf,
    send_sem, recv_sem, sum_send, sum_recv, act_sem, grad_sem,
):
    rows = x_ref.shape[0]
    half = rows // 2
    ff_pad = down_w_ref.shape[0]
    sides = neighbours(n)[1]
    copy = functools.partial(ring_copy, land, send_sem, recv_sem, sides)
    sum_copy = functools.partial(ring_copy, sums, sum_send, sum_recv, sides)

    def grad_load(s):
        place = pl.ds(pl.multiple_of(s * rows, rows), rows)
        slot = lax.rem(s, 2)
        return pltpu.make_async_copy(grad_hbm.at[place], grad_buf.at[slot], grad_sem.at[slot])

    def act_copy(d, s):
        place = pl.ds(pl.multiple_of(s * rows + d * half, half), half)
        return pltpu.make_async_copy(land.at[d, s], act_ref.at[place], act_sem.at[d, s])

    grad_load(0).start()
    grad_load(1).start()
    greet(sides)
    gather_start(x_ref, land)
    ln_sum[...] = jnp.zeros_like(ln_sum)
    scatter_start(sums)

    def by_rows(out, a, w_ref):
        block = 384

        def some(j, carry):
            at = pl.ds(pl.multiple_of(j * block, block), block)
            out[:, at] = dot(a, w_ref[at, :], ((1,), (1,)))
            return carry

        lax.fori_loop(0, w_ref.shape[0] // block, some, 0)

    def term(c):
        place = pl.ds(pl.multiple_of(c * rows, rows), rows)

        def put(at, value):
            term_buf[:, at] = value

        dot_columns(put, d_gu_ref[place, :], gu_w_ref, ((1,), (0,)))

    def finish(at, total):
        d_rows, sums_two = layer_norm_back(hidden_ref[at, :], ln_ref[2:3, :], total)
        d_rows = cot_ref[at, :].astype(F32) * weight_ref[at, :] + d_rows
        out_ref[at, :] = d_rows
        low_ref[at, :] = d_rows.astype(BF)
        ln_sum[...] += sums_two

    def step(s, carry):
        gather_step(n, copy, s)
        for d in range(2):
            act_copy(d, s).start()
        by_rows(gate_up, jnp.concatenate([land[0, s], land[1, s]], axis=0), gu_w_ref)
        grad_load(s).wait()
        by_rows(d_inner, grad_buf[lax.rem(s, 2)], down_w_ref)

        @pl.when(s < n - 2)
        def _():
            grad_load(s + 2).start()

        place = pl.ds(pl.multiple_of(s * rows, rows), rows)
        for at in range(0, ff_pad, 128):
            here, there = slice(at, at + 128), slice(ff_pad + at, ff_pad + at + 128)
            real = real_ref[:, here]
            gate, up = gate_up[:, here], gate_up[:, there]
            value, slope = gelu_pair(gate)
            back = d_inner[:, here] * real
            inner_ref[place, here] = (value * up * real).astype(BF)
            d_gu_ref[place, here] = (back * up * slope).astype(BF)
            d_gu_ref[place, there] = (back * value).astype(BF)

        @pl.when(s > 0)
        def _():
            term(s)
            scatter_step(n, sum_copy, sums, term_buf, finish, s - 1)

        return carry

    lax.fori_loop(0, n, step, 0)
    term(0)
    scatter_step(n, sum_copy, sums, term_buf, finish, n - 1)
    ring_sent(n, copy, range(PIECES))
    ring_sent(n, sum_copy, range(PIECES))

    def written(s, carry):
        for d in range(2):
            act_copy(d, s).wait()
        return carry

    lax.fori_loop(0, n, written, 0)


def both_ways(n, x, gu_w, down_w, real, hidden, cotangent, weight, ln_params, grad):
    rows, width = x.shape
    ff_pad = down_w.shape[0]
    buf, sems = ring_scratch(n, rows, width, PIECES)
    sum_buf, sum_sems = ring_scratch(n, rows, width, PIECES)
    return pl.pallas_call(
        functools.partial(both_kernel, n),
        in_specs=[VMEM_SPEC] * 8 + [ANY_SPEC],
        out_specs=[ANY_SPEC] + [VMEM_SPEC] * 5,
        out_shape=[
            jax.ShapeDtypeStruct((n * rows, width), BF),
            jax.ShapeDtypeStruct((n * rows, ff_pad), BF),
            jax.ShapeDtypeStruct((n * rows, 2 * ff_pad), BF),
            jax.ShapeDtypeStruct((rows, width), F32),
            jax.ShapeDtypeStruct((rows, width), BF),
            jax.ShapeDtypeStruct((2, width), F32),
        ],
        scratch_shapes=buf
        + sum_buf
        + [
            pltpu.VMEM((rows, width), F32),
            pltpu.VMEM((rows, 2 * ff_pad), F32),
            pltpu.VMEM((rows, ff_pad), F32),
            pltpu.VMEM((2, rows, width), BF),
        ]
        + sems
        + sum_sems
        + [pltpu.SemaphoreType.DMA((2, n)), pltpu.SemaphoreType.DMA((2,))],
        compiler_params=pltpu.CompilerParams(
            collective_id=7, has_side_effects=True, vmem_limit_bytes=60 << 20
        ),
        cost_estimate=cost(160),
    )(x, gu_w, down_w, real, hidden, cotangent, weight, ln_params, grad)


def back_kernel(
    n, n_x, x_ref, w_ref, ctx_ref, inner_hbm, d_gu_hbm, grad_hbm, act_hbm,
    d_ctx_ref, out_ref, mine_ref, slots_hbm,
    land, lhs, rhs, part, core_land, out_sum, send_sem, recv_sem, load_sem, core_sem, slot_sem,
):
    rows, ff_pad = x_ref.shape[0], lhs.shape[2]
    ff_rows, half = core_land.shape[1:]
    sides, partner = neighbours(n)[1], other_core()
    core = lax.rem(lax.axis_index("dp"), 2)
    loads = [
        pltpu.make_async_copy(src, dst, load_sem.at[i])
        for i, (src, dst) in enumerate(
            (
                (inner_hbm, lhs.at[0]),
                (grad_hbm, rhs.at[0]),
                (d_gu_hbm.at[:, pl.ds(0, ff_pad)], lhs.at[1]),
                (act_hbm, rhs.at[1]),
                (d_gu_hbm.at[:, pl.ds(ff_pad, ff_pad)], lhs.at[2]),
            )
        )
    ]
    for load in loads:
        load.start()
    out_sum[...] = jnp.zeros_like(out_sum)
    chip, chips = other_chips(n_x)
    greet(sides + [partner] + chips)

    def slot_copy(k):
        return pltpu.make_async_remote_copy(
            src_ref=mine_ref.at[0], dst_ref=slots_hbm.at[chip], send_sem=slot_sem.at[0, k],
            recv_sem=slot_sem.at[1, k], device_id=chips[k], device_id_type=PUSH,
        )

    def core_copy(i):
        return pltpu.make_async_remote_copy(
            src_ref=part.at[i, 1 - core],
            dst_ref=core_land.at[i],
            send_sem=core_sem.at[0, i],
            recv_sem=core_sem.at[1, i],
            device_id=partner,
            device_id_type=PUSH,
        )

    def work(s):
        chunk = jnp.concatenate([land[0, s], land[1, s]], axis=0)
        place = pl.ds(pl.multiple_of(s * rows, rows), rows)
        d_ctx_ref[place, :] = dot(chunk, w_ref[...], ((1,), (1,))).astype(BF)
        out_sum[...] += dot(ctx_ref[place, :], chunk, ((0,), (0,)))
        for i in range(3):
            for turn in range(2):

                @pl.when(s == 2 * i + turn)
                def _():
                    if turn == 0:
                        for load in (loads[:2], loads[2:4], loads[4:])[i]:
                            load.wait()
                    side = slice(turn * half, (turn + 1) * half)

                    def put(at, value):
                        part[i, turn, :, at] = value[:ff_rows].astype(BF)

                    dot_columns(put, lhs[i], rhs.at[min(i, 1), :, side], ((0,), (0,)))
                    if turn == 1:
                        core_copy(i).start()

            @pl.when(s == 2 * i + 3)
            def _():
                core_copy(i).wait()
                total = part[i, core].astype(F32) + core_land[i].astype(F32)
                mine_ref[i] = total.astype(BF)
                if i == 0:
                    for k in range(n_x - 1):
                        slot_copy(k).start()

    ring_gather(n, x_ref, land, send_sem, recv_sem, sides, work)
    out_ref[...] = out_sum[...].astype(BF)
    for k in range(n_x - 1):
        slot_copy(k).wait()


def back_gather(n, n_x, ff_dev, x, w, context, inner, d_gu, grad, act):
    rows, width = x.shape
    ff_pad = inner.shape[1]
    ff_rows = -(-ff_dev // ROW_BLOCK) * ROW_BLOCK
    buf, sems = ring_scratch(n, rows, width, PIECES)
    return pl.pallas_call(
        functools.partial(back_kernel, n, n_x),
        in_specs=[VMEM_SPEC] * 3 + [ANY_SPEC] * 4,
        out_specs=[VMEM_SPEC] * 3 + [ANY_SPEC],
        out_shape=[
            jax.ShapeDtypeStruct((n * rows, w.shape[0]), BF),
            jax.ShapeDtypeStruct(w.shape, BF),
            jax.ShapeDtypeStruct((3, ff_rows, width // 2), BF),
            jax.ShapeDtypeStruct((n_x, ff_rows, width // 2), BF),
        ],
        scratch_shapes=buf
        + [
            pltpu.VMEM((3, n * rows, ff_pad), BF),
            pltpu.VMEM((2, n * rows, width), BF),
            pltpu.VMEM((3, 2, ff_rows, width // 2), BF),
            pltpu.VMEM((3, ff_rows, width // 2), BF),
            pltpu.VMEM(w.shape, F32),
        ]
        + sems
        + [
            pltpu.SemaphoreType.DMA((5,)),
            pltpu.SemaphoreType.DMA((2, 3)),
            pltpu.SemaphoreType.DMA((2, n_x - 1)),
        ],
        compiler_params=pltpu.CompilerParams(
            collective_id=3, has_side_effects=True, vmem_limit_bytes=60 << 20
        ),
        cost_estimate=cost(80),
    )(x, w, context, inner, d_gu, grad, act)


def ffn_kernel(
    n, n_x, heads, inner_ref, w_ref, hidden_ref, thr_ref, qkv_ref, d_ctx_ref, lse_ref,
    out_part_ref, act_hbm, mine_hbm,
    out_ref, d_qkv_ref, slots_hbm, out_slots_hbm, oq_mine_ref,
    land, term_buf, q_ref, k_ref, v_ref, do_ref, dk_sum, dv_sum,
    act_buf, part, qkv_land, out_land,
    send_sem, recv_sem, act_sem, core_sem, slot_sem,
):
    rows = hidden_ref.shape[0]
    pos, sides = neighbours(n)
    partner = other_core()
    core = lax.rem(lax.axis_index("dp"), 2)
    chip, chips = other_chips(n_x)
    block = act_buf.shape[2]
    blocks = act_hbm.shape[1] // block
    qkv_cols, wide = qkv_land.shape
    wide_of = lambda c: pl.ds(pl.multiple_of(c * wide, wide), wide)

    def act_load(j):
        return pltpu.make_async_copy(
            act_hbm.at[:, pl.ds(j * block, block)], act_buf.at[j % 2], act_sem.at[j]
        )

    def core_copy(i):
        src, dst = (
            (part.at[:, wide_of(1 - core)], qkv_land),
            (out_part_ref.at[:, wide_of(1 - core)], out_land),
        )[i]
        return pltpu.make_async_remote_copy(
            src_ref=src, dst_ref=dst, send_sem=core_sem.at[0, i], recv_sem=core_sem.at[1, i],
            device_id=partner, device_id_type=PUSH,
        )

    def slot_copy(i, k):
        src, dst = (
            (mine_hbm.at[pl.ds(1, 2)], slots_hbm),
            (oq_mine_ref.at[pl.ds(qkv_cols, oq_mine_ref.shape[0] - qkv_cols)], out_slots_hbm),
        )[i]
        return pltpu.make_async_remote_copy(
            src_ref=src, dst_ref=dst.at[chip], send_sem=slot_sem.at[0, i, k],
            recv_sem=slot_sem.at[1, i, k], device_id=chips[k], device_id_type=PUSH,
        )

    for j in range(2):
        act_load(j).start()
    greet(sides + [partner] + chips)
    core_copy(1).start()
    for k in range(n_x - 1):
        slot_copy(0, k).start()
    places = chunk_places(n, pos, rows)

    def term(c):
        place = pl.ds(pl.multiple_of(c * rows, rows), rows)

        def put(at, value):
            term_buf[:, at] = value

        dot_columns(put, inner_ref[place, :], w_ref, ((1,), (0,)))

    def work(s):
        for h in range(heads):

            columns = lambda i: slice((i * heads + h) * HD, (i * heads + h + 1) * HD)
            for turn in range(2):

                @pl.when(s == 2 * h + turn)
                def _():
                    if turn == 0:
                        for i, dst in enumerate((q_ref, k_ref, v_ref)):
                            to_order(places, qkv_ref, columns(i), dst)
                        to_order(places, d_ctx_ref, columns(0), do_ref)
                    attn_backward_head(
                        turn, places, thr_ref, lse_ref.at[h], q_ref, k_ref, v_ref, do_ref,
                        dk_sum, dv_sum, d_qkv_ref, columns,
                    )

        @pl.when(s == 1)
        def _():
            core_copy(1).wait()
            total = out_part_ref[:, wide_of(core)].astype(F32) + out_land[...].astype(F32)
            oq_mine_ref[qkv_cols:, :] = total.astype(BF)
            for k in range(n_x - 1):
                slot_copy(1, k).start()

        for turn in range(blocks // 2):

            @pl.when(s == 2 * heads + turn)
            def _():
                for j in (2 * turn, 2 * turn + 1):
                    act_load(j).wait()
                    grad = dot(d_qkv_ref[...], act_buf[j % 2], ((0,), (0,)))
                    part[:, j * block : (j + 1) * block] = grad.astype(BF)
                for j in (2 * turn + 2, 2 * turn + 3):
                    if j < blocks:
                        act_load(j).start()
                if turn == blocks // 2 - 1:
                    core_copy(0).start()

    def finish(at, total):
        out_ref[at, :] = (hidden_ref[at, :] + total).astype(BF)

    ring_scatter(n, land, send_sem, recv_sem, sides, term_buf, term, work, finish)
    core_copy(0).wait()
    total = part[:, wide_of(core)].astype(F32) + qkv_land[...].astype(F32)
    oq_mine_ref[:qkv_cols, :] = total.astype(BF)
    for k in range(n_x - 1):
        slot_copy(0, k).wait()
        slot_copy(1, k).wait()


def ffn_scatter(n, n_x, inner, w, hidden, thr, qkv, d_context, lse, out_part, act, mine):
    rows, width = hidden.shape
    cols, block = d_context.shape[1], 512
    heads = d_context.shape[1] // HD
    buf, sems = ring_scratch(n, rows, width, PIECES)
    return pl.pallas_call(
        functools.partial(ffn_kernel, n, n_x, heads),
        in_specs=[VMEM_SPEC] * 8 + [ANY_SPEC] * 2,
        out_specs=[VMEM_SPEC] * 2 + [ANY_SPEC] * 2 + [VMEM_SPEC],
        out_shape=[
            jax.ShapeDtypeStruct((rows, width), BF),
            jax.ShapeDtypeStruct(qkv.shape, BF),
            jax.ShapeDtypeStruct((n_x, 2) + mine.shape[1:], BF),
            jax.ShapeDtypeStruct((n_x, cols, width // 2), BF),
            jax.ShapeDtypeStruct((4 * cols, width // 2), BF),
        ],
        scratch_shapes=buf
        + [pltpu.VMEM((rows, width), F32)]
        + [pltpu.VMEM((SLOT, HD), BF)] * 4
        + [pltpu.VMEM((SLOT, HD), F32)] * 2
        + [
            pltpu.VMEM((2, n * rows, block), BF),
            pltpu.VMEM((3 * cols, width), BF),
            pltpu.VMEM((3 * cols, width // 2), BF),
            pltpu.VMEM((cols, width // 2), BF),
        ]
        + sems
        + [
            pltpu.SemaphoreType.DMA((width // block,)),
            pltpu.SemaphoreType.DMA((2, 2)),
            pltpu.SemaphoreType.DMA((2, 2, n_x - 1)),
        ],
        compiler_params=pltpu.CompilerParams(
            collective_id=4, has_side_effects=True, vmem_limit_bytes=62 << 20
        ),
        cost_estimate=cost(95),
    )(inner, w, hidden, thr, qkv, d_context, lse, out_part, act, mine)


def row_sums(grad_ref, old_ref, real_ref, new_ref, c_ref, t_ref):
    width = grad_ref.shape[1]
    block = ROW_BLOCK

    def rows(i, carry):
        at = pl.ds(pl.multiple_of(i * block, block), block)
        grad = grad_ref[at, :].astype(F32)
        square = grad * grad
        real = 1.0 if real_ref is None else real_ref[at, :]
        total = (jnp.sum(square, axis=1, keepdims=True) + width * eps_one) * real
        new = DECAY * old_ref[at, :] + (1.0 - DECAY) * (total / width)
        new_ref[at, :] = new
        c = (square + eps_one) * real
        t = square * (real / new)
        c_ref[...] += sum(c[k : k + 8] for k in range(0, block, 8))
        t_ref[...] += sum(t[k : k + 8] for k in range(0, block, 8))
        return carry

    lax.fori_loop(0, grad_ref.shape[0] // block, rows, 0)


def last_kernel(
    n, n_x, d_qkv_ref, w_ref, oq_mine_ref, oq_old, ff_old, ff_real,
    x_ref, d_hidden_ref, ln_ref,
    mine_hbm, down_hbm, gu_hbm, out_hbm,
    out_ref, goq_hbm, gff_hbm, oq_new, ff_new, sums_ref, ln_sum, totals_ref,
    land, term_buf, goq_ref, gff_ref, qkv_land, out_slots, ff_own, ff_slots, c_sum, t_sum,
    send_sem, recv_sem, oq_sem, load_sem, join_sem, write_sem,
):
    rows = term_buf.shape[0]
    cols, width = w_ref.shape[2], term_buf.shape[1]
    sides, partner = neighbours(n)[1], other_core()
    core = lax.rem(lax.axis_index("dp"), 2)
    chip, chips = other_chips(n_x)
    half = width // 2
    own = pl.ds(pl.multiple_of(core * half, half), half)

    qkv_rows, out_rows = pl.ds(0, 3 * cols), pl.ds(3 * cols, cols)
    writes = [
        pltpu.make_async_copy(goq_ref, goq_hbm, write_sem.at[0]),
        pltpu.make_async_copy(gff_ref, gff_hbm, write_sem.at[1]),
    ]

    def loads(i):
        if i == 3:
            return [pltpu.make_async_copy(out_hbm, out_slots, load_sem.at[0, 3])]
        slots = down_hbm if i == 0 else gu_hbm.at[:, i - 1]
        return [
            pltpu.make_async_copy(mine_hbm.at[i], ff_own.at[i], load_sem.at[0, i]),
            pltpu.make_async_copy(slots, ff_slots.at[i], load_sem.at[1, i]),
        ]

    def oq_copy(k):
        return pltpu.make_async_remote_copy(
            src_ref=oq_mine_ref.at[qkv_rows], dst_ref=qkv_land.at[chip], send_sem=oq_sem.at[0, k],
            recv_sem=oq_sem.at[1, k], device_id=chips[k], device_id_type=PUSH,
        )

    def join(i):
        ref = gff_ref.at[i, :, own] if i < 3 else goq_ref.at[(qkv_rows, out_rows)[i - 3], own]
        return pltpu.make_async_remote_copy(
            src_ref=ref, dst_ref=ref, send_sem=join_sem.at[0, i], recv_sem=join_sem.at[1, i],
            device_id=partner, device_id_type=PUSH,
        )

    def chip_sum(own_half, slots):
        total = jnp.zeros(own_half.shape, F32)
        for x in range(n_x):
            total = total + jnp.where(chip == x, own_half, slots[x]).astype(F32)
        return total.astype(BF)

    for i in range(4):
        for load in loads(i):
            load.start()
    ln_sum[...] = jnp.zeros_like(ln_sum)
    greet(sides + [partner] + chips)
    for k in range(n_x - 1):
        oq_copy(k).start()

    def term(c):
        place = pl.ds(pl.multiple_of(c * rows, rows), rows)
        block = 512

        def columns(j, carry):
            at = pl.ds(pl.multiple_of(j * block, block), block)
            term_buf[:, at] = sum(
                dot(d_qkv_ref[place, k * cols : (k + 1) * cols], w_ref[k, at, :], ((1,), (1,)))
                for k in range(3)
            )
            return carry

        lax.fori_loop(0, width // block, columns, 0)

    def sums(group, ref, first=True):
        if first:
            c_sum[...] = jnp.zeros_like(c_sum)
            t_sum[...] = jnp.zeros_like(t_sum)
        row_sums(*ref, c_sum, t_sum)
        sums_ref[2 * group : 2 * group + 1, :] = jnp.sum(c_sum[...], axis=0, keepdims=True)
        sums_ref[2 * group + 1 : 2 * group + 2, :] = jnp.sum(t_sum[...], axis=0, keepdims=True)

    ff_refs = lambda i: (gff_ref.at[i], ff_old.at[i], ff_real, ff_new.at[i])
    oq_refs = lambda at: (goq_ref.at[at], oq_old.at[at], None, oq_new.at[at])

    def work(s):
        for i in range(3):

            @pl.when(s == i)
            def _():
                for load in loads(i):
                    load.wait()
                gff_ref[i, :, own] = chip_sum(ff_own[i], ff_slots.at[i])
                join(i).start()

        @pl.when(s == 0)
        def _():
            for load in loads(3):
                load.wait()
            goq_ref[out_rows, own] = chip_sum(oq_mine_ref[out_rows, :], out_slots)
            join(4).start()

        @pl.when(s == 3)
        def _():
            join(0).wait()
            sums(3, ff_refs(0))

        @pl.when(s == 4)
        def _():
            for k in range(n_x - 1):
                oq_copy(k).wait()
            goq_ref[qkv_rows, own] = chip_sum(oq_mine_ref[qkv_rows, :], qkv_land)
            join(3).start()

        @pl.when(s == 5)
        def _():
            join(1).wait()
            sums(1, ff_refs(1))

        @pl.when(s == 6)
        def _():
            join(2).wait()
            sums(1, ff_refs(2), first=False)
            writes[1].start()
            join(4).wait()
            sums(2, oq_refs(out_rows))
            join(3).wait()
            sums(0, oq_refs(qkv_rows))
            writes[0].start()
            down_new = ff_new[0] * ff_real[: ff_new.shape[1], :]
            for i, new in enumerate((oq_new[out_rows, :], down_new)):
                total = jnp.sum(new, axis=0, keepdims=True)
                totals_ref[i : i + 1, :] = jnp.broadcast_to(total, (1, totals_ref.shape[1]))

    def finish(at, total):
        d_rows, sums_one = layer_norm_back(x_ref[at, :].astype(F32), ln_ref[0:1, :], total)
        out_ref[at, :] = (d_hidden_ref[at, :] + d_rows).astype(BF)
        ln_sum[...] += sums_one

    ring_scatter(n, land, send_sem, recv_sem, sides, term_buf, term, work, finish)
    for write in writes:
        write.wait()


def last_scatter(
    n, n_x, d_qkv, w, oq_mine, oq_old, ff_old, ff_real, ff_mine, down_slots, gu_slots, out_slots,
    x, d_hidden, ln_params,
):
    width, cols = w.shape[1:]
    rows = d_qkv.shape[0] // n
    half = width // 2
    ff_rows = ff_mine.shape[1]
    buf, sems = ring_scratch(n, rows, width, PIECES)
    return pl.pallas_call(
        functools.partial(last_kernel, n, n_x),
        in_specs=[VMEM_SPEC] * 9 + [ANY_SPEC] * 4,
        out_specs=[VMEM_SPEC] + [ANY_SPEC] * 2 + [VMEM_SPEC] * 5,
        out_shape=[
            jax.ShapeDtypeStruct((rows, width), BF),
            jax.ShapeDtypeStruct((4 * cols, width), BF),
            jax.ShapeDtypeStruct((3, ff_rows, width), BF),
            jax.ShapeDtypeStruct(oq_old.shape, F32),
            jax.ShapeDtypeStruct(ff_old.shape, F32),
            jax.ShapeDtypeStruct((8, width), F32),
            jax.ShapeDtypeStruct((2, width), F32),
            jax.ShapeDtypeStruct((8, 128), F32),
        ],
        scratch_shapes=buf
        + [
            pltpu.VMEM((rows, width), F32),
            pltpu.VMEM((4 * cols, width), BF),
            pltpu.VMEM((3, ff_rows, width), BF),
            pltpu.VMEM((n_x, 3 * cols, half), BF),
            pltpu.VMEM((n_x, cols, half), BF),
            pltpu.VMEM((3, ff_rows, half), BF),
            pltpu.VMEM((3, n_x, ff_rows, half), BF),
            pltpu.VMEM((8, width), F32),
            pltpu.VMEM((8, width), F32),
        ]
        + sems
        + [
            pltpu.SemaphoreType.DMA((2, n_x - 1)),
            pltpu.SemaphoreType.DMA((2, 4)),
            pltpu.SemaphoreType.DMA((2, 5)),
            pltpu.SemaphoreType.DMA((2,)),
        ],
        compiler_params=pltpu.CompilerParams(
            collective_id=2, has_side_effects=True, vmem_limit_bytes=62 << 20
        ),
        cost_estimate=cost(90),
    )(
        d_qkv, w, oq_mine, oq_old, ff_old, ff_real, x, d_hidden, ln_params,
        ff_mine, down_slots, gu_slots, out_slots,
    )


def norm_stats(rows):
    mean_row = jnp.mean(rows, axis=-1, keepdims=True)
    centered = rows - mean_row
    variance = jnp.mean(centered * centered, axis=-1, keepdims=True)
    scale = lax.rsqrt(variance + ln_eps)
    return centered * scale, scale


def layer_norm(rows, gain, shift):
    return norm_stats(rows)[0] * gain + shift


def layer_norm_back(rows, gain, e):
    n, scale = norm_stats(rows)
    eg = e * gain
    dv = scale * (
        eg - jnp.mean(eg, axis=-1, keepdims=True) - n * jnp.mean(eg * n, axis=-1, keepdims=True)
    )
    sums = [jnp.sum(x, axis=0, keepdims=True) for x in (e * n, e)]
    return dv, jnp.concatenate(sums, axis=0)


def seen_mask(thr_ref, q0, shape):
    thr = thr_ref[: shape[0], :]
    thr = jnp.concatenate([thr] * (shape[1] // thr.shape[1]), axis=1)
    q_pos = (q0 + lax.broadcasted_iota(jnp.int32, shape, 1)).astype(F32)
    return q_pos >= thr


def q_blocks():
    return [(q0, max(PREFIX_MAX, q0 + Q_BLOCK)) for q0 in range(0, SLOT, Q_BLOCK)]


def to_order(places, src_ref, columns, dst_ref):
    half = SLOT // len(places)
    for j, start in enumerate(places):
        place = pl.ds(pl.multiple_of(start, half), half)
        dst_ref[j * half : (j + 1) * half, :] = src_ref[place, columns]


def from_order(places, q0, value, dst_ref, columns):
    half = SLOT // len(places)
    for i in range(value.shape[0] // half):
        place = pl.ds(pl.multiple_of(places[q0 // half + i], half), half)
        dst_ref[place, columns] = value[i * half : (i + 1) * half, :]


def attn_forward_head(places, thr_ref, lse_ref, q_ref, k_ref, v_ref, o_ref, columns):
    c = HD**-0.5 * LOG2E
    for q0, klim in q_blocks():
        raw = dot(k_ref[:klim, :], q_ref[q0 : q0 + Q_BLOCK, :], ((1,), (1,)))
        raw = jnp.where(seen_mask(thr_ref, q0, raw.shape), raw, masked_score)
        top = jnp.max(raw, axis=0, keepdims=True)
        p = jnp.exp2((raw - top) * c)
        total = jnp.sum(p, axis=0, keepdims=True)
        out = dot(v_ref[:klim, :], p.astype(BF), ((0,), (0,))) / total
        from_order(places, q0, out.T.astype(BF), o_ref, columns)
        lse_ref[:, q0 : q0 + Q_BLOCK] = top * c + jnp.log2(total)


def attn_backward_head(
    turn, places, thr_ref, lse_ref, q_ref, k_ref, v_ref, do_ref, dk_sum, dv_sum, d_ref, columns
):
    scale = HD**-0.5
    blocks = q_blocks()
    if turn == 0:
        dk_sum[...] = jnp.zeros_like(dk_sum)
        dv_sum[...] = jnp.zeros_like(dv_sum)
    for q0, klim in (blocks[-1:] + blocks[:1], blocks[1:-1])[turn]:
        rows = slice(q0, q0 + Q_BLOCK)
        k, q, do = k_ref[:klim, :], q_ref[rows, :], do_ref[rows, :]
        raw = dot(k, q, ((1,), (1,)))
        p = jnp.exp2(raw * (scale * LOG2E) - lse_ref[:, rows])
        p = jnp.where(seen_mask(thr_ref, q0, raw.shape), p, 0.0)
        dv_sum[:klim, :] += dot(p.astype(BF), do, ((1,), (0,)))
        dp = dot(v_ref[:klim, :], do, ((1,), (1,)))
        delta = jnp.sum(p * dp, axis=0, keepdims=True)
        ds = (p * (dp - delta) * scale).astype(BF)
        dk_sum[:klim, :] += dot(ds, q, ((1,), (0,)))
        dq = dot(k, ds, ((0,), (0,))).T.astype(BF)
        from_order(places, q0, dq, d_ref, columns(0))
    if turn == 1:
        from_order(places, 0, dk_sum[...].astype(BF), d_ref, columns(1))
        from_order(places, 0, dv_sum[...].astype(BF), d_ref, columns(2))


def step_rate(update_sq, weight_sq, n_real):
    update_rms = jnp.sqrt(update_sq / n_real)
    weight_rms = jnp.sqrt(weight_sq / n_real)
    return rate_base * jnp.maximum(eps_two, weight_rms) / jnp.maximum(1.0, update_rms / clip_bound)


def results_kernel(
    counts, factor_ref, goq_qkv, goq_out, gff_down, gff_gate, gff_up,
    w_qkv, w_out, w_down, w_gate, w_up, r_qkv, r_out, r_down, r_gate, r_up, *refs,
):
    n_small = (len(refs) - 8) // 2
    small, small_out = refs[:n_small], refs[n_small + 8 :]
    qkv_grad, qkv_new, out_grad, out_new, gu_grad, gu_new, down_grad, down_new = refs[n_small:][:8]
    t = pl.program_id(0)
    n_gu, n_qkv, n_down, n_out = counts

    def after(grad, weight, row, factor):
        return weight.astype(F32) - grad * (lax.rsqrt(row) * factor)

    @pl.when(t == 0)
    def _():
        for src, dst in zip(small, small_out):
            dst[...] = src[...]

    @pl.when(t < n_gu)
    def _():
        factor = factor_ref[1:2, :]
        for i, (g, w, r) in enumerate(((gff_gate, w_gate, r_gate), (gff_up, w_up, r_up))):
            grad = g[0].astype(F32)
            gu_grad[:, i, :] = grad
            gu_new[:, i, :] = after(grad, w[...], r[0], factor)

    start = n_gu
    @pl.when((t >= start) & (t < start + n_qkv))
    def _():
        block = goq_qkv.shape[1]
        at = lax.rem(t - n_gu, factor_ref.shape[1] // block) * block
        factor = factor_ref[0:1, pl.ds(pl.multiple_of(at, block), block)]
        grad = goq_qkv[...].astype(F32).T
        qkv_grad[0] = grad
        down = jnp.broadcast_to(factor, (128, block)).T[:, 0:1]
        along = jnp.broadcast_to(lax.rsqrt(r_qkv[...]), (grad.shape[1], 128)).T[0:1, :]
        qkv_new[0] = w_qkv[0].astype(F32) - grad * (down * along)

    start = n_gu + n_qkv

    @pl.when((t >= start) & (t < start + n_down))
    def _():
        grad = gff_down[0].astype(F32)
        down_grad[...] = grad
        down_new[...] = after(grad, w_down[...], r_down[0], factor_ref[3:4, :])

    @pl.when(t >= n_gu + n_qkv + n_down)
    def _():
        grad = goq_out[...].astype(F32)
        out_grad[...] = grad
        out_new[...] = after(grad, w_out[...], r_out[...], factor_ref[2:3, :])


def results(ff, factors, goq, gff, w_qkv, w_out, w_down, w_gu, oq_new, ff_new, small):
    kinds, width, cols = w_qkv.shape
    rows, wide, high = 192, width, min(256, cols)
    counts = (-(-ff // rows), kinds * width // wide, -(-ff // rows), cols // high)
    starts = [sum(counts[:i]) for i in range(4)]
    per_kind = width // wide
    place = lambda part: lambda t: jnp.clip(t - starts[part], 0, counts[part] - 1)
    gu, qkv, down, out = (place(part) for part in range(4))
    shift = w_gu.shape[0] // 2 // rows
    third = lambda k, part, last: pl.BlockSpec((1, rows, last), lambda t: (k, part(t), 0))
    by_kind = lambda t: (qkv(t) // per_kind, lax.rem(qkv(t), per_kind), 0)
    out_at = 3 * cols // high
    qkv_spec = pl.BlockSpec((1, wide, cols), by_kind)
    out_spec = pl.BlockSpec((high, width), lambda t: (out(t), 0))
    gu_spec = pl.BlockSpec((rows, 2, width), lambda t: (gu(t), 0, 0))
    down_spec = pl.BlockSpec((rows, width), lambda t: (down(t), 0))
    shape = lambda *dims: jax.ShapeDtypeStruct(dims, F32)
    whole = [pl.BlockSpec(x.shape, lambda t: (0, 0)) for x in small]
    return pl.pallas_call(
        functools.partial(results_kernel, counts),
        grid=(sum(counts),),
        in_specs=[
            pl.BlockSpec(factors.shape, lambda t: (0, 0)),
            pl.BlockSpec((cols, wide), lambda t: by_kind(t)[:2]),
            pl.BlockSpec((high, width), lambda t: (out_at + out(t), 0)),
            third(0, down, width),
            third(1, gu, width),
            third(2, gu, width),
            qkv_spec,
            out_spec,
            down_spec,
            pl.BlockSpec((rows, width), lambda t: (gu(t), 0)),
            pl.BlockSpec((rows, width), lambda t: (gu(t) + shift, 0)),
            pl.BlockSpec((cols, 1), lambda t: (by_kind(t)[0], 0)),
            pl.BlockSpec((high, 1), lambda t: (out_at + out(t), 0)),
            third(0, down, 1),
            third(1, gu, 1),
            third(2, gu, 1),
        ]
        + whole,
        out_specs=[qkv_spec, qkv_spec, out_spec, out_spec, gu_spec, gu_spec, down_spec, down_spec]
        + whole,
        out_shape=[shape(kinds, width, cols)] * 2
        + [shape(cols, width)] * 2
        + [shape(ff, 2, width)] * 2
        + [shape(ff, width)] * 2
        + [shape(*x.shape) for x in small],
        compiler_params=pltpu.CompilerParams(vmem_limit_bytes=56 << 20),
        cost_estimate=cost(28),
    )(
        factors, goq, goq, gff, gff, gff, w_qkv, w_out, w_down, w_gu, w_gu,
        oq_new, oq_new, ff_new, ff_new, ff_new, *small,
    )


def exchange_kernel(
    n_dp, n, cells, one_ref, two_ref, sums_ref, totals_ref, squares_ref, old_ref, ln_ref, second_ref,
    factor_ref, qkv_row, gu_row, out_col, down_col, ln_tot, ln_second, ln_new,
    x_ref, o_ref, dp_buf, rows, part_buf, total, whole, sems,
):
    me_d, me = lax.axis_index("dp"), lax.axis_index("tensor")
    width = x_ref.shape[1] // n
    columns = lambda t: pl.ds(pl.multiple_of(t * width, width), width)
    dp_peers = [(k - 1, lax.rem(me_d + k, n_dp)) for k in range(1, n_dp)]
    peers = [(k - 1, lax.rem(me + k, n)) for k in range(1, n)]
    barrier = pltpu.get_barrier_semaphore()
    for _, d in dp_peers:
        pl.semaphore_signal(barrier, inc=1, device_id={"dp": d}, device_id_type=pl.DeviceIdType.MESH)
    for _, t in peers:
        pl.semaphore_signal(barrier, inc=1, device_id={"tensor": t}, device_id_type=pl.DeviceIdType.MESH)
    pl.semaphore_wait(barrier, n_dp + n - 2)

    def push(stage, src, dst, k, device):
        copy = pltpu.make_async_remote_copy(
            src_ref=src, dst_ref=dst, send_sem=sems.at[0, stage, k], recv_sem=sems.at[1, stage, k],
            device_id=device, device_id_type=pl.DeviceIdType.MESH,
        )
        copy.start()
        return copy

    x_ref[0:2, :] = one_ref[...]
    x_ref[2:4, :] = two_ref[...]
    x_ref[4:8, :] = jnp.zeros((4, x_ref.shape[1]), F32)
    lane = lax.broadcasted_iota(jnp.int32, (1, 128), 1)
    add_up = lambda v: jnp.sum(jnp.sum(v, axis=0, keepdims=True), axis=1, keepdims=True)
    scalars = [add_up(squares_ref[i]) for i in range(4)] + [totals_ref[i : i + 1, 0:1] for i in range(2)]
    x_ref[4:5, 0:128] = sum(jnp.where(lane == i, v, 0.0) for i, v in enumerate(scalars)) / n_dp
    x_ref[8:16, :] = sums_ref[...]
    first = [push(0, x_ref.at[pl.ds(0, 8)], dp_buf.at[me_d], k, {"dp": d}) for k, d in dp_peers]
    rows[...] = x_ref[...]
    dp_buf[me_d] = x_ref[0:8, :]
    for copy in first:
        copy.wait()
    rows[0:8, :] = sum(dp_buf[d] for d in range(n_dp))
    second = [push(1, rows.at[:, columns(t)], part_buf.at[me], k, {"tensor": t}) for k, t in peers]
    part_buf[me] = rows[:, columns(me)]
    for copy in second:
        copy.wait()
    total[...] = sum(part_buf[t] for t in range(n))
    third = [push(2, total, whole.at[me], k, {"tensor": t}) for k, t in peers]
    whole[me] = total[...]
    for copy in third:
        copy.wait()
    for t in range(n):
        o_ref[:, t * width : (t + 1) * width] = whole[t]

    columns_all = x_ref.shape[1]
    blend = lambda old, new: DECAY * old + (1.0 - DECAY) * new
    mean_of = lambda v: jnp.sum(v, axis=1, keepdims=True) / columns_all
    at = lambda i: o_ref[i : i + 1, :]
    scalar = lambda i: o_ref[4:5, i : i + 1]
    news = (qkv_row, gu_row, out_col, down_col)
    for i, (new_ref, (count, real, by_row)) in enumerate(zip(news, cells)):
        new = blend(old_ref[i : i + 1, :], at(8 + 2 * i) / count)
        new_ref[...] = new
        mean = mean_of(new) if by_row else scalar(2 + i) / count
        update_sq = jnp.sum(at(9 + 2 * i) / new, axis=1, keepdims=True) * mean
        rate = step_rate(update_sq, scalar(i), real)
        factor_ref[i : i + 1, :] = lax.rsqrt(new) * (rate * jnp.sqrt(mean))
    grad, weight = o_ref[0:4, :], ln_ref[...]
    second = blend(second_ref[...], grad * grad + eps_one)
    update = grad * lax.rsqrt(second)
    update_rms = jnp.sqrt(mean_of(update * update))
    weight_rms = jnp.sqrt(mean_of(weight * weight))
    ln_tot[...] = grad
    ln_second[...] = second
    ln_new[...] = weight - rate_base * jnp.maximum(eps_two, weight_rms) * update / jnp.maximum(
        1.0, update_rms / clip_bound
    )


def exchange(n_dp, n, cells, ln_one, ln_two, sums, totals, squares, old, ln_params, ln_second):
    height, width = 16, sums.shape[1]
    slots = pltpu.VMEM((n, height, width // n), F32)
    shape = lambda *dims: jax.ShapeDtypeStruct(dims, F32)
    return pl.pallas_call(
        functools.partial(exchange_kernel, n_dp, n, cells),
        out_shape=[shape(4, width)] + [shape(1, width)] * 4 + [shape(4, width)] * 3,
        in_specs=[VMEM_SPEC] * 8,
        out_specs=[VMEM_SPEC] * 8,
        scratch_shapes=[
            pltpu.VMEM((height, width), F32),
            pltpu.VMEM((height, width), F32),
            pltpu.VMEM((n_dp, 8, width), F32),
            pltpu.VMEM((height, width), F32),
            slots,
            pltpu.VMEM((height, width // n), F32),
            slots,
            pltpu.SemaphoreType.DMA((2, 3, max(n, n_dp) - 1)),
        ],
        compiler_params=pltpu.CompilerParams(collective_id=0, has_side_effects=True),
        cost_estimate=cost(18),
    )(ln_one, ln_two, sums, totals, squares, old, ln_params, ln_second)


def on_device(
    layer_in,
    cotangent,
    lengths,
    prefix,
    pad_mask,
    clusters,
    qkv_w,
    out_w,
    gate_up_w,
    down_w,
    ln_params,
    qkv_row,
    qkv_col,
    out_row,
    out_col,
    gu_row,
    gu_col,
    down_row,
    down_col,
    ln_second,
):
    n_data = lax.axis_size("dp")
    n_tensor = lax.axis_size("tensor")
    tensor_rank = lax.axis_index("tensor")
    data_rank = lax.axis_index("dp")
    rows_dev, width = layer_in.shape
    cols_dev = qkv_w.shape[2]
    heads_dev = cols_dev // HD
    ff_dev = gate_up_w.shape[2]
    ff_pad = -(-ff_dev // 384) * 384
    n_clusters = max(2, n_data // 2)
    seq_length = lengths[0]
    seq_prefix = prefix[0]

    onehot = (clusters[:, None] == jnp.arange(n_clusters, dtype=jnp.int32)[None, :]).astype(F32)
    counts = jnp.sum(onehot, axis=0)
    own_row = jnp.sum(
        jnp.where((jnp.arange(n_data, dtype=jnp.int32) == data_rank)[:, None], onehot, 0.0), axis=0
    )
    seq_weight = jnp.sum(own_row / jnp.maximum(counts, 1.0))
    own_pos = tensor_rank * rows_dev + jnp.arange(rows_dev, dtype=jnp.int32)
    live_rows = ((own_pos < seq_length) & (pad_mask == 1)).astype(F32)
    row_weight = (live_rows * seq_weight)[:, None]

    key_live = (own_pos == 0) | (own_pos < seq_length) & (pad_mask == 1)
    seen_from = jnp.where(key_live, jnp.where(own_pos < seq_prefix, 0, own_pos), 2 * SLOT)
    seen = jnp.broadcast_to(seen_from.astype(F32)[None], (8, rows_dev))

    col_index = tensor_rank * ff_dev + jnp.arange(ff_pad, dtype=jnp.int32)
    ff_real = ((col_index < FF) & (jnp.arange(ff_pad) < ff_dev)).astype(F32)
    ff_mask = ff_real[:ff_dev]

    act_one_all, qkv, seen_all, w_gu = first_gather(
        n_tensor, layer_in, seen, ln_params, jnp.transpose(qkv_w, (1, 0, 2)),
        jnp.transpose(gate_up_w, (2, 1, 0)),
    )

    pad = ((0, ff_pad - ff_dev), (0, 0))
    w_down = jnp.pad(down_w, pad)
    real_column = ff_real[:, None]
    qkv_t = jnp.transpose(qkv_w, (1, 0, 2))

    grad_all, context, lse, squares, thr = grad_gather(
        n_tensor, cotangent, row_weight, qkv, seen_all, real_column, qkv_t, w_gu, out_w, w_down
    )
    hidden_own, norm_two = mix_scatter(n_tensor, context, out_w, layer_in, ln_params)

    act_two_all, inner_all, d_gu_all, d_hidden, d_hidden_low, ln_two_part = both_ways(
        n_tensor, norm_two, w_gu, w_down, ff_real[None, :], hidden_own, cotangent, row_weight,
        ln_params, grad_all,
    )

    n_x = n_data // 2
    d_context, out_part, ff_mine, down_slots = back_gather(
        n_tensor, n_x, ff_dev, d_hidden_low, out_w, context,
        inner_all, d_gu_all, grad_all, act_two_all,
    )

    layer_out, d_qkv, gu_slots, out_slots, oq_mine = ffn_scatter(
        n_tensor, n_x, inner_all, w_down, hidden_own, thr, qkv, d_context, lse,
        out_part, act_one_all, ff_mine,
    )

    ff_rows = ff_mine.shape[1]
    more = ((0, 0), (0, ff_rows - ff_dev))
    oq_old = jnp.concatenate([qkv_col.reshape(-1), out_row])[:, None]
    ff_old = jnp.pad(jnp.concatenate([down_row[None], gu_col]), more, constant_values=1.0)[:, :, None]
    input_grad, goq, gff, oq_new, ff_new, sums, ln_one_part, totals = last_scatter(
        n_tensor, n_x, d_qkv, qkv_t, oq_mine, oq_old, ff_old, real_column,
        ff_mine, down_slots, gu_slots, out_slots, layer_in, d_hidden, ln_params,
    )
    qkv_col_new, out_row_new = oq_new[: 3 * cols_dev, 0], oq_new[3 * cols_dev :, 0]
    down_row_new, gu_col_new = ff_new[0, :ff_dev, 0], ff_new[1:, :ff_dev, 0]

    rows_all = cols_dev * n_tensor
    cells = (
        (3 * rows_all, width * 3 * rows_all, True),
        (2 * FF, width * 2 * FF, True),
        (rows_all, rows_all * width, False),
        (FF, FF * width, False),
    )
    factors, *small = exchange(
        n_data, n_tensor, cells, ln_one_part, ln_two_part, sums, totals, squares,
        jnp.stack([qkv_row, gu_row, out_col, down_col]), ln_params, ln_second,
    )
    qkv_grad, qkv_new, out_sum, out_new, gu_grad, gu_new, down_sum, down_new, *small = results(
        ff_dev, factors, goq, gff, qkv_t, out_w, w_down, w_gu, oq_new, ff_new, small
    )
    qkv_row_new, gu_row_new, out_col_new, down_col_new, ln_tot, ln_second_new, ln_new = small
    qkv_back = lambda x: jnp.transpose(x, (1, 0, 2))
    return (
        layer_out,
        input_grad,
        qkv_back(qkv_grad),
        qkv_back(qkv_new),
        qkv_row_new[0],
        qkv_col_new.reshape(3, -1),
        out_sum,
        out_new,
        out_row_new,
        out_col_new[0],
        jnp.transpose(gu_grad, (2, 1, 0)),
        jnp.transpose(gu_new, (2, 1, 0)),
        gu_row_new[0],
        gu_col_new,
        down_sum,
        down_new,
        down_row_new,
        down_col_new[0],
        ln_tot,
        ln_second_new,
        ln_new,
    )


def solution(mesh):
    in_specs = (
        P(("dp", "tensor"), None),
        P(("dp", "tensor"), None),
        P("dp"),
        P("dp"),
        P(("dp", "tensor")),
        P(),
        P(None, None, "tensor"),
        P("tensor", None),
        P(None, None, "tensor"),
        P("tensor", None),
        P(),
        P(),
        P(None, "tensor"),
        P("tensor"),
        P(),
        P(),
        P(None, "tensor"),
        P("tensor"),
        P(),
        P(),
    )
    out_specs = (
        P(("dp", "tensor"), None),
        P(("dp", "tensor"), None),
        P(None, None, "tensor"),
        P(None, None, "tensor"),
        P(),
        P(None, "tensor"),
        P("tensor", None),
        P("tensor", None),
        P("tensor"),
        P(),
        P(None, None, "tensor"),
        P(None, None, "tensor"),
        P(),
        P(None, "tensor"),
        P("tensor", None),
        P("tensor", None),
        P("tensor"),
        P(),
        P(),
        P(),
        P(),
    )
    return jax.shard_map(
        on_device, mesh=mesh, in_specs=in_specs, out_specs=out_specs, check_vma=False
    )
```

```python
import functools

import jax
import jax.numpy as jnp
from jax import lax
from jax.experimental import pallas as pl
from jax.experimental.pallas import tpu as pltpu
from jax.sharding import PartitionSpec as P

HD = 128
FF = 5461
SLOT = 2048
STEP = 10
DECAY = 1.0 - STEP ** (-0.8)
PREFIX_MAX = SLOT // 2
Q_BLOCK = 512

ln_eps = 1e-05
eps_one = 1e-30
eps_two = 0.001
clip_bound = 1.0
rate_base = 1.0
masked_score = -1e30
LOG2E = 1.4426950408889634
BF = jnp.bfloat16
F32 = jnp.float32


def dot(a, b, dims):
    return lax.dot_general(a, b, (dims, ((), ())), preferred_element_type=F32)


def ring_order(n):
    b_size = 2 if n <= 8 else 4
    a_size = n // b_size
    order = []
    for a in range(a_size):
        cols = list(range(1, b_size))
        order += [a * b_size + c for c in (cols[::-1] if a % 2 else cols)]
    for a in range(a_size - 1, -1, -1):
        order.append(a * b_size)
    return order


def cost(micros):
    return pl.CostEstimate(flops=int(micros * 1e9), transcendentals=0, bytes_accessed=4 << 20)


PUSH = pl.DeviceIdType.MESH
PIECES = 2
ROW_BLOCK = 64


def pick(index, table):
    out = jnp.int32(table[0])
    for k in range(1, len(table)):
        out = jnp.where(index == k, jnp.int32(table[k]), out)
    return out


def neighbours(n):
    order = ring_order(n)
    pos = pick(lax.axis_index("tensor"), [order.index(t) for t in range(n)])
    ahead = pick(lax.rem(pos + 1, n), order)
    behind = pick(lax.rem(pos + n - 1, n), order)
    return pos, [{"tensor": ahead}, {"tensor": behind}]


def chunk_places(n, pos, rows):
    places = []
    for t in range(n):
        place = ring_order(n).index(t)
        places.append(lax.rem(pos + (n - place), n) * rows)
        places.append(lax.rem(place - pos + n, n) * rows + rows // 2)
    return places


def other_core():
    me = lax.axis_index("dp")
    return {"dp": me + 1 - 2 * lax.rem(me, 2)}


def other_chips(n_x):
    core, chip = lax.rem(lax.axis_index("dp"), 2), lax.axis_index("dp") // 2
    return chip, [{"dp": 2 * lax.rem(chip + k, n_x) + core} for k in range(1, n_x)]


def greet(devices):
    barrier = pltpu.get_barrier_semaphore()
    for device in devices:
        pl.semaphore_signal(barrier, inc=1, device_id=device, device_id_type=PUSH)
    pl.semaphore_wait(barrier, len(devices))


def ring_copy(land, send_sem, recv_sem, sides, d, s, piece=None):
    src, dst, sem = land.at[d, s], land.at[d, s + 1], d
    if piece is not None:
        size = land.shape[2] // PIECES
        rows = pl.ds(piece * size, size)
        src, dst, sem = land.at[d, s, rows], land.at[d, s + 1, rows], d * PIECES + piece
    return pltpu.make_async_remote_copy(
        src_ref=src,
        dst_ref=dst,
        send_sem=send_sem.at[sem, s],
        recv_sem=recv_sem.at[sem, s],
        device_id=sides[d],
        device_id_type=PUSH,
    )


def ring_sent(n, copy, pieces=(None,)):
    def sent(s, carry):
        for d in range(2):
            for piece in pieces:
                copy(d, s, piece).wait_send()
        return carry

    lax.fori_loop(0, n - 1, sent, 0)


def gather_start(x_ref, land):
    half = x_ref.shape[0] // 2
    land[0, 0] = x_ref[:half, :]
    land[1, 0] = x_ref[half:, :]


def gather_step(n, copy, s):
    for piece in range(PIECES):
        for d in range(2):

            @pl.when(s > 0)
            def _():
                copy(d, s - 1, piece).wait_recv()

            @pl.when(s < n - 1)
            def _():
                copy(d, s, piece).start()


def ring_gather(n, x_ref, land, send_sem, recv_sem, sides, work):
    copy = functools.partial(ring_copy, land, send_sem, recv_sem, sides)
    gather_start(x_ref, land)

    def step(s, carry):
        gather_step(n, copy, s)
        work(s)
        return carry

    lax.fori_loop(0, n, step, 0)
    ring_sent(n, copy, range(PIECES))


def scatter_start(land):
    for d in range(2):
        land[d, 0] = jnp.zeros(land.shape[2:], land.dtype)


def scatter_step(n, copy, land, term_buf, finish, s):
    half = term_buf.shape[0] // 2
    size = half // PIECES
    for piece in range(PIECES):
        for d in range(2):
            part = slice(piece * size, (piece + 1) * size)
            rows = slice(d * half + piece * size, d * half + (piece + 1) * size)

            @pl.when(s > 0)
            def _():
                copy(d, s - 1, piece).wait_recv()

            total = land[d, s, part].astype(F32) + term_buf[rows, :]

            @pl.when(s < n - 1)
            def _():
                land[d, s, part] = total.astype(BF)
                copy(d, s, piece).start()

            @pl.when(s == n - 1)
            def _():
                finish(rows, total)


def ring_scatter(n, land, send_sem, recv_sem, sides, term_buf, term, work, finish):
    copy = functools.partial(ring_copy, land, send_sem, recv_sem, sides)
    scatter_start(land)

    def step(s, carry):
        term(lax.rem(s + 1, n))
        scatter_step(n, copy, land, term_buf, finish, s)
        work(s)
        return carry

    lax.fori_loop(0, n, step, 0)
    ring_sent(n, copy, range(PIECES))


def dot_columns(out, a, b, dims, block=512):
    width = b.shape[1]

    def columns(j, carry):
        at = pl.ds(pl.multiple_of(j * block, block), block)
        out(at, dot(a, b[:, at], dims))
        return carry

    lax.fori_loop(0, width // block, columns, 0)


def first_kernel(
    n, x_ref, seen_ref, ln_ref, w_ref, pair_hbm, act_ref, qkv_ref, seen_all, gu_hbm,
    land, act_buf, seen_buf, pair_buf, gu_ref, send_sem, recv_sem, act_sem, seen_sem, pair_sem, gu_sem,
):
    ff, block = pair_hbm.shape[0], pair_buf.shape[1]
    ff_pad = gu_ref.shape[0] // 2
    n_pairs = ff_pad // block

    def pair_load(b):
        rows = min(block, ff - b * block)
        return pltpu.make_async_copy(
            pair_hbm.at[pl.ds(b * block, rows)], pair_buf.at[b % 2, pl.ds(0, rows)], pair_sem.at[b % 2]
        )

    def gu_copy(i, b):
        at = pl.ds(i * ff_pad + b * block, block)
        return pltpu.make_async_copy(gu_ref.at[at], gu_hbm.at[at], gu_sem.at[i, b])

    def pair_start(b):
        if b * block + block > ff:
            pair_buf[b % 2] = jnp.zeros(pair_buf.shape[1:], BF)
        pair_load(b).start()

    for b in range(min(2, n_pairs)):
        pair_start(b)
    rows, cols = x_ref.shape[0], w_ref.shape[2]
    me = lax.axis_index("tensor")
    peers = [lax.rem(me + k, n) for k in range(1, n)]
    sides = neighbours(n)[1]
    greet([{"tensor": t} for t in peers])

    def seen_copy(k):
        return pltpu.make_async_remote_copy(
            src_ref=seen_ref, dst_ref=seen_buf.at[me], send_sem=seen_sem.at[0, k],
            recv_sem=seen_sem.at[1, k], device_id={"tensor": peers[k]}, device_id_type=PUSH,
        )

    def act_copy(s):
        place = pl.ds(pl.multiple_of(s * rows, rows), rows)
        return pltpu.make_async_copy(act_buf.at[s], act_ref.at[place], act_sem.at[s])

    def work(s):
        @pl.when(s == 0)
        def _():
            for k in range(n - 1):
                seen_copy(k).start()

        chunk = jnp.concatenate([land[0, s], land[1, s]], axis=0).astype(F32)
        act = layer_norm(chunk, ln_ref[0:1, :], ln_ref[1:2, :]).astype(BF)
        act_buf[s] = act
        act_copy(s).start()
        place = pl.ds(pl.multiple_of(s * rows, rows), rows)
        for k in range(3):
            qkv_ref[place, k * cols : (k + 1) * cols] = dot(act, w_ref[k], ((1,), (0,))).astype(BF)
        for b in range(n_pairs):

            @pl.when(s == b)
            def _():
                pair_load(b).wait()
                for i in range(2):
                    at = i * ff_pad + b * block
                    gu_ref[at : at + block, :] = pair_buf[b % 2, :, i, :]
                    gu_copy(i, b).start()
                if b + 2 < n_pairs:
                    pair_start(b + 2)

    ring_gather(n, x_ref, land, send_sem, recv_sem, sides, work)
    seen_buf[me] = seen_ref[...]
    for k in range(n - 1):
        seen_copy(k).wait()
    seen_all[...] = seen_buf[...]
    for b in range(n_pairs):
        for i in range(2):
            gu_copy(i, b).wait()

    def written(s, carry):
        act_copy(s).wait()
        return carry

    lax.fori_loop(0, n, written, 0)


def ring_scratch(n, rows, width, pieces):
    return [pltpu.VMEM((2, n, rows // 2, width), BF)], [
        pltpu.SemaphoreType.DMA((2 * pieces, n - 1)),
        pltpu.SemaphoreType.DMA((2 * pieces, n - 1)),
    ]


VMEM_SPEC = pl.BlockSpec(memory_space=pltpu.VMEM)
ANY_SPEC = pl.BlockSpec(memory_space=pl.ANY)


def first_gather(n, x, seen, ln_params, w, pairs):
    rows, width = x.shape
    cols = w.shape[2]
    block = 96
    ff_pad = -(-pairs.shape[0] // block) * block
    buf, sems = ring_scratch(n, rows, width, PIECES)
    return pl.pallas_call(
        functools.partial(first_kernel, n),
        in_specs=[VMEM_SPEC] * 4 + [ANY_SPEC],
        out_specs=[ANY_SPEC] + [VMEM_SPEC] * 2 + [ANY_SPEC],
        out_shape=[
            jax.ShapeDtypeStruct((n * rows, width), BF),
            jax.ShapeDtypeStruct((n * rows, 3 * cols), BF),
            jax.ShapeDtypeStruct((n,) + seen.shape, F32),
            jax.ShapeDtypeStruct((2 * ff_pad, width), BF),
        ],
        scratch_shapes=buf
        + [pltpu.VMEM((n, rows, width), BF), pltpu.VMEM((n,) + seen.shape, F32)]
        + [pltpu.VMEM((2, block, 2, width), BF), pltpu.VMEM((2 * ff_pad, width), BF)]
        + sems
        + [pltpu.SemaphoreType.DMA((n,)), pltpu.SemaphoreType.DMA((2, n - 1))]
        + [pltpu.SemaphoreType.DMA((2,)), pltpu.SemaphoreType.DMA((2, ff_pad // block))],
        compiler_params=pltpu.CompilerParams(
            collective_id=1, has_side_effects=True, vmem_limit_bytes=56 << 20
        ),
        cost_estimate=pl.CostEstimate(
            flops=6 * n * rows * width * cols, transcendentals=0, bytes_accessed=40 << 20
        ),
    )(x, seen, ln_params, w, pairs)


def grad_kernel(
    n, heads, x_ref, weight_ref, qkv_ref, seen_ref, real_ref, out_w_ref, qkv_w_hbm, gu_w_hbm, down_w_hbm,
    all_ref, ctx_ref, lse_ref, square_ref, thr_ref,
    land, own_ref, q_ref, k_ref, v_ref, qkv_w_ref, gu_w_ref, down_w_ref, send_sem, recv_sem, all_sem,
    load_sem,
):
    rows = x_ref.shape[0]
    half = rows // 2
    pos, sides = neighbours(n)
    places = chunk_places(n, pos, rows)
    loads = [
        pltpu.make_async_copy(src, dst, load_sem.at[i])
        for i, (src, dst) in enumerate(
            ((qkv_w_hbm, qkv_w_ref), (gu_w_hbm, gu_w_ref), (down_w_hbm, down_w_ref))
        )
    ]
    for load in loads:
        load.start()
    own_ref[...] = (x_ref[...].astype(F32) * weight_ref[...]).astype(BF)
    for t in range(n):
        column = jnp.broadcast_to(seen_ref[t, 0:1, :], (128, rows)).T
        thr_ref[t * rows : (t + 1) * rows, :] = column
    greet(sides)

    def all_copy(d, s):
        place = pl.ds(pl.multiple_of(s * rows + d * half, half), half)
        return pltpu.make_async_copy(land.at[d, s], all_ref.at[place], all_sem.at[d, s])

    def squares(i, ref, real):
        block, cols = ROW_BLOCK, ref.shape[1]

        def add(j, carry):
            at = pl.multiple_of(j * block, block)
            value = ref[pl.ds(at, block), :].astype(F32)
            value = value * value
            if real is not None:
                value = value * real[pl.ds(lax.rem(at, real.shape[0]), block), :]
            square_ref[i, :, :cols] += sum(value[k : k + 8] for k in range(0, block, 8))
            return carry

        lax.fori_loop(0, ref.shape[0] // block, add, 0)

    def work(s):
        for d in range(2):
            all_copy(d, s).start()
        for h in range(heads):

            @pl.when(s == h)
            def _():
                columns = lambda i: slice((i * heads + h) * HD, (i * heads + h + 1) * HD)
                for i, dst in enumerate((q_ref, k_ref, v_ref)):
                    to_order(places, qkv_ref, columns(i), dst)
                attn_forward_head(
                    places, thr_ref, lse_ref.at[h], q_ref, k_ref, v_ref, ctx_ref, columns(0)
                )

        @pl.when(s == heads)
        def _():
            square_ref[...] = jnp.zeros_like(square_ref)
            loads[0].wait()
            for k in range(3):
                squares(0, qkv_w_ref.at[k], None)

        @pl.when(s == heads + 1)
        def _():
            loads[1].wait()
            squares(1, gu_w_ref, real_ref)

        @pl.when(s == heads + 2)
        def _():
            squares(2, out_w_ref, None)
            loads[2].wait()
            squares(3, down_w_ref, real_ref)

    ring_gather(n, own_ref, land, send_sem, recv_sem, sides, work)

    def written(s, carry):
        for d in range(2):
            all_copy(d, s).wait()
        return carry

    lax.fori_loop(0, n, written, 0)


def grad_gather(n, x, weight, qkv, thr, real, qkv_w, gu_w, out_w, down_w):
    rows, width = x.shape
    cols = out_w.shape[0]
    heads = cols // HD
    buf, sems = ring_scratch(n, rows, width, PIECES)
    return pl.pallas_call(
        functools.partial(grad_kernel, n, heads),
        in_specs=[VMEM_SPEC] * 6 + [ANY_SPEC] * 3,
        out_specs=[ANY_SPEC] + [VMEM_SPEC] * 4,
        out_shape=[
            jax.ShapeDtypeStruct((n * rows, width), BF),
            jax.ShapeDtypeStruct((n * rows, cols), BF),
            jax.ShapeDtypeStruct((heads, 1, SLOT), F32),
            jax.ShapeDtypeStruct((4, 8, width), F32),
            jax.ShapeDtypeStruct((SLOT, 128), F32),
        ],
        scratch_shapes=buf
        + [pltpu.VMEM((rows, width), BF)]
        + [pltpu.VMEM((SLOT, HD), BF)] * 3
        + [pltpu.VMEM(w.shape, BF) for w in (qkv_w, gu_w, down_w)]
        + sems
        + [pltpu.SemaphoreType.DMA((2, n)), pltpu.SemaphoreType.DMA((3,))],
        compiler_params=pltpu.CompilerParams(
            collective_id=5, has_side_effects=True, vmem_limit_bytes=60 << 20
        ),
        cost_estimate=cost(80),
    )(x, weight, qkv, thr, real, out_w, qkv_w, gu_w, down_w)


def mix_kernel(
    n, ctx_ref, w_ref, x_ref, ln_ref, hidden_ref, norm_ref, land, term_buf, send_sem, recv_sem
):
    rows = x_ref.shape[0]
    sides = neighbours(n)[1]
    greet(sides)

    def term(c):
        place = pl.ds(pl.multiple_of(c * rows, rows), rows)

        def put(at, value):
            term_buf[:, at] = value

        dot_columns(put, ctx_ref[place, :], w_ref, ((1,), (0,)))

    def finish(at, total):
        hidden = x_ref[at, :].astype(F32) + total
        hidden_ref[at, :] = hidden
        norm_ref[at, :] = layer_norm(hidden, ln_ref[2:3, :], ln_ref[3:4, :]).astype(BF)

    ring_scatter(n, land, send_sem, recv_sem, sides, term_buf, term, lambda s: None, finish)


def mix_scatter(n, context, w, x, ln_params):
    rows, width = x.shape
    buf, sems = ring_scratch(n, rows, width, PIECES)
    return pl.pallas_call(
        functools.partial(mix_kernel, n),
        in_specs=[VMEM_SPEC] * 4,
        out_specs=[VMEM_SPEC] * 2,
        out_shape=[
            jax.ShapeDtypeStruct((rows, width), F32),
            jax.ShapeDtypeStruct((rows, width), BF),
        ],
        scratch_shapes=buf + [pltpu.VMEM((rows, width), F32)] + sems,
        compiler_params=pltpu.CompilerParams(
            collective_id=6, has_side_effects=True, vmem_limit_bytes=40 << 20
        ),
        cost_estimate=cost(80),
    )(context, w, x, ln_params)


def gelu_pair(gate):
    c, a = (2.0 / jnp.pi) ** 0.5, 0.044715
    square = gate * gate
    t = jnp.tanh(c * gate * (1.0 + a * square))
    value = 0.5 * gate * (1.0 + t)
    slope = 0.5 * (1.0 + t) + 0.5 * gate * (1.0 - t * t) * (c * (1.0 + 3.0 * a * square))
    return value, slope


def both_kernel(
    n, x_ref, real_ref, hidden_ref, cot_ref, weight_ref, ln_ref, gu_w_hbm, down_w_hbm, grad_hbm,
    act_ref, inner_hbm, d_gu_hbm, out_ref, low_ref, ln_sum,
    land, sums, term_buf, gate_up, d_inner, grad_buf, gu_w_ref, down_w_ref, inner_ref, d_gu_ref,
    send_sem, recv_sem, sum_send, sum_recv, act_sem, grad_sem, load_sem, out_sem,
):
    rows = x_ref.shape[0]
    half = rows // 2
    ff_pad = down_w_ref.shape[0]
    sides = neighbours(n)[1]
    copy = functools.partial(ring_copy, land, send_sem, recv_sem, sides)
    sum_copy = functools.partial(ring_copy, sums, sum_send, sum_recv, sides)

    def grad_load(s):
        place = pl.ds(pl.multiple_of(s * rows, rows), rows)
        slot = lax.rem(s, 2)
        return pltpu.make_async_copy(grad_hbm.at[place], grad_buf.at[slot], grad_sem.at[slot])

    def act_copy(d, s):
        place = pl.ds(pl.multiple_of(s * rows + d * half, half), half)
        return pltpu.make_async_copy(land.at[d, s], act_ref.at[place], act_sem.at[d, s])

    def out_copy(i, s):
        place = pl.ds(pl.multiple_of(s * rows, rows), rows)
        src, dst = ((inner_ref, inner_hbm), (d_gu_ref, d_gu_hbm))[i]
        return pltpu.make_async_copy(src.at[place], dst.at[place], out_sem.at[i, s])

    loads = [
        pltpu.make_async_copy(gu_w_hbm, gu_w_ref, load_sem.at[0]),
        pltpu.make_async_copy(down_w_hbm, down_w_ref, load_sem.at[1]),
    ]
    for load in loads:
        load.start()
    grad_load(0).start()
    grad_load(1).start()
    greet(sides)
    gather_start(x_ref, land)
    ln_sum[...] = jnp.zeros_like(ln_sum)
    scatter_start(sums)

    def by_rows(out, a, w_ref):
        block = 384

        def some(j, carry):
            at = pl.ds(pl.multiple_of(j * block, block), block)
            out[:, at] = dot(a, w_ref[at, :], ((1,), (1,)))
            return carry

        lax.fori_loop(0, w_ref.shape[0] // block, some, 0)

    def term(c):
        place = pl.ds(pl.multiple_of(c * rows, rows), rows)

        def put(at, value):
            term_buf[:, at] = value

        dot_columns(put, d_gu_ref[place, :], gu_w_ref, ((1,), (0,)))

    def finish(at, total):
        d_rows, sums_two = layer_norm_back(hidden_ref[at, :], ln_ref[2:3, :], total)
        d_rows = cot_ref[at, :].astype(F32) * weight_ref[at, :] + d_rows
        out_ref[at, :] = d_rows
        low_ref[at, :] = d_rows.astype(BF)
        ln_sum[...] += sums_two

    def step(s, carry):
        gather_step(n, copy, s)
        for d in range(2):
            act_copy(d, s).start()

        @pl.when(s == 0)
        def _():
            for load in loads:
                load.wait()

        by_rows(gate_up, jnp.concatenate([land[0, s], land[1, s]], axis=0), gu_w_ref)
        grad_load(s).wait()
        by_rows(d_inner, grad_buf[lax.rem(s, 2)], down_w_ref)

        @pl.when(s < n - 2)
        def _():
            grad_load(s + 2).start()

        place = pl.ds(pl.multiple_of(s * rows, rows), rows)
        for at in range(0, ff_pad, 128):
            here, there = slice(at, at + 128), slice(ff_pad + at, ff_pad + at + 128)
            real = real_ref[:, here]
            gate, up = gate_up[:, here], gate_up[:, there]
            value, slope = gelu_pair(gate)
            back = d_inner[:, here] * real
            inner_ref[place, here] = (value * up * real).astype(BF)
            d_gu_ref[place, here] = (back * up * slope).astype(BF)
            d_gu_ref[place, there] = (back * value).astype(BF)

        for i in range(2):
            out_copy(i, s).start()

        @pl.when(s > 0)
        def _():
            term(s)
            scatter_step(n, sum_copy, sums, term_buf, finish, s - 1)

        return carry

    lax.fori_loop(0, n, step, 0)
    term(0)
    scatter_step(n, sum_copy, sums, term_buf, finish, n - 1)
    ring_sent(n, copy, range(PIECES))
    ring_sent(n, sum_copy, range(PIECES))

    def written(s, carry):
        for d in range(2):
            act_copy(d, s).wait()
            out_copy(d, s).wait()
        return carry

    lax.fori_loop(0, n, written, 0)


def both_ways(n, x, gu_w, down_w, real, hidden, cotangent, weight, ln_params, grad):
    rows, width = x.shape
    ff_pad = down_w.shape[0]
    buf, sems = ring_scratch(n, rows, width, PIECES)
    sum_buf, sum_sems = ring_scratch(n, rows, width, PIECES)
    return pl.pallas_call(
        functools.partial(both_kernel, n),
        in_specs=[VMEM_SPEC] * 6 + [ANY_SPEC] * 3,
        out_specs=[ANY_SPEC] * 3 + [VMEM_SPEC] * 3,
        out_shape=[
            jax.ShapeDtypeStruct((n * rows, width), BF),
            jax.ShapeDtypeStruct((n * rows, ff_pad), BF),
            jax.ShapeDtypeStruct((n * rows, 2 * ff_pad), BF),
            jax.ShapeDtypeStruct((rows, width), F32),
            jax.ShapeDtypeStruct((rows, width), BF),
            jax.ShapeDtypeStruct((2, width), F32),
        ],
        scratch_shapes=buf
        + sum_buf
        + [
            pltpu.VMEM((rows, width), F32),
            pltpu.VMEM((rows, 2 * ff_pad), F32),
            pltpu.VMEM((rows, ff_pad), F32),
            pltpu.VMEM((2, rows, width), BF),
            pltpu.VMEM(gu_w.shape, BF),
            pltpu.VMEM(down_w.shape, BF),
            pltpu.VMEM((n * rows, ff_pad), BF),
            pltpu.VMEM((n * rows, 2 * ff_pad), BF),
        ]
        + sems
        + sum_sems
        + [pltpu.SemaphoreType.DMA((2, n)), pltpu.SemaphoreType.DMA((2,))]
        + [pltpu.SemaphoreType.DMA((2,)), pltpu.SemaphoreType.DMA((2, n))],
        compiler_params=pltpu.CompilerParams(
            collective_id=7, has_side_effects=True, vmem_limit_bytes=60 << 20
        ),
        cost_estimate=cost(160),
    )(x, real, hidden, cotangent, weight, ln_params, gu_w, down_w, grad)


def back_kernel(
    n, n_x, x_ref, w_ref, ctx_ref, inner_hbm, d_gu_hbm, grad_hbm, act_hbm,
    d_ctx_ref, out_ref, mine_ref, slots_hbm,
    land, lhs, rhs, part, core_land, out_sum, send_sem, recv_sem, load_sem, core_sem, slot_sem,
):
    rows, ff_pad = x_ref.shape[0], lhs.shape[2]
    ff_rows, half = core_land.shape[1:]
    sides, partner = neighbours(n)[1], other_core()
    core = lax.rem(lax.axis_index("dp"), 2)
    loads = [
        pltpu.make_async_copy(src, dst, load_sem.at[i])
        for i, (src, dst) in enumerate(
            (
                (inner_hbm, lhs.at[0]),
                (grad_hbm, rhs.at[0]),
                (d_gu_hbm.at[:, pl.ds(0, ff_pad)], lhs.at[1]),
                (act_hbm, rhs.at[1]),
                (d_gu_hbm.at[:, pl.ds(ff_pad, ff_pad)], lhs.at[2]),
            )
        )
    ]
    for load in loads:
        load.start()
    out_sum[...] = jnp.zeros_like(out_sum)
    chip, chips = other_chips(n_x)
    greet(sides + [partner] + chips)

    def slot_copy(k):
        return pltpu.make_async_remote_copy(
            src_ref=mine_ref.at[0], dst_ref=slots_hbm.at[chip], send_sem=slot_sem.at[0, k],
            recv_sem=slot_sem.at[1, k], device_id=chips[k], device_id_type=PUSH,
        )

    def core_copy(i):
        return pltpu.make_async_remote_copy(
            src_ref=part.at[i, 1 - core],
            dst_ref=core_land.at[i],
            send_sem=core_sem.at[0, i],
            recv_sem=core_sem.at[1, i],
            device_id=partner,
            device_id_type=PUSH,
        )

    def work(s):
        chunk = jnp.concatenate([land[0, s], land[1, s]], axis=0)
        place = pl.ds(pl.multiple_of(s * rows, rows), rows)
        d_ctx_ref[place, :] = dot(chunk, w_ref[...], ((1,), (1,))).astype(BF)
        out_sum[...] += dot(ctx_ref[place, :], chunk, ((0,), (0,)))
        for i in range(3):
            for turn in range(2):

                @pl.when(s == 2 * i + turn)
                def _():
                    if turn == 0:
                        for load in (loads[:2], loads[2:4], loads[4:])[i]:
                            load.wait()
                    side = slice(turn * half, (turn + 1) * half)

                    def put(at, value):
                        part[i, turn, :, at] = value[:ff_rows].astype(BF)

                    dot_columns(put, lhs[i], rhs.at[min(i, 1), :, side], ((0,), (0,)))
                    if turn == 1:
                        core_copy(i).start()

            @pl.when(s == 2 * i + 3)
            def _():
                core_copy(i).wait()
                total = part[i, core].astype(F32) + core_land[i].astype(F32)
                mine_ref[i] = total.astype(BF)
                if i == 0:
                    for k in range(n_x - 1):
                        slot_copy(k).start()

    ring_gather(n, x_ref, land, send_sem, recv_sem, sides, work)
    out_ref[...] = out_sum[...].astype(BF)
    for k in range(n_x - 1):
        slot_copy(k).wait()


def back_gather(n, n_x, ff_dev, x, w, context, inner, d_gu, grad, act):
    rows, width = x.shape
    ff_pad = inner.shape[1]
    ff_rows = -(-ff_dev // ROW_BLOCK) * ROW_BLOCK
    buf, sems = ring_scratch(n, rows, width, PIECES)
    return pl.pallas_call(
        functools.partial(back_kernel, n, n_x),
        in_specs=[VMEM_SPEC] * 3 + [ANY_SPEC] * 4,
        out_specs=[VMEM_SPEC] * 3 + [ANY_SPEC],
        out_shape=[
            jax.ShapeDtypeStruct((n * rows, w.shape[0]), BF),
            jax.ShapeDtypeStruct(w.shape, BF),
            jax.ShapeDtypeStruct((3, ff_rows, width // 2), BF),
            jax.ShapeDtypeStruct((n_x, ff_rows, width // 2), BF),
        ],
        scratch_shapes=buf
        + [
            pltpu.VMEM((3, n * rows, ff_pad), BF),
            pltpu.VMEM((2, n * rows, width), BF),
            pltpu.VMEM((3, 2, ff_rows, width // 2), BF),
            pltpu.VMEM((3, ff_rows, width // 2), BF),
            pltpu.VMEM(w.shape, F32),
        ]
        + sems
        + [
            pltpu.SemaphoreType.DMA((5,)),
            pltpu.SemaphoreType.DMA((2, 3)),
            pltpu.SemaphoreType.DMA((2, n_x - 1)),
        ],
        compiler_params=pltpu.CompilerParams(
            collective_id=3, has_side_effects=True, vmem_limit_bytes=60 << 20
        ),
        cost_estimate=cost(80),
    )(x, w, context, inner, d_gu, grad, act)


def ffn_kernel(
    n, n_x, heads, inner_ref, w_ref, hidden_ref, thr_ref, qkv_ref, d_ctx_ref, lse_ref,
    out_part_ref, act_hbm, mine_hbm,
    out_ref, d_qkv_ref, slots_hbm, out_slots_hbm, oq_mine_ref,
    land, term_buf, q_ref, k_ref, v_ref, do_ref, dk_sum, dv_sum,
    act_buf, part, qkv_land, out_land,
    send_sem, recv_sem, act_sem, core_sem, slot_sem,
):
    rows = hidden_ref.shape[0]
    pos, sides = neighbours(n)
    partner = other_core()
    core = lax.rem(lax.axis_index("dp"), 2)
    chip, chips = other_chips(n_x)
    block = act_buf.shape[2]
    blocks = act_hbm.shape[1] // block
    qkv_cols, wide = qkv_land.shape
    wide_of = lambda c: pl.ds(pl.multiple_of(c * wide, wide), wide)

    def act_load(j):
        return pltpu.make_async_copy(
            act_hbm.at[:, pl.ds(j * block, block)], act_buf.at[j % 2], act_sem.at[j]
        )

    def core_copy(i):
        src, dst = (
            (part.at[:, wide_of(1 - core)], qkv_land),
            (out_part_ref.at[:, wide_of(1 - core)], out_land),
        )[i]
        return pltpu.make_async_remote_copy(
            src_ref=src, dst_ref=dst, send_sem=core_sem.at[0, i], recv_sem=core_sem.at[1, i],
            device_id=partner, device_id_type=PUSH,
        )

    def slot_copy(i, k):
        src, dst = (
            (mine_hbm.at[pl.ds(1, 2)], slots_hbm),
            (oq_mine_ref.at[pl.ds(qkv_cols, oq_mine_ref.shape[0] - qkv_cols)], out_slots_hbm),
        )[i]
        return pltpu.make_async_remote_copy(
            src_ref=src, dst_ref=dst.at[chip], send_sem=slot_sem.at[0, i, k],
            recv_sem=slot_sem.at[1, i, k], device_id=chips[k], device_id_type=PUSH,
        )

    for j in range(2):
        act_load(j).start()
    greet(sides + [partner] + chips)
    core_copy(1).start()
    for k in range(n_x - 1):
        slot_copy(0, k).start()
    places = chunk_places(n, pos, rows)

    def term(c):
        place = pl.ds(pl.multiple_of(c * rows, rows), rows)

        def put(at, value):
            term_buf[:, at] = value

        dot_columns(put, inner_ref[place, :], w_ref, ((1,), (0,)))

    def work(s):
        for h in range(heads):

            columns = lambda i: slice((i * heads + h) * HD, (i * heads + h + 1) * HD)
            for turn in range(2):

                @pl.when(s == 2 * h + turn)
                def _():
                    if turn == 0:
                        for i, dst in enumerate((q_ref, k_ref, v_ref)):
                            to_order(places, qkv_ref, columns(i), dst)
                        to_order(places, d_ctx_ref, columns(0), do_ref)
                    attn_backward_head(
                        turn, places, thr_ref, lse_ref.at[h], q_ref, k_ref, v_ref, do_ref,
                        dk_sum, dv_sum, d_qkv_ref, columns,
                    )

        @pl.when(s == 1)
        def _():
            core_copy(1).wait()
            total = out_part_ref[:, wide_of(core)].astype(F32) + out_land[...].astype(F32)
            oq_mine_ref[qkv_cols:, :] = total.astype(BF)
            for k in range(n_x - 1):
                slot_copy(1, k).start()

        for turn in range(blocks // 2):

            @pl.when(s == 2 * heads + turn)
            def _():
                for j in (2 * turn, 2 * turn + 1):
                    act_load(j).wait()
                    grad = dot(d_qkv_ref[...], act_buf[j % 2], ((0,), (0,)))
                    part[:, j * block : (j + 1) * block] = grad.astype(BF)
                for j in (2 * turn + 2, 2 * turn + 3):
                    if j < blocks:
                        act_load(j).start()
                if turn == blocks // 2 - 1:
                    core_copy(0).start()

    def finish(at, total):
        out_ref[at, :] = (hidden_ref[at, :] + total).astype(BF)

    ring_scatter(n, land, send_sem, recv_sem, sides, term_buf, term, work, finish)
    core_copy(0).wait()
    total = part[:, wide_of(core)].astype(F32) + qkv_land[...].astype(F32)
    oq_mine_ref[:qkv_cols, :] = total.astype(BF)
    for k in range(n_x - 1):
        slot_copy(0, k).wait()
        slot_copy(1, k).wait()


def ffn_scatter(n, n_x, inner, w, hidden, thr, qkv, d_context, lse, out_part, act, mine):
    rows, width = hidden.shape
    cols, block = d_context.shape[1], 512
    heads = d_context.shape[1] // HD
    buf, sems = ring_scratch(n, rows, width, PIECES)
    return pl.pallas_call(
        functools.partial(ffn_kernel, n, n_x, heads),
        in_specs=[VMEM_SPEC] * 8 + [ANY_SPEC] * 2,
        out_specs=[VMEM_SPEC] * 2 + [ANY_SPEC] * 2 + [VMEM_SPEC],
        out_shape=[
            jax.ShapeDtypeStruct((rows, width), BF),
            jax.ShapeDtypeStruct(qkv.shape, BF),
            jax.ShapeDtypeStruct((n_x, 2) + mine.shape[1:], BF),
            jax.ShapeDtypeStruct((n_x, cols, width // 2), BF),
            jax.ShapeDtypeStruct((4 * cols, width // 2), BF),
        ],
        scratch_shapes=buf
        + [pltpu.VMEM((rows, width), F32)]
        + [pltpu.VMEM((SLOT, HD), BF)] * 4
        + [pltpu.VMEM((SLOT, HD), F32)] * 2
        + [
            pltpu.VMEM((2, n * rows, block), BF),
            pltpu.VMEM((3 * cols, width), BF),
            pltpu.VMEM((3 * cols, width // 2), BF),
            pltpu.VMEM((cols, width // 2), BF),
        ]
        + sems
        + [
            pltpu.SemaphoreType.DMA((width // block,)),
            pltpu.SemaphoreType.DMA((2, 2)),
            pltpu.SemaphoreType.DMA((2, 2, n_x - 1)),
        ],
        compiler_params=pltpu.CompilerParams(
            collective_id=4, has_side_effects=True, vmem_limit_bytes=62 << 20
        ),
        cost_estimate=cost(95),
    )(inner, w, hidden, thr, qkv, d_context, lse, out_part, act, mine)


def row_sums(grad_ref, old_ref, real_ref, new_ref, c_ref, t_ref):
    width = grad_ref.shape[1]
    block = ROW_BLOCK

    def rows(i, carry):
        at = pl.ds(pl.multiple_of(i * block, block), block)
        grad = grad_ref[at, :].astype(F32)
        square = grad * grad
        real = 1.0 if real_ref is None else real_ref[at, :]
        total = (jnp.sum(square, axis=1, keepdims=True) + width * eps_one) * real
        new = DECAY * old_ref[at, :] + (1.0 - DECAY) * (total / width)
        new_ref[at, :] = new
        c = (square + eps_one) * real
        t = square * (real / new)
        c_ref[...] += sum(c[k : k + 8] for k in range(0, block, 8))
        t_ref[...] += sum(t[k : k + 8] for k in range(0, block, 8))
        return carry

    lax.fori_loop(0, grad_ref.shape[0] // block, rows, 0)


def last_kernel(
    n, n_x, d_qkv_ref, w_ref, oq_mine_ref, oq_old, ff_old, ff_real,
    x_ref, d_hidden_ref, ln_ref,
    mine_hbm, down_hbm, gu_hbm, out_hbm,
    out_ref, goq_hbm, gff_hbm, oq_new, ff_new, sums_ref, ln_sum, totals_ref,
    land, term_buf, goq_ref, gff_ref, qkv_land, out_slots, ff_own, ff_slots, c_sum, t_sum,
    send_sem, recv_sem, oq_sem, load_sem, join_sem, write_sem,
):
    rows = term_buf.shape[0]
    cols, width = w_ref.shape[2], term_buf.shape[1]
    sides, partner = neighbours(n)[1], other_core()
    core = lax.rem(lax.axis_index("dp"), 2)
    chip, chips = other_chips(n_x)
    half = width // 2
    own = pl.ds(pl.multiple_of(core * half, half), half)

    qkv_rows, out_rows = pl.ds(0, 3 * cols), pl.ds(3 * cols, cols)
    writes = [
        pltpu.make_async_copy(goq_ref, goq_hbm, write_sem.at[0]),
        pltpu.make_async_copy(gff_ref, gff_hbm, write_sem.at[1]),
    ]

    def loads(i):
        if i == 3:
            return [pltpu.make_async_copy(out_hbm, out_slots, load_sem.at[0, 3])]
        slots = down_hbm if i == 0 else gu_hbm.at[:, i - 1]
        return [
            pltpu.make_async_copy(mine_hbm.at[i], ff_own.at[i], load_sem.at[0, i]),
            pltpu.make_async_copy(slots, ff_slots.at[i], load_sem.at[1, i]),
        ]

    def oq_copy(k):
        return pltpu.make_async_remote_copy(
            src_ref=oq_mine_ref.at[qkv_rows], dst_ref=qkv_land.at[chip], send_sem=oq_sem.at[0, k],
            recv_sem=oq_sem.at[1, k], device_id=chips[k], device_id_type=PUSH,
        )

    def join(i):
        ref = gff_ref.at[i, :, own] if i < 3 else goq_ref.at[(qkv_rows, out_rows)[i - 3], own]
        return pltpu.make_async_remote_copy(
            src_ref=ref, dst_ref=ref, send_sem=join_sem.at[0, i], recv_sem=join_sem.at[1, i],
            device_id=partner, device_id_type=PUSH,
        )

    def chip_sum(own_half, slots):
        total = jnp.zeros(own_half.shape, F32)
        for x in range(n_x):
            total = total + jnp.where(chip == x, own_half, slots[x]).astype(F32)
        return total.astype(BF)

    for i in range(4):
        for load in loads(i):
            load.start()
    ln_sum[...] = jnp.zeros_like(ln_sum)
    greet(sides + [partner] + chips)
    for k in range(n_x - 1):
        oq_copy(k).start()

    def term(c):
        place = pl.ds(pl.multiple_of(c * rows, rows), rows)
        block = 512

        def columns(j, carry):
            at = pl.ds(pl.multiple_of(j * block, block), block)
            term_buf[:, at] = sum(
                dot(d_qkv_ref[place, k * cols : (k + 1) * cols], w_ref[k, at, :], ((1,), (1,)))
                for k in range(3)
            )
            return carry

        lax.fori_loop(0, width // block, columns, 0)

    def sums(group, ref, first=True):
        if first:
            c_sum[...] = jnp.zeros_like(c_sum)
            t_sum[...] = jnp.zeros_like(t_sum)
        row_sums(*ref, c_sum, t_sum)
        sums_ref[2 * group : 2 * group + 1, :] = jnp.sum(c_sum[...], axis=0, keepdims=True)
        sums_ref[2 * group + 1 : 2 * group + 2, :] = jnp.sum(t_sum[...], axis=0, keepdims=True)

    ff_refs = lambda i: (gff_ref.at[i], ff_old.at[i], ff_real, ff_new.at[i])
    oq_refs = lambda at: (goq_ref.at[at], oq_old.at[at], None, oq_new.at[at])

    def work(s):
        for i in range(3):

            @pl.when(s == i)
            def _():
                for load in loads(i):
                    load.wait()
                gff_ref[i, :, own] = chip_sum(ff_own[i], ff_slots.at[i])
                join(i).start()

        @pl.when(s == 0)
        def _():
            for load in loads(3):
                load.wait()
            goq_ref[out_rows, own] = chip_sum(oq_mine_ref[out_rows, :], out_slots)
            join(4).start()

        @pl.when(s == 3)
        def _():
            join(0).wait()
            sums(3, ff_refs(0))

        @pl.when(s == 4)
        def _():
            for k in range(n_x - 1):
                oq_copy(k).wait()
            goq_ref[qkv_rows, own] = chip_sum(oq_mine_ref[qkv_rows, :], qkv_land)
            join(3).start()

        @pl.when(s == 5)
        def _():
            join(1).wait()
            sums(1, ff_refs(1))

        @pl.when(s == 6)
        def _():
            join(2).wait()
            sums(1, ff_refs(2), first=False)
            writes[1].start()
            join(4).wait()
            sums(2, oq_refs(out_rows))
            join(3).wait()
            sums(0, oq_refs(qkv_rows))
            writes[0].start()
            down_new = ff_new[0] * ff_real[: ff_new.shape[1], :]
            for i, new in enumerate((oq_new[out_rows, :], down_new)):
                total = jnp.sum(new, axis=0, keepdims=True)
                totals_ref[i : i + 1, :] = jnp.broadcast_to(total, (1, totals_ref.shape[1]))

    def finish(at, total):
        d_rows, sums_one = layer_norm_back(x_ref[at, :].astype(F32), ln_ref[0:1, :], total)
        out_ref[at, :] = (d_hidden_ref[at, :] + d_rows).astype(BF)
        ln_sum[...] += sums_one

    ring_scatter(n, land, send_sem, recv_sem, sides, term_buf, term, work, finish)
    for write in writes:
        write.wait()


def last_scatter(
    n, n_x, d_qkv, w, oq_mine, oq_old, ff_old, ff_real, ff_mine, down_slots, gu_slots, out_slots,
    x, d_hidden, ln_params,
):
    width, cols = w.shape[1:]
    rows = d_qkv.shape[0] // n
    half = width // 2
    ff_rows = ff_mine.shape[1]
    buf, sems = ring_scratch(n, rows, width, PIECES)
    return pl.pallas_call(
        functools.partial(last_kernel, n, n_x),
        in_specs=[VMEM_SPEC] * 9 + [ANY_SPEC] * 4,
        out_specs=[VMEM_SPEC] + [ANY_SPEC] * 2 + [VMEM_SPEC] * 5,
        out_shape=[
            jax.ShapeDtypeStruct((rows, width), BF),
            jax.ShapeDtypeStruct((4 * cols, width), BF),
            jax.ShapeDtypeStruct((3, ff_rows, width), BF),
            jax.ShapeDtypeStruct(oq_old.shape, F32),
            jax.ShapeDtypeStruct(ff_old.shape, F32),
            jax.ShapeDtypeStruct((8, width), F32),
            jax.ShapeDtypeStruct((2, width), F32),
            jax.ShapeDtypeStruct((8, 128), F32),
        ],
        scratch_shapes=buf
        + [
            pltpu.VMEM((rows, width), F32),
            pltpu.VMEM((4 * cols, width), BF),
            pltpu.VMEM((3, ff_rows, width), BF),
            pltpu.VMEM((n_x, 3 * cols, half), BF),
            pltpu.VMEM((n_x, cols, half), BF),
            pltpu.VMEM((3, ff_rows, half), BF),
            pltpu.VMEM((3, n_x, ff_rows, half), BF),
            pltpu.VMEM((8, width), F32),
            pltpu.VMEM((8, width), F32),
        ]
        + sems
        + [
            pltpu.SemaphoreType.DMA((2, n_x - 1)),
            pltpu.SemaphoreType.DMA((2, 4)),
            pltpu.SemaphoreType.DMA((2, 5)),
            pltpu.SemaphoreType.DMA((2,)),
        ],
        compiler_params=pltpu.CompilerParams(
            collective_id=2, has_side_effects=True, vmem_limit_bytes=62 << 20
        ),
        cost_estimate=cost(90),
    )(
        d_qkv, w, oq_mine, oq_old, ff_old, ff_real, x, d_hidden, ln_params,
        ff_mine, down_slots, gu_slots, out_slots,
    )


def norm_stats(rows):
    mean_row = jnp.mean(rows, axis=-1, keepdims=True)
    centered = rows - mean_row
    variance = jnp.mean(centered * centered, axis=-1, keepdims=True)
    scale = lax.rsqrt(variance + ln_eps)
    return centered * scale, scale


def layer_norm(rows, gain, shift):
    return norm_stats(rows)[0] * gain + shift


def layer_norm_back(rows, gain, e):
    n, scale = norm_stats(rows)
    eg = e * gain
    dv = scale * (
        eg - jnp.mean(eg, axis=-1, keepdims=True) - n * jnp.mean(eg * n, axis=-1, keepdims=True)
    )
    sums = [jnp.sum(x, axis=0, keepdims=True) for x in (e * n, e)]
    return dv, jnp.concatenate(sums, axis=0)


def seen_mask(thr_ref, q0, shape):
    thr = thr_ref[: shape[0], :]
    thr = jnp.concatenate([thr] * (shape[1] // thr.shape[1]), axis=1)
    q_pos = (q0 + lax.broadcasted_iota(jnp.int32, shape, 1)).astype(F32)
    return q_pos >= thr


def q_blocks():
    return [(q0, max(PREFIX_MAX, q0 + Q_BLOCK)) for q0 in range(0, SLOT, Q_BLOCK)]


def to_order(places, src_ref, columns, dst_ref):
    half = SLOT // len(places)
    for j, start in enumerate(places):
        place = pl.ds(pl.multiple_of(start, half), half)
        dst_ref[j * half : (j + 1) * half, :] = src_ref[place, columns]


def from_order(places, q0, value, dst_ref, columns):
    half = SLOT // len(places)
    for i in range(value.shape[0] // half):
        place = pl.ds(pl.multiple_of(places[q0 // half + i], half), half)
        dst_ref[place, columns] = value[i * half : (i + 1) * half, :]


def attn_forward_head(places, thr_ref, lse_ref, q_ref, k_ref, v_ref, o_ref, columns):
    c = HD**-0.5 * LOG2E
    for q0, klim in q_blocks():
        raw = dot(k_ref[:klim, :], q_ref[q0 : q0 + Q_BLOCK, :], ((1,), (1,)))
        raw = jnp.where(seen_mask(thr_ref, q0, raw.shape), raw, masked_score)
        top = jnp.max(raw, axis=0, keepdims=True)
        p = jnp.exp2((raw - top) * c)
        total = jnp.sum(p, axis=0, keepdims=True)
        out = dot(v_ref[:klim, :], p.astype(BF), ((0,), (0,))) / total
        from_order(places, q0, out.T.astype(BF), o_ref, columns)
        lse_ref[:, q0 : q0 + Q_BLOCK] = top * c + jnp.log2(total)


def attn_backward_head(
    turn, places, thr_ref, lse_ref, q_ref, k_ref, v_ref, do_ref, dk_sum, dv_sum, d_ref, columns
):
    scale = HD**-0.5
    blocks = q_blocks()
    if turn == 0:
        dk_sum[...] = jnp.zeros_like(dk_sum)
        dv_sum[...] = jnp.zeros_like(dv_sum)
    for q0, klim in (blocks[-1:] + blocks[:1], blocks[1:-1])[turn]:
        rows = slice(q0, q0 + Q_BLOCK)
        k, q, do = k_ref[:klim, :], q_ref[rows, :], do_ref[rows, :]
        raw = dot(k, q, ((1,), (1,)))
        p = jnp.exp2(raw * (scale * LOG2E) - lse_ref[:, rows])
        p = jnp.where(seen_mask(thr_ref, q0, raw.shape), p, 0.0)
        dv_sum[:klim, :] += dot(p.astype(BF), do, ((1,), (0,)))
        dp = dot(v_ref[:klim, :], do, ((1,), (1,)))
        delta = jnp.sum(p * dp, axis=0, keepdims=True)
        ds = (p * (dp - delta) * scale).astype(BF)
        dk_sum[:klim, :] += dot(ds, q, ((1,), (0,)))
        dq = dot(k, ds, ((0,), (0,))).T.astype(BF)
        from_order(places, q0, dq, d_ref, columns(0))
    if turn == 1:
        from_order(places, 0, dk_sum[...].astype(BF), d_ref, columns(1))
        from_order(places, 0, dv_sum[...].astype(BF), d_ref, columns(2))


def step_rate(update_sq, weight_sq, n_real):
    update_rms = jnp.sqrt(update_sq / n_real)
    weight_rms = jnp.sqrt(weight_sq / n_real)
    return rate_base * jnp.maximum(eps_two, weight_rms) / jnp.maximum(1.0, update_rms / clip_bound)


def results_kernel(
    counts, factor_ref, goq_qkv, goq_out, gff_down, gff_gate, gff_up,
    w_qkv, w_out, w_down, w_gate, w_up, r_qkv, r_out, r_down, r_gate, r_up, *refs,
):
    n_small = (len(refs) - 8) // 2
    small, small_out = refs[:n_small], refs[n_small + 8 :]
    qkv_grad, qkv_new, out_grad, out_new, gu_grad, gu_new, down_grad, down_new = refs[n_small:][:8]
    t = pl.program_id(0)
    n_gu, n_qkv, n_down, n_out = counts

    def after(grad, weight, row, factor):
        return weight.astype(F32) - grad * (lax.rsqrt(row) * factor)

    @pl.when(t == 0)
    def _():
        for src, dst in zip(small, small_out):
            dst[...] = src[...]

    @pl.when(t < n_gu)
    def _():
        factor = factor_ref[1:2, :]
        for i, (g, w, r) in enumerate(((gff_gate, w_gate, r_gate), (gff_up, w_up, r_up))):
            grad = g[0].astype(F32)
            gu_grad[:, i, :] = grad
            gu_new[:, i, :] = after(grad, w[...], r[0], factor)

    start = n_gu
    @pl.when((t >= start) & (t < start + n_qkv))
    def _():
        block = goq_qkv.shape[1]
        at = lax.rem(t - n_gu, factor_ref.shape[1] // block) * block
        factor = factor_ref[0:1, pl.ds(pl.multiple_of(at, block), block)]
        grad = goq_qkv[...].astype(F32).T
        qkv_grad[0] = grad
        down = jnp.broadcast_to(factor, (128, block)).T[:, 0:1]
        along = jnp.broadcast_to(lax.rsqrt(r_qkv[...]), (grad.shape[1], 128)).T[0:1, :]
        qkv_new[0] = w_qkv[0].astype(F32) - grad * (down * along)

    start = n_gu + n_qkv

    @pl.when((t >= start) & (t < start + n_down))
    def _():
        grad = gff_down[0].astype(F32)
        down_grad[...] = grad
        down_new[...] = after(grad, w_down[...], r_down[0], factor_ref[3:4, :])

    @pl.when(t >= n_gu + n_qkv + n_down)
    def _():
        grad = goq_out[...].astype(F32)
        out_grad[...] = grad
        out_new[...] = after(grad, w_out[...], r_out[...], factor_ref[2:3, :])


def results(ff, factors, goq, gff, w_qkv, w_out, w_down, w_gu, oq_new, ff_new, small):
    kinds, width, cols = w_qkv.shape
    rows, wide, high = 192, width, min(256, cols)
    counts = (-(-ff // rows), kinds * width // wide, -(-ff // rows), cols // high)
    starts = [sum(counts[:i]) for i in range(4)]
    per_kind = width // wide
    place = lambda part: lambda t: jnp.clip(t - starts[part], 0, counts[part] - 1)
    gu, qkv, down, out = (place(part) for part in range(4))
    shift = w_gu.shape[0] // 2 // rows
    third = lambda k, part, last: pl.BlockSpec((1, rows, last), lambda t: (k, part(t), 0))
    by_kind = lambda t: (qkv(t) // per_kind, lax.rem(qkv(t), per_kind), 0)
    out_at = 3 * cols // high
    qkv_spec = pl.BlockSpec((1, wide, cols), by_kind)
    out_spec = pl.BlockSpec((high, width), lambda t: (out(t), 0))
    gu_spec = pl.BlockSpec((rows, 2, width), lambda t: (gu(t), 0, 0))
    down_spec = pl.BlockSpec((rows, width), lambda t: (down(t), 0))
    shape = lambda *dims: jax.ShapeDtypeStruct(dims, F32)
    whole = [pl.BlockSpec(x.shape, lambda t: (0, 0)) for x in small]
    return pl.pallas_call(
        functools.partial(results_kernel, counts),
        grid=(sum(counts),),
        in_specs=[
            pl.BlockSpec(factors.shape, lambda t: (0, 0)),
            pl.BlockSpec((cols, wide), lambda t: by_kind(t)[:2]),
            pl.BlockSpec((high, width), lambda t: (out_at + out(t), 0)),
            third(0, down, width),
            third(1, gu, width),
            third(2, gu, width),
            qkv_spec,
            out_spec,
            down_spec,
            pl.BlockSpec((rows, width), lambda t: (gu(t), 0)),
            pl.BlockSpec((rows, width), lambda t: (gu(t) + shift, 0)),
            pl.BlockSpec((cols, 1), lambda t: (by_kind(t)[0], 0)),
            pl.BlockSpec((high, 1), lambda t: (out_at + out(t), 0)),
            third(0, down, 1),
            third(1, gu, 1),
            third(2, gu, 1),
        ]
        + whole,
        out_specs=[qkv_spec, qkv_spec, out_spec, out_spec, gu_spec, gu_spec, down_spec, down_spec]
        + whole,
        out_shape=[shape(kinds, width, cols)] * 2
        + [shape(cols, width)] * 2
        + [shape(ff, 2, width)] * 2
        + [shape(ff, width)] * 2
        + [shape(*x.shape) for x in small],
        compiler_params=pltpu.CompilerParams(vmem_limit_bytes=56 << 20),
        cost_estimate=cost(28),
    )(
        factors, goq, goq, gff, gff, gff, w_qkv, w_out, w_down, w_gu, w_gu,
        oq_new, oq_new, ff_new, ff_new, ff_new, *small,
    )


def exchange_kernel(
    n_dp, n, cells, one_ref, two_ref, sums_ref, totals_ref, squares_ref, old_ref, ln_ref, second_ref,
    factor_ref, qkv_row, gu_row, out_col, down_col, ln_tot, ln_second, ln_new,
    x_ref, o_ref, dp_buf, rows, part_buf, total, whole, sems,
):
    me_d, me = lax.axis_index("dp"), lax.axis_index("tensor")
    width = x_ref.shape[1] // n
    columns = lambda t: pl.ds(pl.multiple_of(t * width, width), width)
    dp_peers = [(k - 1, lax.rem(me_d + k, n_dp)) for k in range(1, n_dp)]
    peers = [(k - 1, lax.rem(me + k, n)) for k in range(1, n)]
    barrier = pltpu.get_barrier_semaphore()
    for _, d in dp_peers:
        pl.semaphore_signal(barrier, inc=1, device_id={"dp": d}, device_id_type=pl.DeviceIdType.MESH)
    for _, t in peers:
        pl.semaphore_signal(barrier, inc=1, device_id={"tensor": t}, device_id_type=pl.DeviceIdType.MESH)
    pl.semaphore_wait(barrier, n_dp + n - 2)

    def push(stage, src, dst, k, device):
        copy = pltpu.make_async_remote_copy(
            src_ref=src, dst_ref=dst, send_sem=sems.at[0, stage, k], recv_sem=sems.at[1, stage, k],
            device_id=device, device_id_type=pl.DeviceIdType.MESH,
        )
        copy.start()
        return copy

    x_ref[0:2, :] = one_ref[...]
    x_ref[2:4, :] = two_ref[...]
    x_ref[4:8, :] = jnp.zeros((4, x_ref.shape[1]), F32)
    lane = lax.broadcasted_iota(jnp.int32, (1, 128), 1)
    add_up = lambda v: jnp.sum(jnp.sum(v, axis=0, keepdims=True), axis=1, keepdims=True)
    scalars = [add_up(squares_ref[i]) for i in range(4)] + [totals_ref[i : i + 1, 0:1] for i in range(2)]
    x_ref[4:5, 0:128] = sum(jnp.where(lane == i, v, 0.0) for i, v in enumerate(scalars)) / n_dp
    x_ref[8:16, :] = sums_ref[...]
    first = [push(0, x_ref.at[pl.ds(0, 8)], dp_buf.at[me_d], k, {"dp": d}) for k, d in dp_peers]
    rows[...] = x_ref[...]
    dp_buf[me_d] = x_ref[0:8, :]
    for copy in first:
        copy.wait()
    rows[0:8, :] = sum(dp_buf[d] for d in range(n_dp))
    second = [push(1, rows.at[:, columns(t)], part_buf.at[me], k, {"tensor": t}) for k, t in peers]
    part_buf[me] = rows[:, columns(me)]
    for copy in second:
        copy.wait()
    total[...] = sum(part_buf[t] for t in range(n))
    third = [push(2, total, whole.at[me], k, {"tensor": t}) for k, t in peers]
    whole[me] = total[...]
    for copy in third:
        copy.wait()
    for t in range(n):
        o_ref[:, t * width : (t + 1) * width] = whole[t]

    columns_all = x_ref.shape[1]
    blend = lambda old, new: DECAY * old + (1.0 - DECAY) * new
    mean_of = lambda v: jnp.sum(v, axis=1, keepdims=True) / columns_all
    at = lambda i: o_ref[i : i + 1, :]
    scalar = lambda i: o_ref[4:5, i : i + 1]
    news = (qkv_row, gu_row, out_col, down_col)
    for i, (new_ref, (count, real, by_row)) in enumerate(zip(news, cells)):
        new = blend(old_ref[i : i + 1, :], at(8 + 2 * i) / count)
        new_ref[...] = new
        mean = mean_of(new) if by_row else scalar(2 + i) / count
        update_sq = jnp.sum(at(9 + 2 * i) / new, axis=1, keepdims=True) * mean
        rate = step_rate(update_sq, scalar(i), real)
        factor_ref[i : i + 1, :] = lax.rsqrt(new) * (rate * jnp.sqrt(mean))
    grad, weight = o_ref[0:4, :], ln_ref[...]
    second = blend(second_ref[...], grad * grad + eps_one)
    update = grad * lax.rsqrt(second)
    update_rms = jnp.sqrt(mean_of(update * update))
    weight_rms = jnp.sqrt(mean_of(weight * weight))
    ln_tot[...] = grad
    ln_second[...] = second
    ln_new[...] = weight - rate_base * jnp.maximum(eps_two, weight_rms) * update / jnp.maximum(
        1.0, update_rms / clip_bound
    )


def exchange(n_dp, n, cells, ln_one, ln_two, sums, totals, squares, old, ln_params, ln_second):
    height, width = 16, sums.shape[1]
    slots = pltpu.VMEM((n, height, width // n), F32)
    shape = lambda *dims: jax.ShapeDtypeStruct(dims, F32)
    return pl.pallas_call(
        functools.partial(exchange_kernel, n_dp, n, cells),
        out_shape=[shape(4, width)] + [shape(1, width)] * 4 + [shape(4, width)] * 3,
        in_specs=[VMEM_SPEC] * 8,
        out_specs=[VMEM_SPEC] * 8,
        scratch_shapes=[
            pltpu.VMEM((height, width), F32),
            pltpu.VMEM((height, width), F32),
            pltpu.VMEM((n_dp, 8, width), F32),
            pltpu.VMEM((height, width), F32),
            slots,
            pltpu.VMEM((height, width // n), F32),
            slots,
            pltpu.SemaphoreType.DMA((2, 3, max(n, n_dp) - 1)),
        ],
        compiler_params=pltpu.CompilerParams(collective_id=0, has_side_effects=True),
        cost_estimate=cost(18),
    )(ln_one, ln_two, sums, totals, squares, old, ln_params, ln_second)


def on_device(
    layer_in,
    cotangent,
    lengths,
    prefix,
    pad_mask,
    clusters,
    qkv_w,
    out_w,
    gate_up_w,
    down_w,
    ln_params,
    qkv_row,
    qkv_col,
    out_row,
    out_col,
    gu_row,
    gu_col,
    down_row,
    down_col,
    ln_second,
):
    n_data = lax.axis_size("dp")
    n_tensor = lax.axis_size("tensor")
    tensor_rank = lax.axis_index("tensor")
    data_rank = lax.axis_index("dp")
    rows_dev, width = layer_in.shape
    cols_dev = qkv_w.shape[2]
    heads_dev = cols_dev // HD
    ff_dev = gate_up_w.shape[2]
    ff_pad = -(-ff_dev // 384) * 384
    n_clusters = max(2, n_data // 2)
    seq_length = lengths[0]
    seq_prefix = prefix[0]

    onehot = (clusters[:, None] == jnp.arange(n_clusters, dtype=jnp.int32)[None, :]).astype(F32)
    counts = jnp.sum(onehot, axis=0)
    own_row = jnp.sum(
        jnp.where((jnp.arange(n_data, dtype=jnp.int32) == data_rank)[:, None], onehot, 0.0), axis=0
    )
    seq_weight = jnp.sum(own_row / jnp.maximum(counts, 1.0))
    own_pos = tensor_rank * rows_dev + jnp.arange(rows_dev, dtype=jnp.int32)
    live_rows = ((own_pos < seq_length) & (pad_mask == 1)).astype(F32)
    row_weight = (live_rows * seq_weight)[:, None]

    key_live = (own_pos == 0) | (own_pos < seq_length) & (pad_mask == 1)
    seen_from = jnp.where(key_live, jnp.where(own_pos < seq_prefix, 0, own_pos), 2 * SLOT)
    seen = jnp.broadcast_to(seen_from.astype(F32)[None], (8, rows_dev))

    col_index = tensor_rank * ff_dev + jnp.arange(ff_pad, dtype=jnp.int32)
    ff_real = ((col_index < FF) & (jnp.arange(ff_pad) < ff_dev)).astype(F32)
    ff_mask = ff_real[:ff_dev]

    act_one_all, qkv, seen_all, w_gu = first_gather(
        n_tensor, layer_in, seen, ln_params, jnp.transpose(qkv_w, (1, 0, 2)),
        jnp.transpose(gate_up_w, (2, 1, 0)),
    )

    pad = ((0, ff_pad - ff_dev), (0, 0))
    w_down = jnp.pad(down_w, pad)
    real_column = ff_real[:, None]
    qkv_t = jnp.transpose(qkv_w, (1, 0, 2))

    grad_all, context, lse, squares, thr = grad_gather(
        n_tensor, cotangent, row_weight, qkv, seen_all, real_column, qkv_t, w_gu, out_w, w_down
    )
    hidden_own, norm_two = mix_scatter(n_tensor, context, out_w, layer_in, ln_params)

    act_two_all, inner_all, d_gu_all, d_hidden, d_hidden_low, ln_two_part = both_ways(
        n_tensor, norm_two, w_gu, w_down, ff_real[None, :], hidden_own, cotangent, row_weight,
        ln_params, grad_all,
    )

    n_x = n_data // 2
    d_context, out_part, ff_mine, down_slots = back_gather(
        n_tensor, n_x, ff_dev, d_hidden_low, out_w, context,
        inner_all, d_gu_all, grad_all, act_two_all,
    )

    layer_out, d_qkv, gu_slots, out_slots, oq_mine = ffn_scatter(
        n_tensor, n_x, inner_all, w_down, hidden_own, thr, qkv, d_context, lse,
        out_part, act_one_all, ff_mine,
    )

    ff_rows = ff_mine.shape[1]
    more = ((0, 0), (0, ff_rows - ff_dev))
    oq_old = jnp.concatenate([qkv_col.reshape(-1), out_row])[:, None]
    ff_old = jnp.pad(jnp.concatenate([down_row[None], gu_col]), more, constant_values=1.0)[:, :, None]
    input_grad, goq, gff, oq_new, ff_new, sums, ln_one_part, totals = last_scatter(
        n_tensor, n_x, d_qkv, qkv_t, oq_mine, oq_old, ff_old, real_column,
        ff_mine, down_slots, gu_slots, out_slots, layer_in, d_hidden, ln_params,
    )
    qkv_col_new, out_row_new = oq_new[: 3 * cols_dev, 0], oq_new[3 * cols_dev :, 0]
    down_row_new, gu_col_new = ff_new[0, :ff_dev, 0], ff_new[1:, :ff_dev, 0]

    rows_all = cols_dev * n_tensor
    cells = (
        (3 * rows_all, width * 3 * rows_all, True),
        (2 * FF, width * 2 * FF, True),
        (rows_all, rows_all * width, False),
        (FF, FF * width, False),
    )
    factors, *small = exchange(
        n_data, n_tensor, cells, ln_one_part, ln_two_part, sums, totals, squares,
        jnp.stack([qkv_row, gu_row, out_col, down_col]), ln_params, ln_second,
    )
    qkv_grad, qkv_new, out_sum, out_new, gu_grad, gu_new, down_sum, down_new, *small = results(
        ff_dev, factors, goq, gff, qkv_t, out_w, w_down, w_gu, oq_new, ff_new, small
    )
    qkv_row_new, gu_row_new, out_col_new, down_col_new, ln_tot, ln_second_new, ln_new = small
    qkv_back = lambda x: jnp.transpose(x, (1, 0, 2))
    return (
        layer_out,
        input_grad,
        qkv_back(qkv_grad),
        qkv_back(qkv_new),
        qkv_row_new[0],
        qkv_col_new.reshape(3, -1),
        out_sum,
        out_new,
        out_row_new,
        out_col_new[0],
        jnp.transpose(gu_grad, (2, 1, 0)),
        jnp.transpose(gu_new, (2, 1, 0)),
        gu_row_new[0],
        gu_col_new,
        down_sum,
        down_new,
        down_row_new,
        down_col_new[0],
        ln_tot,
        ln_second_new,
        ln_new,
    )


def solution(mesh):
    in_specs = (
        P(("dp", "tensor"), None),
        P(("dp", "tensor"), None),
        P("dp"),
        P("dp"),
        P(("dp", "tensor")),
        P(),
        P(None, None, "tensor"),
        P("tensor", None),
        P(None, None, "tensor"),
        P("tensor", None),
        P(),
        P(),
        P(None, "tensor"),
        P("tensor"),
        P(),
        P(),
        P(None, "tensor"),
        P("tensor"),
        P(),
        P(),
    )
    out_specs = (
        P(("dp", "tensor"), None),
        P(("dp", "tensor"), None),
        P(None, None, "tensor"),
        P(None, None, "tensor"),
        P(),
        P(None, "tensor"),
        P("tensor", None),
        P("tensor", None),
        P("tensor"),
        P(),
        P(None, None, "tensor"),
        P(None, None, "tensor"),
        P(),
        P(None, "tensor"),
        P("tensor", None),
        P("tensor", None),
        P("tensor"),
        P(),
        P(),
        P(),
        P(),
    )
    return jax.shard_map(
        on_device, mesh=mesh, in_specs=in_specs, out_specs=out_specs, check_vma=False
    )
```
